32 devices in a mesh: ta: 4 (over x, core), ha: 4 (over z), wa: 2 (over y).
Axes of the slice: x: 2, y: 2, z: 4, core: 2. Of those that a mesh axis runs over, the one named last changes fastest.
Arguments:
- queries: bfloat16 [8, 64, 16, 2048], P('ta', 'ha', 'wa'), may hold values from -16 to 16
- keyvals: bfloat16 [2, 8, 64, 16, 2048], P(None, 'ta', 'ha', 'wa'), may hold values from -6 to 6
- far_frames: int32 [8, 8, 2, 2], P('ta', 'ha', 'wa'), may hold values from 0 to 7, as said below
Outputs:
- attended: bfloat16 [8, 64, 16, 2048], P('ta', 'ha', 'wa')
The draws below stay inside these ranges and needn't reach their ends.
Inputs may be any that keep to these rules, and one draw needn't show every extreme that they name: far_frames[t, a, b, :] are 2 different frames, each at a distance of 2 or more from t modulo 8.
All inputs are finite; a program needn't handle non-finite values.
Results may differ from the reference program's by a relative error of at most 0.0049.
Values may be sent and summed in bfloat16 or wider, within the bound.
No kernel may reach another device: no remote copies, remote signals or barrier semaphores. Data moves between devices by JAX's collectives and lax.ppermute only.
A program may use at most 192 MiB of HBM per device.

```python
import jax
import jax.numpy as jnp
from jax import lax

TILE = 8
HEADS = 16
HD = 128
NFAR = 2
NF = 8
NH = 64
NW = 16


def base_keys(key):
    sample_key = jax.random.fold_in(key, 7)
    sampled = jnp.clip(jax.random.normal(sample_key, (NF, NH, NW, HEADS * HD), jnp.float32), -6.0, 6.0)
    return sampled


def draw_keyvals(key, part):
    sampled = base_keys(key)
    value_key = jax.random.fold_in(key, 8)
    key_part = sampled
    value_part = jnp.clip(jax.random.normal(value_key, (NF, NH, NW, HEADS * HD), jnp.float32), -6.0, 6.0)
    return jnp.stack([key_part, value_part]).astype(jnp.bfloat16)


def draw_queries(key, part):
    query_key = jax.random.fold_in(key, 9)
    result = 2.5 * jnp.clip(jax.random.normal(query_key, (NF, NH, NW, HEADS * HD), jnp.float32), -6.0, 6.0)
    return result.astype(jnp.bfloat16)


def draw_far_frames(key, part):
    shape_tiles = (NF, NH // TILE, NW // TILE)
    first_step = 2 + jax.random.randint(jax.random.fold_in(key, 21), shape_tiles, 0, NF - 3)
    extra_step = jax.random.randint(jax.random.fold_in(key, 22), shape_tiles, 1, NF - 3)
    second_step = 2 + (first_step - 2 + extra_step) % (NF - 3)
    frame_ids = jnp.arange(NF, dtype=jnp.int32)[:, None, None]
    return jnp.stack([(frame_ids + first_step) % NF, (frame_ids + second_step) % NF], axis=-1).astype(jnp.int32)


def setup_inputs(seed: int = 0) -> dict:
    splits = jax.random.split(jax.random.key(seed), 4)
    return {
        "queries": draw_queries(jax.random.fold_in(splits[3], 71), 0),
        "keyvals": draw_keyvals(jax.random.fold_in(splits[3], 71), 0),
        "far_frames": draw_far_frames(jax.random.fold_in(splits[3], 71), 0),
    }


def start_at(*values):
    return tuple(jnp.asarray(value).astype(jnp.int32) for value in values)


def reference(queries, keyvals, far_frames):
    tile_rows = NH // TILE
    tile_cols = NW // TILE
    features = HEADS * HD
    scaling = HD ** -0.5
    padded = jnp.pad(keyvals, ((0, 0), (0, 0), (TILE, TILE), (TILE, TILE), (0, 0)))
    offsets = jnp.arange(3 * TILE, dtype=jnp.int32) // TILE - 1

    def attend(tile_index):
        frame_at = tile_index // (tile_rows * tile_cols)
        row_at = (tile_index // tile_cols) % tile_rows
        column = tile_index % tile_cols
        query_rows = lax.dynamic_slice(queries, start_at(frame_at, row_at * TILE, column * TILE, 0), (1, TILE, TILE, features)).reshape(TILE * TILE, HEADS, HD)
        window = jnp.concatenate([lax.dynamic_slice(padded, start_at(0, (frame_at + time_step) % NF, row_at * TILE, column * TILE, 0), (2, 1, 3 * TILE, 3 * TILE, features)) for time_step in (-1, 0, 1)], axis=1)
        distant = jnp.concatenate([lax.dynamic_slice(keyvals, start_at(0, far_frames[frame_at, row_at, column, far_slot], row_at * TILE, column * TILE, 0), (2, 1, TILE, TILE, features)) for far_slot in range(NFAR)], axis=1)
        key_rows = jnp.concatenate([window[0].reshape(-1, HEADS, HD), distant[0].reshape(-1, HEADS, HD)], axis=0)
        values = jnp.concatenate([window[1].reshape(-1, HEADS, HD), distant[1].reshape(-1, HEADS, HD)], axis=0)
        row_valid = (row_at + offsets >= 0) & (row_at + offsets < tile_rows)
        column_valid = (column + offsets >= 0) & (column + offsets < tile_cols)
        inside = jnp.broadcast_to(row_valid[None, :, None] & column_valid[None, None, :], (3, 3 * TILE, 3 * TILE)).reshape(-1)
        inside = jnp.concatenate([inside, jnp.ones((NFAR * TILE * TILE,), dtype=bool)])
        scores = jnp.einsum("qhd,khd->hqk", query_rows.astype(jnp.float32), key_rows.astype(jnp.float32)) * scaling
        scores = jnp.where(inside[None, None, :], scores, jnp.float32(-1e30))
        peak_score = jnp.max(scores, axis=-1, keepdims=True)
        exponent = jnp.exp(scores - peak_score)
        denominator = jnp.sum(exponent, axis=-1, keepdims=True)
        normed = (exponent / denominator).astype(jnp.bfloat16)
        blended = jnp.einsum("hqk,khd->qhd", normed.astype(jnp.float32), values.astype(jnp.float32))
        return blended.reshape(TILE, TILE, features).astype(jnp.bfloat16)

    tile_outputs = lax.map(attend, jnp.arange(NF * tile_rows * tile_cols, dtype=jnp.int32))
    tile_outputs = tile_outputs.reshape(NF, tile_rows, tile_cols, TILE, TILE, features)
    return tile_outputs.transpose(0, 1, 3, 2, 4, 5).reshape(NF, NH, NW, features)
```

```python
import functools

import jax
import jax.numpy as jnp
from jax import lax
from jax.experimental import pallas as pl
from jax.experimental.pallas import tpu as pltpu
from jax.sharding import PartitionSpec as P

TILE = 8
HEADS = 16
HD = 128
NFAR = 2
CHUNKS = 2
SPOT = TILE * TILE
NEGATIVE = -1e30
EXP_SCALE = HD ** (-0.5) * 1.4426950408889634


def contract_last(left, right):
    return lax.dot_general(left, right, (((1,), (1,)), ((), ())), preferred_element_type=jnp.float32)


def attention_kernel(frames, heads, own, first, far_ref, valid_ref, kv_ref, top_ref, bottom_ref, q_ref, out_ref):
    groups, columns = kv_ref.shape[0], kv_ref.shape[1]
    total = groups * frames
    ones = jnp.ones((2 * columns * SPOT, HD), jnp.bfloat16)

    def with_ones(values):
        return jnp.concatenate([values, ones[: values.shape[0]]], axis=1)

    def attend(t, h):
        group, frame = t // frames, t % frames
        queries = [
            jnp.concatenate([q_ref[group, b, h, frame, a * SPOT : (a + 1) * SPOT] for b in range(own)], axis=0)
            for a in range(2)
        ]
        both = jnp.concatenate(queries, axis=0)
        near = [((t + step + total) % total) for step in (-1, 0, 1)]
        near = [(f // frames, f % frames) for f in near]
        split = own == columns
        pieces = [list(range(columns))] if split else [[e] for e in range(columns)]

        def column_valid(piece):
            if split or 0 < piece[0] < columns - 1:
                return None
            return valid_ref[2 if piece[0] == 0 else 3] > 0

        def gather(ref, kind, spot, piece):
            return jnp.concatenate([ref[spot[0], e, h, kind, spot[1]] for e in piece], axis=0)

        blocks = [[], []]
        for spot in near:
            for piece in pieces:
                valid = column_valid(piece)
                scores = contract_last(both, gather(kv_ref, 0, spot, piece))
                values = with_ones(gather(kv_ref, 1, spot, piece))
                half = own * SPOT
                blocks[0].append((valid, scores[:half], values))
                blocks[1].append((valid, scores[half:], values))
        for a, ref in ((0, top_ref), (1, bottom_ref)):
            row_valid = valid_ref[a] > 0
            for spot in near:
                for piece in pieces:
                    valid = column_valid(piece)
                    valid = row_valid if valid is None else jnp.logical_and(valid, row_valid)
                    scores = contract_last(queries[a], gather(ref, 0, spot, piece))
                    blocks[a].append((valid, scores, with_ones(gather(ref, 1, spot, piece))))
        for a in range(2):
            far_scores, far_values = [], []
            for b in range(own):
                keys, values = [], []
                for j in range(NFAR):
                    f = far_ref[((t * 2 + a) * own + b) * NFAR + j]
                    tokens = pl.ds(a * SPOT, SPOT)
                    keys.append(kv_ref[f // frames, first + b, h, 0, f % frames, tokens])
                    values.append(kv_ref[f // frames, first + b, h, 1, f % frames, tokens])
                far_scores.append(contract_last(queries[a][b * SPOT : (b + 1) * SPOT], jnp.concatenate(keys, axis=0)))
                far_values.append(with_ones(jnp.concatenate(values, axis=0)))
            far_all = jnp.concatenate(far_scores, axis=0)
            peak = jnp.max(far_all, axis=-1, keepdims=True)
            for valid, scores, _ in blocks[a]:
                block_peak = jnp.max(scores, axis=-1, keepdims=True)
                if valid is not None:
                    block_peak = jnp.where(valid, block_peak, NEGATIVE)
                peak = jnp.maximum(peak, block_peak)
            weights = jnp.exp2((far_all - peak) * EXP_SCALE).astype(jnp.bfloat16)
            summed = jnp.concatenate(
                [
                    jnp.dot(weights[b * SPOT : (b + 1) * SPOT], far_values[b], preferred_element_type=jnp.float32)
                    for b in range(own)
                ],
                axis=0,
            )
            for valid, scores, values in blocks[a]:
                shift = peak if valid is None else jnp.where(valid, peak, -NEGATIVE)
                weights = jnp.exp2((scores - shift) * EXP_SCALE).astype(jnp.bfloat16)
                summed = summed + jnp.dot(weights, values, preferred_element_type=jnp.float32)
            result = (summed[:, :HD] / summed[:, HD:]).astype(out_ref.dtype)
            for b in range(own):
                out_ref[group, b, h, frame, a * SPOT : (a + 1) * SPOT] = result[b * SPOT : (b + 1) * SPOT]

    def step(t, carry):
        for h in range(heads):
            attend(t, h)
        return carry

    lax.fori_loop(0, total, step, 0)


def attention(far, valid, kv, top, bottom, q, first):
    groups, own, heads, frames = q.shape[:4]
    body = functools.partial(attention_kernel, frames, heads, own, first)
    keys = 2 * SPOT * own * (9 * kv.shape[1] + NFAR) * SPOT * groups * frames * heads
    in_vmem = pl.BlockSpec(memory_space=pltpu.VMEM)
    in_smem = pl.BlockSpec(memory_space=pltpu.SMEM)
    return pl.pallas_call(
        body,
        out_shape=jax.ShapeDtypeStruct(q.shape, q.dtype),
        in_specs=[in_smem, in_smem, in_vmem, in_vmem, in_vmem, in_vmem],
        out_specs=in_vmem,
        compiler_params=pltpu.CompilerParams(vmem_limit_bytes=40 * 1024 * 1024),
        cost_estimate=pl.CostEstimate(flops=keys * HD * 4, bytes_accessed=4 << 20, transcendentals=keys),
    )(far, valid, kv, top, bottom, q)


def per_device(queries, keyvals, far_frames):
    frames, rows, columns, _ = queries.shape
    tokens = rows * columns
    ta_size, ha_size, wa_size = lax.axis_size("ta"), lax.axis_size("ha"), lax.axis_size("wa")
    paired = wa_size == 2
    group = ("ta", "wa") if paired else ("ta",)
    own = wa_size if paired else 1
    members = ta_size * own
    heads = HEADS // (members * CHUNKS)
    ha, wa = lax.axis_index("ha"), lax.axis_index("wa")
    up = [(i, i + 1) for i in range(ha_size - 1)]
    down = [(i + 1, i) for i in range(ha_size - 1)]
    valid = jnp.stack([ha > 0, ha < ha_size - 1, wa > 0, wa < wa_size - 1]).astype(jnp.int32)

    far = lax.all_gather(far_frames[:, :, 0, :], group, axis=0, tiled=False)
    far = far.reshape(ta_size, own, frames, 2, NFAR).transpose(0, 2, 3, 1, 4).reshape(-1)

    kv_split = keyvals.reshape(2, frames, tokens, members, CHUNKS, heads, HD).transpose(4, 3, 5, 0, 1, 2, 6)
    q_split = queries.reshape(frames, tokens, members, CHUNKS, heads, HD).transpose(3, 2, 4, 0, 1, 5)

    def exchange(value):
        return lax.all_to_all(value, group, split_axis=0, concat_axis=0, tiled=True)

    outs = []
    for chunk in range(CHUNKS):
        kv = exchange(kv_split[chunk]).reshape(ta_size, own, heads, 2, frames, tokens, HD)
        first = 0
        if not paired:
            left = lax.ppermute(kv, "wa", [(i, i + 1) for i in range(wa_size - 1)])
            right = lax.ppermute(kv, "wa", [(i + 1, i) for i in range(wa_size - 1)])
            kv = jnp.concatenate([left, kv, right], axis=1)
            first = 1
        top = lax.ppermute(kv[..., tokens - SPOT :, :], "ha", up)
        bottom = lax.ppermute(kv[..., :SPOT, :], "ha", down)
        q = exchange(q_split[chunk]).reshape(ta_size, own, heads, frames, tokens, HD)
        out = attention(far, valid, kv, top, bottom, q, first)
        outs.append(exchange(out.reshape(members, heads, frames, tokens, HD)))
    merged = jnp.stack(outs).transpose(3, 4, 1, 0, 2, 5)
    return merged.reshape(queries.shape)


def solution(mesh):
    placed = (P("ta", "ha", "wa", None), P(None, "ta", "ha", "wa", None), P("ta", "ha", "wa", None))
    return jax.shard_map(
        per_device, mesh=mesh, in_specs=placed, out_specs=P("ta", "ha", "wa", None), check_vma=False
    )
```

```python
import functools

import jax
import jax.numpy as jnp
from jax import lax
from jax.experimental import pallas as pl
from jax.experimental.pallas import tpu as pltpu
from jax.sharding import PartitionSpec as P

TILE = 8
HEADS = 16
HD = 128
NFAR = 2
SPOT = TILE * TILE
NEGATIVE = -1e30
EXP_SCALE = HD ** (-0.5) * 1.4426950408889634
VMEM_LIMIT = 48 * 1024 * 1024


def contract_last(left, right):
    return lax.dot_general(left, right, (((1,), (1,)), ((), ())), preferred_element_type=jnp.float32)


def with_ones(values):
    return jnp.concatenate([values, jnp.ones_like(values)], axis=1)


def head_lanes(h):
    return pl.ds(pl.multiple_of(h * HD, HD), HD)


def lane_index(rows):
    return lax.broadcasted_iota(jnp.int32, (rows, HD), 1)


def near_kernel(sides, meta_ref, own_ref, ext_ref, top_ref, bottom_ref, ext_top_ref, ext_bottom_ref, *refs):
    q_refs, out_refs, sum_refs = refs[:sides], refs[sides : 2 * sides], refs[2 * sides :]
    frame, ext_at = meta_ref[0], meta_ref[1]
    valid = (meta_ref[2] > 0, meta_ref[3] > 0)
    half = sides * SPOT

    def middle(kind, lanes):
        parts = [own_ref[kind, 0, :, lanes], own_ref[kind, 1, :, lanes], ext_ref[kind, ext_at, :, lanes]]
        return jnp.concatenate(parts, axis=0)

    def halo(a, kind, lanes):
        ref, ext = ((top_ref, ext_top_ref), (bottom_ref, ext_bottom_ref))[a]
        return jnp.concatenate([ref[kind, 0, :, lanes], ref[kind, 1, :, lanes], ext[kind, 0, :, lanes]], axis=0)

    def step(h, carry):
        lanes = head_lanes(h)
        queries = [
            jnp.concatenate([ref[frame, a * SPOT : (a + 1) * SPOT, lanes] for ref in q_refs], axis=0) for a in range(2)
        ]
        middle_scores = contract_last(jnp.concatenate(queries, axis=0), middle(0, lanes))
        middle_values = with_ones(middle(1, lanes))
        for a in range(2):
            near = middle_scores[a * half : (a + 1) * half]
            edge = contract_last(queries[a], halo(a, 0, lanes))
            edge_peak = jnp.where(valid[a], jnp.max(edge, axis=-1, keepdims=True), NEGATIVE)
            peak = jnp.maximum(jnp.max(near, axis=-1, keepdims=True), edge_peak)
            near_weights = jnp.exp2((near - peak) * EXP_SCALE).astype(jnp.bfloat16)
            edge_weights = jnp.exp2((edge - jnp.where(valid[a], peak, -NEGATIVE)) * EXP_SCALE).astype(jnp.bfloat16)
            summed = jnp.dot(near_weights, middle_values, preferred_element_type=jnp.float32)
            summed = summed + jnp.dot(
                edge_weights, with_ones(halo(a, 1, lanes)), preferred_element_type=jnp.float32
            )
            total = summed[:, HD:]
            result = summed[:, :HD] / total
            log_sum = peak * EXP_SCALE + jnp.log2(total)
            for s in range(sides):
                tokens, rows = slice(a * SPOT, (a + 1) * SPOT), slice(s * SPOT, (s + 1) * SPOT)
                out_refs[s][tokens, lanes] = result[rows].astype(out_refs[s].dtype)
                sum_refs[s][tokens, :] = jnp.where(lane_index(SPOT) == h, log_sum[rows], sum_refs[s][tokens, :])
        return carry

    for ref in sum_refs:
        ref[...] = jnp.zeros_like(ref)
    lax.fori_loop(0, HEADS, step, 0)


def near_attention(meta, own, ext, top, bottom, ext_top, ext_bottom, queries, out_dtypes):
    sides = len(queries)
    tokens, features = queries[0].shape[1:]
    in_vmem = pl.BlockSpec(memory_space=pltpu.VMEM)
    scores = sides * HEADS * tokens * 9 * SPOT
    outs = [jax.ShapeDtypeStruct((tokens, features), dtype) for dtype in out_dtypes]
    sums = [jax.ShapeDtypeStruct((tokens, HD), jnp.float32) for _ in out_dtypes]
    return pl.pallas_call(
        functools.partial(near_kernel, sides),
        out_shape=outs + sums,
        in_specs=[pl.BlockSpec(memory_space=pltpu.SMEM)] + [in_vmem] * (6 + sides),
        out_specs=[in_vmem] * (2 * sides),
        compiler_params=pltpu.CompilerParams(vmem_limit_bytes=VMEM_LIMIT),
        cost_estimate=pl.CostEstimate(flops=scores * HD * 4, bytes_accessed=8 << 20, transcendentals=scores),
    )(meta, own, ext, top, bottom, ext_top, ext_bottom, *queries)


def far_kernel(meta_ref, code_ref, q_ref, core_ref, cross_ref, last_ref, corner_ref, corner_last_ref, *refs):
    near_refs, near_sums, out_ref, sum_ref, held, sems = refs[:2], refs[2:4], refs[4], refs[5], refs[6], refs[7]
    sources = [(core_ref, 0), (core_ref, 1), (cross_ref, 0), (last_ref, 0), (corner_ref, 0), (corner_last_ref, 0)]

    def for_copies(action):
        for f in range(2):
            for a in range(2):
                for j in range(NFAR):
                    slot = (f * 2 + a) * NFAR + j
                    for code, (ref, at) in enumerate(sources):

                        @pl.when(code_ref[slot] == code)
                        def _(ref=ref, at=at, f=f, a=a, j=j, slot=slot):
                            copy = pltpu.make_async_copy(
                                ref.at[:, at, pl.ds(a * SPOT, SPOT), :],
                                held.at[:, f * 2 + a, pl.ds(j * SPOT, SPOT), :],
                                sems.at[slot],
                            )
                            action(copy)

    for_copies(lambda copy: copy.start())
    for_copies(lambda copy: copy.wait())

    def step(h, carry):
        lanes = head_lanes(h)
        for early in range(2):
            frame = meta_ref[early]
            for a in range(2):
                tokens = slice(a * SPOT, (a + 1) * SPOT)
                scores = contract_last(q_ref[frame, tokens, lanes], held[0, frame * 2 + a, :, lanes])
                peak = jnp.max(scores, axis=-1, keepdims=True)
                weights = jnp.exp2((scores - peak) * EXP_SCALE).astype(jnp.bfloat16)
                values = with_ones(held[1, frame * 2 + a, :, lanes])
                summed = jnp.dot(weights, values, preferred_element_type=jnp.float32)
                mask = lane_index(SPOT) == h
                near_sum = jnp.max(
                    jnp.where(mask, near_sums[early][tokens, :], NEGATIVE), axis=-1, keepdims=True
                )
                far_peak = peak * EXP_SCALE
                top = jnp.maximum(near_sum, far_peak)
                near_scale, far_scale = jnp.exp2(near_sum - top), jnp.exp2(far_peak - top)
                total = near_scale + far_scale * summed[:, HD:]
                joined = near_scale * near_refs[early][tokens, lanes] + far_scale * summed[:, :HD]
                out_ref[early, tokens, lanes] = joined / total
                sum_ref[early, tokens, :] = jnp.where(mask, top + jnp.log2(total), sum_ref[early, tokens, :])
        return carry

    sum_ref[...] = jnp.zeros_like(sum_ref)
    lax.fori_loop(0, HEADS, step, 0)


def far_attention(meta, code, queries, buffers, near):
    tokens, features = queries.shape[1:]
    in_vmem = pl.BlockSpec(memory_space=pltpu.VMEM)
    in_smem = pl.BlockSpec(memory_space=pltpu.SMEM)
    scores = HEADS * 2 * tokens * NFAR * SPOT
    return pl.pallas_call(
        far_kernel,
        out_shape=[
            jax.ShapeDtypeStruct((2, tokens, features), jnp.float32),
            jax.ShapeDtypeStruct((2, tokens, HD), jnp.float32),
        ],
        in_specs=[in_smem, in_smem, in_vmem] + [pl.BlockSpec(memory_space=pl.ANY)] * 5 + [in_vmem] * 4,
        out_specs=[in_vmem] * 2,
        scratch_shapes=[
            pltpu.VMEM((2, 4, NFAR * SPOT, features), jnp.bfloat16),
            pltpu.SemaphoreType.DMA((4 * NFAR,)),
        ],
        compiler_params=pltpu.CompilerParams(vmem_limit_bytes=VMEM_LIMIT),
        cost_estimate=pl.CostEstimate(flops=scores * HD * 4, bytes_accessed=8 << 20, transcendentals=scores),
    )(meta, code, queries, *buffers, *near)


def finish_kernel(sides, meta_ref, own_ref, own_sum_ref, *refs):
    parts, sums, out_ref = refs[: 2 * sides], refs[2 * sides : 4 * sides], refs[4 * sides]
    for early in range(2):
        logs = [own_sum_ref[early]]
        for s in range(sides):
            logs.append(jnp.where(meta_ref[2 + s] > 0, sums[early * sides + s][...], NEGATIVE))
        top = functools.reduce(jnp.maximum, logs)
        scales = [jnp.exp2(value - top) for value in logs]
        total = functools.reduce(jnp.add, scales)
        scales = [value / total for value in scales]
        for h in range(HEADS):
            lanes = slice(h * HD, (h + 1) * HD)
            joined = scales[0][:, h : h + 1] * own_ref[early, :, lanes]
            for s in range(sides):
                joined = joined + scales[1 + s][:, h : h + 1] * parts[early * sides + s][:, lanes].astype(jnp.float32)
            out_ref[meta_ref[early], :, lanes] = joined.astype(out_ref.dtype)


def finish(meta, own, own_sum, parts, sums):
    sides = len(parts) // 2
    in_vmem = pl.BlockSpec(memory_space=pltpu.VMEM)
    return pl.pallas_call(
        functools.partial(finish_kernel, sides),
        out_shape=jax.ShapeDtypeStruct(own.shape, jnp.bfloat16),
        in_specs=[pl.BlockSpec(memory_space=pltpu.SMEM)] + [in_vmem] * (2 + 4 * sides),
        out_specs=in_vmem,
        compiler_params=pltpu.CompilerParams(vmem_limit_bytes=VMEM_LIMIT),
        cost_estimate=pl.CostEstimate(flops=own.size * 8, bytes_accessed=5 << 20, transcendentals=0),
    )(meta, own, own_sum, *parts, *sums)


def per_device(queries, keyvals, far_frames):
    shape = queries.shape
    frames, rows, columns, features = shape
    tokens = rows * columns
    ta_size, ha_size, wa_size = lax.axis_size("ta"), lax.axis_size("ha"), lax.axis_size("wa")
    ta, ha, wa = lax.axis_index("ta"), lax.axis_index("ha"), lax.axis_index("wa")
    parity = ta % 2
    queries = queries.reshape(frames, tokens, features)
    keyvals = keyvals.reshape(2, frames, tokens, features)

    core_pairs = [(i, i ^ 1) for i in range(ta_size)]
    cross_pairs = [(i, ta_size - 1 - i) for i in range(ta_size)]
    up = [(i, i + 1) for i in range(ha_size - 1)]
    down = [(i + 1, i) for i in range(ha_size - 1)]
    if wa_size == 2:
        ways = [([(0, 1), (1, 0)], [(0, 1), (1, 0)], wa >= 0)]
    else:
        right = [(i, i + 1) for i in range(wa_size - 1)]
        left = [(i + 1, i) for i in range(wa_size - 1)]
        ways = [(right, left, wa < wa_size - 1), (left, right, wa > 0)]

    def frame_of(value, index):
        return lax.dynamic_slice_in_dim(value, index, 1, axis=1)

    def halo_rows(value):
        top = lax.ppermute(value[:, :, tokens - SPOT :], "ha", up)
        return top, lax.ppermute(value[:, :, :SPOT], "ha", down)

    cross = lax.ppermute(frame_of(keyvals, parity), "ta", cross_pairs)
    top, bottom = halo_rows(keyvals)
    visitors = [lax.ppermute(queries, "wa", there) for there, _, _ in ways]
    core = lax.ppermute(keyvals, "ta", core_pairs)
    inner_top, inner_bottom = frame_of(top, 1 - parity), frame_of(bottom, 1 - parity)
    core_top = lax.ppermute(inner_top, "ta", core_pairs)
    core_bottom = lax.ppermute(inner_bottom, "ta", core_pairs)
    cross_top, cross_bottom = halo_rows(cross)
    last_frame, cross = lax.optimization_barrier((frame_of(keyvals, 1 - parity), cross))
    last = lax.ppermute(last_frame, "ta", cross_pairs)
    corner = lax.ppermute(cross, "ta", core_pairs)
    corner_last = lax.ppermute(last, "ta", core_pairs)

    has_top, has_bottom = ha > 0, ha < ha_size - 1

    def as_meta(*values):
        return jnp.stack([jnp.asarray(value).astype(jnp.int32) for value in values])

    dtypes = [jnp.bfloat16] * len(ways) + [jnp.float32]
    q_sides = visitors + [queries]
    early = near_attention(
        as_meta(1 - parity, parity, has_top, has_bottom),
        keyvals, core, top, bottom, core_top, core_bottom, q_sides, dtypes,
    )
    late = near_attention(
        as_meta(parity, 0, has_top, has_bottom),
        keyvals, cross, top, bottom, cross_top, cross_bottom, q_sides, dtypes,
    )
    sides = len(ways) + 1

    def send_back(near):
        parts = [lax.ppermute(near[s], "wa", back) for s, (_, back, _) in enumerate(ways)]
        return parts, [lax.ppermute(near[sides + s], "wa", back) for s, (_, back, _) in enumerate(ways)]

    early_parts, early_sums = send_back(early)
    late_parts, late_sums = send_back(late)

    wanted = far_frames[:, :, 0, :]
    owner, place = wanted // frames, wanted % frames
    inner = (place != owner % 2).astype(jnp.int32)
    code = jnp.where(owner == ta ^ 1, place, jnp.where(owner == ta_size - 1 - ta, 2 + inner, 4 + inner))
    own, own_sum = far_attention(
        as_meta(1 - parity, parity),
        code.reshape(-1).astype(jnp.int32),
        queries,
        (core, cross, last, corner, corner_last),
        (early[sides - 1], late[sides - 1], early[2 * sides - 1], late[2 * sides - 1]),
    )
    meta = as_meta(1 - parity, parity, *[valid for _, _, valid in ways])
    out = finish(meta, own, own_sum, early_parts + late_parts, early_sums + late_sums)
    return out.reshape(shape)


def solution(mesh):
    placed = (P("ta", "ha", "wa", None), P(None, "ta", "ha", "wa", None), P("ta", "ha", "wa", None))
    return jax.shard_map(
        per_device, mesh=mesh, in_specs=placed, out_specs=P("ta", "ha", "wa", None), check_vma=False
    )
```

```python
import functools

import jax
import jax.numpy as jnp
from jax import lax
from jax.experimental import pallas as pl
from jax.experimental.pallas import tpu as pltpu
from jax.sharding import PartitionSpec as P

TILE = 8
HEADS = 16
HD = 128
NFAR = 2
SPOT = TILE * TILE
NEGATIVE = -1e30
EXP_SCALE = HD ** (-0.5) * 1.4426950408889634
VMEM_LIMIT = 20 * 1024 * 1024
GROUP = 4


def contract_last(left, right):
    return lax.dot_general(left, right, (((1,), (1,)), ((), ())), preferred_element_type=jnp.float32)


def with_ones(values):
    return jnp.concatenate([values, jnp.ones_like(values)], axis=1)


def head_lanes(h):
    return pl.ds(pl.multiple_of(h * HD, HD), HD)


def lane_index(rows):
    return lax.broadcasted_iota(jnp.int32, (rows, HD), 1)


def near_kernel(sides, meta_ref, own_ref, ext_ref, top_ref, bottom_ref, ext_top_ref, ext_bottom_ref, *refs):
    q_refs, out_refs, sum_refs = refs[:sides], refs[sides : 2 * sides], refs[2 * sides :]
    frame, ext_at = meta_ref[0], meta_ref[1]
    valid = (meta_ref[2] > 0, meta_ref[3] > 0)
    half = sides * SPOT

    def middle(kind, lanes):
        parts = [own_ref[kind, 0, :, lanes], own_ref[kind, 1, :, lanes], ext_ref[kind, ext_at, :, lanes]]
        return jnp.concatenate(parts, axis=0)

    def halo(a, kind, lanes):
        ref, ext = ((top_ref, ext_top_ref), (bottom_ref, ext_bottom_ref))[a]
        return jnp.concatenate([ref[kind, 0, :, lanes], ref[kind, 1, :, lanes], ext[kind, 0, :, lanes]], axis=0)

    def step(group, carry):
        members = [head_lanes(group * GROUP + i) for i in range(GROUP)]
        scores = []
        for lanes in members:
            queries = [
                jnp.concatenate([ref[frame, a * SPOT : (a + 1) * SPOT, lanes] for ref in q_refs], axis=0)
                for a in range(2)
            ]
            near = contract_last(jnp.concatenate(queries, axis=0), middle(0, lanes))
            edges = [contract_last(queries[a], halo(a, 0, lanes)) for a in range(2)]
            scores.append([(near[a * half : (a + 1) * half], edges[a]) for a in range(2)])
        weights = []
        for pairs in scores:
            for a, (near, edge) in enumerate(pairs):
                best = functools.reduce(jnp.maximum, [near[:, i * HD : (i + 1) * HD] for i in range(3)])
                edge_best = jnp.maximum(edge[:, : 2 * SPOT], jnp.concatenate([edge[:, 2 * SPOT :]] * 2, axis=1))
                best = jnp.maximum(best, jnp.where(valid[a], edge_best, NEGATIVE))
                peak = jnp.max(best, axis=-1, keepdims=True)
                shift = jnp.where(valid[a], peak, -NEGATIVE)
                weights.append(
                    (
                        peak,
                        jnp.exp2((near - peak) * EXP_SCALE).astype(jnp.bfloat16),
                        jnp.exp2((edge - shift) * EXP_SCALE).astype(jnp.bfloat16),
                    )
                )
        peaks, totals = [carry_value for carry_value in carry[0]], [carry_value for carry_value in carry[1]]
        for i, lanes in enumerate(members):
            mask = lane_index(half) == group * GROUP + i
            middle_values = with_ones(middle(1, lanes))
            for a in range(2):
                peak, near, edge = weights[2 * i + a]
                summed = jnp.dot(near, middle_values, preferred_element_type=jnp.float32)
                summed = summed + jnp.dot(edge, with_ones(halo(a, 1, lanes)), preferred_element_type=jnp.float32)
                total = summed[:, HD:]
                result = summed[:, :HD] / total
                peaks[a] = jnp.where(mask, peak, peaks[a])
                totals[a] = jnp.where(mask, total, totals[a])
                for s in range(sides):
                    rows = slice(s * SPOT, (s + 1) * SPOT)
                    out_refs[s][a * SPOT : (a + 1) * SPOT, lanes] = result[rows].astype(out_refs[s].dtype)
        return tuple(peaks), tuple(totals)

    zeros = tuple(jnp.zeros((half, HD), jnp.float32) for _ in range(2))
    ones = tuple(jnp.ones((half, HD), jnp.float32) for _ in range(2))
    peaks, totals = lax.fori_loop(0, HEADS // GROUP, step, (zeros, ones))
    for a in range(2):
        log_sum = peaks[a] * EXP_SCALE + jnp.log2(totals[a])
        for s in range(sides):
            sum_refs[s][a * SPOT : (a + 1) * SPOT, :] = log_sum[s * SPOT : (s + 1) * SPOT]


def near_attention(meta, own, ext, top, bottom, ext_top, ext_bottom, queries, out_dtypes):
    sides = len(queries)
    tokens, features = queries[0].shape[1:]
    in_vmem = pl.BlockSpec(memory_space=pltpu.VMEM)
    scores = sides * HEADS * tokens * 9 * SPOT
    outs = [jax.ShapeDtypeStruct((tokens, features), dtype) for dtype in out_dtypes]
    sums = [jax.ShapeDtypeStruct((tokens, HD), jnp.float32) for _ in out_dtypes]
    return pl.pallas_call(
        functools.partial(near_kernel, sides),
        out_shape=outs + sums,
        in_specs=[pl.BlockSpec(memory_space=pltpu.SMEM)] + [in_vmem] * (6 + sides),
        out_specs=[in_vmem] * (2 * sides),
        compiler_params=pltpu.CompilerParams(vmem_limit_bytes=VMEM_LIMIT),
        cost_estimate=pl.CostEstimate(flops=scores * HD * 4, bytes_accessed=8 << 20, transcendentals=scores),
    )(meta, own, ext, top, bottom, ext_top, ext_bottom, *queries)


def far_kernel(meta_ref, code_ref, q_ref, core_ref, cross_ref, last_ref, corner_ref, corner_last_ref, *refs):
    near_refs, near_sums, out_ref, sum_ref, held, sems = refs[:2], refs[2:4], refs[4], refs[5], refs[6], refs[7]
    sources = [(core_ref, 0), (core_ref, 1), (cross_ref, 0), (last_ref, 0), (corner_ref, 0), (corner_last_ref, 0)]

    def for_copies(action):
        for f in range(2):
            for a in range(2):
                for j in range(NFAR):
                    slot = (f * 2 + a) * NFAR + j
                    for code, (ref, at) in enumerate(sources):

                        @pl.when(code_ref[slot] == code)
                        def _(ref=ref, at=at, f=f, a=a, j=j, slot=slot):
                            copy = pltpu.make_async_copy(
                                ref.at[:, at, pl.ds(a * SPOT, SPOT), :],
                                held.at[:, f * 2 + a, pl.ds(j * SPOT, SPOT), :],
                                sems.at[slot],
                            )
                            action(copy)

    for_copies(lambda copy: copy.start())
    for_copies(lambda copy: copy.wait())

    units = [(early, a) for early in range(2) for a in range(2)]
    collected = [jnp.zeros((SPOT, HD), jnp.float32) for _ in units]
    for first in range(0, HEADS, GROUP):
        work = [(h, u) for h in range(first, first + GROUP) for u in range(len(units))]
        scores = []
        for h, u in work:
            early, a = units[u]
            frame, lanes = meta_ref[early], slice(h * HD, (h + 1) * HD)
            queries = q_ref[frame, a * SPOT : (a + 1) * SPOT, lanes]
            scores.append(contract_last(queries, held[0, frame * 2 + a, :, lanes]))
        peaks = [jnp.max(value, axis=-1, keepdims=True) for value in scores]
        weights = [
            jnp.exp2((value - peak) * EXP_SCALE).astype(jnp.bfloat16) for value, peak in zip(scores, peaks)
        ]
        for (h, u), weight, peak in zip(work, weights, peaks):
            early, a = units[u]
            frame, lanes = meta_ref[early], slice(h * HD, (h + 1) * HD)
            tokens = slice(a * SPOT, (a + 1) * SPOT)
            summed = jnp.dot(
                weight, with_ones(held[1, frame * 2 + a, :, lanes]), preferred_element_type=jnp.float32
            )
            near_sum = near_sums[early][tokens, h : h + 1]
            far_peak = peak * EXP_SCALE
            top = jnp.maximum(near_sum, far_peak)
            near_scale, far_scale = jnp.exp2(near_sum - top), jnp.exp2(far_peak - top)
            total = near_scale + far_scale * summed[:, HD:]
            joined = near_scale * near_refs[early][tokens, lanes] + far_scale * summed[:, :HD]
            out_ref[early, tokens, lanes] = joined / total
            collected[u] = jnp.where(lane_index(SPOT) == h, top + jnp.log2(total), collected[u])
    for (early, a), value in zip(units, collected):
        sum_ref[early, a * SPOT : (a + 1) * SPOT, :] = value


def far_attention(meta, code, queries, buffers, near):
    tokens, features = queries.shape[1:]
    in_vmem = pl.BlockSpec(memory_space=pltpu.VMEM)
    in_smem = pl.BlockSpec(memory_space=pltpu.SMEM)
    scores = HEADS * 2 * tokens * NFAR * SPOT
    return pl.pallas_call(
        far_kernel,
        out_shape=[
            jax.ShapeDtypeStruct((2, tokens, features), jnp.float32),
            jax.ShapeDtypeStruct((2, tokens, HD), jnp.float32),
        ],
        in_specs=[in_smem, in_smem, in_vmem] + [pl.BlockSpec(memory_space=pl.ANY)] * 5 + [in_vmem] * 4,
        out_specs=[in_vmem] * 2,
        scratch_shapes=[
            pltpu.VMEM((2, 4, NFAR * SPOT, features), jnp.bfloat16),
            pltpu.SemaphoreType.DMA((4 * NFAR,)),
        ],
        compiler_params=pltpu.CompilerParams(vmem_limit_bytes=VMEM_LIMIT),
        cost_estimate=pl.CostEstimate(flops=scores * HD * 4, bytes_accessed=8 << 20, transcendentals=scores),
    )(meta, code, queries, *buffers, *near)


def finish_kernel(sides, meta_ref, own_ref, own_sum_ref, *refs):
    parts, sums, out_ref = refs[: 2 * sides], refs[2 * sides : 4 * sides], refs[4 * sides]
    for early in range(2):
        logs = [own_sum_ref[early]]
        for s in range(sides):
            logs.append(jnp.where(meta_ref[2 + s] > 0, sums[early * sides + s][...], NEGATIVE))
        top = functools.reduce(jnp.maximum, logs)
        scales = [jnp.exp2(value - top) for value in logs]
        total = functools.reduce(jnp.add, scales)
        scales = [value / total for value in scales]
        for h in range(HEADS):
            lanes = slice(h * HD, (h + 1) * HD)
            joined = scales[0][:, h : h + 1] * own_ref[early, :, lanes]
            for s in range(sides):
                joined = joined + scales[1 + s][:, h : h + 1] * parts[early * sides + s][:, lanes].astype(jnp.float32)
            out_ref[meta_ref[early], :, lanes] = joined.astype(out_ref.dtype)


def finish(meta, own, own_sum, parts, sums):
    sides = len(parts) // 2
    in_vmem = pl.BlockSpec(memory_space=pltpu.VMEM)
    return pl.pallas_call(
        functools.partial(finish_kernel, sides),
        out_shape=jax.ShapeDtypeStruct(own.shape, jnp.bfloat16),
        in_specs=[pl.BlockSpec(memory_space=pltpu.SMEM)] + [in_vmem] * (2 + 4 * sides),
        out_specs=in_vmem,
        compiler_params=pltpu.CompilerParams(vmem_limit_bytes=VMEM_LIMIT),
        cost_estimate=pl.CostEstimate(flops=own.size * 8, bytes_accessed=5 << 20, transcendentals=0),
    )(meta, own, own_sum, *parts, *sums)


def per_device(queries, keyvals, far_frames):
    shape = queries.shape
    frames, rows, columns, features = shape
    tokens = rows * columns
    ta_size, ha_size, wa_size = lax.axis_size("ta"), lax.axis_size("ha"), lax.axis_size("wa")
    ta, ha, wa = lax.axis_index("ta"), lax.axis_index("ha"), lax.axis_index("wa")
    parity = ta % 2
    queries = queries.reshape(frames, tokens, features)
    keyvals = keyvals.reshape(2, frames, tokens, features)

    core_pairs = [(i, i ^ 1) for i in range(ta_size)]
    cross_pairs = [(i, ta_size - 1 - i) for i in range(ta_size)]
    up = [(i, i + 1) for i in range(ha_size - 1)]
    down = [(i + 1, i) for i in range(ha_size - 1)]
    if wa_size == 2:
        ways = [([(0, 1), (1, 0)], [(0, 1), (1, 0)], wa >= 0)]
    else:
        right = [(i, i + 1) for i in range(wa_size - 1)]
        left = [(i + 1, i) for i in range(wa_size - 1)]
        ways = [(right, left, wa < wa_size - 1), (left, right, wa > 0)]

    def frame_of(value, index):
        return lax.dynamic_slice_in_dim(value, index, 1, axis=1)

    def halo_rows(value):
        top = lax.ppermute(value[:, :, tokens - SPOT :], "ha", up)
        return top, lax.ppermute(value[:, :, :SPOT], "ha", down)

    cross = lax.ppermute(frame_of(keyvals, parity), "ta", cross_pairs)
    top, bottom = halo_rows(keyvals)
    visitors = [lax.ppermute(queries, "wa", there) for there, _, _ in ways]
    core = lax.ppermute(keyvals, "ta", core_pairs)
    inner_top, inner_bottom = frame_of(top, 1 - parity), frame_of(bottom, 1 - parity)
    core_top = lax.ppermute(inner_top, "ta", core_pairs)
    core_bottom = lax.ppermute(inner_bottom, "ta", core_pairs)
    cross_top, cross_bottom = halo_rows(cross)
    last_frame, cross = lax.optimization_barrier((frame_of(keyvals, 1 - parity), cross))
    last = lax.ppermute(last_frame, "ta", cross_pairs)
    corner = lax.ppermute(cross, "ta", core_pairs)
    corner_last = lax.ppermute(last, "ta", core_pairs)

    has_top, has_bottom = ha > 0, ha < ha_size - 1

    def as_meta(*values):
        return jnp.stack([jnp.asarray(value).astype(jnp.int32) for value in values])

    dtypes = [jnp.bfloat16] * len(ways) + [jnp.float32]
    q_sides = visitors + [queries]
    early = near_attention(
        as_meta(1 - parity, parity, has_top, has_bottom),
        keyvals, core, top, bottom, core_top, core_bottom, q_sides, dtypes,
    )
    late_meta, early_first = lax.optimization_barrier((as_meta(parity, 0, has_top, has_bottom), early[0]))
    early = [early_first] + list(early[1:])
    late = near_attention(
        late_meta,
        keyvals, cross, top, bottom, cross_top, cross_bottom, q_sides, dtypes,
    )
    sides = len(ways) + 1

    def send_back(near):
        parts = [lax.ppermute(near[s], "wa", back) for s, (_, back, _) in enumerate(ways)]
        return parts, [lax.ppermute(near[sides + s], "wa", back) for s, (_, back, _) in enumerate(ways)]

    early_parts, early_sums = send_back(early)
    late_parts, late_sums = send_back(late)

    wanted = far_frames[:, :, 0, :]
    owner, place = wanted // frames, wanted % frames
    inner = (place != owner % 2).astype(jnp.int32)
    code = jnp.where(owner == ta ^ 1, place, jnp.where(owner == ta_size - 1 - ta, 2 + inner, 4 + inner))
    own, own_sum = far_attention(
        as_meta(1 - parity, parity),
        code.reshape(-1).astype(jnp.int32),
        queries,
        (core, cross, last, corner, corner_last),
        (early[sides - 1], late[sides - 1], early[2 * sides - 1], late[2 * sides - 1]),
    )
    meta = as_meta(1 - parity, parity, *[valid for _, _, valid in ways])
    out = finish(meta, own, own_sum, early_parts + late_parts, early_sums + late_sums)
    return out.reshape(shape)


def solution(mesh):
    placed = (P("ta", "ha", "wa", None), P(None, "ta", "ha", "wa", None), P("ta", "ha", "wa", None))
    return jax.shard_map(
        per_device, mesh=mesh, in_specs=placed, out_specs=P("ta", "ha", "wa", None), check_vma=False
    )
```

```python
import functools

import jax
import jax.numpy as jnp
from jax import lax
from jax.experimental import pallas as pl
from jax.experimental.pallas import tpu as pltpu
from jax.sharding import PartitionSpec as P

TILE = 8
HEADS = 16
HD = 128
NFAR = 2
SPOT = TILE * TILE
NEGATIVE = -1e30
EXP_SCALE = HD ** (-0.5) * 1.4426950408889634
VMEM_LIMIT = 24 * 1024 * 1024
GROUP = 4
FINISH_COST = 4 << 30
LATE_COST = 16 << 30


def contract_last(left, right):
    return lax.dot_general(left, right, (((1,), (1,)), ((), ())), preferred_element_type=jnp.float32)


def with_ones(values):
    return jnp.concatenate([values, jnp.ones_like(values)], axis=1)


def lane_index(rows):
    return lax.broadcasted_iota(jnp.int32, (rows, HD), 1)


def split_sums(value):
    high = value.astype(jnp.bfloat16).astype(jnp.float32)
    rest = value - high
    middle = rest.astype(jnp.bfloat16).astype(jnp.float32)
    low = rest - middle
    return (high + pltpu.roll(middle, HEADS, 1) + pltpu.roll(low, 2 * HEADS, 1)).astype(jnp.bfloat16)


def join_sums(value):
    terms = value.astype(jnp.float32)
    return terms + (pltpu.roll(terms, HD - HEADS, 1) + pltpu.roll(terms, HD - 2 * HEADS, 1))


def near_kernel(sides, meta_ref, own_ref, ext_ref, top_ref, bottom_ref, *refs):
    ext_halos, refs = (refs[:2], refs[2:4]), refs[4:]
    q_refs, out_refs, own_sum_ref, log_ref = refs[:sides], refs[sides : 2 * sides], refs[2 * sides], refs[2 * sides + 1]
    group = pl.program_id(0)
    valid = (meta_ref[2] > 0, meta_ref[3] > 0)
    half = sides * SPOT

    def middle(kind, lanes):
        parts = [own_ref[kind, 0, :, lanes], own_ref[kind, 1, :, lanes], ext_ref[kind, 0, :, lanes]]
        return jnp.concatenate(parts, axis=0)

    def halo(a, kind, lanes):
        ref, ext = (top_ref, bottom_ref)[a], ext_halos[a][kind]
        return jnp.concatenate([ref[kind, 0, :, lanes], ref[kind, 1, :, lanes], ext[0, 0, :, lanes]], axis=0)

    members = [slice(i * HD, (i + 1) * HD) for i in range(GROUP)]
    scores = []
    for lanes in members:
        queries = [
            jnp.concatenate([ref[0, a * SPOT : (a + 1) * SPOT, lanes] for ref in q_refs], axis=0) for a in range(2)
        ]
        near = contract_last(jnp.concatenate(queries, axis=0), middle(0, lanes))
        edges = [contract_last(queries[a], halo(a, 0, lanes)) for a in range(2)]
        scores.append([(near[a * half : (a + 1) * half], edges[a]) for a in range(2)])
    weights = []
    for pairs in scores:
        for a, (near, edge) in enumerate(pairs):
            best = functools.reduce(jnp.maximum, [near[:, i * HD : (i + 1) * HD] for i in range(3)])
            edge_best = jnp.maximum(edge[:, : 2 * SPOT], jnp.concatenate([edge[:, 2 * SPOT :]] * 2, axis=1))
            best = jnp.maximum(best, jnp.where(valid[a], edge_best, NEGATIVE))
            peak = jnp.max(best, axis=-1, keepdims=True)
            shift = jnp.where(valid[a], peak, -NEGATIVE)
            weights.append(
                (
                    peak,
                    jnp.exp2((near - peak) * EXP_SCALE).astype(jnp.bfloat16),
                    jnp.exp2((edge - shift) * EXP_SCALE).astype(jnp.bfloat16),
                )
            )
    peaks = [jnp.zeros((half, HD), jnp.float32) for _ in range(2)]
    totals = [jnp.ones((half, HD), jnp.float32) for _ in range(2)]
    for i, lanes in enumerate(members):
        mask = lane_index(half) == group * GROUP + i
        middle_values = with_ones(middle(1, lanes))
        for a in range(2):
            peak, near, edge = weights[2 * i + a]
            summed = jnp.dot(near, middle_values, preferred_element_type=jnp.float32)
            summed = summed + jnp.dot(edge, with_ones(halo(a, 1, lanes)), preferred_element_type=jnp.float32)
            total = summed[:, HD:]
            result = summed[:, :HD] / total
            peaks[a] = jnp.where(mask, peak, peaks[a])
            totals[a] = jnp.where(mask, total, totals[a])
            for s in range(sides):
                rows = slice(s * SPOT, (s + 1) * SPOT)
                at = pl.ds(pl.multiple_of((group * GROUP + i) * HD, HD), HD)
                out_refs[s][a * SPOT : (a + 1) * SPOT, at] = result[rows].astype(out_refs[s].dtype)

    @pl.when(group == 0)
    def _():
        log_ref[...] = jnp.zeros_like(log_ref)

    for a in range(2):
        log_sum = peaks[a] * EXP_SCALE + jnp.log2(totals[a])
        for s in range(sides):
            log_ref[s, a * SPOT : (a + 1) * SPOT, :] += log_sum[s * SPOT : (s + 1) * SPOT]

    @pl.when(group == pl.num_programs(0) - 1)
    def _():
        own_sum_ref[...] = log_ref[sides - 1]
        for s in range(sides - 1):
            out_refs[s][:, HEADS * HD :] = split_sums(log_ref[s])


def near_attention(meta, own, ext, top, bottom, ext_halos, queries, cost):
    sides = len(queries)
    tokens, features = queries[0].shape[1:]
    width = GROUP * HD
    outs = [jax.ShapeDtypeStruct((tokens, features + HD), jnp.bfloat16) for _ in queries[1:]]
    outs += [jax.ShapeDtypeStruct((tokens, features), jnp.float32), jax.ShapeDtypeStruct((tokens, HD), jnp.float32)]

    def block(value, count, at):
        return pl.BlockSpec((2, count, value.shape[2], width), lambda g, meta: (0, at(meta), 0, g))

    def first(meta):
        return 0

    in_specs = [block(own, 2, first), block(ext, 1, lambda meta: meta[1])]
    in_specs += [block(top, 2, first), block(bottom, 2, first)]
    for _, lead in ext_halos:
        in_specs.append(pl.BlockSpec((1, 1, SPOT, width), lambda g, meta, lead=lead: (lead, 0, 0, g)))
    in_specs += [pl.BlockSpec((1, tokens, width), lambda g, meta: (meta[0], 0, g)) for _ in queries]
    out_specs = [pl.BlockSpec(out.shape, lambda g, meta: (0, 0)) for out in outs]
    return pl.pallas_call(
        functools.partial(near_kernel, sides),
        out_shape=outs,
        grid_spec=pltpu.PrefetchScalarGridSpec(
            num_scalar_prefetch=1,
            grid=(HEADS // GROUP,),
            in_specs=in_specs,
            out_specs=out_specs,
            scratch_shapes=[pltpu.VMEM((sides, tokens, HD), jnp.float32)],
        ),
        compiler_params=pltpu.CompilerParams(vmem_limit_bytes=VMEM_LIMIT),
        cost_estimate=pl.CostEstimate(flops=cost, bytes_accessed=1, transcendentals=0),
    )(meta, own, ext, top, bottom, *[value for value, _ in ext_halos], *queries)


def far_kernel(meta_ref, code_ref, q_ref, core_ref, cross_ref, last_ref, corner_ref, corner_last_ref, *refs):
    near_refs, near_sums, out_ref, sum_ref, held, sems = refs[:2], refs[2:4], refs[4], refs[5], refs[6], refs[7]
    sources = [(core_ref, 0), (core_ref, 1), (cross_ref, 0), (last_ref, 0), (corner_ref, 0), (corner_last_ref, 0)]

    def for_copies(first, action):
        lanes = pl.ds(first * HD, GROUP * HD)
        for f in range(2):
            for a in range(2):
                for j in range(NFAR):
                    slot = (f * 2 + a) * NFAR + j
                    for code, (ref, at) in enumerate(sources):

                        @pl.when(code_ref[slot] == code)
                        def _(ref=ref, at=at, f=f, a=a, j=j, slot=slot):
                            copy = pltpu.make_async_copy(
                                ref.at[:, at, pl.ds(a * SPOT, SPOT), lanes],
                                held.at[:, f * 2 + a, pl.ds(j * SPOT, SPOT), lanes],
                                sems.at[slot, first // GROUP],
                            )
                            action(copy)

    for first in range(0, HEADS, GROUP):
        for_copies(first, lambda copy: copy.start())

    units = [(early, a) for early in range(2) for a in range(2)]
    collected = [jnp.zeros((SPOT, HD), jnp.float32) for _ in units]
    for first in range(0, HEADS, GROUP):
        for_copies(first, lambda copy: copy.wait())
        work = [(h, u) for h in range(first, first + GROUP) for u in range(len(units))]
        scores = []
        for h, u in work:
            early, a = units[u]
            frame, lanes = meta_ref[early], slice(h * HD, (h + 1) * HD)
            queries = q_ref[frame, a * SPOT : (a + 1) * SPOT, lanes]
            scores.append(contract_last(queries, held[0, frame * 2 + a, :, lanes]))
        peaks = [jnp.max(value, axis=-1, keepdims=True) for value in scores]
        weights = [
            jnp.exp2((value - peak) * EXP_SCALE).astype(jnp.bfloat16) for value, peak in zip(scores, peaks)
        ]
        for (h, u), weight, peak in zip(work, weights, peaks):
            early, a = units[u]
            frame, lanes = meta_ref[early], slice(h * HD, (h + 1) * HD)
            tokens = slice(a * SPOT, (a + 1) * SPOT)
            summed = jnp.dot(
                weight, with_ones(held[1, frame * 2 + a, :, lanes]), preferred_element_type=jnp.float32
            )
            near_sum = near_sums[early][tokens, h : h + 1]
            far_peak = peak * EXP_SCALE
            top = jnp.maximum(near_sum, far_peak)
            near_scale, far_scale = jnp.exp2(near_sum - top), jnp.exp2(far_peak - top)
            total = near_scale + far_scale * summed[:, HD:]
            joined = near_scale * near_refs[early][tokens, lanes] + far_scale * summed[:, :HD]
            out_ref[early, tokens, lanes] = joined / total
            collected[u] = jnp.where(lane_index(SPOT) == h, top + jnp.log2(total), collected[u])
    for (early, a), value in zip(units, collected):
        sum_ref[early, a * SPOT : (a + 1) * SPOT, :] = value


def far_attention(meta, code, queries, buffers, near):
    tokens, features = queries.shape[1:]
    in_vmem = pl.BlockSpec(memory_space=pltpu.VMEM)
    in_smem = pl.BlockSpec(memory_space=pltpu.SMEM)
    scores = HEADS * 2 * tokens * NFAR * SPOT
    return pl.pallas_call(
        far_kernel,
        out_shape=[
            jax.ShapeDtypeStruct((2, tokens, features), jnp.float32),
            jax.ShapeDtypeStruct((2, tokens, HD), jnp.float32),
        ],
        in_specs=[in_smem, in_smem, in_vmem] + [pl.BlockSpec(memory_space=pl.ANY)] * 5 + [in_vmem] * 4,
        out_specs=[in_vmem] * 2,
        scratch_shapes=[
            pltpu.VMEM((2, 4, NFAR * SPOT, features), jnp.bfloat16),
            pltpu.SemaphoreType.DMA((4 * NFAR, HEADS // GROUP)),
        ],
        compiler_params=pltpu.CompilerParams(vmem_limit_bytes=VMEM_LIMIT),
        cost_estimate=pl.CostEstimate(flops=1, bytes_accessed=1, transcendentals=0),
    )(meta, code, queries, *buffers, *near)


def finish_kernel(sides, aliased, meta_ref, own_ref, own_sum_ref, *refs):
    parts, out_ref = refs[:sides], refs[sides + aliased]
    logs = [own_sum_ref[0]]
    for s in range(sides):
        logs.append(jnp.where(meta_ref[1 + s] > 0, join_sums(parts[s][:, HEADS * HD :]), NEGATIVE))
    top = functools.reduce(jnp.maximum, logs)
    scales = [jnp.exp2(value - top) for value in logs]
    total = functools.reduce(jnp.add, scales)
    scales = [value / total for value in scales]
    for h in range(HEADS):
        lanes = slice(h * HD, (h + 1) * HD)
        joined = scales[0][:, h : h + 1] * own_ref[0, :, lanes]
        for s in range(sides):
            joined = joined + scales[1 + s][:, h : h + 1] * parts[s][:, lanes].astype(jnp.float32)
        out_ref[0, :, lanes] = joined.astype(out_ref.dtype)


def finish(meta, at, own, own_sum, parts, earlier, cost):
    sides, rows = len(parts), 32
    _, tokens, features = own.shape
    in_specs = [
        pl.BlockSpec((1, rows, features), lambda i, meta: (at, i, 0)),
        pl.BlockSpec((1, rows, HD), lambda i, meta: (at, i, 0)),
    ]
    in_specs += [pl.BlockSpec((rows, features + HD), lambda i, meta: (i, 0)) for _ in parts]
    extra = () if earlier is None else (earlier,)
    in_specs += [pl.BlockSpec(memory_space=pl.ANY) for _ in extra]
    return pl.pallas_call(
        functools.partial(finish_kernel, sides, len(extra)),
        out_shape=jax.ShapeDtypeStruct(own.shape, jnp.bfloat16),
        grid_spec=pltpu.PrefetchScalarGridSpec(
            num_scalar_prefetch=1,
            grid=(tokens // rows,),
            in_specs=in_specs,
            out_specs=pl.BlockSpec((1, rows, features), lambda i, meta: (meta[0], i, 0)),
        ),
        input_output_aliases={} if earlier is None else {3 + sides: 0},
        compiler_params=pltpu.CompilerParams(vmem_limit_bytes=VMEM_LIMIT),
        cost_estimate=pl.CostEstimate(flops=cost, bytes_accessed=1, transcendentals=0),
    )(meta, own, own_sum, *parts, *extra)


def per_device(queries, keyvals, far_frames):
    shape = queries.shape
    frames, rows, columns, features = shape
    tokens = rows * columns
    ta_size, ha_size, wa_size = lax.axis_size("ta"), lax.axis_size("ha"), lax.axis_size("wa")
    ta, ha, wa = lax.axis_index("ta"), lax.axis_index("ha"), lax.axis_index("wa")
    parity = ta % 2
    queries = queries.reshape(frames, tokens, features)
    keyvals = keyvals.reshape(2, frames, tokens, features)

    core_pairs = [(i, i ^ 1) for i in range(ta_size)]
    cross_pairs = [(i, ta_size - 1 - i) for i in range(ta_size)]
    up = [(i, i + 1) for i in range(ha_size - 1)]
    down = [(i + 1, i) for i in range(ha_size - 1)]
    if wa_size == 2:
        ways = [([(0, 1), (1, 0)], [(0, 1), (1, 0)], wa >= 0)]
    else:
        right = [(i, i + 1) for i in range(wa_size - 1)]
        left = [(i + 1, i) for i in range(wa_size - 1)]
        ways = [(right, left, wa < wa_size - 1), (left, right, wa > 0)]

    def frame_of(value, index):
        return lax.dynamic_slice_in_dim(value, index, 1, axis=1)

    visitors = [lax.ppermute(queries, "wa", there) for there, _, _ in ways]
    last_rows, first_rows, held = lax.optimization_barrier(
        (keyvals[:, :, tokens - SPOT :], keyvals[:, :, :SPOT], keyvals)
    )
    top = lax.ppermute(last_rows, "ha", up)
    bottom = lax.ppermute(first_rows, "ha", down)
    cross = lax.ppermute(frame_of(held, parity), "ta", cross_pairs)
    core = lax.ppermute(keyvals, "ta", core_pairs)
    core_top = lax.ppermute(frame_of(top, 1 - parity), "ta", core_pairs)
    core_bottom = lax.ppermute(frame_of(bottom, 1 - parity), "ta", core_pairs)
    last_frame, cross, core_top, core_bottom = lax.optimization_barrier(
        (frame_of(keyvals, 1 - parity), cross, core_top, core_bottom)
    )
    last = lax.ppermute(last_frame, "ta", cross_pairs)
    cross_top = lax.ppermute(cross[:, :, tokens - SPOT :], "ha", up)
    cross_bottom = lax.ppermute(cross[:, :, :SPOT], "ha", down)
    core_halos = [(value, kind) for value in (core_top, core_bottom) for kind in range(2)]
    cross_halos = [(value, kind) for value in (cross_top, cross_bottom) for kind in range(2)]

    has_top, has_bottom = ha > 0, ha < ha_size - 1

    def as_meta(*values):
        return jnp.stack([jnp.asarray(value).astype(jnp.int32) for value in values])

    q_sides = visitors + [queries]
    early = near_attention(
        as_meta(1 - parity, parity, has_top, has_bottom),
        keyvals, core, top, bottom, core_halos, q_sides, 1,
    )
    late_meta, _ = lax.optimization_barrier((as_meta(parity, 0, has_top, has_bottom), early[0]))
    late = near_attention(
        late_meta,
        keyvals, cross, top, bottom, cross_halos, q_sides, LATE_COST,
    )
    early_parts = [lax.ppermute(early[s], "wa", back) for s, (_, back, _) in enumerate(ways)]
    late_results, early_parts, cross, last = lax.optimization_barrier((late[: len(ways)], early_parts, cross, last))
    late_parts = [lax.ppermute(late_results[s], "wa", back) for s, (_, back, _) in enumerate(ways)]
    corner = lax.ppermute(cross, "ta", core_pairs)
    corner_last = lax.ppermute(last, "ta", core_pairs)

    wanted = far_frames[:, :, 0, :]
    owner, place = wanted // frames, wanted % frames
    inner = (place != owner % 2).astype(jnp.int32)
    code = jnp.where(owner == ta ^ 1, place, jnp.where(owner == ta_size - 1 - ta, 2 + inner, 4 + inner))
    own, own_sum = far_attention(
        as_meta(1 - parity, parity),
        code.reshape(-1).astype(jnp.int32),
        queries,
        (core, cross, last, corner, corner_last),
        (early[-2], late[-2], early[-1], late[-1]),
    )
    exists = [valid for _, _, valid in ways]
    out = finish(as_meta(1 - parity, *exists), 0, own, own_sum, early_parts, None, FINISH_COST)
    out = finish(as_meta(parity, *exists), 1, own, own_sum, late_parts, out, 1)
    return out.reshape(shape)


def solution(mesh):
    placed = (P("ta", "ha", "wa", None), P(None, "ta", "ha", "wa", None), P("ta", "ha", "wa", None))
    return jax.shard_map(
        per_device, mesh=mesh, in_specs=placed, out_specs=P("ta", "ha", "wa", None), check_vma=False
    )
```

```python
import functools

import jax
import jax.numpy as jnp
from jax import lax
from jax.experimental import pallas as pl
from jax.experimental.pallas import tpu as pltpu
from jax.sharding import PartitionSpec as P

TILE = 8
HEADS = 16
HD = 128
NFAR = 2
SPOT = TILE * TILE
NEGATIVE = -1e30
EXP_SCALE = HD ** (-0.5) * 1.4426950408889634
VMEM_LIMIT = 16 * 1024 * 1024
GROUP = 4
FINISH_COST = 4 << 30
LATE_COST = 7 << 30


def contract_last(left, right):
    return lax.dot_general(left, right, (((1,), (1,)), ((), ())), preferred_element_type=jnp.float32)


def with_ones(values):
    return jnp.concatenate([values, jnp.ones_like(values)], axis=1)


def lane_index(rows):
    return lax.broadcasted_iota(jnp.int32, (rows, HD), 1)


def split_sums(value):
    high = value.astype(jnp.bfloat16).astype(jnp.float32)
    rest = value - high
    middle = rest.astype(jnp.bfloat16).astype(jnp.float32)
    low = rest - middle
    return (high + pltpu.roll(middle, HEADS, 1) + pltpu.roll(low, 2 * HEADS, 1)).astype(jnp.bfloat16)


def join_sums(value):
    terms = value.astype(jnp.float32)
    return terms + (pltpu.roll(terms, HD - HEADS, 1) + pltpu.roll(terms, HD - 2 * HEADS, 1))


def kernel_cost(flops):
    return pl.CostEstimate(flops=flops, bytes_accessed=1, transcendentals=0)


def cut_kernel(keyvals_ref, last_rows_ref, first_rows_ref, outer_last_ref, outer_first_ref, inner_ref, sems):
    outer = lax.axis_index("ta") % 2
    first, last = pl.ds(0, SPOT), pl.ds(SPOT, SPOT)
    pieces = [
        (keyvals_ref.at[:, :, last], last_rows_ref),
        (keyvals_ref.at[:, :, first], first_rows_ref),
        (keyvals_ref.at[:, outer, last], outer_last_ref),
        (keyvals_ref.at[:, outer, first], outer_first_ref),
        (keyvals_ref.at[:, 1 - outer], inner_ref),
    ]
    copies = [pltpu.make_async_copy(source, target, sems.at[i]) for i, (source, target) in enumerate(pieces)]
    for copy in copies:
        copy.start()
    for copy in copies:
        copy.wait()


def cut(keyvals):
    two, frames, tokens, features = keyvals.shape
    shapes = [(two, frames, SPOT, features)] * 2 + [(two, SPOT, features)] * 2 + [(two, tokens, features)]
    return pl.pallas_call(
        cut_kernel,
        out_shape=[jax.ShapeDtypeStruct(shape, keyvals.dtype) for shape in shapes],
        in_specs=[pl.BlockSpec(memory_space=pl.ANY)],
        out_specs=[pl.BlockSpec(memory_space=pltpu.VMEM)] * 5,
        scratch_shapes=[pltpu.SemaphoreType.DMA((5,))],
        compiler_params=pltpu.CompilerParams(vmem_limit_bytes=VMEM_LIMIT),
        cost_estimate=kernel_cost(1),
    )(keyvals)


def near_kernel(sides, early, has_rows, own_ref, top_ref, bottom_ref, *refs):
    parity = lax.axis_index("ta") % 2
    ha = lax.axis_index("ha")
    valid = (ha > 0, ha < has_rows - 1)
    if early:
        ext_ref, ext_top_ref, ext_bottom_ref, refs = refs[0], refs[1], refs[2], refs[3:]
        frame = 1 - parity
    else:
        ext_first_ref, ext_last_ref, ext_top_ref, ext_bottom_ref, refs = refs[0], refs[1], refs[2], refs[3], refs[4:]
        frame = parity
    q_refs, out_refs, own_sum_ref, log_ref = refs[:sides], refs[sides : 2 * sides], refs[2 * sides], refs[2 * sides + 1]
    group = pl.program_id(0)
    half = sides * SPOT

    def middle(kind, lanes):
        parts = [own_ref[kind, 0, :, lanes], own_ref[kind, 1, :, lanes]]
        if early:
            parts.append(ext_ref[kind, parity, :, lanes])
        else:
            parts += [ext_first_ref[kind, :, lanes], ext_last_ref[kind, :, lanes]]
        return jnp.concatenate(parts, axis=0)

    def halo(a, kind, lanes):
        ref, ext = ((top_ref, ext_top_ref), (bottom_ref, ext_bottom_ref))[a]
        third = ext[kind, parity, :, lanes] if early else ext[kind, :, lanes]
        return jnp.concatenate([ref[kind, 0, :, lanes], ref[kind, 1, :, lanes], third], axis=0)

    members = [slice(i * HD, (i + 1) * HD) for i in range(GROUP)]
    scores = []
    for lanes in members:
        queries = [
            jnp.concatenate([ref[frame, a * SPOT : (a + 1) * SPOT, lanes] for ref in q_refs], axis=0) for a in range(2)
        ]
        near = contract_last(jnp.concatenate(queries, axis=0), middle(0, lanes))
        edges = [contract_last(queries[a], halo(a, 0, lanes)) for a in range(2)]
        scores.append([(near[a * half : (a + 1) * half], edges[a]) for a in range(2)])
    weights = []
    for pairs in scores:
        for a, (near, edge) in enumerate(pairs):
            best = functools.reduce(jnp.maximum, [near[:, i * HD : (i + 1) * HD] for i in range(3)])
            edge_best = jnp.maximum(edge[:, : 2 * SPOT], jnp.concatenate([edge[:, 2 * SPOT :]] * 2, axis=1))
            best = jnp.maximum(best, jnp.where(valid[a], edge_best, NEGATIVE))
            peak = jnp.max(best, axis=-1, keepdims=True)
            shift = jnp.where(valid[a], peak, -NEGATIVE)
            weights.append(
                (
                    peak,
                    jnp.exp2((near - peak) * EXP_SCALE).astype(jnp.bfloat16),
                    jnp.exp2((edge - shift) * EXP_SCALE).astype(jnp.bfloat16),
                )
            )
    peaks = [jnp.zeros((half, HD), jnp.float32) for _ in range(2)]
    totals = [jnp.ones((half, HD), jnp.float32) for _ in range(2)]
    for i, lanes in enumerate(members):
        mask = lane_index(half) == group * GROUP + i
        middle_values = with_ones(middle(1, lanes))
        for a in range(2):
            peak, near, edge = weights[2 * i + a]
            summed = jnp.dot(near, middle_values, preferred_element_type=jnp.float32)
            summed = summed + jnp.dot(edge, with_ones(halo(a, 1, lanes)), preferred_element_type=jnp.float32)
            total = summed[:, HD:]
            result = summed[:, :HD] / total
            peaks[a] = jnp.where(mask, peak, peaks[a])
            totals[a] = jnp.where(mask, total, totals[a])
            for s in range(sides):
                rows = slice(s * SPOT, (s + 1) * SPOT)
                at = pl.ds(pl.multiple_of((group * GROUP + i) * HD, HD), HD)
                out_refs[s][a * SPOT : (a + 1) * SPOT, at] = result[rows].astype(out_refs[s].dtype)

    @pl.when(group == 0)
    def _():
        log_ref[...] = jnp.zeros_like(log_ref)

    for a in range(2):
        log_sum = peaks[a] * EXP_SCALE + jnp.log2(totals[a])
        for s in range(sides):
            log_ref[s, a * SPOT : (a + 1) * SPOT, :] += log_sum[s * SPOT : (s + 1) * SPOT]

    @pl.when(group == pl.num_programs(0) - 1)
    def _():
        own_sum_ref[...] = log_ref[sides - 1]
        for s in range(sides - 1):
            out_refs[s][:, HEADS * HD :] = split_sums(log_ref[s])


def near_attention(early, has_rows, own, top, bottom, third, queries, cost):
    sides = len(queries)
    tokens, features = queries[0].shape[1:]
    width = GROUP * HD
    operands = [own, top, bottom, *third, *queries]
    outs = [jax.ShapeDtypeStruct((tokens, features + HD), jnp.bfloat16) for _ in queries[1:]]
    outs += [jax.ShapeDtypeStruct((tokens, features), jnp.float32), jax.ShapeDtypeStruct((tokens, HD), jnp.float32)]

    def lanes_of_group(value):
        lead = value.ndim - 1
        return pl.BlockSpec(value.shape[:-1] + (width,), lambda g: (0,) * lead + (g,))

    return pl.pallas_call(
        functools.partial(near_kernel, sides, early, has_rows),
        out_shape=outs,
        grid=(HEADS // GROUP,),
        in_specs=[lanes_of_group(value) for value in operands],
        out_specs=[pl.BlockSpec(out.shape, lambda g: (0, 0)) for out in outs],
        scratch_shapes=[pltpu.VMEM((sides, tokens, HD), jnp.float32)],
        compiler_params=pltpu.CompilerParams(vmem_limit_bytes=VMEM_LIMIT),
        cost_estimate=kernel_cost(cost),
    )(*operands)


def far_kernel(members, far_ref, q_ref, core_ref, cross_first_ref, cross_last_ref, last_ref, *refs):
    corner_first_ref, corner_last_ref, corner_inner_ref, *refs = refs
    near_refs, near_sums, out_ref, sum_ref, held, sems = refs[:2], refs[2:4], refs[4], refs[5], refs[6], refs[7]
    ta = lax.axis_index("ta")
    parity = ta % 2

    def for_copies(first, action):
        lanes = pl.ds(first * HD, GROUP * HD)
        for f in range(2):
            for a in range(2):
                rows = pl.ds(a * SPOT, SPOT)
                by_rows = (cross_first_ref, cross_last_ref)[a], (corner_first_ref, corner_last_ref)[a]
                for j in range(NFAR):
                    slot = (f * 2 + a) * NFAR + j
                    wanted = far_ref[f, a, 0, j]
                    owner, place = wanted // 2, wanted % 2
                    inner = place != owner % 2
                    is_core, is_cross = owner == ta + 1 - 2 * parity, owner == members - 1 - ta
                    is_corner = jnp.logical_not(jnp.logical_or(is_core, is_cross))
                    sources = [
                        (jnp.logical_and(is_core, place == 0), core_ref.at[:, 0, rows, lanes]),
                        (jnp.logical_and(is_core, place == 1), core_ref.at[:, 1, rows, lanes]),
                        (jnp.logical_and(is_cross, jnp.logical_not(inner)), by_rows[0].at[:, :, lanes]),
                        (jnp.logical_and(is_cross, inner), last_ref.at[:, rows, lanes]),
                        (jnp.logical_and(is_corner, jnp.logical_not(inner)), by_rows[1].at[:, :, lanes]),
                        (jnp.logical_and(is_corner, inner), corner_inner_ref.at[:, rows, lanes]),
                    ]
                    for chosen, source in sources:

                        @pl.when(chosen)
                        def _(source=source, f=f, a=a, j=j, slot=slot):
                            copy = pltpu.make_async_copy(
                                source,
                                held.at[:, f * 2 + a, pl.ds(j * SPOT, SPOT), lanes],
                                sems.at[slot, first // GROUP],
                            )
                            action(copy)

    for first in range(0, HEADS, GROUP):
        for_copies(first, lambda copy: copy.start())

    units = [(early, a) for early in range(2) for a in range(2)]
    frames = (1 - parity, parity)
    collected = [jnp.zeros((SPOT, HD), jnp.float32) for _ in units]
    for first in range(0, HEADS, GROUP):
        for_copies(first, lambda copy: copy.wait())
        work = [(h, u) for h in range(first, first + GROUP) for u in range(len(units))]
        scores = []
        for h, u in work:
            early, a = units[u]
            frame, lanes = frames[early], slice(h * HD, (h + 1) * HD)
            queries = q_ref[frame, a * SPOT : (a + 1) * SPOT, lanes]
            scores.append(contract_last(queries, held[0, frame * 2 + a, :, lanes]))
        peaks = [jnp.max(value, axis=-1, keepdims=True) for value in scores]
        weights = [
            jnp.exp2((value - peak) * EXP_SCALE).astype(jnp.bfloat16) for value, peak in zip(scores, peaks)
        ]
        for (h, u), weight, peak in zip(work, weights, peaks):
            early, a = units[u]
            frame, lanes = frames[early], slice(h * HD, (h + 1) * HD)
            tokens = slice(a * SPOT, (a + 1) * SPOT)
            summed = jnp.dot(
                weight, with_ones(held[1, frame * 2 + a, :, lanes]), preferred_element_type=jnp.float32
            )
            near_sum = near_sums[early][tokens, h : h + 1]
            far_peak = peak * EXP_SCALE
            top = jnp.maximum(near_sum, far_peak)
            near_scale, far_scale = jnp.exp2(near_sum - top), jnp.exp2(far_peak - top)
            total = near_scale + far_scale * summed[:, HD:]
            joined = near_scale * near_refs[early][tokens, lanes] + far_scale * summed[:, :HD]
            out_ref[early, tokens, lanes] = joined / total
            collected[u] = jnp.where(lane_index(SPOT) == h, top + jnp.log2(total), collected[u])
    for (early, a), value in zip(units, collected):
        sum_ref[early, a * SPOT : (a + 1) * SPOT, :] = value


def far_attention(members, far_frames, queries, buffers, near):
    tokens, features = queries.shape[1:]
    in_vmem = pl.BlockSpec(memory_space=pltpu.VMEM)
    in_specs = [pl.BlockSpec(memory_space=pltpu.SMEM), in_vmem]
    in_specs += [pl.BlockSpec(memory_space=pl.ANY)] * len(buffers) + [in_vmem] * len(near)
    return pl.pallas_call(
        functools.partial(far_kernel, members),
        out_shape=[
            jax.ShapeDtypeStruct((2, tokens, features), jnp.float32),
            jax.ShapeDtypeStruct((2, tokens, HD), jnp.float32),
        ],
        in_specs=in_specs,
        out_specs=[in_vmem] * 2,
        scratch_shapes=[
            pltpu.VMEM((2, 4, NFAR * SPOT, features), jnp.bfloat16),
            pltpu.SemaphoreType.DMA((4 * NFAR, HEADS // GROUP)),
        ],
        compiler_params=pltpu.CompilerParams(vmem_limit_bytes=VMEM_LIMIT),
        cost_estimate=kernel_cost(1),
    )(far_frames, queries, *buffers, *near)


def finish_kernel(sides, columns, early, own_ref, own_sum_ref, *refs):
    parts, refs = refs[:sides], refs[sides:]
    wa = lax.axis_index("wa")
    logs = [own_sum_ref[0]]
    for s in range(sides):
        value = join_sums(parts[s][:, HEADS * HD :])
        if columns > 2:
            value = jnp.where(wa < columns - 1 if s == 0 else wa > 0, value, NEGATIVE)
        logs.append(value)
    top = functools.reduce(jnp.maximum, logs)
    scales = [jnp.exp2(value - top) for value in logs]
    total = functools.reduce(jnp.add, scales)
    scales = [value / total for value in scales]
    if not early:
        parity = lax.axis_index("ta") % 2
        refs[1][1 - parity] = refs[0][...]
    for h in range(HEADS):
        lanes = slice(h * HD, (h + 1) * HD)
        joined = scales[0][:, h : h + 1] * own_ref[0, :, lanes]
        for s in range(sides):
            joined = joined + scales[1 + s][:, h : h + 1] * parts[s][:, lanes].astype(jnp.float32)
        if early:
            refs[0][:, lanes] = joined.astype(jnp.bfloat16)
        else:
            refs[1][parity, :, lanes] = joined.astype(jnp.bfloat16)


def finish(columns, own, own_sum, parts, early_out, cost):
    sides, rows = len(parts), 32
    frames, tokens, features = own.shape
    early = early_out is None
    at = 0 if early else 1
    in_specs = [
        pl.BlockSpec((1, rows, features), lambda i: (at, i, 0)),
        pl.BlockSpec((1, rows, HD), lambda i: (at, i, 0)),
    ]
    in_specs += [pl.BlockSpec((rows, features + HD), lambda i: (i, 0)) for _ in parts]
    one_frame = pl.BlockSpec((rows, features), lambda i: (i, 0))
    if early:
        extra, out_spec, out_shape = (), one_frame, (tokens, features)
    else:
        extra, out_spec = (early_out,), pl.BlockSpec((frames, rows, features), lambda i: (0, i, 0))
        in_specs.append(one_frame)
        out_shape = own.shape
    return pl.pallas_call(
        functools.partial(finish_kernel, sides, columns, early),
        out_shape=jax.ShapeDtypeStruct(out_shape, jnp.bfloat16),
        grid=(tokens // rows,),
        in_specs=in_specs,
        out_specs=out_spec,
        compiler_params=pltpu.CompilerParams(vmem_limit_bytes=VMEM_LIMIT),
        cost_estimate=kernel_cost(cost),
    )(own, own_sum, *parts, *extra)


def per_device(queries, keyvals, far_frames):
    shape = queries.shape
    frames, rows, columns, features = shape
    tokens = rows * columns
    ta_size, ha_size, wa_size = lax.axis_size("ta"), lax.axis_size("ha"), lax.axis_size("wa")
    queries = queries.reshape(frames, tokens, features)
    keyvals = keyvals.reshape(2, frames, tokens, features)

    core_pairs = [(i, i ^ 1) for i in range(ta_size)]
    cross_pairs = [(i, ta_size - 1 - i) for i in range(ta_size)]
    up = [(i, i + 1) for i in range(ha_size - 1)]
    down = [(i + 1, i) for i in range(ha_size - 1)]
    if wa_size == 2:
        ways = [([(0, 1), (1, 0)], [(0, 1), (1, 0)])]
    else:
        right = [(i, i + 1) for i in range(wa_size - 1)]
        left = [(i + 1, i) for i in range(wa_size - 1)]
        ways = [(right, left), (left, right)]
    tie = lax.optimization_barrier

    visitors = [lax.ppermute(queries, "wa", there) for there, _ in ways]
    core = lax.ppermute(keyvals, "ta", core_pairs)
    last_rows, first_rows, outer_last, outer_first, inner = cut(keyvals)
    top = lax.ppermute(last_rows, "ha", up)
    bottom = lax.ppermute(first_rows, "ha", down)
    cross_last = lax.ppermute(outer_last, "ta", cross_pairs)
    outer_first, core = tie((outer_first, core))
    cross_first = lax.ppermute(outer_first, "ta", cross_pairs)
    top, bottom, visitors, cross_first, cross_last = tie((top, bottom, visitors, cross_first, cross_last))
    core_top = lax.ppermute(top, "ta", core_pairs)
    core_bottom = lax.ppermute(bottom, "ta", core_pairs)
    inner, cross_first, cross_last, core_top, core_bottom = tie((inner, cross_first, cross_last, core_top, core_bottom))
    cross_top = lax.ppermute(cross_last, "ha", up)
    cross_bottom = lax.ppermute(cross_first, "ha", down)
    last = lax.ppermute(inner, "ta", cross_pairs)

    q_sides = visitors + [queries]
    early = near_attention(
        True, ha_size, keyvals, top, bottom, (core, core_top, core_bottom), q_sides, 1
    )
    early_parts = [lax.ppermute(early[s], "wa", back) for s, (_, back) in enumerate(ways)]
    cross_top, cross_bottom, _ = tie((cross_top, cross_bottom, early[0]))
    late = near_attention(
        False, ha_size, keyvals, top, bottom, (cross_first, cross_last, cross_top, cross_bottom), q_sides, LATE_COST
    )
    late_results, early_parts, cross_first, cross_last, last = tie(
        (late[: len(ways)], early_parts, cross_first, cross_last, last)
    )
    late_parts = [lax.ppermute(late_results[s], "wa", back) for s, (_, back) in enumerate(ways)]
    corner_first = lax.ppermute(cross_first, "ta", core_pairs)
    corner_last = lax.ppermute(cross_last, "ta", core_pairs)
    corner_inner = lax.ppermute(last, "ta", core_pairs)
    own, own_sum = far_attention(
        ta_size,
        far_frames,
        queries,
        (core, cross_first, cross_last, last, corner_first, corner_last, corner_inner),
        (early[-2], late[-2], early[-1], late[-1]),
    )
    out = finish(wa_size, own, own_sum, early_parts, None, FINISH_COST)
    out = finish(wa_size, own, own_sum, late_parts, out, 1)
    return out.reshape(shape)


def solution(mesh):
    placed = (P("ta", "ha", "wa", None), P(None, "ta", "ha", "wa", None), P("ta", "ha", "wa", None))
    return jax.shard_map(
        per_device, mesh=mesh, in_specs=placed, out_specs=P("ta", "ha", "wa", None), check_vma=False
    )
```

```python
import functools

import jax
import jax.numpy as jnp
from jax import lax
from jax.experimental import pallas as pl
from jax.experimental.pallas import tpu as pltpu
from jax.sharding import PartitionSpec as P

TILE = 8
HEADS = 16
HD = 128
NFAR = 2
SPOT = TILE * TILE
NEGATIVE = -1e30
EXP_SCALE = HD ** (-0.5) * 1.4426950408889634
VMEM_LIMIT = 16 * 1024 * 1024
GROUP = 4
FINISH_COST = 1
LATE_COST = 8 << 30


def contract_last(left, right):
    return lax.dot_general(left, right, (((1,), (1,)), ((), ())), preferred_element_type=jnp.float32)


def with_ones(values):
    return jnp.concatenate([values, jnp.ones_like(values)], axis=1)


def lane_index(rows):
    return lax.broadcasted_iota(jnp.int32, (rows, HD), 1)


def split_sums(value):
    high = value.astype(jnp.bfloat16).astype(jnp.float32)
    rest = value - high
    middle = rest.astype(jnp.bfloat16).astype(jnp.float32)
    low = rest - middle
    return (high + pltpu.roll(middle, HEADS, 1) + pltpu.roll(low, 2 * HEADS, 1)).astype(jnp.bfloat16)


def join_sums(value):
    terms = value.astype(jnp.float32)
    return terms + (pltpu.roll(terms, HD - HEADS, 1) + pltpu.roll(terms, HD - 2 * HEADS, 1))


def kernel_cost(flops):
    return pl.CostEstimate(flops=flops, bytes_accessed=1, transcendentals=0)


def cut_kernel(keyvals_ref, last_rows_ref, first_rows_ref, outer_last_ref, outer_first_ref, *refs):
    inner_keys_ref, inner_values_ref, sems = refs
    outer = lax.axis_index("ta") % 2
    first, last = pl.ds(0, SPOT), pl.ds(SPOT, SPOT)
    pieces = [
        (keyvals_ref.at[:, :, last], last_rows_ref),
        (keyvals_ref.at[:, :, first], first_rows_ref),
        (keyvals_ref.at[:, outer, last], outer_last_ref),
        (keyvals_ref.at[:, outer, first], outer_first_ref),
        (keyvals_ref.at[0, 1 - outer], inner_keys_ref),
        (keyvals_ref.at[1, 1 - outer], inner_values_ref),
    ]
    copies = [pltpu.make_async_copy(source, target, sems.at[i]) for i, (source, target) in enumerate(pieces)]
    for copy in copies:
        copy.start()
    for copy in copies:
        copy.wait()


def cut(keyvals):
    two, frames, tokens, features = keyvals.shape
    shapes = [(two, frames, SPOT, features)] * 2 + [(two, SPOT, features)] * 2 + [(tokens, features)] * 2
    return pl.pallas_call(
        cut_kernel,
        out_shape=[jax.ShapeDtypeStruct(shape, keyvals.dtype) for shape in shapes],
        in_specs=[pl.BlockSpec(memory_space=pl.ANY)],
        out_specs=[pl.BlockSpec(memory_space=pltpu.VMEM)] * 6,
        scratch_shapes=[pltpu.SemaphoreType.DMA((6,))],
        compiler_params=pltpu.CompilerParams(vmem_limit_bytes=VMEM_LIMIT),
        cost_estimate=kernel_cost(1),
    )(keyvals)


def near_kernel(sides, early, home, has_rows, own_ref, top_ref, bottom_ref, *refs):
    parity = lax.axis_index("ta") % 2
    ha = lax.axis_index("ha")
    valid = (ha > 0, ha < has_rows - 1)
    if early:
        ext_ref, ext_top_ref, ext_bottom_ref, refs = refs[0], refs[1], refs[2], refs[3:]
        frame = 1 - parity
    else:
        ext_first_ref, ext_last_ref, ext_top_ref, ext_bottom_ref, refs = refs[0], refs[1], refs[2], refs[3], refs[4:]
        frame = parity
    q_refs, out_refs, refs, log_ref = refs[:sides], refs[sides : 2 * sides], refs[2 * sides : -1], refs[-1]
    group = pl.program_id(0)
    half = sides * SPOT

    def middle(kind, lanes):
        parts = [own_ref[kind, 0, :, lanes], own_ref[kind, 1, :, lanes]]
        if early:
            parts.append(ext_ref[kind, parity, :, lanes])
        else:
            parts += [ext_first_ref[kind, :, lanes], ext_last_ref[kind, :, lanes]]
        return jnp.concatenate(parts, axis=0)

    def halo(a, kind, lanes):
        ref, ext = ((top_ref, ext_top_ref), (bottom_ref, ext_bottom_ref))[a]
        third = ext[kind, parity, :, lanes] if early else ext[kind, :, lanes]
        return jnp.concatenate([ref[kind, 0, :, lanes], ref[kind, 1, :, lanes], third], axis=0)

    members = [slice(i * HD, (i + 1) * HD) for i in range(GROUP)]
    scores = []
    for lanes in members:
        queries = [
            jnp.concatenate([ref[frame, a * SPOT : (a + 1) * SPOT, lanes] for ref in q_refs], axis=0) for a in range(2)
        ]
        near = contract_last(jnp.concatenate(queries, axis=0), middle(0, lanes))
        edges = [contract_last(queries[a], halo(a, 0, lanes)) for a in range(2)]
        scores.append([(near[a * half : (a + 1) * half], edges[a]) for a in range(2)])
    weights = []
    for pairs in scores:
        for a, (near, edge) in enumerate(pairs):
            best = functools.reduce(jnp.maximum, [near[:, i * HD : (i + 1) * HD] for i in range(3)])
            edge_best = jnp.maximum(edge[:, : 2 * SPOT], jnp.concatenate([edge[:, 2 * SPOT :]] * 2, axis=1))
            best = jnp.maximum(best, jnp.where(valid[a], edge_best, NEGATIVE))
            peak = jnp.max(best, axis=-1, keepdims=True)
            shift = jnp.where(valid[a], peak, -NEGATIVE)
            weights.append(
                (
                    peak,
                    jnp.exp2((near - peak) * EXP_SCALE).astype(jnp.bfloat16),
                    jnp.exp2((edge - shift) * EXP_SCALE).astype(jnp.bfloat16),
                )
            )
    peaks = [jnp.zeros((half, HD), jnp.float32) for _ in range(2)]
    totals = [jnp.ones((half, HD), jnp.float32) for _ in range(2)]
    for i, lanes in enumerate(members):
        mask = lane_index(half) == group * GROUP + i
        middle_values = with_ones(middle(1, lanes))
        for a in range(2):
            peak, near, edge = weights[2 * i + a]
            summed = jnp.dot(near, middle_values, preferred_element_type=jnp.float32)
            summed = summed + jnp.dot(edge, with_ones(halo(a, 1, lanes)), preferred_element_type=jnp.float32)
            total = summed[:, HD:]
            result = summed[:, :HD] / total
            peaks[a] = jnp.where(mask, peak, peaks[a])
            totals[a] = jnp.where(mask, total, totals[a])
            for s in range(sides):
                rows = slice(s * SPOT, (s + 1) * SPOT)
                at = pl.ds(pl.multiple_of((group * GROUP + i) * HD, HD), HD)
                out_refs[s][a * SPOT : (a + 1) * SPOT, at] = result[rows].astype(out_refs[s].dtype)

    @pl.when(group == 0)
    def _():
        log_ref[...] = jnp.zeros_like(log_ref)

    for a in range(2):
        log_sum = peaks[a] * EXP_SCALE + jnp.log2(totals[a])
        for s in range(sides):
            log_ref[s, a * SPOT : (a + 1) * SPOT, :] += log_sum[s * SPOT : (s + 1) * SPOT]

    @pl.when(group == pl.num_programs(0) - 1)
    def _():
        if home:
            refs[0][...] = log_ref[0]
        else:
            for s in range(sides):
                out_refs[s][:, HEADS * HD :] = split_sums(log_ref[s])


def near_attention(early, home, has_rows, own, top, bottom, third, queries, cost):
    sides = len(queries)
    tokens, features = queries[0].shape[1:]
    width = GROUP * HD
    operands = [own, top, bottom, *third, *queries]
    if home:
        outs = [jax.ShapeDtypeStruct((tokens, lanes), jnp.float32) for lanes in (features, HD)]
    else:
        outs = [jax.ShapeDtypeStruct((tokens, features + HD), jnp.bfloat16) for _ in queries]

    def lanes_of_group(value):
        lead = value.ndim - 1
        return pl.BlockSpec(value.shape[:-1] + (width,), lambda g: (0,) * lead + (g,))

    return pl.pallas_call(
        functools.partial(near_kernel, sides, early, home, has_rows),
        out_shape=outs,
        grid=(HEADS // GROUP,),
        in_specs=[lanes_of_group(value) for value in operands],
        out_specs=[pl.BlockSpec(out.shape, lambda g: (0, 0)) for out in outs],
        scratch_shapes=[pltpu.VMEM((sides, tokens, HD), jnp.float32)],
        compiler_params=pltpu.CompilerParams(vmem_limit_bytes=VMEM_LIMIT),
        cost_estimate=kernel_cost(cost),
    )(*operands)


def far_kernel(members, far_ref, q_ref, core_ref, cross_first_ref, cross_last_ref, *refs):
    last_refs, corner_first_ref, corner_last_ref, corner_inner_refs, refs = refs[:2], refs[2], refs[3], refs[4:6], refs[6:]
    near_refs, near_sums, out_ref, sum_ref, held, sems = refs[:2], refs[2:4], refs[4], refs[5], refs[6], refs[7]
    ta = lax.axis_index("ta")
    parity = ta % 2

    def tile_copy(source, kind, tile, j, slot, group):
        lanes = pl.ds(group * GROUP * HD, GROUP * HD)
        target = held.at[kind, tile, pl.ds(j * SPOT, SPOT), lanes]
        return pltpu.make_async_copy(source.at[:, lanes], target, sems.at[kind, slot, group])

    for f in range(2):
        for a in range(2):
            rows = pl.ds(a * SPOT, SPOT)
            by_rows = (cross_first_ref, cross_last_ref)[a], (corner_first_ref, corner_last_ref)[a]
            for j in range(NFAR):
                slot = (f * 2 + a) * NFAR + j
                wanted = far_ref[f, a, 0, j]
                owner, place = wanted // 2, wanted % 2
                inner = place != owner % 2
                is_core, is_cross = owner == ta + 1 - 2 * parity, owner == members - 1 - ta
                is_corner = jnp.logical_not(jnp.logical_or(is_core, is_cross))
                sources = [
                    (jnp.logical_and(is_core, place == 0), [core_ref.at[kind, 0, rows] for kind in range(2)]),
                    (jnp.logical_and(is_core, place == 1), [core_ref.at[kind, 1, rows] for kind in range(2)]),
                    (jnp.logical_and(is_cross, jnp.logical_not(inner)), [by_rows[0].at[kind] for kind in range(2)]),
                    (jnp.logical_and(is_cross, inner), [ref.at[rows] for ref in last_refs]),
                    (jnp.logical_and(is_corner, jnp.logical_not(inner)), [by_rows[1].at[kind] for kind in range(2)]),
                    (jnp.logical_and(is_corner, inner), [ref.at[rows] for ref in corner_inner_refs]),
                ]
                for chosen, pair in sources:

                    @pl.when(chosen)
                    def _(pair=pair, f=f, a=a, j=j, slot=slot):
                        for group in range(HEADS // GROUP):
                            for kind, source in enumerate(pair):
                                tile_copy(source, kind, f * 2 + a, j, slot, group).start()

    units = [(early, a) for early in range(2) for a in range(2)]
    frames = (1 - parity, parity)
    collected = [jnp.zeros((SPOT, HD), jnp.float32) for _ in units]
    for first in range(0, HEADS, GROUP):
        for slot in range(4 * NFAR):
            for kind in range(2):
                tile_copy(cross_first_ref.at[kind], kind, slot // NFAR, slot % NFAR, slot, first // GROUP).wait()
        work = [(h, u) for h in range(first, first + GROUP) for u in range(len(units))]
        scores = []
        for h, u in work:
            early, a = units[u]
            frame, lanes = frames[early], slice(h * HD, (h + 1) * HD)
            queries = q_ref[frame, a * SPOT : (a + 1) * SPOT, lanes]
            scores.append(contract_last(queries, held[0, frame * 2 + a, :, lanes]))
        peaks = [jnp.max(value, axis=-1, keepdims=True) for value in scores]
        weights = [
            jnp.exp2((value - peak) * EXP_SCALE).astype(jnp.bfloat16) for value, peak in zip(scores, peaks)
        ]
        for (h, u), weight, peak in zip(work, weights, peaks):
            early, a = units[u]
            frame, lanes = frames[early], slice(h * HD, (h + 1) * HD)
            tokens = slice(a * SPOT, (a + 1) * SPOT)
            summed = jnp.dot(
                weight, with_ones(held[1, frame * 2 + a, :, lanes]), preferred_element_type=jnp.float32
            )
            near_sum = near_sums[early][tokens, h : h + 1]
            far_peak = peak * EXP_SCALE
            top = jnp.maximum(near_sum, far_peak)
            near_scale, far_scale = jnp.exp2(near_sum - top), jnp.exp2(far_peak - top)
            total = near_scale + far_scale * summed[:, HD:]
            joined = near_scale * near_refs[early][tokens, lanes] + far_scale * summed[:, :HD]
            out_ref[early, tokens, lanes] = joined / total
            collected[u] = jnp.where(lane_index(SPOT) == h, top + jnp.log2(total), collected[u])
    for (early, a), value in zip(units, collected):
        sum_ref[early, a * SPOT : (a + 1) * SPOT, :] = value


def far_attention(members, far_frames, queries, buffers, near):
    tokens, features = queries.shape[1:]
    in_vmem = pl.BlockSpec(memory_space=pltpu.VMEM)
    in_specs = [pl.BlockSpec(memory_space=pltpu.SMEM), in_vmem]
    in_specs += [pl.BlockSpec(memory_space=pl.ANY)] * len(buffers) + [in_vmem] * len(near)
    return pl.pallas_call(
        functools.partial(far_kernel, members),
        out_shape=[
            jax.ShapeDtypeStruct((2, tokens, features), jnp.float32),
            jax.ShapeDtypeStruct((2, tokens, HD), jnp.float32),
        ],
        in_specs=in_specs,
        out_specs=[in_vmem] * 2,
        scratch_shapes=[
            pltpu.VMEM((2, 4, NFAR * SPOT, features), jnp.bfloat16),
            pltpu.SemaphoreType.DMA((2, 4 * NFAR, HEADS // GROUP)),
        ],
        compiler_params=pltpu.CompilerParams(vmem_limit_bytes=VMEM_LIMIT),
        cost_estimate=kernel_cost(1),
    )(far_frames, queries, *buffers, *near)


def finish_kernel(sides, columns, early, own_ref, own_sum_ref, *refs):
    parts, refs = refs[:sides], refs[sides:]
    wa = lax.axis_index("wa")
    logs = [own_sum_ref[0]]
    for s in range(sides):
        value = join_sums(parts[s][:, HEADS * HD :])
        if columns > 2:
            value = jnp.where(wa < columns - 1 if s == 0 else wa > 0, value, NEGATIVE)
        logs.append(value)
    top = functools.reduce(jnp.maximum, logs)
    scales = [jnp.exp2(value - top) for value in logs]
    total = functools.reduce(jnp.add, scales)
    scales = [value / total for value in scales]
    if not early:
        parity = lax.axis_index("ta") % 2
        refs[1][1 - parity] = refs[0][...]
    for h in range(HEADS):
        lanes = slice(h * HD, (h + 1) * HD)
        joined = scales[0][:, h : h + 1] * own_ref[0, :, lanes]
        for s in range(sides):
            joined = joined + scales[1 + s][:, h : h + 1] * parts[s][:, lanes].astype(jnp.float32)
        if early:
            refs[0][:, lanes] = joined.astype(jnp.bfloat16)
        else:
            refs[1][parity, :, lanes] = joined.astype(jnp.bfloat16)


def finish(columns, own, own_sum, parts, early_out, cost):
    sides, rows = len(parts), 32
    frames, tokens, features = own.shape
    early = early_out is None
    at = 0 if early else 1
    in_specs = [
        pl.BlockSpec((1, rows, features), lambda i: (at, i, 0)),
        pl.BlockSpec((1, rows, HD), lambda i: (at, i, 0)),
    ]
    in_specs += [pl.BlockSpec((rows, features + HD), lambda i: (i, 0)) for _ in parts]
    one_frame = pl.BlockSpec((rows, features), lambda i: (i, 0))
    if early:
        extra, out_spec, out_shape = (), one_frame, (tokens, features)
    else:
        extra, out_spec = (early_out,), pl.BlockSpec((frames, rows, features), lambda i: (0, i, 0))
        in_specs.append(one_frame)
        out_shape = own.shape
    return pl.pallas_call(
        functools.partial(finish_kernel, sides, columns, early),
        out_shape=jax.ShapeDtypeStruct(out_shape, jnp.bfloat16),
        grid=(tokens // rows,),
        in_specs=in_specs,
        out_specs=out_spec,
        compiler_params=pltpu.CompilerParams(vmem_limit_bytes=VMEM_LIMIT),
        cost_estimate=kernel_cost(cost),
    )(own, own_sum, *parts, *extra)


def per_device(queries, keyvals, far_frames):
    shape = queries.shape
    frames, rows, columns, features = shape
    tokens = rows * columns
    ta_size, ha_size, wa_size = lax.axis_size("ta"), lax.axis_size("ha"), lax.axis_size("wa")
    queries = queries.reshape(frames, tokens, features)
    keyvals = keyvals.reshape(2, frames, tokens, features)

    core_pairs = [(i, i ^ 1) for i in range(ta_size)]
    cross_pairs = [(i, ta_size - 1 - i) for i in range(ta_size)]
    up = [(i, i + 1) for i in range(ha_size - 1)]
    down = [(i + 1, i) for i in range(ha_size - 1)]
    if wa_size == 2:
        ways = [([(0, 1), (1, 0)], [(0, 1), (1, 0)])]
    else:
        right = [(i, i + 1) for i in range(wa_size - 1)]
        left = [(i + 1, i) for i in range(wa_size - 1)]
        ways = [(right, left), (left, right)]
    tie = lax.optimization_barrier

    core = lax.ppermute(keyvals, "ta", core_pairs)
    last_rows, first_rows, outer_last, outer_first, *inner = cut(keyvals)
    top = lax.ppermute(last_rows, "ha", up)
    bottom = lax.ppermute(first_rows, "ha", down)
    cross_last = lax.ppermute(outer_last, "ta", cross_pairs)
    outer_first, core, sent = tie((outer_first, core, queries))
    cross_first = lax.ppermute(outer_first, "ta", cross_pairs)
    visitors = [lax.ppermute(sent, "wa", there) for there, _ in ways]
    top, bottom, cross_first, cross_last, inner = tie((top, bottom, cross_first, cross_last, inner))
    core_top = lax.ppermute(top, "ta", core_pairs)
    core_bottom = lax.ppermute(bottom, "ta", core_pairs)
    cross_top = lax.ppermute(cross_last, "ha", up)
    cross_bottom = lax.ppermute(cross_first, "ha", down)
    last = [lax.ppermute(value, "ta", cross_pairs) for value in inner]

    early_third = (core, core_top, core_bottom)
    early = near_attention(True, False, ha_size, keyvals, top, bottom, early_third, visitors, 1)
    early_parts = [lax.ppermute(result, "wa", back) for result, (_, back) in zip(early, ways)]
    core_top, _ = tie((core_top, early[0]))
    early_third = (core, core_top, core_bottom)
    early_home = near_attention(True, True, ha_size, keyvals, top, bottom, early_third, [queries], 1)
    cross_top, cross_bottom, _ = tie((cross_top, cross_bottom, early_home[1]))
    late_third = (cross_first, cross_last, cross_top, cross_bottom)
    late = near_attention(False, False, ha_size, keyvals, top, bottom, late_third, visitors, LATE_COST)
    late_parts = [lax.ppermute(result, "wa", back) for result, (_, back) in zip(late, ways)]
    cross_top, _ = tie((cross_top, late[0]))
    late_third = (cross_first, cross_last, cross_top, cross_bottom)
    late_home = near_attention(False, True, ha_size, keyvals, top, bottom, late_third, [queries], 1)
    cross_first, cross_last, last, early_parts, _ = tie((cross_first, cross_last, last, early_parts, late_home[1]))
    corner_first = lax.ppermute(cross_first, "ta", core_pairs)
    corner_last = lax.ppermute(cross_last, "ta", core_pairs)
    corner_inner = [lax.ppermute(value, "ta", core_pairs) for value in last]
    own, own_sum = far_attention(
        ta_size,
        far_frames,
        queries,
        (core, cross_first, cross_last, *last, corner_first, corner_last, *corner_inner),
        (early_home[0], late_home[0], early_home[1], late_home[1]),
    )
    out = finish(wa_size, own, own_sum, early_parts, None, FINISH_COST)
    out = finish(wa_size, own, own_sum, late_parts, out, 1)
    return out.reshape(shape)


def solution(mesh):
    placed = (P("ta", "ha", "wa", None), P(None, "ta", "ha", "wa", None), P("ta", "ha", "wa", None))
    return jax.shard_map(
        per_device, mesh=mesh, in_specs=placed, out_specs=P("ta", "ha", "wa", None), check_vma=False
    )
```

```python
import functools

import jax
import jax.numpy as jnp
from jax import lax
from jax.experimental import pallas as pl
from jax.experimental.pallas import tpu as pltpu
from jax.sharding import PartitionSpec as P

TILE = 8
HEADS = 16
HD = 128
NFAR = 2
SPOT = TILE * TILE
NEGATIVE = -1e30
EXP_SCALE = HD ** (-0.5) * 1.4426950408889634
VMEM_LIMIT = 16 * 1024 * 1024
GROUP = 4
FINISH_COST = 1
LATE_COST = 8 << 30


def contract_last(left, right):
    return lax.dot_general(left, right, (((1,), (1,)), ((), ())), preferred_element_type=jnp.float32)


def lane_index(rows):
    return lax.broadcasted_iota(jnp.int32, (rows, HD), 1)


def split_sums(value):
    high = value.astype(jnp.bfloat16).astype(jnp.float32)
    rest = value - high
    middle = rest.astype(jnp.bfloat16).astype(jnp.float32)
    low = rest - middle
    return (high + pltpu.roll(middle, HEADS, 1) + pltpu.roll(low, 2 * HEADS, 1)).astype(jnp.bfloat16)


def join_sums(value):
    terms = value.astype(jnp.float32)
    return terms + (pltpu.roll(terms, HD - HEADS, 1) + pltpu.roll(terms, HD - 2 * HEADS, 1))


def kernel_cost(flops):
    return pl.CostEstimate(flops=flops, bytes_accessed=1, transcendentals=0)


def cut_kernel(keyvals_ref, last_rows_ref, first_rows_ref, outer_last_ref, outer_first_ref, *refs):
    inner_last_ref, inner_first_ref, sems = refs
    outer = lax.axis_index("ta") % 2
    first, last = pl.ds(0, SPOT), pl.ds(SPOT, SPOT)
    pieces = [
        (keyvals_ref.at[:, :, last], last_rows_ref),
        (keyvals_ref.at[:, :, first], first_rows_ref),
        (keyvals_ref.at[:, outer, last], outer_last_ref),
        (keyvals_ref.at[:, outer, first], outer_first_ref),
        (keyvals_ref.at[:, 1 - outer, last], inner_last_ref),
        (keyvals_ref.at[:, 1 - outer, first], inner_first_ref),
    ]
    copies = [pltpu.make_async_copy(source, target, sems.at[i]) for i, (source, target) in enumerate(pieces)]
    for copy in copies:
        copy.start()
    for copy in copies:
        copy.wait()


def cut(keyvals):
    two, frames, tokens, features = keyvals.shape
    shapes = [(two, frames, SPOT, features)] * 2 + [(two, SPOT, features)] * 4
    return pl.pallas_call(
        cut_kernel,
        out_shape=[jax.ShapeDtypeStruct(shape, keyvals.dtype) for shape in shapes],
        in_specs=[pl.BlockSpec(memory_space=pl.ANY)],
        out_specs=[pl.BlockSpec(memory_space=pltpu.VMEM)] * 6,
        scratch_shapes=[pltpu.SemaphoreType.DMA((6,))],
        compiler_params=pltpu.CompilerParams(vmem_limit_bytes=VMEM_LIMIT),
        cost_estimate=kernel_cost(1),
    )(keyvals)


def near_kernel(sides, home, early, has_rows, own_ref, top_ref, bottom_ref, *refs):
    parity = lax.axis_index("ta") % 2
    ha = lax.axis_index("ha")
    valid = (ha > 0, ha < has_rows - 1)
    if early:
        ext_ref, ext_top_ref, ext_bottom_ref, refs = refs[0], refs[1], refs[2], refs[3:]
        frame = 1 - parity
    else:
        ext_first_ref, ext_last_ref, ext_top_ref, ext_bottom_ref, refs = refs[0], refs[1], refs[2], refs[3], refs[4:]
        frame = parity
    count = sides + home
    q_refs, out_refs, peak_ref, total_ref = refs[:count], refs[count:-2], refs[-2], refs[-1]
    group = pl.program_id(0)
    half = count * SPOT

    def middle(kind, lanes):
        parts = [own_ref[kind, 0, :, lanes], own_ref[kind, 1, :, lanes]]
        if early:
            parts.append(ext_ref[kind, parity, :, lanes])
        else:
            parts += [ext_first_ref[kind, :, lanes], ext_last_ref[kind, :, lanes]]
        return jnp.concatenate(parts, axis=0)

    def halo(a, kind, lanes):
        ref, ext = ((top_ref, ext_top_ref), (bottom_ref, ext_bottom_ref))[a]
        third = ext[kind, parity, :, lanes] if early else ext[kind, :, lanes]
        return jnp.concatenate([ref[kind, 0, :, lanes], ref[kind, 1, :, lanes], third], axis=0)

    members = [slice(i * HD, (i + 1) * HD) for i in range(GROUP)]
    scores = []
    for lanes in members:
        queries = [
            jnp.concatenate([ref[frame, a * SPOT : (a + 1) * SPOT, lanes] for ref in q_refs], axis=0) for a in range(2)
        ]
        near = contract_last(jnp.concatenate(queries, axis=0), middle(0, lanes))
        edges = [contract_last(queries[a], halo(a, 0, lanes)) for a in range(2)]
        scores.append([(near[a * half : (a + 1) * half], edges[a]) for a in range(2)])
    weights = []
    for pairs in scores:
        for a, (near, edge) in enumerate(pairs):
            best = functools.reduce(jnp.maximum, [near[:, i * HD : (i + 1) * HD] for i in range(3)])
            edge_best = jnp.maximum(edge[:, : 2 * SPOT], jnp.concatenate([edge[:, 2 * SPOT :]] * 2, axis=1))
            best = jnp.maximum(best, jnp.where(valid[a], edge_best, NEGATIVE))
            peak = jnp.max(best, axis=-1, keepdims=True)
            shift = jnp.where(valid[a], peak, -NEGATIVE)
            near = jnp.exp2((near - peak) * EXP_SCALE)
            edge = jnp.exp2((edge - shift) * EXP_SCALE)
            total = functools.reduce(jnp.add, [near[:, i * HD : (i + 1) * HD] for i in range(3)] + [edge[:, :HD]])
            total = jnp.sum(total, axis=-1, keepdims=True) + jnp.sum(edge[:, HD:], axis=-1, keepdims=True)
            weights.append((peak, total, near.astype(jnp.bfloat16), edge.astype(jnp.bfloat16)))
    peaks = [jnp.zeros((half, HD), jnp.float32) for _ in range(2)]
    totals = [jnp.zeros((half, HD), jnp.float32) for _ in range(2)]
    for i, lanes in enumerate(members):
        mask = lane_index(half) == group * GROUP + i
        at = pl.ds(pl.multiple_of((group * GROUP + i) * HD, HD), HD)
        middle_values = middle(1, lanes)
        for a in range(2):
            peak, total, near, edge = weights[2 * i + a]
            summed = jnp.dot(near, middle_values, preferred_element_type=jnp.float32)
            summed = summed + jnp.dot(edge, halo(a, 1, lanes), preferred_element_type=jnp.float32)
            peaks[a] = jnp.where(mask, peak, peaks[a])
            totals[a] = jnp.where(mask, total, totals[a])
            inverse = 1.0 / total
            for s in range(count):
                rows = slice(s * SPOT, (s + 1) * SPOT)
                result = summed[rows]
                if s < sides:
                    result = result * inverse[rows]
                out_refs[s][a * SPOT : (a + 1) * SPOT, at] = result.astype(out_refs[s].dtype)

    @pl.when(group == 0)
    def _():
        peak_ref[...] = jnp.zeros_like(peak_ref)
        total_ref[...] = jnp.zeros_like(total_ref)

    for a in range(2):
        for s in range(count):
            rows = slice(s * SPOT, (s + 1) * SPOT)
            peak_ref[s, a * SPOT : (a + 1) * SPOT, :] += peaks[a][rows] * EXP_SCALE
            total_ref[s, a * SPOT : (a + 1) * SPOT, :] += totals[a][rows]

    @pl.when(group == pl.num_programs(0) - 1)
    def _():
        for s in range(sides):
            heads = lane_index(2 * SPOT) < HEADS
            out_refs[s][:, HEADS * HD :] = split_sums(
                jnp.where(heads, peak_ref[s] + jnp.log2(jnp.where(heads, total_ref[s], 1.0)), 0.0)
            )
        if home:
            out_refs[sides + 1][...] = peak_ref[sides]
            out_refs[sides + 2][...] = total_ref[sides]


def near_attention(early, has_rows, own, top, bottom, third, visitors, queries, cost):
    home = len(queries)
    tokens, features = own.shape[2:]
    width = GROUP * HD
    operands = [own, top, bottom, *third, *visitors, *queries]
    outs = [jax.ShapeDtypeStruct((tokens, features + HD), jnp.bfloat16) for _ in visitors]
    for _ in queries:
        outs += [jax.ShapeDtypeStruct((tokens, lanes), jnp.float32) for lanes in (features, HD, HD)]

    def lanes_of_group(value):
        lead = value.ndim - 1
        return pl.BlockSpec(value.shape[:-1] + (width,), lambda g: (0,) * lead + (g,))

    return pl.pallas_call(
        functools.partial(near_kernel, len(visitors), home, early, has_rows),
        out_shape=outs,
        grid=(HEADS // GROUP,),
        in_specs=[lanes_of_group(value) for value in operands],
        out_specs=[pl.BlockSpec(out.shape, lambda g: (0, 0)) for out in outs],
        scratch_shapes=[pltpu.VMEM((len(visitors) + home, tokens, HD), jnp.float32)] * 2,
        compiler_params=pltpu.CompilerParams(vmem_limit_bytes=VMEM_LIMIT),
        cost_estimate=kernel_cost(cost),
    )(*operands)


def far_kernel(members, far_ref, q_ref, core_ref, *refs):
    cross, cross_inner, corner, corner_inner = refs[:2], refs[2:4], refs[4:6], refs[6:8]
    near_refs, (out_ref, peak_ref, total_ref, held, sems) = (refs[8:11], refs[11:14]), refs[14:]
    ta = lax.axis_index("ta")
    parity = ta % 2

    def tile_copy(source, tile, j, slot, group):
        lanes = pl.ds(group * GROUP * HD, GROUP * HD)
        target = held.at[:, tile, pl.ds(j * SPOT, SPOT), lanes]
        return pltpu.make_async_copy(source.at[:, :, lanes], target, sems.at[slot, group])

    for f in range(2):
        for a in range(2):
            rows = pl.ds(a * SPOT, SPOT)
            for j in range(NFAR):
                slot = (f * 2 + a) * NFAR + j
                wanted = far_ref[f, a, 0, j]
                owner, place = wanted // 2, wanted % 2
                inner = place != owner % 2
                is_core, is_cross = owner == ta + 1 - 2 * parity, owner == members - 1 - ta
                is_corner = jnp.logical_not(jnp.logical_or(is_core, is_cross))
                sources = [
                    (jnp.logical_and(is_core, place == 0), core_ref.at[:, 0, rows]),
                    (jnp.logical_and(is_core, place == 1), core_ref.at[:, 1, rows]),
                    (jnp.logical_and(is_cross, jnp.logical_not(inner)), cross[a]),
                    (jnp.logical_and(is_cross, inner), cross_inner[a]),
                    (jnp.logical_and(is_corner, jnp.logical_not(inner)), corner[a]),
                    (jnp.logical_and(is_corner, inner), corner_inner[a]),
                ]
                for chosen, source in sources:

                    @pl.when(chosen)
                    def _(source=source, f=f, a=a, j=j, slot=slot):
                        for group in range(HEADS // GROUP):
                            tile_copy(source, f * 2 + a, j, slot, group).start()

    units = [(early, a) for early in range(2) for a in range(2)]
    frames = (1 - parity, parity)
    collected = [(jnp.zeros((SPOT, HD), jnp.float32), jnp.zeros((SPOT, HD), jnp.float32)) for _ in units]
    for first in range(0, HEADS, GROUP):
        for slot in range(4 * NFAR):
            tile_copy(cross[0], slot // NFAR, slot % NFAR, slot, first // GROUP).wait()
        work = [(h, u) for h in range(first, first + GROUP) for u in range(len(units))]
        scores = []
        for h, u in work:
            early, a = units[u]
            frame, lanes = frames[early], slice(h * HD, (h + 1) * HD)
            queries = q_ref[frame, a * SPOT : (a + 1) * SPOT, lanes]
            scores.append(contract_last(queries, held[0, frame * 2 + a, :, lanes]))
        weights = []
        for (h, u), value in zip(work, scores):
            early, a = units[u]
            near_peak = near_refs[early][1][a * SPOT : (a + 1) * SPOT, h : h + 1]
            value = value * EXP_SCALE
            peak = jnp.maximum(jnp.max(value, axis=-1, keepdims=True), near_peak)
            value = jnp.exp2(value - peak)
            total = jnp.sum(value, axis=-1, keepdims=True)
            weights.append((peak, jnp.exp2(near_peak - peak), total, value.astype(jnp.bfloat16)))
        for (h, u), (peak, near_scale, total, weight) in zip(work, weights):
            early, a = units[u]
            frame, lanes, tokens = frames[early], slice(h * HD, (h + 1) * HD), slice(a * SPOT, (a + 1) * SPOT)
            summed = jnp.dot(weight, held[1, frame * 2 + a, :, lanes], preferred_element_type=jnp.float32)
            total = total + near_scale * near_refs[early][2][tokens, h : h + 1]
            out_ref[early, tokens, lanes] = summed + near_scale * near_refs[early][0][tokens, lanes]
            mask = lane_index(SPOT) == h
            collected[u] = jnp.where(mask, peak, collected[u][0]), jnp.where(mask, total, collected[u][1])
    for (early, a), (peak, total) in zip(units, collected):
        peak_ref[early, a * SPOT : (a + 1) * SPOT, :] = peak
        total_ref[early, a * SPOT : (a + 1) * SPOT, :] = total


def far_attention(members, far_frames, queries, buffers, near):
    tokens, features = queries.shape[1:]
    in_vmem = pl.BlockSpec(memory_space=pltpu.VMEM)
    in_specs = [pl.BlockSpec(memory_space=pltpu.SMEM), in_vmem]
    in_specs += [pl.BlockSpec(memory_space=pl.ANY)] * len(buffers) + [in_vmem] * len(near)
    return pl.pallas_call(
        functools.partial(far_kernel, members),
        out_shape=[jax.ShapeDtypeStruct((2, tokens, lanes), jnp.float32) for lanes in (features, HD, HD)],
        in_specs=in_specs,
        out_specs=[in_vmem] * 3,
        scratch_shapes=[
            pltpu.VMEM((2, 4, NFAR * SPOT, features), jnp.bfloat16),
            pltpu.SemaphoreType.DMA((4 * NFAR, HEADS // GROUP)),
        ],
        compiler_params=pltpu.CompilerParams(vmem_limit_bytes=VMEM_LIMIT),
        cost_estimate=kernel_cost(1),
    )(far_frames, queries, *buffers, *near)


def finish_kernel(sides, columns, early, own_ref, own_peak_ref, own_total_ref, *refs):
    parts, refs = refs[:sides], refs[sides:]
    wa = lax.axis_index("wa")
    logs = [own_peak_ref[0]]
    for s in range(sides):
        value = join_sums(parts[s][:, HEADS * HD :])
        if columns > 2:
            value = jnp.where(wa < columns - 1 if s == 0 else wa > 0, value, NEGATIVE)
        logs.append(value)
    top = functools.reduce(jnp.maximum, logs)
    scales = [jnp.exp2(value - top) for value in logs]
    total = functools.reduce(jnp.add, [scales[0] * own_total_ref[0]] + scales[1:])
    scales = [value / total for value in scales]
    if not early:
        parity = lax.axis_index("ta") % 2
        refs[1][1 - parity] = refs[0][...]
    for h in range(HEADS):
        lanes = slice(h * HD, (h + 1) * HD)
        joined = scales[0][:, h : h + 1] * own_ref[0, :, lanes]
        for s in range(sides):
            joined = joined + scales[1 + s][:, h : h + 1] * parts[s][:, lanes].astype(jnp.float32)
        if early:
            refs[0][:, lanes] = joined.astype(jnp.bfloat16)
        else:
            refs[1][parity, :, lanes] = joined.astype(jnp.bfloat16)


def finish(columns, own, parts, early_out, cost):
    sides, rows = len(parts), 32
    frames, tokens, features = own[0].shape
    early = early_out is None
    at = 0 if early else 1
    in_specs = [
        pl.BlockSpec((1, rows, features), lambda i: (at, i, 0)),
        pl.BlockSpec((1, rows, HD), lambda i: (at, i, 0)),
        pl.BlockSpec((1, rows, HD), lambda i: (at, i, 0)),
    ]
    in_specs += [pl.BlockSpec((rows, features + HD), lambda i: (i, 0)) for _ in parts]
    one_frame = pl.BlockSpec((rows, features), lambda i: (i, 0))
    if early:
        extra, out_spec, out_shape = (), one_frame, (tokens, features)
    else:
        extra, out_spec = (early_out,), pl.BlockSpec((frames, rows, features), lambda i: (0, i, 0))
        in_specs.append(one_frame)
        out_shape = own[0].shape
    return pl.pallas_call(
        functools.partial(finish_kernel, sides, columns, early),
        out_shape=jax.ShapeDtypeStruct(out_shape, jnp.bfloat16),
        grid=(tokens // rows,),
        in_specs=in_specs,
        out_specs=out_spec,
        compiler_params=pltpu.CompilerParams(vmem_limit_bytes=VMEM_LIMIT),
        cost_estimate=kernel_cost(cost),
    )(*own, *parts, *extra)


def per_device(queries, keyvals, far_frames):
    shape = queries.shape
    frames, rows, columns, features = shape
    tokens = rows * columns
    ta_size, ha_size, wa_size = lax.axis_size("ta"), lax.axis_size("ha"), lax.axis_size("wa")
    queries = queries.reshape(frames, tokens, features)
    keyvals = keyvals.reshape(2, frames, tokens, features)

    core_pairs = [(i, i ^ 1) for i in range(ta_size)]
    cross_pairs = [(i, ta_size - 1 - i) for i in range(ta_size)]
    up = [(i, i + 1) for i in range(ha_size - 1)]
    down = [(i + 1, i) for i in range(ha_size - 1)]
    if wa_size == 2:
        ways = [([(0, 1), (1, 0)], [(0, 1), (1, 0)])]
    else:
        right = [(i, i + 1) for i in range(wa_size - 1)]
        left = [(i + 1, i) for i in range(wa_size - 1)]
        ways = [(right, left), (left, right)]
    tie = lax.optimization_barrier

    core = lax.ppermute(keyvals, "ta", core_pairs)
    last_rows, first_rows, outer_last, outer_first, *inner = cut(keyvals)
    top = lax.ppermute(last_rows, "ha", up)
    bottom = lax.ppermute(first_rows, "ha", down)
    cross_last = lax.ppermute(outer_last, "ta", cross_pairs)
    outer_first, core, sent = tie((outer_first, core, queries))
    cross_first = lax.ppermute(outer_first, "ta", cross_pairs)
    visitors = [lax.ppermute(sent, "wa", there) for there, _ in ways]
    top, bottom, cross_first, cross_last, inner = tie((top, bottom, cross_first, cross_last, inner))
    core_top = lax.ppermute(top, "ta", core_pairs)
    core_bottom = lax.ppermute(bottom, "ta", core_pairs)
    cross_top = lax.ppermute(cross_last, "ha", up)
    cross_bottom = lax.ppermute(cross_first, "ha", down)
    inner_last, inner_first = [lax.ppermute(value, "ta", cross_pairs) for value in inner]

    early_third = (core, core_top, core_bottom)
    early = near_attention(True, ha_size, keyvals, top, bottom, early_third, visitors, [], 1)
    early_parts = [lax.ppermute(result, "wa", back) for result, (_, back) in zip(early, ways)]
    core_top, _ = tie((core_top, early[0]))
    early_third = (core, core_top, core_bottom)
    early_home = near_attention(True, ha_size, keyvals, top, bottom, early_third, [], [queries], 1)
    cross_top, cross_bottom, _ = tie((cross_top, cross_bottom, early_home[1]))
    late_third = (cross_first, cross_last, cross_top, cross_bottom)
    late = near_attention(False, ha_size, keyvals, top, bottom, late_third, visitors, [queries], LATE_COST)
    late_parts = [lax.ppermute(result, "wa", back) for result, (_, back) in zip(late, ways)]
    frames_here = (cross_first, cross_last, inner_first, inner_last)
    frames_here, early_parts, _ = tie((frames_here, early_parts, late[0]))
    corner = [lax.ppermute(value, "ta", core_pairs) for value in frames_here]
    buffers = (core, *frames_here, *corner)
    own = far_attention(ta_size, far_frames, queries, buffers, (*early_home, *late[-3:]))
    out = finish(wa_size, own, early_parts, None, FINISH_COST)
    out = finish(wa_size, own, late_parts, out, 1)
    return out.reshape(shape)


def solution(mesh):
    placed = (P("ta", "ha", "wa", None), P(None, "ta", "ha", "wa", None), P("ta", "ha", "wa", None))
    return jax.shard_map(
        per_device, mesh=mesh, in_specs=placed, out_specs=P("ta", "ha", "wa", None), check_vma=False
    )
```

```python
import functools

import jax
import jax.numpy as jnp
from jax import lax
from jax.experimental import pallas as pl
from jax.experimental.pallas import tpu as pltpu
from jax.sharding import PartitionSpec as P

TILE = 8
HEADS = 16
HD = 128
NFAR = 2
SPOT = TILE * TILE
NEGATIVE = -1e30
EXP_SCALE = HD ** (-0.5) * 1.4426950408889634
VMEM_LIMIT = 16 * 1024 * 1024
GROUP = 4
FINISH_COST = 1
LATE_COST = 4 << 30


def contract_last(left, right):
    return lax.dot_general(left, right, (((1,), (1,)), ((), ())), preferred_element_type=jnp.float32)


def with_ones(values):
    return jnp.concatenate([values, jnp.ones_like(values)], axis=1)


def lane_index(rows):
    return lax.broadcasted_iota(jnp.int32, (rows, HD), 1)


def split_sums(value):
    high = value.astype(jnp.bfloat16).astype(jnp.float32)
    rest = value - high
    middle = rest.astype(jnp.bfloat16).astype(jnp.float32)
    low = rest - middle
    return (high + pltpu.roll(middle, HEADS, 1) + pltpu.roll(low, 2 * HEADS, 1)).astype(jnp.bfloat16)


def join_sums(value):
    terms = value.astype(jnp.float32)
    return terms + (pltpu.roll(terms, HD - HEADS, 1) + pltpu.roll(terms, HD - 2 * HEADS, 1))


def kernel_cost(flops):
    return pl.CostEstimate(flops=flops, bytes_accessed=1, transcendentals=0)


def cut_kernel(keyvals_ref, last_rows_ref, first_rows_ref, outer_last_ref, outer_first_ref, inner_ref, sems):
    outer = lax.axis_index("ta") % 2
    first, last = pl.ds(0, SPOT), pl.ds(SPOT, SPOT)
    pieces = [
        (keyvals_ref.at[:, :, last], last_rows_ref),
        (keyvals_ref.at[:, :, first], first_rows_ref),
        (keyvals_ref.at[:, outer, last], outer_last_ref),
        (keyvals_ref.at[:, outer, first], outer_first_ref),
        (keyvals_ref.at[:, 1 - outer], inner_ref),
    ]
    copies = [pltpu.make_async_copy(source, target, sems.at[i]) for i, (source, target) in enumerate(pieces)]
    for copy in copies:
        copy.start()
    for copy in copies:
        copy.wait()


def cut(keyvals):
    two, frames, tokens, features = keyvals.shape
    shapes = [(two, frames, SPOT, features)] * 2 + [(two, SPOT, features)] * 2 + [(two, tokens, features)]
    return pl.pallas_call(
        cut_kernel,
        out_shape=[jax.ShapeDtypeStruct(shape, keyvals.dtype) for shape in shapes],
        in_specs=[pl.BlockSpec(memory_space=pl.ANY)],
        out_specs=[pl.BlockSpec(memory_space=pltpu.VMEM)] * 5,
        scratch_shapes=[pltpu.SemaphoreType.DMA((5,))],
        compiler_params=pltpu.CompilerParams(vmem_limit_bytes=VMEM_LIMIT),
        cost_estimate=kernel_cost(1),
    )(keyvals)


def inner_rows_kernel(top_ref, bottom_ref, out_top_ref, out_bottom_ref, sems):
    inner = 1 - lax.axis_index("ta") % 2
    pairs = ((top_ref, out_top_ref), (bottom_ref, out_bottom_ref))
    copies = [pltpu.make_async_copy(ref.at[:, inner], out, sems.at[i]) for i, (ref, out) in enumerate(pairs)]
    for copy in copies:
        copy.start()
    for copy in copies:
        copy.wait()


def inner_rows(top, bottom):
    shape = jax.ShapeDtypeStruct((top.shape[0],) + top.shape[2:], top.dtype)
    in_vmem = pl.BlockSpec(memory_space=pltpu.VMEM)
    return pl.pallas_call(
        inner_rows_kernel,
        out_shape=[shape] * 2,
        in_specs=[in_vmem] * 2,
        out_specs=[in_vmem] * 2,
        scratch_shapes=[pltpu.SemaphoreType.DMA((2,))],
        compiler_params=pltpu.CompilerParams(vmem_limit_bytes=VMEM_LIMIT),
        cost_estimate=kernel_cost(1),
    )(top, bottom)


def near_kernel(sides, home, early, has_rows, own_ref, top_ref, bottom_ref, *refs):
    parity = lax.axis_index("ta") % 2
    ha = lax.axis_index("ha")
    valid = (ha > 0, ha < has_rows - 1)
    if early:
        ext_ref, ext_top_ref, ext_bottom_ref, refs = refs[0], refs[1], refs[2], refs[3:]
        frame = 1 - parity
    else:
        ext_first_ref, ext_last_ref, ext_top_ref, ext_bottom_ref, refs = refs[0], refs[1], refs[2], refs[3], refs[4:]
        frame = parity
    count = sides + home
    q_refs, out_refs = refs[:count], refs[count:]
    half = count * SPOT

    def middle(kind, lanes):
        parts = [own_ref[kind, 0, :, lanes], own_ref[kind, 1, :, lanes]]
        if early:
            parts.append(ext_ref[kind, parity, :, lanes])
        else:
            parts += [ext_first_ref[kind, :, lanes], ext_last_ref[kind, :, lanes]]
        return jnp.concatenate(parts, axis=0)

    def halo(a, kind, lanes):
        ref, ext = ((top_ref, ext_top_ref), (bottom_ref, ext_bottom_ref))[a]
        return jnp.concatenate([ref[kind, 0, :, lanes], ref[kind, 1, :, lanes], ext[kind, :, lanes]], axis=0)

    peaks = [jnp.zeros((half, HD), jnp.float32) for _ in range(2)]
    totals = [jnp.ones((half, HD), jnp.float32) for _ in range(2)]
    for first in range(0, HEADS, GROUP):
        members = [slice(h * HD, (h + 1) * HD) for h in range(first, first + GROUP)]
        scores = []
        for lanes in members:
            queries = [
                jnp.concatenate([ref[frame, a * SPOT : (a + 1) * SPOT, lanes] for ref in q_refs], axis=0)
                for a in range(2)
            ]
            near = contract_last(jnp.concatenate(queries, axis=0), middle(0, lanes))
            edges = [contract_last(queries[a], halo(a, 0, lanes)) for a in range(2)]
            scores.append([(near[a * half : (a + 1) * half], edges[a]) for a in range(2)])
        weights = []
        for pairs in scores:
            for a, (near, edge) in enumerate(pairs):
                best = functools.reduce(jnp.maximum, [near[:, i * HD : (i + 1) * HD] for i in range(3)])
                edge_best = jnp.maximum(edge[:, : 2 * SPOT], jnp.concatenate([edge[:, 2 * SPOT :]] * 2, axis=1))
                best = jnp.maximum(best, jnp.where(valid[a], edge_best, NEGATIVE))
                peak = jnp.max(best, axis=-1, keepdims=True)
                shift = jnp.where(valid[a], peak, -NEGATIVE)
                near = jnp.exp2((near - peak) * EXP_SCALE).astype(jnp.bfloat16)
                edge = jnp.exp2((edge - shift) * EXP_SCALE).astype(jnp.bfloat16)
                weights.append((peak, near, edge))
        for i, lanes in enumerate(members):
            mask = lane_index(half) == first + i
            middle_values = with_ones(middle(1, lanes))
            for a in range(2):
                peak, near, edge = weights[2 * i + a]
                summed = jnp.dot(near, middle_values, preferred_element_type=jnp.float32)
                summed = summed + jnp.dot(edge, with_ones(halo(a, 1, lanes)), preferred_element_type=jnp.float32)
                total = summed[:, HD:]
                peaks[a] = jnp.where(mask, peak, peaks[a])
                totals[a] = jnp.where(mask, total, totals[a])
                for s in range(count):
                    rows = slice(s * SPOT, (s + 1) * SPOT)
                    result = summed[rows, :HD]
                    if s < sides:
                        result = result / total[rows]
                    out_refs[s][a * SPOT : (a + 1) * SPOT, lanes] = result.astype(out_refs[s].dtype)
    for a in range(2):
        tokens = slice(a * SPOT, (a + 1) * SPOT)
        for s in range(count):
            rows = slice(s * SPOT, (s + 1) * SPOT)
            if s < sides:
                log_sum = peaks[a][rows] * EXP_SCALE + jnp.log2(totals[a][rows])
                out_refs[s][tokens, HEADS * HD :] = split_sums(log_sum)
            else:
                out_refs[s + 1][tokens, :] = peaks[a][rows] * EXP_SCALE
                out_refs[s + 2][tokens, :] = totals[a][rows]


def near_attention(early, has_rows, own, top, bottom, third, visitors, queries, cost):
    tokens, features = own.shape[2:]
    operands = [own, top, bottom, *third, *visitors, *queries]
    outs = [jax.ShapeDtypeStruct((tokens, features + HD), jnp.bfloat16) for _ in visitors]
    for _ in queries:
        outs += [jax.ShapeDtypeStruct((tokens, lanes), jnp.float32) for lanes in (features, HD, HD)]
    in_vmem = pl.BlockSpec(memory_space=pltpu.VMEM)
    return pl.pallas_call(
        functools.partial(near_kernel, len(visitors), len(queries), early, has_rows),
        out_shape=outs,
        in_specs=[in_vmem] * len(operands),
        out_specs=[in_vmem] * len(outs),
        compiler_params=pltpu.CompilerParams(vmem_limit_bytes=VMEM_LIMIT),
        cost_estimate=kernel_cost(cost),
    )(*operands)


def far_kernel(members, far_ref, q_ref, core_ref, *refs):
    cross, cross_inner, corner, corner_inner = refs[:2], refs[2], refs[3:5], refs[5]
    near_refs, (out_ref, peak_ref, total_ref, held, sems) = (refs[6:9], refs[9:12]), refs[12:]
    ta = lax.axis_index("ta")
    parity = ta % 2

    def tile_copy(source, tile, j, slot, group):
        lanes = pl.ds(group * GROUP * HD, GROUP * HD)
        target = held.at[:, tile, pl.ds(j * SPOT, SPOT), lanes]
        return pltpu.make_async_copy(source.at[:, :, lanes], target, sems.at[slot, group])

    for f in range(2):
        for a in range(2):
            rows = pl.ds(a * SPOT, SPOT)
            for j in range(NFAR):
                slot = (f * 2 + a) * NFAR + j
                wanted = far_ref[f, a, 0, j]
                owner, place = wanted // 2, wanted % 2
                inner = place != owner % 2
                is_core, is_cross = owner == ta + 1 - 2 * parity, owner == members - 1 - ta
                is_corner = jnp.logical_not(jnp.logical_or(is_core, is_cross))
                sources = [
                    (jnp.logical_and(is_core, place == 0), core_ref.at[:, 0, rows]),
                    (jnp.logical_and(is_core, place == 1), core_ref.at[:, 1, rows]),
                    (jnp.logical_and(is_cross, jnp.logical_not(inner)), cross[a]),
                    (jnp.logical_and(is_cross, inner), cross_inner.at[:, rows]),
                    (jnp.logical_and(is_corner, jnp.logical_not(inner)), corner[a]),
                    (jnp.logical_and(is_corner, inner), corner_inner.at[:, rows]),
                ]
                for chosen, source in sources:

                    @pl.when(chosen)
                    def _(source=source, f=f, a=a, j=j, slot=slot):
                        for group in range(HEADS // GROUP):
                            tile_copy(source, f * 2 + a, j, slot, group).start()

    units = [(early, a) for early in range(2) for a in range(2)]
    frames = (1 - parity, parity)
    collected = [(jnp.zeros((SPOT, HD), jnp.float32), jnp.zeros((SPOT, HD), jnp.float32)) for _ in units]
    for first in range(0, HEADS, GROUP):
        for slot in range(4 * NFAR):
            tile_copy(cross[0], slot // NFAR, slot % NFAR, slot, first // GROUP).wait()
        work = [(h, u) for h in range(first, first + GROUP) for u in range(len(units))]
        scores = []
        for h, u in work:
            early, a = units[u]
            frame, lanes = frames[early], slice(h * HD, (h + 1) * HD)
            queries = q_ref[frame, a * SPOT : (a + 1) * SPOT, lanes]
            scores.append(contract_last(queries, held[0, frame * 2 + a, :, lanes]))
        weights = []
        for (h, u), value in zip(work, scores):
            early, a = units[u]
            near_peak = near_refs[early][1][a * SPOT : (a + 1) * SPOT, h : h + 1]
            value = value * EXP_SCALE
            peak = jnp.maximum(jnp.max(value, axis=-1, keepdims=True), near_peak)
            weights.append((peak, jnp.exp2(near_peak - peak), jnp.exp2(value - peak).astype(jnp.bfloat16)))
        for (h, u), (peak, near_scale, weight) in zip(work, weights):
            early, a = units[u]
            frame, lanes, tokens = frames[early], slice(h * HD, (h + 1) * HD), slice(a * SPOT, (a + 1) * SPOT)
            values = with_ones(held[1, frame * 2 + a, :, lanes])
            summed = jnp.dot(weight, values, preferred_element_type=jnp.float32)
            total = summed[:, HD:]
            out_ref[early, tokens, lanes] = summed[:, :HD] + near_scale * near_refs[early][0][tokens, lanes]
            mask = lane_index(SPOT) == h
            collected[u] = jnp.where(mask, peak, collected[u][0]), jnp.where(mask, total, collected[u][1])
    for (early, a), (peak, total) in zip(units, collected):
        tokens = slice(a * SPOT, (a + 1) * SPOT)
        near_scale = jnp.exp2(near_refs[early][1][tokens, :] - peak)
        peak_ref[early, tokens, :] = peak
        total_ref[early, tokens, :] = total + near_scale * near_refs[early][2][tokens, :]


def far_attention(members, far_frames, queries, buffers, near):
    tokens, features = queries.shape[1:]
    in_vmem = pl.BlockSpec(memory_space=pltpu.VMEM)
    in_specs = [pl.BlockSpec(memory_space=pltpu.SMEM), in_vmem]
    in_specs += [pl.BlockSpec(memory_space=pl.ANY)] * len(buffers) + [in_vmem] * len(near)
    return pl.pallas_call(
        functools.partial(far_kernel, members),
        out_shape=[jax.ShapeDtypeStruct((2, tokens, lanes), jnp.float32) for lanes in (features, HD, HD)],
        in_specs=in_specs,
        out_specs=[in_vmem] * 3,
        scratch_shapes=[
            pltpu.VMEM((2, 4, NFAR * SPOT, features), jnp.bfloat16),
            pltpu.SemaphoreType.DMA((4 * NFAR, HEADS // GROUP)),
        ],
        compiler_params=pltpu.CompilerParams(vmem_limit_bytes=VMEM_LIMIT),
        cost_estimate=kernel_cost(1),
    )(far_frames, queries, *buffers, *near)


def finish_kernel(sides, columns, early, own_ref, own_peak_ref, own_total_ref, *refs):
    parts, refs = refs[:sides], refs[sides:]
    wa = lax.axis_index("wa")
    logs = [own_peak_ref[0]]
    for s in range(sides):
        value = join_sums(parts[s][:, HEADS * HD :])
        if columns > 2:
            value = jnp.where(wa < columns - 1 if s == 0 else wa > 0, value, NEGATIVE)
        logs.append(value)
    top = functools.reduce(jnp.maximum, logs)
    scales = [jnp.exp2(value - top) for value in logs]
    total = functools.reduce(jnp.add, [scales[0] * own_total_ref[0]] + scales[1:])
    scales = [value / total for value in scales]
    if not early:
        parity = lax.axis_index("ta") % 2
        refs[1][1 - parity] = refs[0][...]
    for h in range(HEADS):
        lanes = slice(h * HD, (h + 1) * HD)
        joined = scales[0][:, h : h + 1] * own_ref[0, :, lanes]
        for s in range(sides):
            joined = joined + scales[1 + s][:, h : h + 1] * parts[s][:, lanes].astype(jnp.float32)
        if early:
            refs[0][:, lanes] = joined.astype(jnp.bfloat16)
        else:
            refs[1][parity, :, lanes] = joined.astype(jnp.bfloat16)


def finish(columns, own, parts, early_out, cost):
    sides, rows = len(parts), 32
    frames, tokens, features = own[0].shape
    early = early_out is None
    at = 0 if early else 1
    in_specs = [
        pl.BlockSpec((1, rows, features), lambda i: (at, i, 0)),
        pl.BlockSpec((1, rows, HD), lambda i: (at, i, 0)),
        pl.BlockSpec((1, rows, HD), lambda i: (at, i, 0)),
    ]
    in_specs += [pl.BlockSpec((rows, features + HD), lambda i: (i, 0)) for _ in parts]
    one_frame = pl.BlockSpec((rows, features), lambda i: (i, 0))
    if early:
        extra, out_spec, out_shape = (), one_frame, (tokens, features)
    else:
        extra, out_spec = (early_out,), pl.BlockSpec((frames, rows, features), lambda i: (0, i, 0))
        in_specs.append(one_frame)
        out_shape = own[0].shape
    return pl.pallas_call(
        functools.partial(finish_kernel, sides, columns, early),
        out_shape=jax.ShapeDtypeStruct(out_shape, jnp.bfloat16),
        grid=(tokens // rows,),
        in_specs=in_specs,
        out_specs=out_spec,
        compiler_params=pltpu.CompilerParams(vmem_limit_bytes=VMEM_LIMIT),
        cost_estimate=kernel_cost(cost),
    )(*own, *parts, *extra)


def per_device(queries, keyvals, far_frames):
    shape = queries.shape
    frames, rows, columns, features = shape
    tokens = rows * columns
    ta_size, ha_size, wa_size = lax.axis_size("ta"), lax.axis_size("ha"), lax.axis_size("wa")
    queries = queries.reshape(frames, tokens, features)
    keyvals = keyvals.reshape(2, frames, tokens, features)

    core_pairs = [(i, i ^ 1) for i in range(ta_size)]
    cross_pairs = [(i, ta_size - 1 - i) for i in range(ta_size)]
    up = [(i, i + 1) for i in range(ha_size - 1)]
    down = [(i + 1, i) for i in range(ha_size - 1)]
    if wa_size == 2:
        ways = [([(0, 1), (1, 0)], [(0, 1), (1, 0)])]
    else:
        right = [(i, i + 1) for i in range(wa_size - 1)]
        left = [(i + 1, i) for i in range(wa_size - 1)]
        ways = [(right, left), (left, right)]
    tie = lax.optimization_barrier

    core = lax.ppermute(keyvals, "ta", core_pairs)
    last_rows, first_rows, outer_last, outer_first, inner = cut(keyvals)
    top = lax.ppermute(last_rows, "ha", up)
    bottom = lax.ppermute(first_rows, "ha", down)
    cross_last = lax.ppermute(outer_last, "ta", cross_pairs)
    outer_first, core, sent = tie((outer_first, core, queries))
    cross_first = lax.ppermute(outer_first, "ta", cross_pairs)
    visitors = [lax.ppermute(sent, "wa", there) for there, _ in ways]
    inner, cross_last = tie((inner, cross_last))
    last = lax.ppermute(inner, "ta", cross_pairs)
    top, bottom, cross_first, cross_last, visitors = tie((top, bottom, cross_first, cross_last, visitors))
    core_top, core_bottom = [lax.ppermute(value, "ta", core_pairs) for value in inner_rows(top, bottom)]
    cross_top = lax.ppermute(cross_last, "ha", up)
    cross_bottom = lax.ppermute(cross_first, "ha", down)

    early_third = (core, core_top, core_bottom)
    early = near_attention(True, ha_size, keyvals, top, bottom, early_third, visitors, [], 1)
    early_parts = [lax.ppermute(result, "wa", back) for result, (_, back) in zip(early, ways)]
    core_top, _ = tie((core_top, early[0]))
    early_third = (core, core_top, core_bottom)
    early_home = near_attention(True, ha_size, keyvals, top, bottom, early_third, [], [queries], 1)
    cross_top, cross_bottom, last, _ = tie((cross_top, cross_bottom, last, early_home[1]))
    late_third = (cross_first, cross_last, cross_top, cross_bottom)
    late = near_attention(False, ha_size, keyvals, top, bottom, late_third, visitors, [queries], LATE_COST)
    late_parts = [lax.ppermute(result, "wa", back) for result, (_, back) in zip(late, ways)]
    frames_here = (cross_first, cross_last, last)
    frames_here, early_parts, _ = tie((frames_here, early_parts, late[0]))
    corner = [lax.ppermute(value, "ta", core_pairs) for value in frames_here]
    buffers = (core, *frames_here, *corner)
    own = far_attention(ta_size, far_frames, queries, buffers, (*early_home, *late[-3:]))
    out = finish(wa_size, own, early_parts, None, FINISH_COST)
    out = finish(wa_size, own, late_parts, out, 1)
    return out.reshape(shape)


def solution(mesh):
    placed = (P("ta", "ha", "wa", None), P(None, "ta", "ha", "wa", None), P("ta", "ha", "wa", None))
    return jax.shard_map(
        per_device, mesh=mesh, in_specs=placed, out_specs=P("ta", "ha", "wa", None), check_vma=False
    )
```

```python
import functools

import jax
import jax.numpy as jnp
from jax import lax
from jax.experimental import pallas as pl
from jax.experimental.pallas import tpu as pltpu
from jax.sharding import PartitionSpec as P

TILE = 8
HEADS = 16
HD = 128
NFAR = 2
SPOT = TILE * TILE
NEGATIVE = -1e30
EXP_SCALE = HD ** (-0.5) * 1.4426950408889634
VMEM_LIMIT = 16 * 1024 * 1024
GROUP = 4
FINISH_COST = 1
LATE_COST = 8 << 30


def contract_last(left, right):
    return lax.dot_general(left, right, (((1,), (1,)), ((), ())), preferred_element_type=jnp.float32)


def with_ones(values):
    return jnp.concatenate([values, jnp.ones_like(values)], axis=1)


def lane_index(rows):
    return lax.broadcasted_iota(jnp.int32, (rows, HD), 1)


def split_sums(value):
    high = value.astype(jnp.bfloat16).astype(jnp.float32)
    rest = value - high
    middle = rest.astype(jnp.bfloat16).astype(jnp.float32)
    low = rest - middle
    return (high + pltpu.roll(middle, HEADS, 1) + pltpu.roll(low, 2 * HEADS, 1)).astype(jnp.bfloat16)


def join_sums(value):
    terms = value.astype(jnp.float32)
    return terms + (pltpu.roll(terms, HD - HEADS, 1) + pltpu.roll(terms, HD - 2 * HEADS, 1))


def kernel_cost(flops):
    return pl.CostEstimate(flops=flops, bytes_accessed=1, transcendentals=0)


def cut_kernel(keyvals_ref, last_rows_ref, first_rows_ref, outer_last_ref, outer_first_ref, inner_ref, sems):
    outer = lax.axis_index("ta") % 2
    first, last = pl.ds(0, SPOT), pl.ds(SPOT, SPOT)
    pieces = [
        (keyvals_ref.at[:, :, last], last_rows_ref),
        (keyvals_ref.at[:, :, first], first_rows_ref),
        (keyvals_ref.at[:, outer, last], outer_last_ref),
        (keyvals_ref.at[:, outer, first], outer_first_ref),
        (keyvals_ref.at[:, 1 - outer], inner_ref),
    ]
    copies = [pltpu.make_async_copy(source, target, sems.at[i]) for i, (source, target) in enumerate(pieces)]
    for copy in copies:
        copy.start()
    for copy in copies:
        copy.wait()


def cut(keyvals):
    two, frames, tokens, features = keyvals.shape
    shapes = [(two, frames, SPOT, features)] * 2 + [(two, SPOT, features)] * 2 + [(two, tokens, features)]
    return pl.pallas_call(
        cut_kernel,
        out_shape=[jax.ShapeDtypeStruct(shape, keyvals.dtype) for shape in shapes],
        in_specs=[pl.BlockSpec(memory_space=pl.ANY)],
        out_specs=[pl.BlockSpec(memory_space=pltpu.VMEM)] * 5,
        scratch_shapes=[pltpu.SemaphoreType.DMA((5,))],
        compiler_params=pltpu.CompilerParams(vmem_limit_bytes=VMEM_LIMIT),
        cost_estimate=kernel_cost(1),
    )(keyvals)


def widen_kernel(rows_ref, out_ref, sems):
    tokens = rows_ref.shape[1]
    extra = out_ref.shape[1] - tokens
    copies = [
        pltpu.make_async_copy(rows_ref, out_ref.at[:, pl.ds(0, tokens)], sems.at[0]),
        pltpu.make_async_copy(rows_ref.at[:, pl.ds(0, extra)], out_ref.at[:, pl.ds(tokens, extra)], sems.at[1]),
    ]
    for copy in copies:
        copy.start()
    for copy in copies:
        copy.wait()


def widen(rows):
    two, tokens, features = rows.shape
    in_vmem = pl.BlockSpec(memory_space=pltpu.VMEM)
    return pl.pallas_call(
        widen_kernel,
        out_shape=jax.ShapeDtypeStruct((two, tokens + tokens // 2, features), rows.dtype),
        in_specs=[in_vmem],
        out_specs=in_vmem,
        scratch_shapes=[pltpu.SemaphoreType.DMA((2,))],
        compiler_params=pltpu.CompilerParams(vmem_limit_bytes=VMEM_LIMIT),
        cost_estimate=kernel_cost(1),
    )(rows)


def by_rows_kernel(frame_ref, first_ref, last_ref, sems):
    pairs = ((pl.ds(0, SPOT), first_ref), (pl.ds(SPOT, SPOT), last_ref))
    copies = [pltpu.make_async_copy(frame_ref.at[:, rows], out, sems.at[i]) for i, (rows, out) in enumerate(pairs)]
    for copy in copies:
        copy.start()
    for copy in copies:
        copy.wait()


def by_rows(frame):
    two, _, features = frame.shape
    in_vmem = pl.BlockSpec(memory_space=pltpu.VMEM)
    return pl.pallas_call(
        by_rows_kernel,
        out_shape=[jax.ShapeDtypeStruct((two, SPOT, features), frame.dtype)] * 2,
        in_specs=[in_vmem],
        out_specs=[in_vmem] * 2,
        scratch_shapes=[pltpu.SemaphoreType.DMA((2,))],
        compiler_params=pltpu.CompilerParams(vmem_limit_bytes=VMEM_LIMIT),
        cost_estimate=kernel_cost(1),
    )(frame)


def inner_rows_kernel(top_ref, bottom_ref, out_top_ref, out_bottom_ref, sems):
    inner = 1 - lax.axis_index("ta") % 2
    pairs = ((top_ref, out_top_ref), (bottom_ref, out_bottom_ref))
    copies = [pltpu.make_async_copy(ref.at[:, inner], out, sems.at[i]) for i, (ref, out) in enumerate(pairs)]
    for copy in copies:
        copy.start()
    for copy in copies:
        copy.wait()


def inner_rows(top, bottom):
    shape = jax.ShapeDtypeStruct((top.shape[0],) + top.shape[2:], top.dtype)
    in_vmem = pl.BlockSpec(memory_space=pltpu.VMEM)
    return pl.pallas_call(
        inner_rows_kernel,
        out_shape=[shape] * 2,
        in_specs=[in_vmem] * 2,
        out_specs=[in_vmem] * 2,
        scratch_shapes=[pltpu.SemaphoreType.DMA((2,))],
        compiler_params=pltpu.CompilerParams(vmem_limit_bytes=VMEM_LIMIT),
        cost_estimate=kernel_cost(1),
    )(top, bottom)


def near_kernel(sides, home, early, has_rows, own_ref, top_ref, bottom_ref, *refs):
    parity = lax.axis_index("ta") % 2
    ha = lax.axis_index("ha")
    valid = (ha > 0, ha < has_rows - 1)
    if early:
        ext_ref, ext_top_ref, ext_bottom_ref, refs = refs[0], refs[1], refs[2], refs[3:]
        frame = 1 - parity
    else:
        ext_first_ref, ext_last_ref, ext_top_ref, ext_bottom_ref, refs = refs[0], refs[1], refs[2], refs[3], refs[4:]
        frame = parity
    count = sides + home
    q_refs, out_refs = refs[:count], refs[count:]
    half = count * SPOT

    def middle(kind, lanes):
        parts = [own_ref[kind, 0, :, lanes], own_ref[kind, 1, :, lanes]]
        if early:
            parts.append(ext_ref[kind, parity, :, lanes])
        else:
            parts += [ext_first_ref[kind, :, lanes], ext_last_ref[kind, :, lanes]]
        return jnp.concatenate(parts, axis=0)

    def halo(a, kind, lanes):
        ref, ext = ((top_ref, ext_top_ref), (bottom_ref, ext_bottom_ref))[a]
        return jnp.concatenate([ref[kind, 0, :, lanes], ref[kind, 1, :, lanes], ext[kind, :SPOT, lanes]], axis=0)

    peaks = [jnp.zeros((half, HD), jnp.float32) for _ in range(2)]
    totals = [jnp.ones((half, HD), jnp.float32) for _ in range(2)]
    for first in range(0, HEADS, GROUP):
        members = [slice(h * HD, (h + 1) * HD) for h in range(first, first + GROUP)]
        scores = []
        for lanes in members:
            queries = [
                jnp.concatenate([ref[frame, a * SPOT : (a + 1) * SPOT, lanes] for ref in q_refs], axis=0)
                for a in range(2)
            ]
            near = contract_last(jnp.concatenate(queries, axis=0), middle(0, lanes))
            edges = [contract_last(queries[a], halo(a, 0, lanes)) for a in range(2)]
            scores.append([(near[a * half : (a + 1) * half], edges[a]) for a in range(2)])
        weights = []
        for pairs in scores:
            for a, (near, edge) in enumerate(pairs):
                best = functools.reduce(jnp.maximum, [near[:, i * HD : (i + 1) * HD] for i in range(3)])
                edge_best = jnp.maximum(edge[:, : 2 * SPOT], jnp.concatenate([edge[:, 2 * SPOT :]] * 2, axis=1))
                best = jnp.maximum(best, jnp.where(valid[a], edge_best, NEGATIVE))
                peak = jnp.max(best, axis=-1, keepdims=True)
                shift = jnp.where(valid[a], peak, -NEGATIVE)
                near = jnp.exp2((near - peak) * EXP_SCALE).astype(jnp.bfloat16)
                edge = jnp.exp2((edge - shift) * EXP_SCALE).astype(jnp.bfloat16)
                weights.append((peak, near, edge))
        for i, lanes in enumerate(members):
            mask = lane_index(half) == first + i
            middle_values = with_ones(middle(1, lanes))
            for a in range(2):
                peak, near, edge = weights[2 * i + a]
                summed = jnp.dot(near, middle_values, preferred_element_type=jnp.float32)
                summed = summed + jnp.dot(edge, with_ones(halo(a, 1, lanes)), preferred_element_type=jnp.float32)
                total = summed[:, HD:]
                peaks[a] = jnp.where(mask, peak, peaks[a])
                totals[a] = jnp.where(mask, total, totals[a])
                for s in range(count):
                    rows = slice(s * SPOT, (s + 1) * SPOT)
                    result = summed[rows, :HD]
                    if s < sides:
                        result = result / total[rows]
                    else:
                        filled = jnp.broadcast_to(peak[rows] * EXP_SCALE, (SPOT, HD))
                        out_refs[s + 3][a * SPOT : (a + 1) * SPOT, lanes] = filled
                    out_refs[s][a * SPOT : (a + 1) * SPOT, lanes] = result.astype(out_refs[s].dtype)
    for a in range(2):
        tokens = slice(a * SPOT, (a + 1) * SPOT)
        for s in range(count):
            rows = slice(s * SPOT, (s + 1) * SPOT)
            if s < sides:
                log_sum = peaks[a][rows] * EXP_SCALE + jnp.log2(totals[a][rows])
                out_refs[s][tokens, HEADS * HD :] = split_sums(log_sum)
            else:
                out_refs[s + 1][tokens, :] = peaks[a][rows] * EXP_SCALE
                out_refs[s + 2][tokens, :] = totals[a][rows]


def near_attention(early, has_rows, own, top, bottom, third, visitors, queries, cost):
    tokens, features = own.shape[2:]
    operands = [own, top, bottom, *third, *visitors, *queries]
    outs = [jax.ShapeDtypeStruct((tokens, features + HD), jnp.bfloat16) for _ in visitors]
    for _ in queries:
        outs += [jax.ShapeDtypeStruct((tokens, lanes), jnp.float32) for lanes in (features, HD, HD, features)]
    in_vmem = pl.BlockSpec(memory_space=pltpu.VMEM)
    return pl.pallas_call(
        functools.partial(near_kernel, len(visitors), len(queries), early, has_rows),
        out_shape=outs,
        in_specs=[in_vmem] * len(operands),
        out_specs=[in_vmem] * len(outs),
        compiler_params=pltpu.CompilerParams(vmem_limit_bytes=VMEM_LIMIT),
        cost_estimate=kernel_cost(cost),
    )(*operands)


def far_kernel(members, far_ref, q_ref, core_ref, *refs):
    cross, cross_inner, corner, corner_inner = refs[:2], refs[2:4], refs[4:6], refs[6:8]
    near_refs, (out_ref, peak_ref, total_ref, held, sems) = (refs[8:12], refs[12:16]), refs[16:]
    ta = lax.axis_index("ta")
    parity = ta % 2

    def tile_copy(source, tile, j, slot, group):
        lanes = pl.ds(group * GROUP * HD, GROUP * HD)
        target = held.at[:, tile, pl.ds(j * SPOT, SPOT), lanes]
        return pltpu.make_async_copy(source.at[:, :, lanes], target, sems.at[slot, group])

    for f in range(2):
        for a in range(2):
            rows = pl.ds(a * SPOT, SPOT)
            for j in range(NFAR):
                slot = (f * 2 + a) * NFAR + j
                wanted = far_ref[f, a, 0, j]
                owner, place = wanted // 2, wanted % 2
                inner = place != owner % 2
                is_core, is_cross = owner == ta + 1 - 2 * parity, owner == members - 1 - ta
                is_corner = jnp.logical_not(jnp.logical_or(is_core, is_cross))
                sources = [
                    (jnp.logical_and(is_core, place == 0), core_ref.at[:, 0, rows]),
                    (jnp.logical_and(is_core, place == 1), core_ref.at[:, 1, rows]),
                    (jnp.logical_and(is_cross, jnp.logical_not(inner)), cross[a]),
                    (jnp.logical_and(is_cross, inner), cross_inner[a]),
                    (jnp.logical_and(is_corner, jnp.logical_not(inner)), corner[a]),
                    (jnp.logical_and(is_corner, inner), corner_inner[a]),
                ]
                for chosen, source in sources:

                    @pl.when(chosen)
                    def _(source=source, f=f, a=a, j=j, slot=slot):
                        for group in range(HEADS // GROUP):
                            tile_copy(source, f * 2 + a, j, slot, group).start()

    units = [(early, a) for early in range(2) for a in range(2)]
    frames = (1 - parity, parity)
    collected = [(jnp.zeros((SPOT, HD), jnp.float32), jnp.zeros((SPOT, HD), jnp.float32)) for _ in units]
    for first in range(0, HEADS, GROUP):
        for slot in range(4 * NFAR):
            tile_copy(cross[0], slot // NFAR, slot % NFAR, slot, first // GROUP).wait()
        work = [(h, u) for h in range(first, first + GROUP) for u in range(len(units))]
        scores = []
        for h, u in work:
            early, a = units[u]
            frame, lanes = frames[early], slice(h * HD, (h + 1) * HD)
            queries = q_ref[frame, a * SPOT : (a + 1) * SPOT, lanes]
            scores.append(contract_last(queries, held[0, frame * 2 + a, :, lanes]))
        weights = []
        for (h, u), value in zip(work, scores):
            early, a = units[u]
            near_peak = near_refs[early][3][a * SPOT : (a + 1) * SPOT, h * HD : (h + 1) * HD]
            value = value * EXP_SCALE
            peak = jnp.maximum(jnp.max(value, axis=-1, keepdims=True), near_peak)
            weights.append((peak, jnp.exp2(near_peak - peak), jnp.exp2(value - peak).astype(jnp.bfloat16)))
        for (h, u), (peak, near_scale, weight) in zip(work, weights):
            early, a = units[u]
            frame, lanes, tokens = frames[early], slice(h * HD, (h + 1) * HD), slice(a * SPOT, (a + 1) * SPOT)
            values = with_ones(held[1, frame * 2 + a, :, lanes])
            summed = jnp.dot(weight, values, preferred_element_type=jnp.float32)
            total = summed[:, HD:]
            out_ref[early, tokens, lanes] = summed[:, :HD] + near_scale * near_refs[early][0][tokens, lanes]
            mask = lane_index(SPOT) == h
            collected[u] = jnp.where(mask, peak, collected[u][0]), jnp.where(mask, total, collected[u][1])
    for (early, a), (peak, total) in zip(units, collected):
        tokens = slice(a * SPOT, (a + 1) * SPOT)
        near_scale = jnp.exp2(near_refs[early][1][tokens, :] - peak)
        peak_ref[early, tokens, :] = peak
        total_ref[early, tokens, :] = total + near_scale * near_refs[early][2][tokens, :]


def far_attention(members, far_frames, queries, buffers, near):
    tokens, features = queries.shape[1:]
    in_vmem = pl.BlockSpec(memory_space=pltpu.VMEM)
    in_specs = [pl.BlockSpec(memory_space=pltpu.SMEM), in_vmem]
    in_specs += [pl.BlockSpec(memory_space=pl.ANY)] * len(buffers) + [in_vmem] * len(near)
    return pl.pallas_call(
        functools.partial(far_kernel, members),
        out_shape=[jax.ShapeDtypeStruct((2, tokens, lanes), jnp.float32) for lanes in (features, HD, HD)],
        in_specs=in_specs,
        out_specs=[in_vmem] * 3,
        scratch_shapes=[
            pltpu.VMEM((2, 4, NFAR * SPOT, features), jnp.bfloat16),
            pltpu.SemaphoreType.DMA((4 * NFAR, HEADS // GROUP)),
        ],
        compiler_params=pltpu.CompilerParams(vmem_limit_bytes=VMEM_LIMIT),
        cost_estimate=kernel_cost(1),
    )(far_frames, queries, *buffers, *near)


def finish_kernel(sides, columns, early, own_ref, own_peak_ref, own_total_ref, *refs):
    parts, refs = refs[:sides], refs[sides:]
    wa = lax.axis_index("wa")
    logs = [own_peak_ref[0]]
    for s in range(sides):
        value = join_sums(parts[s][:, HEADS * HD :])
        if columns > 2:
            value = jnp.where(wa < columns - 1 if s == 0 else wa > 0, value, NEGATIVE)
        logs.append(value)
    top = functools.reduce(jnp.maximum, logs)
    scales = [jnp.exp2(value - top) for value in logs]
    total = functools.reduce(jnp.add, [scales[0] * own_total_ref[0]] + scales[1:])
    scales = [value / total for value in scales]
    if not early:
        parity = lax.axis_index("ta") % 2
        refs[1][1 - parity] = refs[0][...]
    for h in range(HEADS):
        lanes = slice(h * HD, (h + 1) * HD)
        joined = scales[0][:, h : h + 1] * own_ref[0, :, lanes]
        for s in range(sides):
            joined = joined + scales[1 + s][:, h : h + 1] * parts[s][:, lanes].astype(jnp.float32)
        if early:
            refs[0][:, lanes] = joined.astype(jnp.bfloat16)
        else:
            refs[1][parity, :, lanes] = joined.astype(jnp.bfloat16)


def finish(columns, own, parts, early_out, cost):
    sides, rows = len(parts), 32
    frames, tokens, features = own[0].shape
    early = early_out is None
    at = 0 if early else 1
    in_specs = [
        pl.BlockSpec((1, rows, features), lambda i: (at, i, 0)),
        pl.BlockSpec((1, rows, HD), lambda i: (at, i, 0)),
        pl.BlockSpec((1, rows, HD), lambda i: (at, i, 0)),
    ]
    in_specs += [pl.BlockSpec((rows, features + HD), lambda i: (i, 0)) for _ in parts]
    one_frame = pl.BlockSpec((rows, features), lambda i: (i, 0))
    if early:
        extra, out_spec, out_shape = (), one_frame, (tokens, features)
    else:
        extra, out_spec = (early_out,), pl.BlockSpec((frames, rows, features), lambda i: (0, i, 0))
        in_specs.append(one_frame)
        out_shape = own[0].shape
    return pl.pallas_call(
        functools.partial(finish_kernel, sides, columns, early),
        out_shape=jax.ShapeDtypeStruct(out_shape, jnp.bfloat16),
        grid=(tokens // rows,),
        in_specs=in_specs,
        out_specs=out_spec,
        compiler_params=pltpu.CompilerParams(vmem_limit_bytes=VMEM_LIMIT),
        cost_estimate=kernel_cost(cost),
    )(*own, *parts, *extra)


def per_device(queries, keyvals, far_frames):
    shape = queries.shape
    frames, rows, columns, features = shape
    tokens = rows * columns
    ta_size, ha_size, wa_size = lax.axis_size("ta"), lax.axis_size("ha"), lax.axis_size("wa")
    queries = queries.reshape(frames, tokens, features)
    keyvals = keyvals.reshape(2, frames, tokens, features)

    core_pairs = [(i, i ^ 1) for i in range(ta_size)]
    cross_pairs = [(i, ta_size - 1 - i) for i in range(ta_size)]
    up = [(i, i + 1) for i in range(ha_size - 1)]
    down = [(i + 1, i) for i in range(ha_size - 1)]
    if wa_size == 2:
        ways = [([(0, 1), (1, 0)], [(0, 1), (1, 0)])]
    else:
        right = [(i, i + 1) for i in range(wa_size - 1)]
        left = [(i + 1, i) for i in range(wa_size - 1)]
        ways = [(right, left), (left, right)]
    tie = lax.optimization_barrier

    core = lax.ppermute(keyvals, "ta", core_pairs)
    last_rows, first_rows, outer_last, outer_first, inner = cut(keyvals)
    top = lax.ppermute(last_rows, "ha", up)
    bottom = lax.ppermute(first_rows, "ha", down)
    cross_last = lax.ppermute(outer_last, "ta", cross_pairs)
    outer_first, core, sent = tie((outer_first, core, queries))
    cross_first = lax.ppermute(outer_first, "ta", cross_pairs)
    visitors = [lax.ppermute(sent, "wa", there) for there, _ in ways]
    inner, cross_last = tie((inner, cross_last))
    last = lax.ppermute(inner, "ta", cross_pairs)
    core_top, core_bottom = [lax.ppermute(value, "ta", core_pairs) for value in inner_rows(top, bottom)]
    cross_top = lax.ppermute(widen(cross_last), "ha", up)
    cross_bottom = lax.ppermute(cross_first, "ha", down)

    early_third = (core, core_top, core_bottom)
    early = near_attention(True, ha_size, keyvals, top, bottom, early_third, visitors, [], 1)
    early_parts = [lax.ppermute(result, "wa", back) for result, (_, back) in zip(early, ways)]
    core_top, _ = tie((core_top, early[0]))
    early_third = (core, core_top, core_bottom)
    early_home = near_attention(True, ha_size, keyvals, top, bottom, early_third, [], [queries], 1)
    cross_top, cross_bottom, _ = tie((cross_top, cross_bottom, early_home[1]))
    late_third = (cross_first, cross_last, cross_top, cross_bottom)
    late = near_attention(False, ha_size, keyvals, top, bottom, late_third, visitors, [queries], LATE_COST)
    late_parts = [lax.ppermute(result, "wa", back) for result, (_, back) in zip(late, ways)]
    last, _ = tie((last, late[0]))
    cross_first, cross_last, early_parts, _ = tie((cross_first, cross_last, early_parts, late[0]))
    frames_here = (cross_first, cross_last, *by_rows(last))
    corner = [lax.ppermute(value, "ta", core_pairs) for value in frames_here]
    buffers = (core, *frames_here, *corner)
    own = far_attention(ta_size, far_frames, queries, buffers, (*early_home, *late[-4:]))
    out = finish(wa_size, own, early_parts, None, FINISH_COST)
    out = finish(wa_size, own, late_parts, out, 1)
    return out.reshape(shape)


def solution(mesh):
    placed = (P("ta", "ha", "wa", None), P(None, "ta", "ha", "wa", None), P("ta", "ha", "wa", None))
    return jax.shard_map(
        per_device, mesh=mesh, in_specs=placed, out_specs=P("ta", "ha", "wa", None), check_vma=False
    )
```

```python
import functools

import jax
import jax.numpy as jnp
from jax import lax
from jax.experimental import pallas as pl
from jax.experimental.pallas import tpu as pltpu
from jax.sharding import PartitionSpec as P

TILE = 8
HEADS = 16
HD = 128
NFAR = 2
SPOT = TILE * TILE
ROWS = 32
NEGATIVE = -1e30
EXP_SCALE = HD ** (-0.5) * 1.4426950408889634
VMEM_LIMIT = 16 * 1024 * 1024
GROUP = 4
FINISH_COST = 1
LATE_COST = 16 << 30


def contract_last(left, right):
    return lax.dot_general(left, right, (((1,), (1,)), ((), ())), preferred_element_type=jnp.float32)


def with_ones(values):
    return jnp.concatenate([values, jnp.ones_like(values)], axis=1)


def lane_index(rows):
    return lax.broadcasted_iota(jnp.int32, (rows, HD), 1)


def split_sums(value):
    high = value.astype(jnp.bfloat16).astype(jnp.float32)
    rest = value - high
    middle = rest.astype(jnp.bfloat16).astype(jnp.float32)
    low = rest - middle
    return (high + pltpu.roll(middle, HEADS, 1) + pltpu.roll(low, 2 * HEADS, 1)).astype(jnp.bfloat16)


def join_sums(value):
    terms = value.astype(jnp.float32)
    return terms + (pltpu.roll(terms, HD - HEADS, 1) + pltpu.roll(terms, HD - 2 * HEADS, 1))


def kernel_cost(flops):
    return pl.CostEstimate(flops=flops, bytes_accessed=1, transcendentals=0)


def run_copies(pairs, sems):
    copies = [pltpu.make_async_copy(source, target, sems.at[i]) for i, (source, target) in enumerate(pairs)]
    for copy in copies:
        copy.start()
    for copy in copies:
        copy.wait()


def copying_call(kernel, shapes, copies, *operands):
    in_vmem = pl.BlockSpec(memory_space=pltpu.VMEM)
    return pl.pallas_call(
        kernel,
        out_shape=[jax.ShapeDtypeStruct(shape, operands[0].dtype) for shape in shapes],
        in_specs=[in_vmem] * len(operands),
        out_specs=[in_vmem] * len(shapes),
        scratch_shapes=[pltpu.SemaphoreType.DMA((copies,))],
        compiler_params=pltpu.CompilerParams(vmem_limit_bytes=VMEM_LIMIT),
        cost_estimate=kernel_cost(1),
    )(*operands)


FIRST, LAST = pl.ds(0, SPOT), pl.ds(SPOT, SPOT)


def cut_kernel(keyvals_ref, last_rows_ref, first_rows_ref, outer_ref, inner_ref, sems):
    outer = lax.axis_index("ta") % 2
    pairs = [
        (keyvals_ref.at[:, :, LAST], last_rows_ref),
        (keyvals_ref.at[:, :, FIRST], first_rows_ref),
        (keyvals_ref.at[:, outer], outer_ref),
        (keyvals_ref.at[:, 1 - outer], inner_ref),
    ]
    run_copies(pairs, sems)


def cut(keyvals):
    two, frames, tokens, features = keyvals.shape
    shapes = [(two, frames, SPOT, features)] * 2 + [(two, tokens, features)] * 2
    return copying_call(cut_kernel, shapes, 4, keyvals)


def by_rows_kernel(*refs):
    frame_refs, out_refs, sems = refs[: len(refs) // 3], refs[len(refs) // 3 : -1], refs[-1]
    pairs = []
    for i, frame_ref in enumerate(frame_refs):
        for rows, out_ref in zip((FIRST, LAST), out_refs[2 * i : 2 * i + 2]):
            pairs.append((frame_ref.at[:, rows], out_ref))
    run_copies(pairs, sems)


def by_rows(*frames):
    two, _, features = frames[0].shape
    shapes = [(two, SPOT, features)] * (2 * len(frames))
    return copying_call(by_rows_kernel, shapes, 2 * len(frames), *frames)


def widened_rows_kernel(frame_ref, first_ref, last_ref, sems):
    features = frame_ref.shape[2]
    main, extra = pl.ds(0, features), pl.ds(features, HD)
    pairs = []
    for rows, out_ref in ((FIRST, first_ref), (LAST, last_ref)):
        pairs.append((frame_ref.at[:, rows], out_ref.at[:, :, main]))
        pairs.append((frame_ref.at[:, rows, pl.ds(0, HD)], out_ref.at[:, :, extra]))
    run_copies(pairs, sems)


def widened_rows(frame):
    two, _, features = frame.shape
    return copying_call(widened_rows_kernel, [(two, SPOT, features + HD)] * 2, 4, frame)


def inner_rows_kernel(top_ref, bottom_ref, out_top_ref, out_bottom_ref, sems):
    inner = 1 - lax.axis_index("ta") % 2
    run_copies([(top_ref.at[:, inner], out_top_ref), (bottom_ref.at[:, inner], out_bottom_ref)], sems)


def inner_rows(top, bottom):
    return copying_call(inner_rows_kernel, [top.shape[:1] + top.shape[2:]] * 2, 2, top, bottom)


def near_kernel(sides, home, early, has_rows, own_ref, top_ref, bottom_ref, *refs):
    parity = lax.axis_index("ta") % 2
    ha = lax.axis_index("ha")
    valid = (ha > 0, ha < has_rows - 1)
    ext_ref, ext_top_ref, ext_bottom_ref, refs = refs[0], refs[1], refs[2], refs[3:]
    frame = 1 - parity if early else parity
    count = sides + home
    q_refs, out_refs = refs[:count], refs[count:]
    half = count * SPOT

    def middle(kind, lanes):
        parts = [own_ref[kind, 0, :, lanes], own_ref[kind, 1, :, lanes]]
        parts.append(ext_ref[kind, parity, :, lanes] if early else ext_ref[kind, :, lanes])
        return jnp.concatenate(parts, axis=0)

    def halo(a, kind, lanes):
        ref, ext = ((top_ref, ext_top_ref), (bottom_ref, ext_bottom_ref))[a]
        return jnp.concatenate([ref[kind, 0, :, lanes], ref[kind, 1, :, lanes], ext[kind, :, lanes]], axis=0)

    peaks = [jnp.zeros((half, HD), jnp.float32) for _ in range(2)]
    totals = [jnp.ones((half, HD), jnp.float32) for _ in range(2)]
    for first in range(0, HEADS, GROUP):
        members = [slice(h * HD, (h + 1) * HD) for h in range(first, first + GROUP)]
        scores = []
        for lanes in members:
            queries = [
                jnp.concatenate([ref[frame, a * SPOT : (a + 1) * SPOT, lanes] for ref in q_refs], axis=0)
                for a in range(2)
            ]
            near = contract_last(jnp.concatenate(queries, axis=0), middle(0, lanes))
            edges = [contract_last(queries[a], halo(a, 0, lanes)) for a in range(2)]
            scores.append([(near[a * half : (a + 1) * half], edges[a]) for a in range(2)])
        weights = []
        for pairs in scores:
            for a, (near, edge) in enumerate(pairs):
                best = functools.reduce(jnp.maximum, [near[:, i * HD : (i + 1) * HD] for i in range(3)])
                edge_best = jnp.maximum(edge[:, : 2 * SPOT], jnp.concatenate([edge[:, 2 * SPOT :]] * 2, axis=1))
                best = jnp.maximum(best, jnp.where(valid[a], edge_best, NEGATIVE))
                peak = jnp.max(best, axis=-1, keepdims=True)
                shift = jnp.where(valid[a], peak, -NEGATIVE)
                near = jnp.exp2((near - peak) * EXP_SCALE).astype(jnp.bfloat16)
                edge = jnp.exp2((edge - shift) * EXP_SCALE).astype(jnp.bfloat16)
                weights.append((peak, near, edge))
        for i, lanes in enumerate(members):
            mask = lane_index(half) == first + i
            middle_values = with_ones(middle(1, lanes))
            for a in range(2):
                peak, near, edge = weights[2 * i + a]
                summed = jnp.dot(near, middle_values, preferred_element_type=jnp.float32)
                summed = summed + jnp.dot(edge, with_ones(halo(a, 1, lanes)), preferred_element_type=jnp.float32)
                total = summed[:, HD:]
                peaks[a] = jnp.where(mask, peak, peaks[a])
                totals[a] = jnp.where(mask, total, totals[a])
                for s in range(count):
                    rows = slice(s * SPOT, (s + 1) * SPOT)
                    result = summed[rows, :HD]
                    if s < sides:
                        result = result / total[rows]
                    else:
                        filled = jnp.broadcast_to(peak[rows] * EXP_SCALE, (SPOT, HD))
                        out_refs[s + 3][a * SPOT : (a + 1) * SPOT, lanes] = filled
                    out_refs[s][a * SPOT : (a + 1) * SPOT, lanes] = result.astype(out_refs[s].dtype)
    for a in range(2):
        tokens = slice(a * SPOT, (a + 1) * SPOT)
        for s in range(count):
            rows = slice(s * SPOT, (s + 1) * SPOT)
            if s < sides:
                log_sum = peaks[a][rows] * EXP_SCALE + jnp.log2(totals[a][rows])
                out_refs[s][tokens, HEADS * HD :] = split_sums(log_sum)
            else:
                out_refs[s + 1][tokens, :] = peaks[a][rows] * EXP_SCALE
                out_refs[s + 2][tokens, :] = totals[a][rows]


def near_attention(early, has_rows, own, top, bottom, third, visitors, queries, cost):
    tokens, features = own.shape[2:]
    operands = [own, top, bottom, *third, *visitors, *queries]
    outs = [jax.ShapeDtypeStruct((tokens, features + HD), jnp.bfloat16) for _ in visitors]
    for _ in queries:
        outs += [jax.ShapeDtypeStruct((tokens, lanes), jnp.float32) for lanes in (features, HD, HD, features)]
    in_vmem = pl.BlockSpec(memory_space=pltpu.VMEM)
    return pl.pallas_call(
        functools.partial(near_kernel, len(visitors), len(queries), early, has_rows),
        out_shape=outs,
        in_specs=[in_vmem] * len(operands),
        out_specs=[in_vmem] * len(outs),
        compiler_params=pltpu.CompilerParams(vmem_limit_bytes=VMEM_LIMIT),
        cost_estimate=kernel_cost(cost),
    )(*operands)


def far_kernel(members, far_ref, q_ref, core_ref, *refs):
    cross_ref, cross_inner_ref, corner, corner_inner = refs[0], refs[1], refs[2:4], refs[4:6]
    near_refs, (out_ref, peak_ref, total_ref, held, sems) = (refs[6:10], refs[10:14]), refs[14:]
    ta = lax.axis_index("ta")
    parity = ta % 2

    def tile_copy(source, tile, j, slot, group):
        lanes = pl.ds(group * GROUP * HD, GROUP * HD)
        target = held.at[:, tile, pl.ds(j * SPOT, SPOT), lanes]
        return pltpu.make_async_copy(source.at[:, :, lanes], target, sems.at[slot, group])

    for f in range(2):
        for a in range(2):
            rows = pl.ds(a * SPOT, SPOT)
            for j in range(NFAR):
                slot = (f * 2 + a) * NFAR + j
                wanted = far_ref[f, a, 0, j]
                owner, place = wanted // 2, wanted % 2
                inner = place != owner % 2
                is_core, is_cross = owner == ta + 1 - 2 * parity, owner == members - 1 - ta
                is_corner = jnp.logical_not(jnp.logical_or(is_core, is_cross))
                sources = [
                    (jnp.logical_and(is_core, place == 0), core_ref.at[:, 0, rows]),
                    (jnp.logical_and(is_core, place == 1), core_ref.at[:, 1, rows]),
                    (jnp.logical_and(is_cross, jnp.logical_not(inner)), cross_ref.at[:, rows]),
                    (jnp.logical_and(is_cross, inner), cross_inner_ref.at[:, rows]),
                    (jnp.logical_and(is_corner, jnp.logical_not(inner)), corner[a]),
                    (jnp.logical_and(is_corner, inner), corner_inner[a]),
                ]
                for chosen, source in sources:

                    @pl.when(chosen)
                    def _(source=source, f=f, a=a, j=j, slot=slot):
                        for group in range(HEADS // GROUP):
                            tile_copy(source, f * 2 + a, j, slot, group).start()

    units = [(early, a) for early in range(2) for a in range(2)]
    frames = (1 - parity, parity)
    collected = [(jnp.zeros((SPOT, HD), jnp.float32), jnp.zeros((SPOT, HD), jnp.float32)) for _ in units]
    for first in range(0, HEADS, GROUP):
        for slot in range(4 * NFAR):
            tile_copy(corner[0], slot // NFAR, slot % NFAR, slot, first // GROUP).wait()
        work = [(h, u) for h in range(first, first + GROUP) for u in range(len(units))]
        scores = []
        for h, u in work:
            early, a = units[u]
            frame, lanes = frames[early], slice(h * HD, (h + 1) * HD)
            queries = q_ref[frame, a * SPOT : (a + 1) * SPOT, lanes]
            scores.append(contract_last(queries, held[0, frame * 2 + a, :, lanes]))
        weights = []
        for (h, u), value in zip(work, scores):
            early, a = units[u]
            near_peak = near_refs[early][3][a * SPOT : (a + 1) * SPOT, h * HD : (h + 1) * HD]
            value = value * EXP_SCALE
            peak = jnp.maximum(jnp.max(value, axis=-1, keepdims=True), near_peak)
            weights.append((peak, jnp.exp2(near_peak - peak), jnp.exp2(value - peak).astype(jnp.bfloat16)))
        for (h, u), (peak, near_scale, weight) in zip(work, weights):
            early, a = units[u]
            frame, lanes, tokens = frames[early], slice(h * HD, (h + 1) * HD), slice(a * SPOT, (a + 1) * SPOT)
            values = with_ones(held[1, frame * 2 + a, :, lanes])
            summed = jnp.dot(weight, values, preferred_element_type=jnp.float32)
            total = summed[:, HD:]
            out_ref[early, tokens, lanes] = summed[:, :HD] + near_scale * near_refs[early][0][tokens, lanes]
            mask = lane_index(SPOT) == h
            collected[u] = jnp.where(mask, peak, collected[u][0]), jnp.where(mask, total, collected[u][1])
    for (early, a), (peak, total) in zip(units, collected):
        tokens = slice(a * SPOT, (a + 1) * SPOT)
        near_scale = jnp.exp2(near_refs[early][1][tokens, :] - peak)
        peak_ref[early, tokens, :] = peak
        total_ref[early, tokens, :] = total + near_scale * near_refs[early][2][tokens, :]


def far_attention(members, far_frames, queries, buffers, near):
    tokens, features = queries.shape[1:]
    in_vmem = pl.BlockSpec(memory_space=pltpu.VMEM)
    in_specs = [pl.BlockSpec(memory_space=pltpu.SMEM), in_vmem]
    in_specs += [pl.BlockSpec(memory_space=pl.ANY)] * len(buffers) + [in_vmem] * len(near)
    return pl.pallas_call(
        functools.partial(far_kernel, members),
        out_shape=[jax.ShapeDtypeStruct((2, tokens, lanes), jnp.float32) for lanes in (features, HD, HD)],
        in_specs=in_specs,
        out_specs=[in_vmem] * 3,
        scratch_shapes=[
            pltpu.VMEM((2, 4, NFAR * SPOT, features), jnp.bfloat16),
            pltpu.SemaphoreType.DMA((4 * NFAR, HEADS // GROUP)),
        ],
        compiler_params=pltpu.CompilerParams(vmem_limit_bytes=VMEM_LIMIT),
        cost_estimate=kernel_cost(1),
    )(far_frames, queries, *buffers, *near)


def joined_frame(sides, columns, at, own_refs, parts, rows, store):
    own_ref, own_peak_ref, own_total_ref = own_refs
    wa = lax.axis_index("wa")
    logs = [own_peak_ref[at, rows, :]]
    for s in range(sides):
        value = join_sums(parts[s][rows, HEADS * HD :])
        if columns > 2:
            value = jnp.where(wa < columns - 1 if s == 0 else wa > 0, value, NEGATIVE)
        logs.append(value)
    top = functools.reduce(jnp.maximum, logs)
    scales = [jnp.exp2(value - top) for value in logs]
    total = functools.reduce(jnp.add, [scales[0] * own_total_ref[at, rows, :]] + scales[1:])
    scales = [value / total for value in scales]
    for h in range(HEADS):
        lanes = slice(h * HD, (h + 1) * HD)
        joined = scales[0][:, h : h + 1] * own_ref[at, rows, lanes]
        for s in range(sides):
            joined = joined + scales[1 + s][:, h : h + 1] * parts[s][rows, lanes].astype(jnp.float32)
        store(lanes, joined.astype(jnp.bfloat16))


def finish_early_kernel(sides, columns, *refs):
    own_refs, parts, out_ref = refs[:3], refs[3 : 3 + sides], refs[-1]
    for first in range(0, out_ref.shape[0], ROWS):
        rows = slice(first, first + ROWS)

        def store(lanes, value, rows=rows):
            out_ref[rows, lanes] = value

        joined_frame(sides, columns, 0, own_refs, parts, rows, store)


def finish_late_kernel(sides, columns, *refs):
    own_refs, parts, (early_ref, out_ref, held, sems) = refs[:3], refs[3 : 3 + sides], refs[3 + sides :]
    parity = lax.axis_index("ta") % 2
    copies = [pltpu.make_async_copy(early_ref, out_ref.at[1 - parity], sems.at[0])]
    copies[0].start()
    for i, first in enumerate(range(0, held.shape[0], ROWS)):
        rows, span = slice(first, first + ROWS), pl.ds(first, ROWS)

        def store(lanes, value, rows=rows):
            held[rows, lanes] = value

        joined_frame(sides, columns, 1, own_refs, parts, rows, store)
        copies.append(pltpu.make_async_copy(held.at[span], out_ref.at[parity, span], sems.at[1 + i]))
        copies[-1].start()
    for copy in copies:
        copy.wait()


def finish(columns, own, parts, early_out, cost):
    sides = len(parts)
    frames, tokens, features = own[0].shape
    in_vmem = pl.BlockSpec(memory_space=pltpu.VMEM)
    early = early_out is None
    operands = [*own, *parts] + ([] if early else [early_out])
    one_frame = (tokens, features)
    if early:
        kernel, out_shape, out_spec, scratch = finish_early_kernel, one_frame, in_vmem, []
    else:
        kernel, out_shape, out_spec = finish_late_kernel, (frames, *one_frame), pl.BlockSpec(memory_space=pl.ANY)
        scratch = [pltpu.VMEM(one_frame, jnp.bfloat16), pltpu.SemaphoreType.DMA((1 + tokens // ROWS,))]
    return pl.pallas_call(
        functools.partial(kernel, sides, columns),
        out_shape=jax.ShapeDtypeStruct(out_shape, jnp.bfloat16),
        in_specs=[in_vmem] * len(operands),
        out_specs=out_spec,
        scratch_shapes=scratch,
        compiler_params=pltpu.CompilerParams(vmem_limit_bytes=VMEM_LIMIT),
        cost_estimate=kernel_cost(cost),
    )(*operands)


def per_device(queries, keyvals, far_frames):
    shape = queries.shape
    frames, rows, columns, features = shape
    tokens = rows * columns
    ta_size, ha_size, wa_size = lax.axis_size("ta"), lax.axis_size("ha"), lax.axis_size("wa")
    queries = queries.reshape(frames, tokens, features)
    keyvals = keyvals.reshape(2, frames, tokens, features)

    core_pairs = [(i, i ^ 1) for i in range(ta_size)]
    cross_pairs = [(i, ta_size - 1 - i) for i in range(ta_size)]
    up = [(i, i + 1) for i in range(ha_size - 1)]
    down = [(i + 1, i) for i in range(ha_size - 1)]
    if wa_size == 2:
        ways = [([(0, 1), (1, 0)], [(0, 1), (1, 0)])]
    else:
        right = [(i, i + 1) for i in range(wa_size - 1)]
        left = [(i + 1, i) for i in range(wa_size - 1)]
        ways = [(right, left), (left, right)]
    tie = lax.optimization_barrier

    core = lax.ppermute(keyvals, "ta", core_pairs)
    last_rows, first_rows, outer, inner = cut(keyvals)
    cross = lax.ppermute(outer, "ta", cross_pairs)
    top = lax.ppermute(last_rows, "ha", up)
    bottom = lax.ppermute(first_rows, "ha", down)
    sent, core = tie((queries, core))
    visitors = [lax.ppermute(sent, "wa", there) for there, _ in ways]
    cross_first, cross_last = widened_rows(cross)
    cross_top = lax.ppermute(cross_last, "ha", up)
    cross_bottom = lax.ppermute(cross_first, "ha", down)
    inner, cross = tie((inner, cross))
    last = lax.ppermute(inner, "ta", cross_pairs)
    core_top, core_bottom = [lax.ppermute(value, "ta", core_pairs) for value in inner_rows(top, bottom)]

    early_third = (core, core_top, core_bottom)
    early = near_attention(True, ha_size, keyvals, top, bottom, early_third, visitors, [], 1)
    early_parts = [lax.ppermute(result, "wa", back) for result, (_, back) in zip(early, ways)]
    core_top, _ = tie((core_top, early[0]))
    early_third = (core, core_top, core_bottom)
    early_home = near_attention(True, ha_size, keyvals, top, bottom, early_third, [], [queries], 1)
    cross_top, cross_bottom, _ = tie((cross_top, cross_bottom, early_home[1]))
    late_third = (cross, cross_top, cross_bottom)
    late = near_attention(False, ha_size, keyvals, top, bottom, late_third, visitors, [queries], LATE_COST)
    late_parts = [lax.ppermute(result, "wa", back) for result, (_, back) in zip(late, ways)]
    last, _ = tie((last, late[0]))
    *cross_rows, inner_first, inner_last = by_rows(cross, last)
    cross_rows, early_parts, _ = tie((cross_rows, early_parts, late[0]))
    corner = [lax.ppermute(value, "ta", core_pairs) for value in (*cross_rows, inner_first, inner_last)]
    buffers = (core, cross, last, *corner)
    own = far_attention(ta_size, far_frames, queries, buffers, (*early_home, *late[-4:]))
    out = finish(wa_size, own, early_parts, None, FINISH_COST)
    out = finish(wa_size, own, late_parts, out, 1)
    return out.reshape(shape)


def solution(mesh):
    placed = (P("ta", "ha", "wa", None), P(None, "ta", "ha", "wa", None), P("ta", "ha", "wa", None))
    return jax.shard_map(
        per_device, mesh=mesh, in_specs=placed, out_specs=P("ta", "ha", "wa", None), check_vma=False
    )
```

```python
import functools

import jax
import jax.numpy as jnp
from jax import lax
from jax.experimental import pallas as pl
from jax.experimental.pallas import tpu as pltpu
from jax.sharding import PartitionSpec as P

TILE = 8
HEADS = 16
HD = 128
NFAR = 2
SPOT = TILE * TILE
NEGATIVE = -1e30
EXP_SCALE = HD ** (-0.5) * 1.4426950408889634
VMEM_LIMIT = 16 * 1024 * 1024
GROUP = 4
FINISH_COST = 1
LATE_COST = 28 << 30


def contract_last(left, right):
    return lax.dot_general(left, right, (((1,), (1,)), ((), ())), preferred_element_type=jnp.float32)


def with_ones(values):
    return jnp.concatenate([values, jnp.ones_like(values)], axis=1)


def lane_index(rows):
    return lax.broadcasted_iota(jnp.int32, (rows, HD), 1)


def split_sums(value):
    high = value.astype(jnp.bfloat16).astype(jnp.float32)
    rest = value - high
    middle = rest.astype(jnp.bfloat16).astype(jnp.float32)
    low = rest - middle
    return (high + pltpu.roll(middle, HEADS, 1) + pltpu.roll(low, 2 * HEADS, 1)).astype(jnp.bfloat16)


def join_sums(value):
    terms = value.astype(jnp.float32)
    return terms + (pltpu.roll(terms, HD - HEADS, 1) + pltpu.roll(terms, HD - 2 * HEADS, 1))


def kernel_cost(flops):
    return pl.CostEstimate(flops=flops, bytes_accessed=1, transcendentals=0)


def run_copies(pairs, sems):
    copies = [pltpu.make_async_copy(source, target, sems.at[i]) for i, (source, target) in enumerate(pairs)]
    for copy in copies:
        copy.start()
    for copy in copies:
        copy.wait()


def copying_call(kernel, shapes, copies, *operands):
    in_vmem = pl.BlockSpec(memory_space=pltpu.VMEM)
    return pl.pallas_call(
        kernel,
        out_shape=[jax.ShapeDtypeStruct(shape, operands[0].dtype) for shape in shapes],
        in_specs=[in_vmem] * len(operands),
        out_specs=[in_vmem] * len(shapes),
        scratch_shapes=[pltpu.SemaphoreType.DMA((copies,))],
        compiler_params=pltpu.CompilerParams(vmem_limit_bytes=VMEM_LIMIT),
        cost_estimate=kernel_cost(1),
    )(*operands)


FIRST, LAST = pl.ds(0, SPOT), pl.ds(SPOT, SPOT)


def cut_kernel(keyvals_ref, last_rows_ref, first_rows_ref, outer_ref, inner_ref, sems):
    outer = lax.axis_index("ta") % 2
    pairs = [
        (keyvals_ref.at[:, :, LAST], last_rows_ref),
        (keyvals_ref.at[:, :, FIRST], first_rows_ref),
        (keyvals_ref.at[:, outer], outer_ref),
        (keyvals_ref.at[:, 1 - outer], inner_ref),
    ]
    run_copies(pairs, sems)


def cut(keyvals):
    two, frames, tokens, features = keyvals.shape
    shapes = [(two, frames, SPOT, features)] * 2 + [(two, tokens, features)] * 2
    return copying_call(cut_kernel, shapes, 4, keyvals)


def by_rows_kernel(*refs):
    frame_refs, out_refs, sems = refs[: len(refs) // 3], refs[len(refs) // 3 : -1], refs[-1]
    pairs = []
    for i, frame_ref in enumerate(frame_refs):
        for rows, out_ref in zip((FIRST, LAST), out_refs[2 * i : 2 * i + 2]):
            pairs.append((frame_ref.at[:, rows], out_ref))
    run_copies(pairs, sems)


def by_rows(*frames):
    two, _, features = frames[0].shape
    shapes = [(two, SPOT, features)] * (2 * len(frames))
    return copying_call(by_rows_kernel, shapes, 2 * len(frames), *frames)


def widened_rows_kernel(frame_ref, first_ref, last_ref, sems):
    features = frame_ref.shape[2]
    main, extra = pl.ds(0, features), pl.ds(features, HD)
    pairs = []
    for rows, out_ref in ((FIRST, first_ref), (LAST, last_ref)):
        pairs.append((frame_ref.at[:, rows], out_ref.at[:, :, main]))
        pairs.append((frame_ref.at[:, rows, pl.ds(0, HD)], out_ref.at[:, :, extra]))
    run_copies(pairs, sems)


def widened_rows(frame):
    two, _, features = frame.shape
    return copying_call(widened_rows_kernel, [(two, SPOT, features + HD)] * 2, 4, frame)


def inner_rows_kernel(top_ref, bottom_ref, out_top_ref, out_bottom_ref, sems):
    inner = 1 - lax.axis_index("ta") % 2
    run_copies([(top_ref.at[:, inner], out_top_ref), (bottom_ref.at[:, inner], out_bottom_ref)], sems)


def inner_rows(top, bottom):
    return copying_call(inner_rows_kernel, [top.shape[:1] + top.shape[2:]] * 2, 2, top, bottom)


def near_kernel(sides, home, early, has_rows, own_ref, top_ref, bottom_ref, *refs):
    parity = lax.axis_index("ta") % 2
    ha = lax.axis_index("ha")
    valid = (ha > 0, ha < has_rows - 1)
    ext_ref, ext_top_ref, ext_bottom_ref, refs = refs[0], refs[1], refs[2], refs[3:]
    frame = 1 - parity if early else parity
    count = sides + home
    q_refs, out_refs = refs[:count], refs[count:]
    half = count * SPOT

    def middle(kind, lanes):
        parts = [own_ref[kind, 0, :, lanes], own_ref[kind, 1, :, lanes]]
        parts.append(ext_ref[kind, parity, :, lanes] if early else ext_ref[kind, :, lanes])
        return jnp.concatenate(parts, axis=0)

    def halo(a, kind, lanes):
        ref, ext = ((top_ref, ext_top_ref), (bottom_ref, ext_bottom_ref))[a]
        return jnp.concatenate([ref[kind, 0, :, lanes], ref[kind, 1, :, lanes], ext[kind, :, lanes]], axis=0)

    peaks = [jnp.zeros((half, HD), jnp.float32) for _ in range(2)]
    totals = [jnp.ones((half, HD), jnp.float32) for _ in range(2)]
    for first in range(0, HEADS, GROUP):
        members = [slice(h * HD, (h + 1) * HD) for h in range(first, first + GROUP)]
        scores = []
        for lanes in members:
            queries = [
                jnp.concatenate([ref[frame, a * SPOT : (a + 1) * SPOT, lanes] for ref in q_refs], axis=0)
                for a in range(2)
            ]
            near = contract_last(jnp.concatenate(queries, axis=0), middle(0, lanes))
            edges = [contract_last(queries[a], halo(a, 0, lanes)) for a in range(2)]
            scores.append([(near[a * half : (a + 1) * half], edges[a]) for a in range(2)])
        weights = []
        for pairs in scores:
            for a, (near, edge) in enumerate(pairs):
                best = functools.reduce(jnp.maximum, [near[:, i * HD : (i + 1) * HD] for i in range(3)])
                edge_best = jnp.maximum(edge[:, : 2 * SPOT], jnp.concatenate([edge[:, 2 * SPOT :]] * 2, axis=1))
                best = jnp.maximum(best, jnp.where(valid[a], edge_best, NEGATIVE))
                peak = jnp.max(best, axis=-1, keepdims=True)
                shift = jnp.where(valid[a], peak, -NEGATIVE)
                near = jnp.exp2((near - peak) * EXP_SCALE).astype(jnp.bfloat16)
                edge = jnp.exp2((edge - shift) * EXP_SCALE).astype(jnp.bfloat16)
                weights.append((peak, near, edge))
        for i, lanes in enumerate(members):
            mask = lane_index(half) == first + i
            middle_values = with_ones(middle(1, lanes))
            for a in range(2):
                peak, near, edge = weights[2 * i + a]
                summed = jnp.dot(near, middle_values, preferred_element_type=jnp.float32)
                summed = summed + jnp.dot(edge, with_ones(halo(a, 1, lanes)), preferred_element_type=jnp.float32)
                total = summed[:, HD:]
                peaks[a] = jnp.where(mask, peak, peaks[a])
                totals[a] = jnp.where(mask, total, totals[a])
                for s in range(count):
                    rows = slice(s * SPOT, (s + 1) * SPOT)
                    result = summed[rows, :HD]
                    if s < sides:
                        result = result / total[rows]
                    else:
                        filled = jnp.broadcast_to(peak[rows] * EXP_SCALE, (SPOT, HD))
                        out_refs[s + 3][a * SPOT : (a + 1) * SPOT, lanes] = filled
                    out_refs[s][a * SPOT : (a + 1) * SPOT, lanes] = result.astype(out_refs[s].dtype)
    for a in range(2):
        tokens = slice(a * SPOT, (a + 1) * SPOT)
        for s in range(count):
            rows = slice(s * SPOT, (s + 1) * SPOT)
            if s < sides:
                log_sum = peaks[a][rows] * EXP_SCALE + jnp.log2(totals[a][rows])
                out_refs[s][tokens, HEADS * HD :] = split_sums(log_sum)
            else:
                out_refs[s + 1][tokens, :] = peaks[a][rows] * EXP_SCALE
                out_refs[s + 2][tokens, :] = totals[a][rows]


def near_attention(early, has_rows, own, top, bottom, third, visitors, queries, cost):
    tokens, features = own.shape[2:]
    operands = [own, top, bottom, *third, *visitors, *queries]
    outs = [jax.ShapeDtypeStruct((tokens, features + HD), jnp.bfloat16) for _ in visitors]
    for _ in queries:
        outs += [jax.ShapeDtypeStruct((tokens, lanes), jnp.float32) for lanes in (features, HD, HD, features)]
    in_vmem = pl.BlockSpec(memory_space=pltpu.VMEM)
    return pl.pallas_call(
        functools.partial(near_kernel, len(visitors), len(queries), early, has_rows),
        out_shape=outs,
        in_specs=[in_vmem] * len(operands),
        out_specs=[in_vmem] * len(outs),
        compiler_params=pltpu.CompilerParams(vmem_limit_bytes=VMEM_LIMIT),
        cost_estimate=kernel_cost(cost),
    )(*operands)


def far_kernel(members, far_ref, q_ref, core_ref, *refs):
    cross_ref, cross_inner_ref, corner, corner_inner = refs[0], refs[1], refs[2:4], refs[4:6]
    near_refs, (out_ref, peak_ref, total_ref, held, sems) = (refs[6:10], refs[10:14]), refs[14:]
    ta = lax.axis_index("ta")
    parity = ta % 2

    def tile_copy(source, tile, j, slot, group):
        lanes = pl.ds(group * GROUP * HD, GROUP * HD)
        target = held.at[:, tile, pl.ds(j * SPOT, SPOT), lanes]
        return pltpu.make_async_copy(source.at[:, :, lanes], target, sems.at[slot, group])

    for f in range(2):
        for a in range(2):
            rows = pl.ds(a * SPOT, SPOT)
            for j in range(NFAR):
                slot = (f * 2 + a) * NFAR + j
                wanted = far_ref[f, a, 0, j]
                owner, place = wanted // 2, wanted % 2
                inner = place != owner % 2
                is_core, is_cross = owner == ta + 1 - 2 * parity, owner == members - 1 - ta
                is_corner = jnp.logical_not(jnp.logical_or(is_core, is_cross))
                sources = [
                    (jnp.logical_and(is_core, place == 0), core_ref.at[:, 0, rows]),
                    (jnp.logical_and(is_core, place == 1), core_ref.at[:, 1, rows]),
                    (jnp.logical_and(is_cross, jnp.logical_not(inner)), cross_ref.at[:, rows]),
                    (jnp.logical_and(is_cross, inner), cross_inner_ref.at[:, rows]),
                    (jnp.logical_and(is_corner, jnp.logical_not(inner)), corner[a]),
                    (jnp.logical_and(is_corner, inner), corner_inner[a]),
                ]
                for chosen, source in sources:

                    @pl.when(chosen)
                    def _(source=source, f=f, a=a, j=j, slot=slot):
                        for group in range(HEADS // GROUP):
                            tile_copy(source, f * 2 + a, j, slot, group).start()

    units = [(early, a) for early in range(2) for a in range(2)]
    frames = (1 - parity, parity)
    collected = [(jnp.zeros((SPOT, HD), jnp.float32), jnp.zeros((SPOT, HD), jnp.float32)) for _ in units]
    for first in range(0, HEADS, GROUP):
        for slot in range(4 * NFAR):
            tile_copy(corner[0], slot // NFAR, slot % NFAR, slot, first // GROUP).wait()
        work = [(h, u) for h in range(first, first + GROUP) for u in range(len(units))]
        scores = []
        for h, u in work:
            early, a = units[u]
            frame, lanes = frames[early], slice(h * HD, (h + 1) * HD)
            queries = q_ref[frame, a * SPOT : (a + 1) * SPOT, lanes]
            scores.append(contract_last(queries, held[0, frame * 2 + a, :, lanes]))
        weights = []
        for (h, u), value in zip(work, scores):
            early, a = units[u]
            near_peak = near_refs[early][3][a * SPOT : (a + 1) * SPOT, h * HD : (h + 1) * HD]
            value = value * EXP_SCALE
            peak = jnp.maximum(jnp.max(value, axis=-1, keepdims=True), near_peak)
            weights.append((peak, jnp.exp2(near_peak - peak), jnp.exp2(value - peak).astype(jnp.bfloat16)))
        for (h, u), (peak, near_scale, weight) in zip(work, weights):
            early, a = units[u]
            frame, lanes, tokens = frames[early], slice(h * HD, (h + 1) * HD), slice(a * SPOT, (a + 1) * SPOT)
            values = with_ones(held[1, frame * 2 + a, :, lanes])
            summed = jnp.dot(weight, values, preferred_element_type=jnp.float32)
            total = summed[:, HD:]
            out_ref[early, tokens, lanes] = summed[:, :HD] + near_scale * near_refs[early][0][tokens, lanes]
            mask = lane_index(SPOT) == h
            collected[u] = jnp.where(mask, peak, collected[u][0]), jnp.where(mask, total, collected[u][1])
    for (early, a), (peak, total) in zip(units, collected):
        tokens = slice(a * SPOT, (a + 1) * SPOT)
        near_scale = jnp.exp2(near_refs[early][1][tokens, :] - peak)
        peak_ref[early, tokens, :] = peak
        total_ref[early, tokens, :] = total + near_scale * near_refs[early][2][tokens, :]


def far_attention(members, far_frames, queries, buffers, near):
    tokens, features = queries.shape[1:]
    in_vmem = pl.BlockSpec(memory_space=pltpu.VMEM)
    in_specs = [pl.BlockSpec(memory_space=pltpu.SMEM), in_vmem]
    in_specs += [pl.BlockSpec(memory_space=pl.ANY)] * len(buffers) + [in_vmem] * len(near)
    return pl.pallas_call(
        functools.partial(far_kernel, members),
        out_shape=[jax.ShapeDtypeStruct((2, tokens, lanes), jnp.float32) for lanes in (features, HD, HD)],
        in_specs=in_specs,
        out_specs=[in_vmem] * 3,
        scratch_shapes=[
            pltpu.VMEM((2, 4, NFAR * SPOT, features), jnp.bfloat16),
            pltpu.SemaphoreType.DMA((4 * NFAR, HEADS // GROUP)),
        ],
        compiler_params=pltpu.CompilerParams(vmem_limit_bytes=VMEM_LIMIT),
        cost_estimate=kernel_cost(1),
    )(far_frames, queries, *buffers, *near)


def frame_scales(sides, columns, at, own_refs, parts):
    _, own_peak_ref, own_total_ref = own_refs
    wa = lax.axis_index("wa")
    logs = [own_peak_ref[at]]
    for s in range(sides):
        value = join_sums(parts[s][:, HEADS * HD :])
        if columns > 2:
            value = jnp.where(wa < columns - 1 if s == 0 else wa > 0, value, NEGATIVE)
        logs.append(value)
    top = functools.reduce(jnp.maximum, logs)
    scales = [jnp.exp2(value - top) for value in logs]
    total = functools.reduce(jnp.add, [scales[0] * own_total_ref[at]] + scales[1:])
    heads = lane_index(top.shape[0]) < HEADS
    return [split_sums(jnp.where(heads, value / total, 0.0)) for value in scales]


def joined_head(h, at, own_ref, parts, scales):
    row = lax.broadcasted_iota(jnp.int32, (HD, HD), 0)
    spread = jnp.where(jnp.logical_and(row % HEADS == h, row < 3 * HEADS), 1.0, 0.0).astype(jnp.bfloat16)
    lanes = slice(h * HD, (h + 1) * HD)
    factors = [jnp.dot(value, spread, preferred_element_type=jnp.float32) for value in scales]
    joined = factors[0] * own_ref[at, :, lanes]
    for factor, part in zip(factors[1:], parts):
        joined = joined + factor * part[:, lanes].astype(jnp.float32)
    return joined.astype(jnp.bfloat16)


def finish_early_kernel(sides, columns, *refs):
    own_refs, parts, out_ref = refs[:3], refs[3 : 3 + sides], refs[-1]
    scales = frame_scales(sides, columns, 0, own_refs, parts)
    for h in range(HEADS):
        out_ref[:, h * HD : (h + 1) * HD] = joined_head(h, 0, own_refs[0], parts, scales)


def finish_late_kernel(sides, columns, *refs):
    own_refs, parts, (early_ref, out_ref, held, sems) = refs[:3], refs[3 : 3 + sides], refs[3 + sides :]
    parity = lax.axis_index("ta") % 2
    copies = [pltpu.make_async_copy(early_ref, out_ref.at[1 - parity], sems.at[0])]
    copies[0].start()
    scales = frame_scales(sides, columns, 1, own_refs, parts)
    for first in range(0, HEADS, GROUP):
        for h in range(first, first + GROUP):
            held[:, h * HD : (h + 1) * HD] = joined_head(h, 1, own_refs[0], parts, scales)
        lanes = pl.ds(first * HD, GROUP * HD)
        copy = pltpu.make_async_copy(held.at[:, lanes], out_ref.at[parity, :, lanes], sems.at[1 + first // GROUP])
        copy.start()
        copies.append(copy)
    for copy in copies:
        copy.wait()


def finish(columns, own, parts, early_out, cost):
    sides = len(parts)
    frames, tokens, features = own[0].shape
    in_vmem = pl.BlockSpec(memory_space=pltpu.VMEM)
    early = early_out is None
    operands = [*own, *parts] + ([] if early else [early_out])
    one_frame = (tokens, features)
    if early:
        kernel, out_shape, out_spec, scratch = finish_early_kernel, one_frame, in_vmem, []
    else:
        kernel, out_shape, out_spec = finish_late_kernel, (frames, *one_frame), pl.BlockSpec(memory_space=pl.ANY)
        scratch = [pltpu.VMEM(one_frame, jnp.bfloat16), pltpu.SemaphoreType.DMA((1 + HEADS // GROUP,))]
    return pl.pallas_call(
        functools.partial(kernel, sides, columns),
        out_shape=jax.ShapeDtypeStruct(out_shape, jnp.bfloat16),
        in_specs=[in_vmem] * len(operands),
        out_specs=out_spec,
        scratch_shapes=scratch,
        compiler_params=pltpu.CompilerParams(vmem_limit_bytes=VMEM_LIMIT),
        cost_estimate=kernel_cost(cost),
    )(*operands)


def per_device(queries, keyvals, far_frames):
    shape = queries.shape
    frames, rows, columns, features = shape
    tokens = rows * columns
    ta_size, ha_size, wa_size = lax.axis_size("ta"), lax.axis_size("ha"), lax.axis_size("wa")
    queries = queries.reshape(frames, tokens, features)
    keyvals = keyvals.reshape(2, frames, tokens, features)

    core_pairs = [(i, i ^ 1) for i in range(ta_size)]
    cross_pairs = [(i, ta_size - 1 - i) for i in range(ta_size)]
    up = [(i, i + 1) for i in range(ha_size - 1)]
    down = [(i + 1, i) for i in range(ha_size - 1)]
    if wa_size == 2:
        ways = [([(0, 1), (1, 0)], [(0, 1), (1, 0)])]
    else:
        right = [(i, i + 1) for i in range(wa_size - 1)]
        left = [(i + 1, i) for i in range(wa_size - 1)]
        ways = [(right, left), (left, right)]
    tie = lax.optimization_barrier

    core = lax.ppermute(keyvals, "ta", core_pairs)
    last_rows, first_rows, outer, inner = cut(keyvals)
    cross = lax.ppermute(outer, "ta", cross_pairs)
    top = lax.ppermute(last_rows, "ha", up)
    bottom = lax.ppermute(first_rows, "ha", down)
    sent, core = tie((queries, core))
    visitors = [lax.ppermute(sent, "wa", there) for there, _ in ways]
    cross_first, cross_last = widened_rows(cross)
    cross_top = lax.ppermute(cross_last, "ha", up)
    cross_bottom = lax.ppermute(cross_first, "ha", down)
    inner, cross = tie((inner, cross))
    last = lax.ppermute(inner, "ta", cross_pairs)
    top, bottom, visitors = tie((top, bottom, visitors))
    core_top, core_bottom = [lax.ppermute(value, "ta", core_pairs) for value in inner_rows(top, bottom)]

    early_third = (core, core_top, core_bottom)
    early = near_attention(True, ha_size, keyvals, top, bottom, early_third, visitors, [], 1)
    early_parts = [lax.ppermute(result, "wa", back) for result, (_, back) in zip(early, ways)]
    core_top, _ = tie((core_top, early[0]))
    early_third = (core, core_top, core_bottom)
    early_home = near_attention(True, ha_size, keyvals, top, bottom, early_third, [], [queries], 1)
    cross_top, cross_bottom, _ = tie((cross_top, cross_bottom, early_home[1]))
    late_third = (cross, cross_top, cross_bottom)
    late = near_attention(False, ha_size, keyvals, top, bottom, late_third, visitors, [], 1)
    late_parts = [lax.ppermute(result, "wa", back) for result, (_, back) in zip(late, ways)]
    cross_top, last, _ = tie((cross_top, last, late[0]))
    late_third = (cross, cross_top, cross_bottom)
    late_home = near_attention(False, ha_size, keyvals, top, bottom, late_third, [], [queries], LATE_COST)
    inner_corner = [lax.ppermute(value, "ta", core_pairs) for value in widened_rows(last)]
    sent, early_parts, _ = tie((cross, early_parts, late_home[1]))
    cross_rows = by_rows(sent)
    corner = [lax.ppermute(value, "ta", core_pairs) for value in cross_rows]
    buffers = (core, cross, last, *corner, *inner_corner)
    own = far_attention(ta_size, far_frames, queries, buffers, (*early_home, *late_home))
    out = finish(wa_size, own, early_parts, None, FINISH_COST)
    out = finish(wa_size, own, late_parts, out, 1)
    return out.reshape(shape)


def solution(mesh):
    placed = (P("ta", "ha", "wa", None), P(None, "ta", "ha", "wa", None), P("ta", "ha", "wa", None))
    return jax.shard_map(
        per_device, mesh=mesh, in_specs=placed, out_specs=P("ta", "ha", "wa", None), check_vma=False
    )
```

```python
import functools

import jax
import jax.numpy as jnp
from jax import lax
from jax.experimental import pallas as pl
from jax.experimental.pallas import tpu as pltpu
from jax.sharding import PartitionSpec as P

TILE = 8
HEADS = 16
HD = 128
NFAR = 2
SPOT = TILE * TILE
NEGATIVE = -1e30
EXP_SCALE = HD ** (-0.5) * 1.4426950408889634
VMEM_LIMIT = 16 * 1024 * 1024
GROUP = 4
FINISH_COST = 1
LATE_COST = 28 << 30


def contract_last(left, right):
    return lax.dot_general(left, right, (((1,), (1,)), ((), ())), preferred_element_type=jnp.float32)


def with_ones(values):
    return jnp.concatenate([values, jnp.ones_like(values)], axis=1)


def lane_index(rows):
    return lax.broadcasted_iota(jnp.int32, (rows, HD), 1)


def split_sums(value):
    high = value.astype(jnp.bfloat16).astype(jnp.float32)
    rest = value - high
    middle = rest.astype(jnp.bfloat16).astype(jnp.float32)
    low = rest - middle
    return (high + pltpu.roll(middle, HEADS, 1) + pltpu.roll(low, 2 * HEADS, 1)).astype(jnp.bfloat16)


def join_sums(value):
    terms = value.astype(jnp.float32)
    return terms + (pltpu.roll(terms, HD - HEADS, 1) + pltpu.roll(terms, HD - 2 * HEADS, 1))


def kernel_cost(flops):
    return pl.CostEstimate(flops=flops, bytes_accessed=1, transcendentals=0)


def run_copies(pairs, sems):
    copies = [pltpu.make_async_copy(source, target, sems.at[i]) for i, (source, target) in enumerate(pairs)]
    for copy in copies:
        copy.start()
    for copy in copies:
        copy.wait()


def copying_call(kernel, shapes, copies, *operands):
    in_vmem = pl.BlockSpec(memory_space=pltpu.VMEM)
    return pl.pallas_call(
        kernel,
        out_shape=[jax.ShapeDtypeStruct(shape, operands[0].dtype) for shape in shapes],
        in_specs=[in_vmem] * len(operands),
        out_specs=[in_vmem] * len(shapes),
        scratch_shapes=[pltpu.SemaphoreType.DMA((copies,))],
        compiler_params=pltpu.CompilerParams(vmem_limit_bytes=VMEM_LIMIT),
        cost_estimate=kernel_cost(1),
    )(*operands)


FIRST, LAST = pl.ds(0, SPOT), pl.ds(SPOT, SPOT)


def cut_kernel(keyvals_ref, last_rows_ref, first_rows_ref, outer_ref, inner_ref, sems):
    outer = lax.axis_index("ta") % 2
    pairs = [
        (keyvals_ref.at[:, :, LAST], last_rows_ref),
        (keyvals_ref.at[:, :, FIRST], first_rows_ref),
        (keyvals_ref.at[:, outer], outer_ref),
        (keyvals_ref.at[:, 1 - outer], inner_ref),
    ]
    run_copies(pairs, sems)


def cut(keyvals):
    two, frames, tokens, features = keyvals.shape
    shapes = [(two, frames, SPOT, features)] * 2 + [(two, tokens, features)] * 2
    return copying_call(cut_kernel, shapes, 4, keyvals)


def by_rows_kernel(*refs):
    frame_refs, out_refs, sems = refs[: len(refs) // 3], refs[len(refs) // 3 : -1], refs[-1]
    pairs = []
    for i, frame_ref in enumerate(frame_refs):
        for rows, out_ref in zip((FIRST, LAST), out_refs[2 * i : 2 * i + 2]):
            pairs.append((frame_ref.at[:, rows], out_ref))
    run_copies(pairs, sems)


def by_rows(*frames):
    two, _, features = frames[0].shape
    shapes = [(two, SPOT, features)] * (2 * len(frames))
    return copying_call(by_rows_kernel, shapes, 2 * len(frames), *frames)


def widened_rows_kernel(frame_ref, first_ref, last_ref, sems):
    features = frame_ref.shape[2]
    main, extra = pl.ds(0, features), pl.ds(features, HD)
    pairs = []
    for rows, out_ref in ((FIRST, first_ref), (LAST, last_ref)):
        pairs.append((frame_ref.at[:, rows], out_ref.at[:, :, main]))
        pairs.append((frame_ref.at[:, rows, pl.ds(0, HD)], out_ref.at[:, :, extra]))
    run_copies(pairs, sems)


def widened_rows(frame):
    two, _, features = frame.shape
    return copying_call(widened_rows_kernel, [(two, SPOT, features + HD)] * 2, 4, frame)


def inner_rows_kernel(top_ref, bottom_ref, out_top_ref, out_bottom_ref, sems):
    inner = 1 - lax.axis_index("ta") % 2
    run_copies([(top_ref.at[:, inner], out_top_ref), (bottom_ref.at[:, inner], out_bottom_ref)], sems)


def inner_rows(top, bottom):
    return copying_call(inner_rows_kernel, [top.shape[:1] + top.shape[2:]] * 2, 2, top, bottom)


def near_kernel(sides, home, early, has_rows, own_ref, top_ref, bottom_ref, *refs):
    parity = lax.axis_index("ta") % 2
    ha = lax.axis_index("ha")
    valid = (ha > 0, ha < has_rows - 1)
    ext_ref, ext_top_ref, ext_bottom_ref, refs = refs[0], refs[1], refs[2], refs[3:]
    frame = 1 - parity if early else parity
    count = sides + home
    q_refs, out_refs = refs[:count], refs[count:]
    half = count * SPOT

    def middle(kind, lanes):
        parts = [own_ref[kind, 0, :, lanes], own_ref[kind, 1, :, lanes]]
        parts.append(ext_ref[kind, parity, :, lanes] if early else ext_ref[kind, :, lanes])
        return jnp.concatenate(parts, axis=0)

    def halo(a, kind, lanes):
        ref, ext = ((top_ref, ext_top_ref), (bottom_ref, ext_bottom_ref))[a]
        return jnp.concatenate([ref[kind, 0, :, lanes], ref[kind, 1, :, lanes], ext[kind, :, lanes]], axis=0)

    peaks = [jnp.zeros((half, HD), jnp.float32) for _ in range(2)]
    totals = [jnp.ones((half, HD), jnp.float32) for _ in range(2)]
    for first in range(0, HEADS, GROUP):
        members = [slice(h * HD, (h + 1) * HD) for h in range(first, first + GROUP)]
        scores = []
        for lanes in members:
            queries = [
                jnp.concatenate([ref[frame, a * SPOT : (a + 1) * SPOT, lanes] for ref in q_refs], axis=0)
                for a in range(2)
            ]
            near = contract_last(jnp.concatenate(queries, axis=0), middle(0, lanes))
            edges = [contract_last(queries[a], halo(a, 0, lanes)) for a in range(2)]
            scores.append([(near[a * half : (a + 1) * half], edges[a]) for a in range(2)])
        weights = []
        for pairs in scores:
            for a, (near, edge) in enumerate(pairs):
                best = functools.reduce(jnp.maximum, [near[:, i * HD : (i + 1) * HD] for i in range(3)])
                edge_best = jnp.maximum(edge[:, : 2 * SPOT], jnp.concatenate([edge[:, 2 * SPOT :]] * 2, axis=1))
                best = jnp.maximum(best, jnp.where(valid[a], edge_best, NEGATIVE))
                peak = jnp.max(best, axis=-1, keepdims=True)
                shift = jnp.where(valid[a], peak, -NEGATIVE)
                near = jnp.exp2((near - peak) * EXP_SCALE).astype(jnp.bfloat16)
                edge = jnp.exp2((edge - shift) * EXP_SCALE).astype(jnp.bfloat16)
                weights.append((peak, near, edge))
        for i, lanes in enumerate(members):
            mask = lane_index(half) == first + i
            pair = weights[2 * i : 2 * i + 2]
            middle_weights = jnp.concatenate([near for _, near, _ in pair], axis=0)
            middle_sums = jnp.dot(middle_weights, with_ones(middle(1, lanes)), preferred_element_type=jnp.float32)
            for a, (peak, _, edge) in enumerate(pair):
                summed = jnp.dot(edge, with_ones(halo(a, 1, lanes)), preferred_element_type=jnp.float32)
                summed = summed + middle_sums[a * half : (a + 1) * half]
                total = summed[:, HD:]
                peaks[a] = jnp.where(mask, peak, peaks[a])
                totals[a] = jnp.where(mask, total, totals[a])
                for s in range(count):
                    rows = slice(s * SPOT, (s + 1) * SPOT)
                    result = summed[rows, :HD]
                    if s < sides:
                        result = result / total[rows]
                    else:
                        filled = jnp.broadcast_to(peak[rows] * EXP_SCALE, (SPOT, HD))
                        out_refs[s + 3][a * SPOT : (a + 1) * SPOT, lanes] = filled
                    out_refs[s][a * SPOT : (a + 1) * SPOT, lanes] = result.astype(out_refs[s].dtype)
    for a in range(2):
        tokens = slice(a * SPOT, (a + 1) * SPOT)
        for s in range(count):
            rows = slice(s * SPOT, (s + 1) * SPOT)
            if s < sides:
                log_sum = peaks[a][rows] * EXP_SCALE + jnp.log2(totals[a][rows])
                out_refs[s][tokens, HEADS * HD :] = split_sums(log_sum)
            else:
                out_refs[s + 1][tokens, :] = peaks[a][rows] * EXP_SCALE
                out_refs[s + 2][tokens, :] = totals[a][rows]


def near_attention(early, has_rows, own, top, bottom, third, visitors, queries, cost):
    tokens, features = own.shape[2:]
    operands = [own, top, bottom, *third, *visitors, *queries]
    outs = [jax.ShapeDtypeStruct((tokens, features + HD), jnp.bfloat16) for _ in visitors]
    for _ in queries:
        outs += [jax.ShapeDtypeStruct((tokens, lanes), jnp.float32) for lanes in (features, HD, HD, features)]
    in_vmem = pl.BlockSpec(memory_space=pltpu.VMEM)
    return pl.pallas_call(
        functools.partial(near_kernel, len(visitors), len(queries), early, has_rows),
        out_shape=outs,
        in_specs=[in_vmem] * len(operands),
        out_specs=[in_vmem] * len(outs),
        compiler_params=pltpu.CompilerParams(vmem_limit_bytes=VMEM_LIMIT),
        cost_estimate=kernel_cost(cost),
    )(*operands)


def far_kernel(members, far_ref, q_ref, core_ref, *refs):
    cross_ref, cross_inner_ref, corner, corner_inner = refs[0], refs[1], refs[2:4], refs[4:6]
    near_refs, (out_ref, peak_ref, total_ref, held, sems) = (refs[6:10], refs[10:14]), refs[14:]
    ta = lax.axis_index("ta")
    parity = ta % 2

    def tile_copy(source, tile, j, slot, group):
        lanes = pl.ds(group * GROUP * HD, GROUP * HD)
        target = held.at[:, tile, pl.ds(j * SPOT, SPOT), lanes]
        return pltpu.make_async_copy(source.at[:, :, lanes], target, sems.at[slot, group])

    for f in range(2):
        for a in range(2):
            rows = pl.ds(a * SPOT, SPOT)
            for j in range(NFAR):
                slot = (f * 2 + a) * NFAR + j
                wanted = far_ref[f, a, 0, j]
                owner, place = wanted // 2, wanted % 2
                inner = place != owner % 2
                is_core, is_cross = owner == ta + 1 - 2 * parity, owner == members - 1 - ta
                is_corner = jnp.logical_not(jnp.logical_or(is_core, is_cross))
                sources = [
                    (jnp.logical_and(is_core, place == 0), core_ref.at[:, 0, rows]),
                    (jnp.logical_and(is_core, place == 1), core_ref.at[:, 1, rows]),
                    (jnp.logical_and(is_cross, jnp.logical_not(inner)), cross_ref.at[:, rows]),
                    (jnp.logical_and(is_cross, inner), cross_inner_ref.at[:, rows]),
                    (jnp.logical_and(is_corner, jnp.logical_not(inner)), corner[a]),
                    (jnp.logical_and(is_corner, inner), corner_inner[a]),
                ]
                for chosen, source in sources:

                    @pl.when(chosen)
                    def _(source=source, f=f, a=a, j=j, slot=slot):
                        for group in range(HEADS // GROUP):
                            tile_copy(source, f * 2 + a, j, slot, group).start()

    units = [(early, a) for early in range(2) for a in range(2)]
    frames = (1 - parity, parity)
    collected = [(jnp.zeros((SPOT, HD), jnp.float32), jnp.zeros((SPOT, HD), jnp.float32)) for _ in units]
    for first in range(0, HEADS, GROUP):
        for slot in range(4 * NFAR):
            tile_copy(corner[0], slot // NFAR, slot % NFAR, slot, first // GROUP).wait()
        work = [(h, u) for h in range(first, first + GROUP) for u in range(len(units))]
        scores = []
        for h, u in work:
            early, a = units[u]
            frame, lanes = frames[early], slice(h * HD, (h + 1) * HD)
            queries = q_ref[frame, a * SPOT : (a + 1) * SPOT, lanes]
            scores.append(contract_last(queries, held[0, frame * 2 + a, :, lanes]))
        weights = []
        for (h, u), value in zip(work, scores):
            early, a = units[u]
            near_peak = near_refs[early][3][a * SPOT : (a + 1) * SPOT, h * HD : (h + 1) * HD]
            value = value * EXP_SCALE
            peak = jnp.maximum(jnp.max(value, axis=-1, keepdims=True), near_peak)
            weights.append((peak, jnp.exp2(near_peak - peak), jnp.exp2(value - peak).astype(jnp.bfloat16)))
        for (h, u), (peak, near_scale, weight) in zip(work, weights):
            early, a = units[u]
            frame, lanes, tokens = frames[early], slice(h * HD, (h + 1) * HD), slice(a * SPOT, (a + 1) * SPOT)
            values = with_ones(held[1, frame * 2 + a, :, lanes])
            summed = jnp.dot(weight, values, preferred_element_type=jnp.float32)
            total = summed[:, HD:]
            out_ref[early, tokens, lanes] = summed[:, :HD] + near_scale * near_refs[early][0][tokens, lanes]
            mask = lane_index(SPOT) == h
            collected[u] = jnp.where(mask, peak, collected[u][0]), jnp.where(mask, total, collected[u][1])
    for (early, a), (peak, total) in zip(units, collected):
        tokens = slice(a * SPOT, (a + 1) * SPOT)
        near_scale = jnp.exp2(near_refs[early][1][tokens, :] - peak)
        peak_ref[early, tokens, :] = peak
        total_ref[early, tokens, :] = total + near_scale * near_refs[early][2][tokens, :]


def far_attention(members, far_frames, queries, buffers, near):
    tokens, features = queries.shape[1:]
    in_vmem = pl.BlockSpec(memory_space=pltpu.VMEM)
    in_specs = [pl.BlockSpec(memory_space=pltpu.SMEM), in_vmem]
    in_specs += [pl.BlockSpec(memory_space=pl.ANY)] * len(buffers) + [in_vmem] * len(near)
    return pl.pallas_call(
        functools.partial(far_kernel, members),
        out_shape=[jax.ShapeDtypeStruct((2, tokens, lanes), jnp.float32) for lanes in (features, HD, HD)],
        in_specs=in_specs,
        out_specs=[in_vmem] * 3,
        scratch_shapes=[
            pltpu.VMEM((2, 4, NFAR * SPOT, features), jnp.bfloat16),
            pltpu.SemaphoreType.DMA((4 * NFAR, HEADS // GROUP)),
        ],
        compiler_params=pltpu.CompilerParams(vmem_limit_bytes=VMEM_LIMIT),
        cost_estimate=kernel_cost(1),
    )(far_frames, queries, *buffers, *near)


def frame_scales(sides, columns, at, own_refs, parts):
    _, own_peak_ref, own_total_ref = own_refs
    wa = lax.axis_index("wa")
    logs = [own_peak_ref[at]]
    for s in range(sides):
        value = join_sums(parts[s][:, HEADS * HD :])
        if columns > 2:
            value = jnp.where(wa < columns - 1 if s == 0 else wa > 0, value, NEGATIVE)
        logs.append(value)
    top = functools.reduce(jnp.maximum, logs)
    scales = [jnp.exp2(value - top) for value in logs]
    total = functools.reduce(jnp.add, [scales[0] * own_total_ref[at]] + scales[1:])
    heads = lane_index(top.shape[0]) < HEADS
    return [split_sums(jnp.where(heads, value / total, 0.0)) for value in scales]


def joined_head(h, at, own_ref, parts, scales):
    row = lax.broadcasted_iota(jnp.int32, (HD, HD), 0)
    spread = jnp.where(jnp.logical_and(row % HEADS == h, row < 3 * HEADS), 1.0, 0.0).astype(jnp.bfloat16)
    lanes = slice(h * HD, (h + 1) * HD)
    factors = [jnp.dot(value, spread, preferred_element_type=jnp.float32) for value in scales]
    joined = factors[0] * own_ref[at, :, lanes]
    for factor, part in zip(factors[1:], parts):
        joined = joined + factor * part[:, lanes].astype(jnp.float32)
    return joined.astype(jnp.bfloat16)


def finish_early_kernel(sides, columns, *refs):
    own_refs, parts, out_ref = refs[:3], refs[3 : 3 + sides], refs[-1]
    scales = frame_scales(sides, columns, 0, own_refs, parts)
    for h in range(HEADS):
        out_ref[:, h * HD : (h + 1) * HD] = joined_head(h, 0, own_refs[0], parts, scales)


def finish_late_kernel(sides, columns, *refs):
    own_refs, parts, (early_ref, out_ref, held, sems) = refs[:3], refs[3 : 3 + sides], refs[3 + sides :]
    parity = lax.axis_index("ta") % 2
    copies = [pltpu.make_async_copy(early_ref, out_ref.at[1 - parity], sems.at[0])]
    copies[0].start()
    scales = frame_scales(sides, columns, 1, own_refs, parts)
    for first in range(0, HEADS, GROUP):
        for h in range(first, first + GROUP):
            held[:, h * HD : (h + 1) * HD] = joined_head(h, 1, own_refs[0], parts, scales)
        lanes = pl.ds(first * HD, GROUP * HD)
        copy = pltpu.make_async_copy(held.at[:, lanes], out_ref.at[parity, :, lanes], sems.at[1 + first // GROUP])
        copy.start()
        copies.append(copy)
    for copy in copies:
        copy.wait()


def finish(columns, own, parts, early_out, cost):
    sides = len(parts)
    frames, tokens, features = own[0].shape
    in_vmem = pl.BlockSpec(memory_space=pltpu.VMEM)
    early = early_out is None
    operands = [*own, *parts] + ([] if early else [early_out])
    one_frame = (tokens, features)
    if early:
        kernel, out_shape, out_spec, scratch = finish_early_kernel, one_frame, in_vmem, []
    else:
        kernel, out_shape, out_spec = finish_late_kernel, (frames, *one_frame), pl.BlockSpec(memory_space=pl.ANY)
        scratch = [pltpu.VMEM(one_frame, jnp.bfloat16), pltpu.SemaphoreType.DMA((1 + HEADS // GROUP,))]
    return pl.pallas_call(
        functools.partial(kernel, sides, columns),
        out_shape=jax.ShapeDtypeStruct(out_shape, jnp.bfloat16),
        in_specs=[in_vmem] * len(operands),
        out_specs=out_spec,
        scratch_shapes=scratch,
        compiler_params=pltpu.CompilerParams(vmem_limit_bytes=VMEM_LIMIT),
        cost_estimate=kernel_cost(cost),
    )(*operands)


def per_device(queries, keyvals, far_frames):
    shape = queries.shape
    frames, rows, columns, features = shape
    tokens = rows * columns
    ta_size, ha_size, wa_size = lax.axis_size("ta"), lax.axis_size("ha"), lax.axis_size("wa")
    queries = queries.reshape(frames, tokens, features)
    keyvals = keyvals.reshape(2, frames, tokens, features)

    core_pairs = [(i, i ^ 1) for i in range(ta_size)]
    cross_pairs = [(i, ta_size - 1 - i) for i in range(ta_size)]
    up = [(i, i + 1) for i in range(ha_size - 1)]
    down = [(i + 1, i) for i in range(ha_size - 1)]
    if wa_size == 2:
        ways = [([(0, 1), (1, 0)], [(0, 1), (1, 0)])]
    else:
        right = [(i, i + 1) for i in range(wa_size - 1)]
        left = [(i + 1, i) for i in range(wa_size - 1)]
        ways = [(right, left), (left, right)]
    tie = lax.optimization_barrier

    core = lax.ppermute(keyvals, "ta", core_pairs)
    last_rows, first_rows, outer, inner = cut(keyvals)
    cross = lax.ppermute(outer, "ta", cross_pairs)
    top = lax.ppermute(last_rows, "ha", up)
    bottom = lax.ppermute(first_rows, "ha", down)
    sent, core = tie((queries, core))
    visitors = [lax.ppermute(sent, "wa", there) for there, _ in ways]
    cross_first, cross_last = widened_rows(cross)
    cross_top = lax.ppermute(cross_last, "ha", up)
    cross_bottom = lax.ppermute(cross_first, "ha", down)
    inner, cross = tie((inner, cross))
    last = lax.ppermute(inner, "ta", cross_pairs)
    top, bottom, visitors = tie((top, bottom, visitors))
    core_top, core_bottom = [lax.ppermute(value, "ta", core_pairs) for value in inner_rows(top, bottom)]

    early_third = (core, core_top, core_bottom)
    early = near_attention(True, ha_size, keyvals, top, bottom, early_third, visitors, [], 1)
    early_parts = [lax.ppermute(result, "wa", back) for result, (_, back) in zip(early, ways)]
    core_top, _ = tie((core_top, early[0]))
    early_third = (core, core_top, core_bottom)
    early_home = near_attention(True, ha_size, keyvals, top, bottom, early_third, [], [queries], 1)
    cross_top, cross_bottom, _ = tie((cross_top, cross_bottom, early_home[1]))
    late_third = (cross, cross_top, cross_bottom)
    late = near_attention(False, ha_size, keyvals, top, bottom, late_third, visitors, [], 1)
    late_parts = [lax.ppermute(result, "wa", back) for result, (_, back) in zip(late, ways)]
    cross_top, last, _ = tie((cross_top, last, late[0]))
    late_third = (cross, cross_top, cross_bottom)
    late_home = near_attention(False, ha_size, keyvals, top, bottom, late_third, [], [queries], LATE_COST)
    inner_corner = [lax.ppermute(value, "ta", core_pairs) for value in widened_rows(last)]
    sent, early_parts, _ = tie((cross, early_parts, late_home[1]))
    cross_rows = by_rows(sent)
    corner = [lax.ppermute(value, "ta", core_pairs) for value in cross_rows]
    buffers = (core, cross, last, *corner, *inner_corner)
    own = far_attention(ta_size, far_frames, queries, buffers, (*early_home, *late_home))
    out = finish(wa_size, own, early_parts, None, FINISH_COST)
    out = finish(wa_size, own, late_parts, out, 1)
    return out.reshape(shape)


def solution(mesh):
    placed = (P("ta", "ha", "wa", None), P(None, "ta", "ha", "wa", None), P("ta", "ha", "wa", None))
    return jax.shard_map(
        per_device, mesh=mesh, in_specs=placed, out_specs=P("ta", "ha", "wa", None), check_vma=False
    )
```

```python
import functools

import jax
import jax.numpy as jnp
from jax import lax
from jax.experimental import pallas as pl
from jax.experimental.pallas import tpu as pltpu
from jax.sharding import PartitionSpec as P

TILE = 8
HEADS = 16
HD = 128
NFAR = 2
SPOT = TILE * TILE
NEGATIVE = -1e30
EXP_SCALE = HD ** (-0.5) * 1.4426950408889634
VMEM_LIMIT = 16 * 1024 * 1024
GROUP = 4
FINISH_COST = 1
LATE_COST = 28 << 30


def contract_last(left, right):
    return lax.dot_general(left, right, (((1,), (1,)), ((), ())), preferred_element_type=jnp.float32)


def with_ones(values):
    return jnp.concatenate([values, jnp.ones_like(values)], axis=1)


def lane_index(rows):
    return lax.broadcasted_iota(jnp.int32, (rows, HD), 1)


def split_sums(value):
    high = value.astype(jnp.bfloat16).astype(jnp.float32)
    rest = value - high
    middle = rest.astype(jnp.bfloat16).astype(jnp.float32)
    low = rest - middle
    return (high + pltpu.roll(middle, HEADS, 1) + pltpu.roll(low, 2 * HEADS, 1)).astype(jnp.bfloat16)


def join_sums(value):
    terms = value.astype(jnp.float32)
    return terms + (pltpu.roll(terms, HD - HEADS, 1) + pltpu.roll(terms, HD - 2 * HEADS, 1))


def kernel_cost(flops):
    return pl.CostEstimate(flops=flops, bytes_accessed=1, transcendentals=0)


def run_copies(pairs, sems):
    copies = [pltpu.make_async_copy(source, target, sems.at[i]) for i, (source, target) in enumerate(pairs)]
    for copy in copies:
        copy.start()
    for copy in copies:
        copy.wait()


def copying_call(kernel, shapes, copies, *operands):
    in_vmem = pl.BlockSpec(memory_space=pltpu.VMEM)
    return pl.pallas_call(
        kernel,
        out_shape=[jax.ShapeDtypeStruct(shape, operands[0].dtype) for shape in shapes],
        in_specs=[in_vmem] * len(operands),
        out_specs=[in_vmem] * len(shapes),
        scratch_shapes=[pltpu.SemaphoreType.DMA((copies,))],
        compiler_params=pltpu.CompilerParams(vmem_limit_bytes=VMEM_LIMIT),
        cost_estimate=kernel_cost(1),
    )(*operands)


FIRST, LAST = pl.ds(0, SPOT), pl.ds(SPOT, SPOT)


def cut_kernel(keyvals_ref, last_rows_ref, first_rows_ref, outer_ref, inner_ref, sems):
    outer = lax.axis_index("ta") % 2
    pairs = [
        (keyvals_ref.at[:, :, LAST], last_rows_ref),
        (keyvals_ref.at[:, :, FIRST], first_rows_ref),
        (keyvals_ref.at[:, outer], outer_ref),
        (keyvals_ref.at[:, 1 - outer], inner_ref),
    ]
    run_copies(pairs, sems)


def cut(keyvals):
    two, frames, tokens, features = keyvals.shape
    shapes = [(two, frames, SPOT, features)] * 2 + [(two, tokens, features)] * 2
    return copying_call(cut_kernel, shapes, 4, keyvals)


def by_rows_kernel(*refs):
    frame_refs, out_refs, sems = refs[: len(refs) // 3], refs[len(refs) // 3 : -1], refs[-1]
    pairs = []
    for i, frame_ref in enumerate(frame_refs):
        for rows, out_ref in zip((FIRST, LAST), out_refs[2 * i : 2 * i + 2]):
            pairs.append((frame_ref.at[:, rows], out_ref))
    run_copies(pairs, sems)


def by_rows(*frames):
    two, _, features = frames[0].shape
    shapes = [(two, SPOT, features)] * (2 * len(frames))
    return copying_call(by_rows_kernel, shapes, 2 * len(frames), *frames)


def widened_rows_kernel(frame_ref, first_ref, last_ref, sems):
    features = frame_ref.shape[2]
    main, extra = pl.ds(0, features), pl.ds(features, HD)
    pairs = []
    for rows, out_ref in ((FIRST, first_ref), (LAST, last_ref)):
        pairs.append((frame_ref.at[:, rows], out_ref.at[:, :, main]))
        pairs.append((frame_ref.at[:, rows, pl.ds(0, HD)], out_ref.at[:, :, extra]))
    run_copies(pairs, sems)


def widened_rows(frame):
    two, _, features = frame.shape
    return copying_call(widened_rows_kernel, [(two, SPOT, features + HD)] * 2, 4, frame)


def inner_rows_kernel(top_ref, bottom_ref, out_top_ref, out_bottom_ref, sems):
    inner = 1 - lax.axis_index("ta") % 2
    run_copies([(top_ref.at[:, inner], out_top_ref), (bottom_ref.at[:, inner], out_bottom_ref)], sems)


def inner_rows(top, bottom):
    return copying_call(inner_rows_kernel, [top.shape[:1] + top.shape[2:]] * 2, 2, top, bottom)


def near_kernel(sides, home, early, has_rows, own_ref, top_ref, bottom_ref, *refs):
    parity = lax.axis_index("ta") % 2
    ha = lax.axis_index("ha")
    valid = (ha > 0, ha < has_rows - 1)
    ext_ref, ext_top_ref, ext_bottom_ref, refs = refs[0], refs[1], refs[2], refs[3:]
    frame = 1 - parity if early else parity
    count = sides + home
    q_refs, out_refs = refs[:count], refs[count:]
    half = count * SPOT

    def middle(kind, lanes):
        parts = [own_ref[kind, 0, :, lanes], own_ref[kind, 1, :, lanes]]
        parts.append(ext_ref[kind, parity, :, lanes] if early else ext_ref[kind, :, lanes])
        return jnp.concatenate(parts, axis=0)

    def halo(a, kind, lanes, copies):
        ref, ext = ((top_ref, ext_top_ref), (bottom_ref, ext_bottom_ref))[a]
        blocks = [ref[kind, 0, :, lanes], ref[kind, 1, :, lanes]] + [ext[kind, :, lanes]] * copies
        return jnp.concatenate(blocks, axis=0)

    peaks = [jnp.zeros((half, HD), jnp.float32) for _ in range(2)]
    totals = [jnp.ones((half, HD), jnp.float32) for _ in range(2)]
    for first in range(0, HEADS, GROUP):
        members = [slice(h * HD, (h + 1) * HD) for h in range(first, first + GROUP)]
        scores = []
        for lanes in members:
            queries = [
                jnp.concatenate([ref[frame, a * SPOT : (a + 1) * SPOT, lanes] for ref in q_refs], axis=0)
                for a in range(2)
            ]
            near = contract_last(jnp.concatenate(queries, axis=0), middle(0, lanes))
            edges = [contract_last(queries[a], halo(a, 0, lanes, 2)) for a in range(2)]
            scores.append([(near[a * half : (a + 1) * half], edges[a]) for a in range(2)])
        weights = []
        for pairs in scores:
            for a, (near, edge) in enumerate(pairs):
                best = functools.reduce(jnp.maximum, [near[:, i * HD : (i + 1) * HD] for i in range(3)])
                edge_best = jnp.maximum(edge[:, : 2 * SPOT], edge[:, 2 * SPOT :])
                best = jnp.maximum(best, jnp.where(valid[a], edge_best, NEGATIVE))
                peak = jnp.max(best, axis=-1, keepdims=True)
                shift = jnp.where(valid[a], peak, -NEGATIVE)
                near = jnp.exp2((near - peak) * EXP_SCALE).astype(jnp.bfloat16)
                edge = jnp.exp2((edge[:, : 3 * SPOT] - shift) * EXP_SCALE).astype(jnp.bfloat16)
                weights.append((peak, near, edge))
        for i, lanes in enumerate(members):
            mask = lane_index(half) == first + i
            pair = weights[2 * i : 2 * i + 2]
            middle_weights = jnp.concatenate([near for _, near, _ in pair], axis=0)
            middle_sums = jnp.dot(middle_weights, with_ones(middle(1, lanes)), preferred_element_type=jnp.float32)
            for a, (peak, _, edge) in enumerate(pair):
                summed = jnp.dot(edge, with_ones(halo(a, 1, lanes, 1)), preferred_element_type=jnp.float32)
                summed = summed + middle_sums[a * half : (a + 1) * half]
                total = summed[:, HD:]
                peaks[a] = jnp.where(mask, peak, peaks[a])
                totals[a] = jnp.where(mask, total, totals[a])
                for s in range(count):
                    rows = slice(s * SPOT, (s + 1) * SPOT)
                    result = summed[rows, :HD]
                    if s < sides:
                        result = result / total[rows]
                    else:
                        filled = jnp.broadcast_to(peak[rows] * EXP_SCALE, (SPOT, HD))
                        out_refs[s + 3][a * SPOT : (a + 1) * SPOT, lanes] = filled
                    out_refs[s][a * SPOT : (a + 1) * SPOT, lanes] = result.astype(out_refs[s].dtype)
    for a in range(2):
        tokens = slice(a * SPOT, (a + 1) * SPOT)
        for s in range(count):
            rows = slice(s * SPOT, (s + 1) * SPOT)
            if s < sides:
                log_sum = peaks[a][rows] * EXP_SCALE + jnp.log2(totals[a][rows])
                out_refs[s][tokens, HEADS * HD :] = split_sums(log_sum)
            else:
                out_refs[s + 1][tokens, :] = peaks[a][rows] * EXP_SCALE
                out_refs[s + 2][tokens, :] = totals[a][rows]


def near_attention(early, has_rows, own, top, bottom, third, visitors, queries, cost):
    tokens, features = own.shape[2:]
    operands = [own, top, bottom, *third, *visitors, *queries]
    outs = [jax.ShapeDtypeStruct((tokens, features + HD), jnp.bfloat16) for _ in visitors]
    for _ in queries:
        outs += [jax.ShapeDtypeStruct((tokens, lanes), jnp.float32) for lanes in (features, HD, HD, features)]
    in_vmem = pl.BlockSpec(memory_space=pltpu.VMEM)
    return pl.pallas_call(
        functools.partial(near_kernel, len(visitors), len(queries), early, has_rows),
        out_shape=outs,
        in_specs=[in_vmem] * len(operands),
        out_specs=[in_vmem] * len(outs),
        compiler_params=pltpu.CompilerParams(vmem_limit_bytes=VMEM_LIMIT),
        cost_estimate=kernel_cost(cost),
    )(*operands)


def far_kernel(members, far_ref, q_ref, core_ref, *refs):
    cross_ref, cross_inner_ref, corner, corner_inner = refs[0], refs[1], refs[2:4], refs[4:6]
    near_refs, (out_ref, peak_ref, total_ref, held, sems) = (refs[6:10], refs[10:14]), refs[14:]
    ta = lax.axis_index("ta")
    parity = ta % 2

    def tile_copy(source, tile, j, slot, group):
        lanes = pl.ds(group * GROUP * HD, GROUP * HD)
        target = held.at[:, tile, pl.ds(j * SPOT, SPOT), lanes]
        return pltpu.make_async_copy(source.at[:, :, lanes], target, sems.at[slot, group])

    for f in range(2):
        for a in range(2):
            rows = pl.ds(a * SPOT, SPOT)
            for j in range(NFAR):
                slot = (f * 2 + a) * NFAR + j
                wanted = far_ref[f, a, 0, j]
                owner, place = wanted // 2, wanted % 2
                inner = place != owner % 2
                is_core, is_cross = owner == ta + 1 - 2 * parity, owner == members - 1 - ta
                is_corner = jnp.logical_not(jnp.logical_or(is_core, is_cross))
                sources = [
                    (jnp.logical_and(is_core, place == 0), core_ref.at[:, 0, rows]),
                    (jnp.logical_and(is_core, place == 1), core_ref.at[:, 1, rows]),
                    (jnp.logical_and(is_cross, jnp.logical_not(inner)), cross_ref.at[:, rows]),
                    (jnp.logical_and(is_cross, inner), cross_inner_ref.at[:, rows]),
                    (jnp.logical_and(is_corner, jnp.logical_not(inner)), corner[a]),
                    (jnp.logical_and(is_corner, inner), corner_inner[a]),
                ]
                for chosen, source in sources:

                    @pl.when(chosen)
                    def _(source=source, f=f, a=a, j=j, slot=slot):
                        for group in range(HEADS // GROUP):
                            tile_copy(source, f * 2 + a, j, slot, group).start()

    units = [(early, a) for early in range(2) for a in range(2)]
    frames = (1 - parity, parity)
    collected = [(jnp.zeros((SPOT, HD), jnp.float32), jnp.zeros((SPOT, HD), jnp.float32)) for _ in units]
    for first in range(0, HEADS, GROUP):
        for slot in range(4 * NFAR):
            tile_copy(corner[0], slot // NFAR, slot % NFAR, slot, first // GROUP).wait()
        work = [(h, u) for h in range(first, first + GROUP) for u in range(len(units))]
        scores = []
        for h, u in work:
            early, a = units[u]
            frame, lanes = frames[early], slice(h * HD, (h + 1) * HD)
            queries = q_ref[frame, a * SPOT : (a + 1) * SPOT, lanes]
            scores.append(contract_last(queries, held[0, frame * 2 + a, :, lanes]))
        weights = []
        for (h, u), value in zip(work, scores):
            early, a = units[u]
            near_peak = near_refs[early][3][a * SPOT : (a + 1) * SPOT, h * HD : (h + 1) * HD]
            value = value * EXP_SCALE
            peak = jnp.maximum(jnp.max(value, axis=-1, keepdims=True), near_peak)
            weights.append((peak, jnp.exp2(near_peak - peak), jnp.exp2(value - peak).astype(jnp.bfloat16)))
        for (h, u), (peak, near_scale, weight) in zip(work, weights):
            early, a = units[u]
            frame, lanes, tokens = frames[early], slice(h * HD, (h + 1) * HD), slice(a * SPOT, (a + 1) * SPOT)
            values = with_ones(held[1, frame * 2 + a, :, lanes])
            summed = jnp.dot(weight, values, preferred_element_type=jnp.float32)
            total = summed[:, HD:]
            out_ref[early, tokens, lanes] = summed[:, :HD] + near_scale * near_refs[early][0][tokens, lanes]
            mask = lane_index(SPOT) == h
            collected[u] = jnp.where(mask, peak, collected[u][0]), jnp.where(mask, total, collected[u][1])
    for (early, a), (peak, total) in zip(units, collected):
        tokens = slice(a * SPOT, (a + 1) * SPOT)
        near_scale = jnp.exp2(near_refs[early][1][tokens, :] - peak)
        peak_ref[early, tokens, :] = peak
        total_ref[early, tokens, :] = total + near_scale * near_refs[early][2][tokens, :]


def far_attention(members, far_frames, queries, buffers, near):
    tokens, features = queries.shape[1:]
    in_vmem = pl.BlockSpec(memory_space=pltpu.VMEM)
    in_specs = [pl.BlockSpec(memory_space=pltpu.SMEM), in_vmem]
    in_specs += [pl.BlockSpec(memory_space=pl.ANY)] * len(buffers) + [in_vmem] * len(near)
    return pl.pallas_call(
        functools.partial(far_kernel, members),
        out_shape=[jax.ShapeDtypeStruct((2, tokens, lanes), jnp.float32) for lanes in (features, HD, HD)],
        in_specs=in_specs,
        out_specs=[in_vmem] * 3,
        scratch_shapes=[
            pltpu.VMEM((2, 4, NFAR * SPOT, features), jnp.bfloat16),
            pltpu.SemaphoreType.DMA((4 * NFAR, HEADS // GROUP)),
        ],
        compiler_params=pltpu.CompilerParams(vmem_limit_bytes=VMEM_LIMIT),
        cost_estimate=kernel_cost(1),
    )(far_frames, queries, *buffers, *near)


def frame_scales(sides, columns, at, own_refs, parts):
    _, own_peak_ref, own_total_ref = own_refs
    wa = lax.axis_index("wa")
    logs = [own_peak_ref[at]]
    for s in range(sides):
        value = join_sums(parts[s][:, HEADS * HD :])
        if columns > 2:
            value = jnp.where(wa < columns - 1 if s == 0 else wa > 0, value, NEGATIVE)
        logs.append(value)
    top = functools.reduce(jnp.maximum, logs)
    scales = [jnp.exp2(value - top) for value in logs]
    total = functools.reduce(jnp.add, [scales[0] * own_total_ref[at]] + scales[1:])
    heads = lane_index(top.shape[0]) < HEADS
    return [split_sums(jnp.where(heads, value / total, 0.0)) for value in scales]


def joined_head(h, at, own_ref, parts, scales):
    row = lax.broadcasted_iota(jnp.int32, (HD, HD), 0)
    spread = jnp.where(jnp.logical_and(row % HEADS == h, row < 3 * HEADS), 1.0, 0.0).astype(jnp.bfloat16)
    lanes = slice(h * HD, (h + 1) * HD)
    factors = [jnp.dot(value, spread, preferred_element_type=jnp.float32) for value in scales]
    joined = factors[0] * own_ref[at, :, lanes]
    for factor, part in zip(factors[1:], parts):
        joined = joined + factor * part[:, lanes].astype(jnp.float32)
    return joined.astype(jnp.bfloat16)


def finish_early_kernel(sides, columns, *refs):
    own_refs, parts, out_ref = refs[:3], refs[3 : 3 + sides], refs[-1]
    scales = frame_scales(sides, columns, 0, own_refs, parts)
    for h in range(HEADS):
        out_ref[:, h * HD : (h + 1) * HD] = joined_head(h, 0, own_refs[0], parts, scales)


def finish_late_kernel(sides, columns, *refs):
    own_refs, parts, (early_ref, out_ref, held, sems) = refs[:3], refs[3 : 3 + sides], refs[3 + sides :]
    parity = lax.axis_index("ta") % 2
    copies = [pltpu.make_async_copy(early_ref, out_ref.at[1 - parity], sems.at[0])]
    copies[0].start()
    scales = frame_scales(sides, columns, 1, own_refs, parts)
    for first in range(0, HEADS, GROUP):
        for h in range(first, first + GROUP):
            held[:, h * HD : (h + 1) * HD] = joined_head(h, 1, own_refs[0], parts, scales)
        lanes = pl.ds(first * HD, GROUP * HD)
        copy = pltpu.make_async_copy(held.at[:, lanes], out_ref.at[parity, :, lanes], sems.at[1 + first // GROUP])
        copy.start()
        copies.append(copy)
    for copy in copies:
        copy.wait()


def finish(columns, own, parts, early_out, cost):
    sides = len(parts)
    frames, tokens, features = own[0].shape
    in_vmem = pl.BlockSpec(memory_space=pltpu.VMEM)
    early = early_out is None
    operands = [*own, *parts] + ([] if early else [early_out])
    one_frame = (tokens, features)
    if early:
        kernel, out_shape, out_spec, scratch = finish_early_kernel, one_frame, in_vmem, []
    else:
        kernel, out_shape, out_spec = finish_late_kernel, (frames, *one_frame), pl.BlockSpec(memory_space=pl.ANY)
        scratch = [pltpu.VMEM(one_frame, jnp.bfloat16), pltpu.SemaphoreType.DMA((1 + HEADS // GROUP,))]
    return pl.pallas_call(
        functools.partial(kernel, sides, columns),
        out_shape=jax.ShapeDtypeStruct(out_shape, jnp.bfloat16),
        in_specs=[in_vmem] * len(operands),
        out_specs=out_spec,
        scratch_shapes=scratch,
        compiler_params=pltpu.CompilerParams(vmem_limit_bytes=VMEM_LIMIT),
        cost_estimate=kernel_cost(cost),
    )(*operands)


def per_device(queries, keyvals, far_frames):
    shape = queries.shape
    frames, rows, columns, features = shape
    tokens = rows * columns
    ta_size, ha_size, wa_size = lax.axis_size("ta"), lax.axis_size("ha"), lax.axis_size("wa")
    queries = queries.reshape(frames, tokens, features)
    keyvals = keyvals.reshape(2, frames, tokens, features)

    core_pairs = [(i, i ^ 1) for i in range(ta_size)]
    cross_pairs = [(i, ta_size - 1 - i) for i in range(ta_size)]
    up = [(i, i + 1) for i in range(ha_size - 1)]
    down = [(i + 1, i) for i in range(ha_size - 1)]
    if wa_size == 2:
        ways = [([(0, 1), (1, 0)], [(0, 1), (1, 0)])]
    else:
        right = [(i, i + 1) for i in range(wa_size - 1)]
        left = [(i + 1, i) for i in range(wa_size - 1)]
        ways = [(right, left), (left, right)]
    tie = lax.optimization_barrier

    core = lax.ppermute(keyvals, "ta", core_pairs)
    last_rows, first_rows, outer, inner = cut(keyvals)
    cross = lax.ppermute(outer, "ta", cross_pairs)
    top = lax.ppermute(last_rows, "ha", up)
    bottom = lax.ppermute(first_rows, "ha", down)
    sent, core = tie((queries, core))
    visitors = [lax.ppermute(sent, "wa", there) for there, _ in ways]
    cross_first, cross_last = widened_rows(cross)
    cross_top = lax.ppermute(cross_last, "ha", up)
    cross_bottom = lax.ppermute(cross_first, "ha", down)
    last = lax.ppermute(inner, "ta", cross_pairs)
    top, bottom, visitors = tie((top, bottom, visitors))
    core_top, core_bottom = [lax.ppermute(value, "ta", core_pairs) for value in inner_rows(top, bottom)]

    early_third = (core, core_top, core_bottom)
    early = near_attention(True, ha_size, keyvals, top, bottom, early_third, visitors, [], 1)
    early_parts = [lax.ppermute(result, "wa", back) for result, (_, back) in zip(early, ways)]
    core_top, _ = tie((core_top, early[0]))
    early_third = (core, core_top, core_bottom)
    early_home = near_attention(True, ha_size, keyvals, top, bottom, early_third, [], [queries], 1)
    cross_top, cross_bottom, _ = tie((cross_top, cross_bottom, early_home[1]))
    late_third = (cross, cross_top, cross_bottom)
    late = near_attention(False, ha_size, keyvals, top, bottom, late_third, visitors, [], 1)
    late_parts = [lax.ppermute(result, "wa", back) for result, (_, back) in zip(late, ways)]
    cross_top, last, _ = tie((cross_top, last, late[0]))
    late_third = (cross, cross_top, cross_bottom)
    late_home = near_attention(False, ha_size, keyvals, top, bottom, late_third, [], [queries], LATE_COST)
    inner_corner = [lax.ppermute(value, "ta", core_pairs) for value in widened_rows(last)]
    sent, early_parts, _ = tie((cross, early_parts, late_home[1]))
    cross_rows = by_rows(sent)
    corner = [lax.ppermute(value, "ta", core_pairs) for value in cross_rows]
    buffers = (core, cross, last, *corner, *inner_corner)
    own = far_attention(ta_size, far_frames, queries, buffers, (*early_home, *late_home))
    out = finish(wa_size, own, early_parts, None, FINISH_COST)
    out = finish(wa_size, own, late_parts, out, 1)
    return out.reshape(shape)


def solution(mesh):
    placed = (P("ta", "ha", "wa", None), P(None, "ta", "ha", "wa", None), P("ta", "ha", "wa", None))
    return jax.shard_map(
        per_device, mesh=mesh, in_specs=placed, out_specs=P("ta", "ha", "wa", None), check_vma=False
    )
```

```python
import functools

import jax
import jax.numpy as jnp
from jax import lax
from jax.experimental import pallas as pl
from jax.experimental.pallas import tpu as pltpu
from jax.sharding import PartitionSpec as P

TILE = 8
HEADS = 16
HD = 128
NFAR = 2
SPOT = TILE * TILE
NEGATIVE = -1e30
EXP_SCALE = HD ** (-0.5) * 1.4426950408889634
VMEM_LIMIT = 16 * 1024 * 1024
GROUP = 4
FINISH_COST = 1
LATE_COST = 28 << 30


def contract_last(left, right):
    return lax.dot_general(left, right, (((1,), (1,)), ((), ())), preferred_element_type=jnp.float32)


def with_ones(values):
    return jnp.concatenate([values, jnp.ones_like(values)], axis=1)


def lane_index(rows):
    return lax.broadcasted_iota(jnp.int32, (rows, HD), 1)


def three_terms(value):
    high = value.astype(jnp.bfloat16).astype(jnp.float32)
    rest = value - high
    middle = rest.astype(jnp.bfloat16).astype(jnp.float32)
    return high, middle, rest - middle


def split_sums(value):
    high, middle, low = three_terms(value)
    return (high + pltpu.roll(middle, HEADS, 1) + pltpu.roll(low, 2 * HEADS, 1)).astype(jnp.bfloat16)


def store_sums(ref, value):
    turned = value.T[:HEADS]
    for i, term in enumerate(three_terms(turned)):
        start = HEADS * 2 * SPOT + i * HEADS
        ref[start : start + HEADS, :] = term.astype(jnp.bfloat16)


def load_sums(ref):
    start = HEADS * 2 * SPOT
    terms = [ref[start + i * HEADS : start + (i + 1) * HEADS, :].astype(jnp.float32) for i in range(3)]
    turned = terms[0] + (terms[1] + terms[2])
    return jnp.concatenate([turned, jnp.zeros((HD - HEADS, turned.shape[1]), jnp.float32)], axis=0).T


def kernel_cost(flops):
    return pl.CostEstimate(flops=flops, bytes_accessed=1, transcendentals=0)


def run_copies(pairs, sems):
    copies = [pltpu.make_async_copy(source, target, sems.at[i]) for i, (source, target) in enumerate(pairs)]
    for copy in copies:
        copy.start()
    for copy in copies:
        copy.wait()


def copying_call(kernel, shapes, copies, *operands):
    in_vmem = pl.BlockSpec(memory_space=pltpu.VMEM)
    return pl.pallas_call(
        kernel,
        out_shape=[jax.ShapeDtypeStruct(shape, operands[0].dtype) for shape in shapes],
        in_specs=[in_vmem] * len(operands),
        out_specs=[in_vmem] * len(shapes),
        scratch_shapes=[pltpu.SemaphoreType.DMA((copies,))],
        compiler_params=pltpu.CompilerParams(vmem_limit_bytes=VMEM_LIMIT),
        cost_estimate=kernel_cost(1),
    )(*operands)


FIRST, LAST = pl.ds(0, SPOT), pl.ds(SPOT, SPOT)


def cut_kernel(keyvals_ref, first_rows_ref, last_rows_ref, outer_ref, inner_ref, sems):
    outer = lax.axis_index("ta") % 2
    pairs = [
        (keyvals_ref.at[:, :, FIRST], first_rows_ref),
        (keyvals_ref.at[:, :, LAST], last_rows_ref),
        (keyvals_ref.at[:, outer], outer_ref),
        (keyvals_ref.at[:, 1 - outer], inner_ref),
    ]
    run_copies(pairs, sems)


def cut(keyvals):
    two, frames, tokens, features = keyvals.shape
    shapes = [(two, frames, SPOT, features)] * 2 + [(two, tokens, features)] * 2
    return copying_call(cut_kernel, shapes, 4, keyvals)


def by_rows_kernel(*refs):
    frame_refs, out_refs, sems = refs[: len(refs) // 3], refs[len(refs) // 3 : -1], refs[-1]
    pairs = []
    for i, frame_ref in enumerate(frame_refs):
        for rows, out_ref in zip((FIRST, LAST), out_refs[2 * i : 2 * i + 2]):
            pairs.append((frame_ref.at[:, rows], out_ref))
    run_copies(pairs, sems)


def by_rows(*frames):
    two, _, features = frames[0].shape
    shapes = [(two, SPOT, features)] * (2 * len(frames))
    return copying_call(by_rows_kernel, shapes, 2 * len(frames), *frames)


def widened_rows_kernel(frame_ref, last_ref, first_ref, sems):
    features = frame_ref.shape[2]
    main, extra = pl.ds(0, features), pl.ds(features, HD)
    pairs = []
    for rows, out_ref in ((LAST, last_ref), (FIRST, first_ref)):
        pairs.append((frame_ref.at[:, rows], out_ref.at[:, :, main]))
        pairs.append((frame_ref.at[:, rows, pl.ds(0, HD)], out_ref.at[:, :, extra]))
    run_copies(pairs, sems)


def widened_rows(frame):
    two, _, features = frame.shape
    return copying_call(widened_rows_kernel, [(two, SPOT, features + HD)] * 2, 4, frame)


def inner_rows_kernel(bottom_ref, top_ref, out_bottom_ref, out_top_ref, sems):
    inner = 1 - lax.axis_index("ta") % 2
    run_copies([(bottom_ref.at[:, inner], out_bottom_ref), (top_ref.at[:, inner], out_top_ref)], sems)


def inner_rows(bottom, top):
    return copying_call(inner_rows_kernel, [top.shape[:1] + top.shape[2:]] * 2, 2, bottom, top)


def near_kernel(sides, home, early, has_rows, own_ref, top_ref, bottom_ref, *refs):
    parity = lax.axis_index("ta") % 2
    ha = lax.axis_index("ha")
    valid = (ha > 0, ha < has_rows - 1)
    ext_ref, ext_top_ref, ext_bottom_ref, refs = refs[0], refs[1], refs[2], refs[3:]
    frame = 1 - parity if early else parity
    count = sides + home
    q_refs, out_refs = refs[:count], refs[count:]
    half = count * SPOT

    def middle(kind, lanes):
        parts = [own_ref[kind, 0, :, lanes], own_ref[kind, 1, :, lanes]]
        parts.append(ext_ref[kind, parity, :, lanes] if early else ext_ref[kind, :, lanes])
        return jnp.concatenate(parts, axis=0)

    def halo(a, kind, lanes, copies):
        ref, ext = ((top_ref, ext_top_ref), (bottom_ref, ext_bottom_ref))[a]
        blocks = [ref[kind, 0, :, lanes], ref[kind, 1, :, lanes]] + [ext[kind, :, lanes]] * copies
        return jnp.concatenate(blocks, axis=0)

    peaks = [jnp.zeros((half, HD), jnp.float32) for _ in range(2)]
    totals = [jnp.ones((half, HD), jnp.float32) for _ in range(2)]
    for first in range(0, HEADS, GROUP):
        members = [slice(h * HD, (h + 1) * HD) for h in range(first, first + GROUP)]
        scores = []
        for lanes in members:
            queries = [
                jnp.concatenate([ref[frame, a * SPOT : (a + 1) * SPOT, lanes] for ref in q_refs], axis=0)
                for a in range(2)
            ]
            near = contract_last(jnp.concatenate(queries, axis=0), middle(0, lanes))
            edges = [contract_last(queries[a], halo(a, 0, lanes, 2)) for a in range(2)]
            scores.append([(near[a * half : (a + 1) * half], edges[a]) for a in range(2)])
        weights = []
        for pairs in scores:
            for a, (near, edge) in enumerate(pairs):
                best = functools.reduce(jnp.maximum, [near[:, i * HD : (i + 1) * HD] for i in range(3)])
                edge_best = jnp.maximum(edge[:, : 2 * SPOT], edge[:, 2 * SPOT :])
                best = jnp.maximum(best, jnp.where(valid[a], edge_best, NEGATIVE))
                peak = jnp.max(best, axis=-1, keepdims=True)
                shift = jnp.where(valid[a], peak, -NEGATIVE)
                near = jnp.exp2((near - peak) * EXP_SCALE).astype(jnp.bfloat16)
                edge = jnp.exp2((edge[:, : 3 * SPOT] - shift) * EXP_SCALE).astype(jnp.bfloat16)
                weights.append((peak, near, edge))
        for i, lanes in enumerate(members):
            mask = lane_index(half) == first + i
            pair = weights[2 * i : 2 * i + 2]
            middle_weights = jnp.concatenate([near for _, near, _ in pair], axis=0)
            middle_sums = jnp.dot(middle_weights, with_ones(middle(1, lanes)), preferred_element_type=jnp.float32)
            for a, (peak, _, edge) in enumerate(pair):
                summed = jnp.dot(edge, with_ones(halo(a, 1, lanes, 1)), preferred_element_type=jnp.float32)
                summed = summed + middle_sums[a * half : (a + 1) * half]
                total = summed[:, HD:]
                peaks[a] = jnp.where(mask, peak, peaks[a])
                totals[a] = jnp.where(mask, total, totals[a])
                for s in range(count):
                    rows = slice(s * SPOT, (s + 1) * SPOT)
                    result = summed[rows, :HD]
                    if s < sides:
                        result = result / total[rows]
                    else:
                        filled = jnp.broadcast_to(peak[rows] * EXP_SCALE, (SPOT, HD))
                        out_refs[s + 3][a * SPOT : (a + 1) * SPOT, lanes] = filled
                        out_refs[s][a * SPOT : (a + 1) * SPOT, lanes] = result
                    if s < sides:
                        start = (first + i) * 2 * SPOT + a * SPOT
                        out_refs[s][start : start + SPOT, :] = result.astype(jnp.bfloat16)
    for s in range(count):
        rows = slice(s * SPOT, (s + 1) * SPOT)
        peak = jnp.concatenate([value[rows] for value in peaks], axis=0) * EXP_SCALE
        total = jnp.concatenate([value[rows] for value in totals], axis=0)
        if s < sides:
            store_sums(out_refs[s], peak + jnp.log2(total))
        else:
            out_refs[s + 1][...] = peak
            out_refs[s + 2][...] = total


def near_attention(early, has_rows, own, top, bottom, third, visitors, queries, cost):
    tokens, features = own.shape[2:]
    operands = [own, top, bottom, *third, *visitors, *queries]
    payload = jax.ShapeDtypeStruct((HEADS * (tokens + 3), HD), jnp.bfloat16)
    outs = [payload for _ in visitors]
    for _ in queries:
        outs += [jax.ShapeDtypeStruct((tokens, lanes), jnp.float32) for lanes in (features, HD, HD, features)]
    in_vmem = pl.BlockSpec(memory_space=pltpu.VMEM)
    return pl.pallas_call(
        functools.partial(near_kernel, len(visitors), len(queries), early, has_rows),
        out_shape=outs,
        in_specs=[in_vmem] * len(operands),
        out_specs=[in_vmem] * len(outs),
        compiler_params=pltpu.CompilerParams(vmem_limit_bytes=VMEM_LIMIT),
        cost_estimate=kernel_cost(cost),
    )(*operands)


def far_kernel(members, far_ref, q_ref, core_ref, *refs):
    cross_ref, cross_inner_ref, corner, corner_inner = refs[0], refs[1], refs[2:4], refs[4:6]
    near_refs, (out_ref, peak_ref, total_ref, held, sems) = (refs[6:10], refs[10:14]), refs[14:]
    ta = lax.axis_index("ta")
    parity = ta % 2

    def tile_copy(source, tile, j, slot, group):
        lanes = pl.ds(group * GROUP * HD, GROUP * HD)
        target = held.at[:, tile, pl.ds(j * SPOT, SPOT), lanes]
        return pltpu.make_async_copy(source.at[:, :, lanes], target, sems.at[slot, group])

    for f in range(2):
        for a in range(2):
            rows = pl.ds(a * SPOT, SPOT)
            for j in range(NFAR):
                slot = (f * 2 + a) * NFAR + j
                wanted = far_ref[f, a, 0, j]
                owner, place = wanted // 2, wanted % 2
                inner = place != owner % 2
                is_core, is_cross = owner == ta + 1 - 2 * parity, owner == members - 1 - ta
                is_corner = jnp.logical_not(jnp.logical_or(is_core, is_cross))
                sources = [
                    (jnp.logical_and(is_core, place == 0), core_ref.at[:, 0, rows]),
                    (jnp.logical_and(is_core, place == 1), core_ref.at[:, 1, rows]),
                    (jnp.logical_and(is_cross, jnp.logical_not(inner)), cross_ref.at[:, rows]),
                    (jnp.logical_and(is_cross, inner), cross_inner_ref.at[:, rows]),
                    (jnp.logical_and(is_corner, jnp.logical_not(inner)), corner[a]),
                    (jnp.logical_and(is_corner, inner), corner_inner[a]),
                ]
                for chosen, source in sources:

                    @pl.when(chosen)
                    def _(source=source, f=f, a=a, j=j, slot=slot):
                        for group in range(HEADS // GROUP):
                            tile_copy(source, f * 2 + a, j, slot, group).start()

    units = [(early, a) for early in range(2) for a in range(2)]
    frames = (1 - parity, parity)
    collected = [(jnp.zeros((SPOT, HD), jnp.float32), jnp.zeros((SPOT, HD), jnp.float32)) for _ in units]
    for first in range(0, HEADS, GROUP):
        for slot in range(4 * NFAR):
            tile_copy(corner[0], slot // NFAR, slot % NFAR, slot, first // GROUP).wait()
        work = [(h, u) for h in range(first, first + GROUP) for u in range(len(units))]
        scores = []
        for h, u in work:
            early, a = units[u]
            frame, lanes = frames[early], slice(h * HD, (h + 1) * HD)
            queries = q_ref[frame, a * SPOT : (a + 1) * SPOT, lanes]
            scores.append(contract_last(queries, held[0, frame * 2 + a, :, lanes]))
        weights = []
        for (h, u), value in zip(work, scores):
            early, a = units[u]
            near_peak = near_refs[early][3][a * SPOT : (a + 1) * SPOT, h * HD : (h + 1) * HD]
            value = value * EXP_SCALE
            peak = jnp.maximum(jnp.max(value, axis=-1, keepdims=True), near_peak)
            weights.append((peak, jnp.exp2(near_peak - peak), jnp.exp2(value - peak).astype(jnp.bfloat16)))
        for (h, u), (peak, near_scale, weight) in zip(work, weights):
            early, a = units[u]
            frame, lanes, tokens = frames[early], slice(h * HD, (h + 1) * HD), slice(a * SPOT, (a + 1) * SPOT)
            values = with_ones(held[1, frame * 2 + a, :, lanes])
            summed = jnp.dot(weight, values, preferred_element_type=jnp.float32)
            total = summed[:, HD:]
            out_ref[early, tokens, lanes] = summed[:, :HD] + near_scale * near_refs[early][0][tokens, lanes]
            mask = lane_index(SPOT) == h
            collected[u] = jnp.where(mask, peak, collected[u][0]), jnp.where(mask, total, collected[u][1])
    for (early, a), (peak, total) in zip(units, collected):
        tokens = slice(a * SPOT, (a + 1) * SPOT)
        near_scale = jnp.exp2(near_refs[early][1][tokens, :] - peak)
        peak_ref[early, tokens, :] = peak
        total_ref[early, tokens, :] = total + near_scale * near_refs[early][2][tokens, :]


def far_attention(members, far_frames, queries, buffers, near):
    tokens, features = queries.shape[1:]
    in_vmem = pl.BlockSpec(memory_space=pltpu.VMEM)
    in_specs = [pl.BlockSpec(memory_space=pltpu.SMEM), in_vmem]
    in_specs += [pl.BlockSpec(memory_space=pl.ANY)] * len(buffers) + [in_vmem] * len(near)
    return pl.pallas_call(
        functools.partial(far_kernel, members),
        out_shape=[jax.ShapeDtypeStruct((2, tokens, lanes), jnp.float32) for lanes in (features, HD, HD)],
        in_specs=in_specs,
        out_specs=[in_vmem] * 3,
        scratch_shapes=[
            pltpu.VMEM((2, 4, NFAR * SPOT, features), jnp.bfloat16),
            pltpu.SemaphoreType.DMA((4 * NFAR, HEADS // GROUP)),
        ],
        compiler_params=pltpu.CompilerParams(vmem_limit_bytes=VMEM_LIMIT),
        cost_estimate=kernel_cost(1),
    )(far_frames, queries, *buffers, *near)


def frame_scales(sides, columns, at, own_refs, parts):
    _, own_peak_ref, own_total_ref = own_refs
    wa = lax.axis_index("wa")
    logs = [own_peak_ref[at]]
    for s in range(sides):
        value = load_sums(parts[s])
        if columns > 2:
            value = jnp.where(wa < columns - 1 if s == 0 else wa > 0, value, NEGATIVE)
        logs.append(value)
    top = functools.reduce(jnp.maximum, logs)
    scales = [jnp.exp2(value - top) for value in logs]
    total = functools.reduce(jnp.add, [scales[0] * own_total_ref[at]] + scales[1:])
    heads = lane_index(top.shape[0]) < HEADS
    return [split_sums(jnp.where(heads, value / total, 0.0)) for value in scales]


def joined_head(h, at, own_ref, parts, scales):
    row = lax.broadcasted_iota(jnp.int32, (HD, HD), 0)
    spread = jnp.where(jnp.logical_and(row % HEADS == h, row < 3 * HEADS), 1.0, 0.0).astype(jnp.bfloat16)
    lanes = slice(h * HD, (h + 1) * HD)
    factors = [jnp.dot(value, spread, preferred_element_type=jnp.float32) for value in scales]
    joined = factors[0] * own_ref[at, :, lanes]
    for factor, part in zip(factors[1:], parts):
        joined = joined + factor * part[h * 2 * SPOT : (h + 1) * 2 * SPOT, :].astype(jnp.float32)
    return joined.astype(jnp.bfloat16)


def finish_early_kernel(sides, columns, *refs):
    own_refs, parts, out_ref = refs[:3], refs[3 : 3 + sides], refs[-1]
    scales = frame_scales(sides, columns, 0, own_refs, parts)
    for h in range(HEADS):
        out_ref[:, h * HD : (h + 1) * HD] = joined_head(h, 0, own_refs[0], parts, scales)


def finish_late_kernel(sides, columns, *refs):
    own_refs, parts, (early_ref, out_ref, held, sems) = refs[:3], refs[3 : 3 + sides], refs[3 + sides :]
    parity = lax.axis_index("ta") % 2
    copies = [pltpu.make_async_copy(early_ref, out_ref.at[1 - parity], sems.at[0])]
    copies[0].start()
    scales = frame_scales(sides, columns, 1, own_refs, parts)
    for first in range(0, HEADS, GROUP):
        for h in range(first, first + GROUP):
            held[:, h * HD : (h + 1) * HD] = joined_head(h, 1, own_refs[0], parts, scales)
        lanes = pl.ds(first * HD, GROUP * HD)
        copy = pltpu.make_async_copy(held.at[:, lanes], out_ref.at[parity, :, lanes], sems.at[1 + first // GROUP])
        copy.start()
        copies.append(copy)
    for copy in copies:
        copy.wait()


def finish(columns, own, parts, early_out, cost):
    sides = len(parts)
    frames, tokens, features = own[0].shape
    in_vmem = pl.BlockSpec(memory_space=pltpu.VMEM)
    early = early_out is None
    operands = [*own, *parts] + ([] if early else [early_out])
    one_frame = (tokens, features)
    if early:
        kernel, out_shape, out_spec, scratch = finish_early_kernel, one_frame, in_vmem, []
    else:
        kernel, out_shape, out_spec = finish_late_kernel, (frames, *one_frame), pl.BlockSpec(memory_space=pl.ANY)
        scratch = [pltpu.VMEM(one_frame, jnp.bfloat16), pltpu.SemaphoreType.DMA((1 + HEADS // GROUP,))]
    return pl.pallas_call(
        functools.partial(kernel, sides, columns),
        out_shape=jax.ShapeDtypeStruct(out_shape, jnp.bfloat16),
        in_specs=[in_vmem] * len(operands),
        out_specs=out_spec,
        scratch_shapes=scratch,
        compiler_params=pltpu.CompilerParams(vmem_limit_bytes=VMEM_LIMIT),
        cost_estimate=kernel_cost(cost),
    )(*operands)


def per_device(queries, keyvals, far_frames):
    shape = queries.shape
    frames, rows, columns, features = shape
    tokens = rows * columns
    ta_size, ha_size, wa_size = lax.axis_size("ta"), lax.axis_size("ha"), lax.axis_size("wa")
    queries = queries.reshape(frames, tokens, features)
    keyvals = keyvals.reshape(2, frames, tokens, features)

    core_pairs = [(i, i ^ 1) for i in range(ta_size)]
    cross_pairs = [(i, ta_size - 1 - i) for i in range(ta_size)]
    up = [(i, i + 1) for i in range(ha_size - 1)]
    down = [(i + 1, i) for i in range(ha_size - 1)]
    if wa_size == 2:
        ways = [([(0, 1), (1, 0)], [(0, 1), (1, 0)])]
    else:
        right = [(i, i + 1) for i in range(wa_size - 1)]
        left = [(i + 1, i) for i in range(wa_size - 1)]
        ways = [(right, left), (left, right)]
    tie = lax.optimization_barrier

    core = lax.ppermute(keyvals, "ta", core_pairs)
    first_rows, last_rows, outer, inner = cut(keyvals)
    cross = lax.ppermute(outer, "ta", cross_pairs)
    bottom = lax.ppermute(first_rows, "ha", down)
    top = lax.ppermute(last_rows, "ha", up)
    sent, core = tie((queries, core))
    visitors = [lax.ppermute(sent, "wa", there) for there, _ in ways]
    cross_last, cross_first = widened_rows(cross)
    cross_top = lax.ppermute(cross_last, "ha", up)
    cross_bottom = lax.ppermute(cross_first, "ha", down)
    last = lax.ppermute(inner, "ta", cross_pairs)
    bottom, top, visitors = tie((bottom, top, visitors))
    core_bottom, core_top = [lax.ppermute(value, "ta", core_pairs) for value in inner_rows(bottom, top)]

    early_third = (core, core_top, core_bottom)
    early = near_attention(True, ha_size, keyvals, top, bottom, early_third, visitors, [], 1)
    early_parts = [lax.ppermute(result, "wa", back) for result, (_, back) in zip(early, ways)]
    core_top, _ = tie((core_top, early[0]))
    early_third = (core, core_top, core_bottom)
    early_home = near_attention(True, ha_size, keyvals, top, bottom, early_third, [], [queries], 1)
    cross_top, cross_bottom, _ = tie((cross_top, cross_bottom, early_home[1]))
    late_third = (cross, cross_top, cross_bottom)
    late = near_attention(False, ha_size, keyvals, top, bottom, late_third, visitors, [], 1)
    late_parts = [lax.ppermute(result, "wa", back) for result, (_, back) in zip(late, ways)]
    cross_top, last, _ = tie((cross_top, last, late[0]))
    late_third = (cross, cross_top, cross_bottom)
    late_home = near_attention(False, ha_size, keyvals, top, bottom, late_third, [], [queries], LATE_COST)
    inner_corner = [lax.ppermute(value, "ta", core_pairs) for value in reversed(widened_rows(last))]
    sent, early_parts, _ = tie((cross, early_parts, late_home[1]))
    cross_rows = by_rows(sent)
    corner = [lax.ppermute(value, "ta", core_pairs) for value in cross_rows]
    buffers = (core, cross, last, *corner, *inner_corner)
    own = far_attention(ta_size, far_frames, queries, buffers, (*early_home, *late_home))
    out = finish(wa_size, own, early_parts, None, FINISH_COST)
    out = finish(wa_size, own, late_parts, out, 1)
    return out.reshape(shape)


def solution(mesh):
    placed = (P("ta", "ha", "wa", None), P(None, "ta", "ha", "wa", None), P("ta", "ha", "wa", None))
    return jax.shard_map(
        per_device, mesh=mesh, in_specs=placed, out_specs=P("ta", "ha", "wa", None), check_vma=False
    )
```

```python
import functools

import jax
import jax.numpy as jnp
from jax import lax
from jax.experimental import pallas as pl
from jax.experimental.pallas import tpu as pltpu
from jax.sharding import PartitionSpec as P

TILE = 8
HEADS = 16
HD = 128
NFAR = 2
SPOT = TILE * TILE
NEGATIVE = -1e30
EXP_SCALE = HD ** (-0.5) * 1.4426950408889634
VMEM_LIMIT = 16 * 1024 * 1024
GROUP = 4
FINISH_COST = 1
LATE_COST = 28 << 30


def contract_last(left, right):
    return lax.dot_general(left, right, (((1,), (1,)), ((), ())), preferred_element_type=jnp.float32)


def with_ones(values):
    return jnp.concatenate([values, jnp.ones_like(values)], axis=1)


def lane_index(rows):
    return lax.broadcasted_iota(jnp.int32, (rows, HD), 1)


def three_terms(value):
    high = value.astype(jnp.bfloat16).astype(jnp.float32)
    rest = value - high
    middle = rest.astype(jnp.bfloat16).astype(jnp.float32)
    return high, middle, rest - middle


def split_sums(value):
    high, middle, low = three_terms(value)
    return (high + pltpu.roll(middle, HEADS, 1) + pltpu.roll(low, 2 * HEADS, 1)).astype(jnp.bfloat16)


def store_sums(ref, value):
    turned = value.T[:HEADS]
    for i, term in enumerate(three_terms(turned)):
        start = HEADS * 2 * SPOT + i * HEADS
        ref[start : start + HEADS, :] = term.astype(jnp.bfloat16)


def load_sums(ref):
    start = HEADS * 2 * SPOT
    terms = [ref[start + i * HEADS : start + (i + 1) * HEADS, :].astype(jnp.float32) for i in range(3)]
    turned = terms[0] + (terms[1] + terms[2])
    return jnp.concatenate([turned, jnp.zeros((HD - HEADS, turned.shape[1]), jnp.float32)], axis=0).T


def kernel_cost(flops):
    return pl.CostEstimate(flops=flops, bytes_accessed=1, transcendentals=0)


def run_copies(pairs, sems):
    copies = [pltpu.make_async_copy(source, target, sems.at[i]) for i, (source, target) in enumerate(pairs)]
    for copy in copies:
        copy.start()
    for copy in copies:
        copy.wait()


def copying_call(kernel, shapes, copies, *operands):
    in_vmem = pl.BlockSpec(memory_space=pltpu.VMEM)
    return pl.pallas_call(
        kernel,
        out_shape=[jax.ShapeDtypeStruct(shape, operands[0].dtype) for shape in shapes],
        in_specs=[in_vmem] * len(operands),
        out_specs=[in_vmem] * len(shapes),
        scratch_shapes=[pltpu.SemaphoreType.DMA((copies,))],
        compiler_params=pltpu.CompilerParams(vmem_limit_bytes=VMEM_LIMIT),
        cost_estimate=kernel_cost(1),
    )(*operands)


FIRST, LAST = pl.ds(0, SPOT), pl.ds(SPOT, SPOT)


def cut_kernel(keyvals_ref, first_rows_ref, last_rows_ref, outer_ref, inner_ref, sems):
    outer = lax.axis_index("ta") % 2
    pairs = [
        (keyvals_ref.at[:, :, FIRST], first_rows_ref),
        (keyvals_ref.at[:, :, LAST], last_rows_ref),
        (keyvals_ref.at[:, outer], outer_ref),
        (keyvals_ref.at[:, 1 - outer], inner_ref),
    ]
    run_copies(pairs, sems)


def cut(keyvals):
    two, frames, tokens, features = keyvals.shape
    shapes = [(two, frames, SPOT, features)] * 2 + [(two, tokens, features)] * 2
    return copying_call(cut_kernel, shapes, 4, keyvals)


def first_rows_kernel(frame_ref, out_ref, sems):
    run_copies([(frame_ref.at[:, FIRST], out_ref)], sems)


def first_rows_of(frame):
    two, _, features = frame.shape
    return copying_call(first_rows_kernel, [(two, SPOT, features)], 1, frame)[0]


def widened_rows_kernel(frame_ref, last_ref, first_ref, sems):
    features = frame_ref.shape[2]
    main, extra = pl.ds(0, features), pl.ds(features, HD)
    pairs = []
    for rows, out_ref in ((LAST, last_ref), (FIRST, first_ref)):
        pairs.append((frame_ref.at[:, rows], out_ref.at[:, :, main]))
        pairs.append((frame_ref.at[:, rows, pl.ds(0, HD)], out_ref.at[:, :, extra]))
    run_copies(pairs, sems)


def widened_rows(frame):
    two, _, features = frame.shape
    return copying_call(widened_rows_kernel, [(two, SPOT, features + HD)] * 2, 4, frame)


def inner_rows_kernel(bottom_ref, top_ref, out_bottom_ref, out_top_ref, sems):
    inner = 1 - lax.axis_index("ta") % 2
    run_copies([(bottom_ref.at[:, inner], out_bottom_ref), (top_ref.at[:, inner], out_top_ref)], sems)


def inner_rows(bottom, top):
    return copying_call(inner_rows_kernel, [top.shape[:1] + top.shape[2:]] * 2, 2, bottom, top)


def near_kernel(sides, home, early, has_rows, own_ref, top_ref, bottom_ref, *refs):
    parity = lax.axis_index("ta") % 2
    ha = lax.axis_index("ha")
    valid = (ha > 0, ha < has_rows - 1)
    ext_ref, ext_top_ref, ext_bottom_ref, refs = refs[0], refs[1], refs[2], refs[3:]
    frame = 1 - parity if early else parity
    count = sides + home
    q_refs, out_refs = refs[:count], refs[count:]
    half = count * SPOT

    def middle(kind, lanes):
        parts = [own_ref[kind, 0, :, lanes], own_ref[kind, 1, :, lanes]]
        parts.append(ext_ref[kind, parity, :, lanes] if early else ext_ref[kind, :, lanes])
        return jnp.concatenate(parts, axis=0)

    def halo(a, kind, lanes, copies):
        ref, ext = ((top_ref, ext_top_ref), (bottom_ref, ext_bottom_ref))[a]
        blocks = [ref[kind, 0, :, lanes], ref[kind, 1, :, lanes]] + [ext[kind, :, lanes]] * copies
        return jnp.concatenate(blocks, axis=0)

    peaks = [jnp.zeros((half, HD), jnp.float32) for _ in range(2)]
    totals = [jnp.ones((half, HD), jnp.float32) for _ in range(2)]
    for first in range(0, HEADS, GROUP):
        members = [slice(h * HD, (h + 1) * HD) for h in range(first, first + GROUP)]
        scores = []
        for lanes in members:
            queries = [
                jnp.concatenate([ref[frame, a * SPOT : (a + 1) * SPOT, lanes] for ref in q_refs], axis=0)
                for a in range(2)
            ]
            near = contract_last(jnp.concatenate(queries, axis=0), middle(0, lanes))
            edges = [contract_last(queries[a], halo(a, 0, lanes, 2)) for a in range(2)]
            scores.append([(near[a * half : (a + 1) * half], edges[a]) for a in range(2)])
        weights = []
        for pairs in scores:
            for a, (near, edge) in enumerate(pairs):
                best = functools.reduce(jnp.maximum, [near[:, i * HD : (i + 1) * HD] for i in range(3)])
                edge_best = jnp.maximum(edge[:, : 2 * SPOT], edge[:, 2 * SPOT :])
                best = jnp.maximum(best, jnp.where(valid[a], edge_best, NEGATIVE))
                peak = jnp.max(best, axis=-1, keepdims=True)
                shift = jnp.where(valid[a], peak, -NEGATIVE)
                near = jnp.exp2((near - peak) * EXP_SCALE).astype(jnp.bfloat16)
                edge = jnp.exp2((edge[:, : 3 * SPOT] - shift) * EXP_SCALE).astype(jnp.bfloat16)
                weights.append((peak, near, edge))
        for i, lanes in enumerate(members):
            mask = lane_index(half) == first + i
            pair = weights[2 * i : 2 * i + 2]
            middle_weights = jnp.concatenate([near for _, near, _ in pair], axis=0)
            middle_sums = jnp.dot(middle_weights, with_ones(middle(1, lanes)), preferred_element_type=jnp.float32)
            for a, (peak, _, edge) in enumerate(pair):
                summed = jnp.dot(edge, with_ones(halo(a, 1, lanes, 1)), preferred_element_type=jnp.float32)
                summed = summed + middle_sums[a * half : (a + 1) * half]
                total = summed[:, HD:]
                peaks[a] = jnp.where(mask, peak, peaks[a])
                totals[a] = jnp.where(mask, total, totals[a])
                for s in range(count):
                    rows = slice(s * SPOT, (s + 1) * SPOT)
                    result = summed[rows, :HD]
                    if s < sides:
                        result = result / total[rows]
                    else:
                        filled = jnp.broadcast_to(peak[rows] * EXP_SCALE, (SPOT, HD))
                        out_refs[s + 3][a * SPOT : (a + 1) * SPOT, lanes] = filled
                        out_refs[s][a * SPOT : (a + 1) * SPOT, lanes] = result
                    if s < sides:
                        start = (first + i) * 2 * SPOT + a * SPOT
                        out_refs[s][start : start + SPOT, :] = result.astype(jnp.bfloat16)
    for s in range(count):
        rows = slice(s * SPOT, (s + 1) * SPOT)
        peak = jnp.concatenate([value[rows] for value in peaks], axis=0) * EXP_SCALE
        total = jnp.concatenate([value[rows] for value in totals], axis=0)
        if s < sides:
            store_sums(out_refs[s], peak + jnp.log2(total))
        else:
            out_refs[s + 1][...] = peak
            out_refs[s + 2][...] = total


def near_attention(early, has_rows, own, top, bottom, third, visitors, queries, cost):
    tokens, features = own.shape[2:]
    operands = [own, top, bottom, *third, *visitors, *queries]
    payload = jax.ShapeDtypeStruct((HEADS * (tokens + 3), HD), jnp.bfloat16)
    outs = [payload for _ in visitors]
    for _ in queries:
        outs += [jax.ShapeDtypeStruct((tokens, lanes), jnp.float32) for lanes in (features, HD, HD, features)]
    in_vmem = pl.BlockSpec(memory_space=pltpu.VMEM)
    return pl.pallas_call(
        functools.partial(near_kernel, len(visitors), len(queries), early, has_rows),
        out_shape=outs,
        in_specs=[in_vmem] * len(operands),
        out_specs=[in_vmem] * len(outs),
        compiler_params=pltpu.CompilerParams(vmem_limit_bytes=VMEM_LIMIT),
        cost_estimate=kernel_cost(cost),
    )(*operands)


def far_kernel(members, far_ref, q_ref, core_ref, *refs):
    cross_ref, cross_inner_ref, corner, corner_inner = refs[0], refs[1], refs[2:4], refs[4:6]
    near_refs, (out_ref, peak_ref, total_ref, held, sems) = (refs[6:10], refs[10:14]), refs[14:]
    ta = lax.axis_index("ta")
    parity = ta % 2

    def tile_copy(source, tile, j, slot, group):
        lanes = pl.ds(group * GROUP * HD, GROUP * HD)
        target = held.at[:, tile, pl.ds(j * SPOT, SPOT), lanes]
        return pltpu.make_async_copy(source.at[:, :, lanes], target, sems.at[slot, group])

    for f in range(2):
        for a in range(2):
            rows = pl.ds(a * SPOT, SPOT)
            for j in range(NFAR):
                slot = (f * 2 + a) * NFAR + j
                wanted = far_ref[f, a, 0, j]
                owner, place = wanted // 2, wanted % 2
                inner = place != owner % 2
                is_core, is_cross = owner == ta + 1 - 2 * parity, owner == members - 1 - ta
                is_corner = jnp.logical_not(jnp.logical_or(is_core, is_cross))
                sources = [
                    (jnp.logical_and(is_core, place == 0), core_ref.at[:, 0, rows]),
                    (jnp.logical_and(is_core, place == 1), core_ref.at[:, 1, rows]),
                    (jnp.logical_and(is_cross, jnp.logical_not(inner)), cross_ref.at[:, rows]),
                    (jnp.logical_and(is_cross, inner), cross_inner_ref.at[:, rows]),
                    (jnp.logical_and(is_corner, jnp.logical_not(inner)), corner[a]),
                    (jnp.logical_and(is_corner, inner), corner_inner[a]),
                ]
                for chosen, source in sources:

                    @pl.when(chosen)
                    def _(source=source, f=f, a=a, j=j, slot=slot):
                        for group in range(HEADS // GROUP):
                            tile_copy(source, f * 2 + a, j, slot, group).start()

    units = [(early, a) for early in range(2) for a in range(2)]
    frames = (1 - parity, parity)
    collected = [(jnp.zeros((SPOT, HD), jnp.float32), jnp.zeros((SPOT, HD), jnp.float32)) for _ in units]
    for first in range(0, HEADS, GROUP):
        for slot in range(4 * NFAR):
            tile_copy(corner[0], slot // NFAR, slot % NFAR, slot, first // GROUP).wait()
        work = [(h, u) for h in range(first, first + GROUP) for u in range(len(units))]
        scores = []
        for h, u in work:
            early, a = units[u]
            frame, lanes = frames[early], slice(h * HD, (h + 1) * HD)
            queries = q_ref[frame, a * SPOT : (a + 1) * SPOT, lanes]
            scores.append(contract_last(queries, held[0, frame * 2 + a, :, lanes]))
        weights = []
        for (h, u), value in zip(work, scores):
            early, a = units[u]
            near_peak = near_refs[early][3][a * SPOT : (a + 1) * SPOT, h * HD : (h + 1) * HD]
            value = value * EXP_SCALE
            peak = jnp.maximum(jnp.max(value, axis=-1, keepdims=True), near_peak)
            weights.append((peak, jnp.exp2(near_peak - peak), jnp.exp2(value - peak).astype(jnp.bfloat16)))
        for (h, u), (peak, near_scale, weight) in zip(work, weights):
            early, a = units[u]
            frame, lanes, tokens = frames[early], slice(h * HD, (h + 1) * HD), slice(a * SPOT, (a + 1) * SPOT)
            values = with_ones(held[1, frame * 2 + a, :, lanes])
            summed = jnp.dot(weight, values, preferred_element_type=jnp.float32)
            total = summed[:, HD:]
            out_ref[early, tokens, lanes] = summed[:, :HD] + near_scale * near_refs[early][0][tokens, lanes]
            mask = lane_index(SPOT) == h
            collected[u] = jnp.where(mask, peak, collected[u][0]), jnp.where(mask, total, collected[u][1])
    for (early, a), (peak, total) in zip(units, collected):
        tokens = slice(a * SPOT, (a + 1) * SPOT)
        near_scale = jnp.exp2(near_refs[early][1][tokens, :] - peak)
        peak_ref[early, tokens, :] = peak
        total_ref[early, tokens, :] = total + near_scale * near_refs[early][2][tokens, :]


def far_attention(members, far_frames, queries, buffers, near):
    tokens, features = queries.shape[1:]
    in_vmem = pl.BlockSpec(memory_space=pltpu.VMEM)
    in_specs = [pl.BlockSpec(memory_space=pltpu.SMEM), in_vmem]
    in_specs += [pl.BlockSpec(memory_space=pl.ANY)] * len(buffers) + [in_vmem] * len(near)
    return pl.pallas_call(
        functools.partial(far_kernel, members),
        out_shape=[jax.ShapeDtypeStruct((2, tokens, lanes), jnp.float32) for lanes in (features, HD, HD)],
        in_specs=in_specs,
        out_specs=[in_vmem] * 3,
        scratch_shapes=[
            pltpu.VMEM((2, 4, NFAR * SPOT, features), jnp.bfloat16),
            pltpu.SemaphoreType.DMA((4 * NFAR, HEADS // GROUP)),
        ],
        compiler_params=pltpu.CompilerParams(vmem_limit_bytes=VMEM_LIMIT),
        cost_estimate=kernel_cost(1),
    )(far_frames, queries, *buffers, *near)


def frame_scales(sides, columns, at, own_refs, parts):
    _, own_peak_ref, own_total_ref = own_refs
    wa = lax.axis_index("wa")
    logs = [own_peak_ref[at]]
    for s in range(sides):
        value = load_sums(parts[s])
        if columns > 2:
            value = jnp.where(wa < columns - 1 if s == 0 else wa > 0, value, NEGATIVE)
        logs.append(value)
    top = functools.reduce(jnp.maximum, logs)
    scales = [jnp.exp2(value - top) for value in logs]
    total = functools.reduce(jnp.add, [scales[0] * own_total_ref[at]] + scales[1:])
    heads = lane_index(top.shape[0]) < HEADS
    return [split_sums(jnp.where(heads, value / total, 0.0)) for value in scales]


def joined_head(h, at, own_ref, parts, scales):
    row = lax.broadcasted_iota(jnp.int32, (HD, HD), 0)
    spread = jnp.where(jnp.logical_and(row % HEADS == h, row < 3 * HEADS), 1.0, 0.0).astype(jnp.bfloat16)
    lanes = slice(h * HD, (h + 1) * HD)
    factors = [jnp.dot(value, spread, preferred_element_type=jnp.float32) for value in scales]
    joined = factors[0] * own_ref[at, :, lanes]
    for factor, part in zip(factors[1:], parts):
        joined = joined + factor * part[h * 2 * SPOT : (h + 1) * 2 * SPOT, :].astype(jnp.float32)
    return joined.astype(jnp.bfloat16)


def finish_early_kernel(sides, columns, *refs):
    own_refs, parts, out_ref = refs[:3], refs[3 : 3 + sides], refs[-1]
    scales = frame_scales(sides, columns, 0, own_refs, parts)
    for h in range(HEADS):
        out_ref[:, h * HD : (h + 1) * HD] = joined_head(h, 0, own_refs[0], parts, scales)


def finish_late_kernel(sides, columns, *refs):
    own_refs, parts, (early_ref, out_ref, held, sems) = refs[:3], refs[3 : 3 + sides], refs[3 + sides :]
    parity = lax.axis_index("ta") % 2
    copies = [pltpu.make_async_copy(early_ref, out_ref.at[1 - parity], sems.at[0])]
    copies[0].start()
    scales = frame_scales(sides, columns, 1, own_refs, parts)
    for first in range(0, HEADS, GROUP):
        for h in range(first, first + GROUP):
            held[:, h * HD : (h + 1) * HD] = joined_head(h, 1, own_refs[0], parts, scales)
        lanes = pl.ds(first * HD, GROUP * HD)
        copy = pltpu.make_async_copy(held.at[:, lanes], out_ref.at[parity, :, lanes], sems.at[1 + first // GROUP])
        copy.start()
        copies.append(copy)
    for copy in copies:
        copy.wait()


def finish(columns, own, parts, early_out, cost):
    sides = len(parts)
    frames, tokens, features = own[0].shape
    in_vmem = pl.BlockSpec(memory_space=pltpu.VMEM)
    early = early_out is None
    operands = [*own, *parts] + ([] if early else [early_out])
    one_frame = (tokens, features)
    if early:
        kernel, out_shape, out_spec, scratch = finish_early_kernel, one_frame, in_vmem, []
    else:
        kernel, out_shape, out_spec = finish_late_kernel, (frames, *one_frame), pl.BlockSpec(memory_space=pl.ANY)
        scratch = [pltpu.VMEM(one_frame, jnp.bfloat16), pltpu.SemaphoreType.DMA((1 + HEADS // GROUP,))]
    return pl.pallas_call(
        functools.partial(kernel, sides, columns),
        out_shape=jax.ShapeDtypeStruct(out_shape, jnp.bfloat16),
        in_specs=[in_vmem] * len(operands),
        out_specs=out_spec,
        scratch_shapes=scratch,
        compiler_params=pltpu.CompilerParams(vmem_limit_bytes=VMEM_LIMIT),
        cost_estimate=kernel_cost(cost),
    )(*operands)


def per_device(queries, keyvals, far_frames):
    shape = queries.shape
    frames, rows, columns, features = shape
    tokens = rows * columns
    ta_size, ha_size, wa_size = lax.axis_size("ta"), lax.axis_size("ha"), lax.axis_size("wa")
    queries = queries.reshape(frames, tokens, features)
    keyvals = keyvals.reshape(2, frames, tokens, features)

    core_pairs = [(i, i ^ 1) for i in range(ta_size)]
    cross_pairs = [(i, ta_size - 1 - i) for i in range(ta_size)]
    up = [(i, i + 1) for i in range(ha_size - 1)]
    down = [(i + 1, i) for i in range(ha_size - 1)]
    if wa_size == 2:
        ways = [([(0, 1), (1, 0)], [(0, 1), (1, 0)])]
    else:
        right = [(i, i + 1) for i in range(wa_size - 1)]
        left = [(i + 1, i) for i in range(wa_size - 1)]
        ways = [(right, left), (left, right)]
    tie = lax.optimization_barrier

    core = lax.ppermute(keyvals, "ta", core_pairs)
    first_rows, last_rows, outer, inner = cut(keyvals)
    cross = lax.ppermute(outer, "ta", cross_pairs)
    bottom = lax.ppermute(first_rows, "ha", down)
    top = lax.ppermute(last_rows, "ha", up)
    sent, core = tie((queries, core))
    visitors = [lax.ppermute(sent, "wa", there) for there, _ in ways]
    cross_last, cross_first = widened_rows(cross)
    cross_top = lax.ppermute(cross_last, "ha", up)
    cross_bottom = lax.ppermute(cross_first, "ha", down)
    last = lax.ppermute(inner, "ta", cross_pairs)
    bottom, top = tie((bottom, top))
    inner_bottom, inner_top = inner_rows(bottom, top)
    core_bottom = lax.ppermute(inner_bottom, "ta", core_pairs)
    inner_top, visitors = tie((inner_top, visitors))
    core_top = lax.ppermute(inner_top, "ta", core_pairs)

    early_third = (core, core_top, core_bottom)
    early = near_attention(True, ha_size, keyvals, top, bottom, early_third, visitors, [], 1)
    early_parts = [lax.ppermute(result, "wa", back) for result, (_, back) in zip(early, ways)]
    core_top, _ = tie((core_top, early[0]))
    early_third = (core, core_top, core_bottom)
    early_home = near_attention(True, ha_size, keyvals, top, bottom, early_third, [], [queries], 1)
    cross_top, cross_bottom, _ = tie((cross_top, cross_bottom, early_home[1]))
    late_third = (cross, cross_top, cross_bottom)
    late = near_attention(False, ha_size, keyvals, top, bottom, late_third, visitors, [], 1)
    late_parts = [lax.ppermute(result, "wa", back) for result, (_, back) in zip(late, ways)]
    cross_top, last, _ = tie((cross_top, last, late[0]))
    late_third = (cross, cross_top, cross_bottom)
    late_home = near_attention(False, ha_size, keyvals, top, bottom, late_third, [], [queries], LATE_COST)
    inner_corner = [lax.ppermute(value, "ta", core_pairs) for value in reversed(widened_rows(last))]
    cross_last, _ = tie((cross_last, late[0]))
    corner_last = lax.ppermute(cross_last, "ta", core_pairs)
    sent, early_parts, _ = tie((cross, early_parts, late_home[1]))
    corner_first = lax.ppermute(first_rows_of(sent), "ta", core_pairs)
    buffers = (core, cross, last, corner_first, corner_last, *inner_corner)
    own = far_attention(ta_size, far_frames, queries, buffers, (*early_home, *late_home))
    out = finish(wa_size, own, early_parts, None, FINISH_COST)
    out = finish(wa_size, own, late_parts, out, 1)
    return out.reshape(shape)


def solution(mesh):
    placed = (P("ta", "ha", "wa", None), P(None, "ta", "ha", "wa", None), P("ta", "ha", "wa", None))
    return jax.shard_map(
        per_device, mesh=mesh, in_specs=placed, out_specs=P("ta", "ha", "wa", None), check_vma=False
    )
```

```python
import functools

import jax
import jax.numpy as jnp
from jax import lax
from jax.experimental import pallas as pl
from jax.experimental.pallas import tpu as pltpu
from jax.sharding import PartitionSpec as P

TILE = 8
HEADS = 16
HD = 128
NFAR = 2
SPOT = TILE * TILE
NEGATIVE = -1e30
EXP_SCALE = HD ** (-0.5) * 1.4426950408889634
VMEM_LIMIT = 16 * 1024 * 1024
GROUP = 4
FINISH_COST = 1
LATE_COST = 28 << 30


def contract_last(left, right):
    return lax.dot_general(left, right, (((1,), (1,)), ((), ())), preferred_element_type=jnp.float32)


def with_ones(values):
    return jnp.concatenate([values, jnp.ones_like(values)], axis=1)


def lane_index(rows):
    return lax.broadcasted_iota(jnp.int32, (rows, HD), 1)


def three_terms(value):
    high = value.astype(jnp.bfloat16).astype(jnp.float32)
    rest = value - high
    middle = rest.astype(jnp.bfloat16).astype(jnp.float32)
    return high, middle, rest - middle


def split_sums(value):
    high, middle, low = three_terms(value)
    return (high + pltpu.roll(middle, HEADS, 1) + pltpu.roll(low, 2 * HEADS, 1)).astype(jnp.bfloat16)


def store_sums(ref, value):
    turned = value.T[:HEADS]
    for i, term in enumerate(three_terms(turned)):
        start = HEADS * 2 * SPOT + i * HEADS
        ref[start : start + HEADS, :] = term.astype(jnp.bfloat16)


def load_sums(ref):
    start = HEADS * 2 * SPOT
    terms = [ref[start + i * HEADS : start + (i + 1) * HEADS, :].astype(jnp.float32) for i in range(3)]
    turned = terms[0] + (terms[1] + terms[2])
    return jnp.concatenate([turned, jnp.zeros((HD - HEADS, turned.shape[1]), jnp.float32)], axis=0).T


def kernel_cost(flops):
    return pl.CostEstimate(flops=flops, bytes_accessed=1, transcendentals=0)


def run_copies(pairs, sems):
    copies = [pltpu.make_async_copy(source, target, sems.at[i]) for i, (source, target) in enumerate(pairs)]
    for copy in copies:
        copy.start()
    for copy in copies:
        copy.wait()


def copying_call(kernel, shapes, copies, *operands):
    in_vmem = pl.BlockSpec(memory_space=pltpu.VMEM)
    return pl.pallas_call(
        kernel,
        out_shape=[jax.ShapeDtypeStruct(shape, operands[0].dtype) for shape in shapes],
        in_specs=[in_vmem] * len(operands),
        out_specs=[in_vmem] * len(shapes),
        scratch_shapes=[pltpu.SemaphoreType.DMA((copies,))],
        compiler_params=pltpu.CompilerParams(vmem_limit_bytes=VMEM_LIMIT),
        cost_estimate=kernel_cost(1),
    )(*operands)


FIRST, LAST = pl.ds(0, SPOT), pl.ds(SPOT, SPOT)


def cut_kernel(keyvals_ref, first_rows_ref, last_rows_ref, outer_ref, inner_ref, sems):
    outer = lax.axis_index("ta") % 2
    pairs = [
        (keyvals_ref.at[:, :, FIRST], first_rows_ref),
        (keyvals_ref.at[:, :, LAST], last_rows_ref),
        (keyvals_ref.at[:, outer], outer_ref),
        (keyvals_ref.at[:, 1 - outer], inner_ref),
    ]
    run_copies(pairs, sems)


def cut(keyvals):
    two, frames, tokens, features = keyvals.shape
    shapes = [(two, frames, SPOT, features)] * 2 + [(two, tokens, features)] * 2
    return copying_call(cut_kernel, shapes, 4, keyvals)


def last_rows_kernel(frame_ref, out_ref, sems):
    run_copies([(frame_ref.at[:, LAST], out_ref)], sems)


def last_rows_of(frame):
    two, _, features = frame.shape
    return copying_call(last_rows_kernel, [(two, SPOT, features)], 1, frame)[0]


def widened_rows_kernel(frame_ref, last_ref, first_ref, sems):
    features = frame_ref.shape[2]
    main, extra = pl.ds(0, features), pl.ds(features, HD)
    pairs = []
    for rows, out_ref in ((LAST, last_ref), (FIRST, first_ref)):
        pairs.append((frame_ref.at[:, rows], out_ref.at[:, :, main]))
        pairs.append((frame_ref.at[:, rows, pl.ds(0, HD)], out_ref.at[:, :, extra]))
    run_copies(pairs, sems)


def widened_rows(frame):
    two, _, features = frame.shape
    return copying_call(widened_rows_kernel, [(two, SPOT, features + HD)] * 2, 4, frame)


def inner_rows_kernel(bottom_ref, top_ref, out_bottom_ref, out_top_ref, sems):
    inner = 1 - lax.axis_index("ta") % 2
    run_copies([(bottom_ref.at[:, inner], out_bottom_ref), (top_ref.at[:, inner], out_top_ref)], sems)


def inner_rows(bottom, top):
    return copying_call(inner_rows_kernel, [top.shape[:1] + top.shape[2:]] * 2, 2, bottom, top)


def near_kernel(sides, home, early, has_rows, own_ref, top_ref, bottom_ref, *refs):
    parity = lax.axis_index("ta") % 2
    ha = lax.axis_index("ha")
    valid = (ha > 0, ha < has_rows - 1)
    ext_ref, ext_top_ref, ext_bottom_ref, refs = refs[0], refs[1], refs[2], refs[3:]
    frame = 1 - parity if early else parity
    count = sides + home
    q_refs, out_refs = refs[:count], refs[count:]
    half = count * SPOT

    def middle(kind, lanes):
        parts = [own_ref[kind, 0, :, lanes], own_ref[kind, 1, :, lanes]]
        parts.append(ext_ref[kind, parity, :, lanes] if early else ext_ref[kind, :, lanes])
        return jnp.concatenate(parts, axis=0)

    def halo(a, kind, lanes, copies):
        ref, ext = ((top_ref, ext_top_ref), (bottom_ref, ext_bottom_ref))[a]
        blocks = [ref[kind, 0, :, lanes], ref[kind, 1, :, lanes]] + [ext[kind, :, lanes]] * copies
        return jnp.concatenate(blocks, axis=0)

    peaks = [jnp.zeros((half, HD), jnp.float32) for _ in range(2)]
    totals = [jnp.ones((half, HD), jnp.float32) for _ in range(2)]
    for first in range(0, HEADS, GROUP):
        members = [slice(h * HD, (h + 1) * HD) for h in range(first, first + GROUP)]
        scores = []
        for lanes in members:
            queries = [
                jnp.concatenate([ref[frame, a * SPOT : (a + 1) * SPOT, lanes] for ref in q_refs], axis=0)
                for a in range(2)
            ]
            near = contract_last(jnp.concatenate(queries, axis=0), middle(0, lanes))
            edges = [contract_last(queries[a], halo(a, 0, lanes, 2)) for a in range(2)]
            scores.append([(near[a * half : (a + 1) * half], edges[a]) for a in range(2)])
        weights = []
        for pairs in scores:
            for a, (near, edge) in enumerate(pairs):
                best = functools.reduce(jnp.maximum, [near[:, i * HD : (i + 1) * HD] for i in range(3)])
                edge_best = jnp.maximum(edge[:, : 2 * SPOT], edge[:, 2 * SPOT :])
                best = jnp.maximum(best, jnp.where(valid[a], edge_best, NEGATIVE))
                peak = jnp.max(best, axis=-1, keepdims=True)
                shift = jnp.where(valid[a], peak, -NEGATIVE)
                near = jnp.exp2((near - peak) * EXP_SCALE).astype(jnp.bfloat16)
                edge = jnp.exp2((edge[:, : 3 * SPOT] - shift) * EXP_SCALE).astype(jnp.bfloat16)
                weights.append((peak, near, edge))
        for i, lanes in enumerate(members):
            mask = lane_index(half) == first + i
            pair = weights[2 * i : 2 * i + 2]
            middle_weights = jnp.concatenate([near for _, near, _ in pair], axis=0)
            middle_sums = jnp.dot(middle_weights, with_ones(middle(1, lanes)), preferred_element_type=jnp.float32)
            for a, (peak, _, edge) in enumerate(pair):
                summed = jnp.dot(edge, with_ones(halo(a, 1, lanes, 1)), preferred_element_type=jnp.float32)
                summed = summed + middle_sums[a * half : (a + 1) * half]
                total = summed[:, HD:]
                peaks[a] = jnp.where(mask, peak, peaks[a])
                totals[a] = jnp.where(mask, total, totals[a])
                for s in range(count):
                    rows = slice(s * SPOT, (s + 1) * SPOT)
                    result = summed[rows, :HD]
                    if s < sides:
                        result = result / total[rows]
                    else:
                        filled = jnp.broadcast_to(peak[rows] * EXP_SCALE, (SPOT, HD))
                        out_refs[s + 3][a * SPOT : (a + 1) * SPOT, lanes] = filled
                        out_refs[s][a * SPOT : (a + 1) * SPOT, lanes] = result
                    if s < sides:
                        start = (first + i) * 2 * SPOT + a * SPOT
                        out_refs[s][start : start + SPOT, :] = result.astype(jnp.bfloat16)
    for s in range(count):
        rows = slice(s * SPOT, (s + 1) * SPOT)
        peak = jnp.concatenate([value[rows] for value in peaks], axis=0) * EXP_SCALE
        total = jnp.concatenate([value[rows] for value in totals], axis=0)
        if s < sides:
            store_sums(out_refs[s], peak + jnp.log2(total))
        else:
            out_refs[s + 1][...] = peak
            out_refs[s + 2][...] = total


def near_attention(early, has_rows, own, top, bottom, third, visitors, queries, cost):
    tokens, features = own.shape[2:]
    operands = [own, top, bottom, *third, *visitors, *queries]
    payload = jax.ShapeDtypeStruct((HEADS * (tokens + 3), HD), jnp.bfloat16)
    outs = [payload for _ in visitors]
    for _ in queries:
        outs += [jax.ShapeDtypeStruct((tokens, lanes), jnp.float32) for lanes in (features, HD, HD, features)]
    in_vmem = pl.BlockSpec(memory_space=pltpu.VMEM)
    return pl.pallas_call(
        functools.partial(near_kernel, len(visitors), len(queries), early, has_rows),
        out_shape=outs,
        in_specs=[in_vmem] * len(operands),
        out_specs=[in_vmem] * len(outs),
        compiler_params=pltpu.CompilerParams(vmem_limit_bytes=VMEM_LIMIT),
        cost_estimate=kernel_cost(cost),
    )(*operands)


def far_kernel(members, far_ref, q_ref, core_ref, *refs):
    cross_ref, cross_inner_ref, corner, corner_inner = refs[0], refs[1], refs[2:4], refs[4:6]
    near_refs, (out_ref, peak_ref, total_ref, held, sems) = (refs[6:10], refs[10:14]), refs[14:]
    ta = lax.axis_index("ta")
    parity = ta % 2

    def tile_copy(source, tile, j, slot, group):
        lanes = pl.ds(group * GROUP * HD, GROUP * HD)
        target = held.at[:, tile, pl.ds(j * SPOT, SPOT), lanes]
        return pltpu.make_async_copy(source.at[:, :, lanes], target, sems.at[slot, group])

    for f in range(2):
        for a in range(2):
            rows = pl.ds(a * SPOT, SPOT)
            for j in range(NFAR):
                slot = (f * 2 + a) * NFAR + j
                wanted = far_ref[f, a, 0, j]
                owner, place = wanted // 2, wanted % 2
                inner = place != owner % 2
                is_core, is_cross = owner == ta + 1 - 2 * parity, owner == members - 1 - ta
                is_corner = jnp.logical_not(jnp.logical_or(is_core, is_cross))
                sources = [
                    (jnp.logical_and(is_core, place == 0), core_ref.at[:, 0, rows]),
                    (jnp.logical_and(is_core, place == 1), core_ref.at[:, 1, rows]),
                    (jnp.logical_and(is_cross, jnp.logical_not(inner)), cross_ref.at[:, rows]),
                    (jnp.logical_and(is_cross, inner), cross_inner_ref.at[:, rows]),
                    (jnp.logical_and(is_corner, jnp.logical_not(inner)), corner[a]),
                    (jnp.logical_and(is_corner, inner), corner_inner[a]),
                ]
                for chosen, source in sources:

                    @pl.when(chosen)
                    def _(source=source, f=f, a=a, j=j, slot=slot):
                        for group in range(HEADS // GROUP):
                            tile_copy(source, f * 2 + a, j, slot, group).start()

    units = [(early, a) for early in range(2) for a in range(2)]
    frames = (1 - parity, parity)
    collected = [(jnp.zeros((SPOT, HD), jnp.float32), jnp.zeros((SPOT, HD), jnp.float32)) for _ in units]
    for first in range(0, HEADS, GROUP):
        for slot in range(4 * NFAR):
            tile_copy(corner[1], slot // NFAR, slot % NFAR, slot, first // GROUP).wait()
        work = [(h, u) for h in range(first, first + GROUP) for u in range(len(units))]
        scores = []
        for h, u in work:
            early, a = units[u]
            frame, lanes = frames[early], slice(h * HD, (h + 1) * HD)
            queries = q_ref[frame, a * SPOT : (a + 1) * SPOT, lanes]
            scores.append(contract_last(queries, held[0, frame * 2 + a, :, lanes]))
        weights = []
        for (h, u), value in zip(work, scores):
            early, a = units[u]
            near_peak = near_refs[early][3][a * SPOT : (a + 1) * SPOT, h * HD : (h + 1) * HD]
            value = value * EXP_SCALE
            peak = jnp.maximum(jnp.max(value, axis=-1, keepdims=True), near_peak)
            weights.append((peak, jnp.exp2(near_peak - peak), jnp.exp2(value - peak).astype(jnp.bfloat16)))
        for (h, u), (peak, near_scale, weight) in zip(work, weights):
            early, a = units[u]
            frame, lanes, tokens = frames[early], slice(h * HD, (h + 1) * HD), slice(a * SPOT, (a + 1) * SPOT)
            values = with_ones(held[1, frame * 2 + a, :, lanes])
            summed = jnp.dot(weight, values, preferred_element_type=jnp.float32)
            total = summed[:, HD:]
            out_ref[early, tokens, lanes] = summed[:, :HD] + near_scale * near_refs[early][0][tokens, lanes]
            mask = lane_index(SPOT) == h
            collected[u] = jnp.where(mask, peak, collected[u][0]), jnp.where(mask, total, collected[u][1])
    for (early, a), (peak, total) in zip(units, collected):
        tokens = slice(a * SPOT, (a + 1) * SPOT)
        near_scale = jnp.exp2(near_refs[early][1][tokens, :] - peak)
        peak_ref[early, tokens, :] = peak
        total_ref[early, tokens, :] = total + near_scale * near_refs[early][2][tokens, :]


def far_attention(members, far_frames, queries, buffers, near):
    tokens, features = queries.shape[1:]
    in_vmem = pl.BlockSpec(memory_space=pltpu.VMEM)
    in_specs = [pl.BlockSpec(memory_space=pltpu.SMEM), in_vmem]
    in_specs += [pl.BlockSpec(memory_space=pl.ANY)] * len(buffers) + [in_vmem] * len(near)
    return pl.pallas_call(
        functools.partial(far_kernel, members),
        out_shape=[jax.ShapeDtypeStruct((2, tokens, lanes), jnp.float32) for lanes in (features, HD, HD)],
        in_specs=in_specs,
        out_specs=[in_vmem] * 3,
        scratch_shapes=[
            pltpu.VMEM((2, 4, NFAR * SPOT, features), jnp.bfloat16),
            pltpu.SemaphoreType.DMA((4 * NFAR, HEADS // GROUP)),
        ],
        compiler_params=pltpu.CompilerParams(vmem_limit_bytes=VMEM_LIMIT),
        cost_estimate=kernel_cost(1),
    )(far_frames, queries, *buffers, *near)


def frame_scales(sides, columns, at, own_refs, parts):
    _, own_peak_ref, own_total_ref = own_refs
    wa = lax.axis_index("wa")
    logs = [own_peak_ref[at]]
    for s in range(sides):
        value = load_sums(parts[s])
        if columns > 2:
            value = jnp.where(wa < columns - 1 if s == 0 else wa > 0, value, NEGATIVE)
        logs.append(value)
    top = functools.reduce(jnp.maximum, logs)
    scales = [jnp.exp2(value - top) for value in logs]
    total = functools.reduce(jnp.add, [scales[0] * own_total_ref[at]] + scales[1:])
    heads = lane_index(top.shape[0]) < HEADS
    return [split_sums(jnp.where(heads, value / total, 0.0)) for value in scales]


def joined_head(h, at, own_ref, parts, scales):
    row = lax.broadcasted_iota(jnp.int32, (HD, HD), 0)
    spread = jnp.where(jnp.logical_and(row % HEADS == h, row < 3 * HEADS), 1.0, 0.0).astype(jnp.bfloat16)
    lanes = slice(h * HD, (h + 1) * HD)
    factors = [jnp.dot(value, spread, preferred_element_type=jnp.float32) for value in scales]
    joined = factors[0] * own_ref[at, :, lanes]
    for factor, part in zip(factors[1:], parts):
        joined = joined + factor * part[h * 2 * SPOT : (h + 1) * 2 * SPOT, :].astype(jnp.float32)
    return joined.astype(jnp.bfloat16)


def finish_early_kernel(sides, columns, *refs):
    own_refs, parts, out_ref = refs[:3], refs[3 : 3 + sides], refs[-1]
    scales = frame_scales(sides, columns, 0, own_refs, parts)
    for h in range(HEADS):
        out_ref[:, h * HD : (h + 1) * HD] = joined_head(h, 0, own_refs[0], parts, scales)


def finish_late_kernel(sides, columns, *refs):
    own_refs, parts, (early_ref, out_ref, held, sems) = refs[:3], refs[3 : 3 + sides], refs[3 + sides :]
    parity = lax.axis_index("ta") % 2
    copies = [pltpu.make_async_copy(early_ref, out_ref.at[1 - parity], sems.at[0])]
    copies[0].start()
    scales = frame_scales(sides, columns, 1, own_refs, parts)
    for first in range(0, HEADS, GROUP):
        for h in range(first, first + GROUP):
            held[:, h * HD : (h + 1) * HD] = joined_head(h, 1, own_refs[0], parts, scales)
        lanes = pl.ds(first * HD, GROUP * HD)
        copy = pltpu.make_async_copy(held.at[:, lanes], out_ref.at[parity, :, lanes], sems.at[1 + first // GROUP])
        copy.start()
        copies.append(copy)
    for copy in copies:
        copy.wait()


def finish(columns, own, parts, early_out, cost):
    sides = len(parts)
    frames, tokens, features = own[0].shape
    in_vmem = pl.BlockSpec(memory_space=pltpu.VMEM)
    early = early_out is None
    operands = [*own, *parts] + ([] if early else [early_out])
    one_frame = (tokens, features)
    if early:
        kernel, out_shape, out_spec, scratch = finish_early_kernel, one_frame, in_vmem, []
    else:
        kernel, out_shape, out_spec = finish_late_kernel, (frames, *one_frame), pl.BlockSpec(memory_space=pl.ANY)
        scratch = [pltpu.VMEM(one_frame, jnp.bfloat16), pltpu.SemaphoreType.DMA((1 + HEADS // GROUP,))]
    return pl.pallas_call(
        functools.partial(kernel, sides, columns),
        out_shape=jax.ShapeDtypeStruct(out_shape, jnp.bfloat16),
        in_specs=[in_vmem] * len(operands),
        out_specs=out_spec,
        scratch_shapes=scratch,
        compiler_params=pltpu.CompilerParams(vmem_limit_bytes=VMEM_LIMIT),
        cost_estimate=kernel_cost(cost),
    )(*operands)


def per_device(queries, keyvals, far_frames):
    shape = queries.shape
    frames, rows, columns, features = shape
    tokens = rows * columns
    ta_size, ha_size, wa_size = lax.axis_size("ta"), lax.axis_size("ha"), lax.axis_size("wa")
    queries = queries.reshape(frames, tokens, features)
    keyvals = keyvals.reshape(2, frames, tokens, features)

    core_pairs = [(i, i ^ 1) for i in range(ta_size)]
    cross_pairs = [(i, ta_size - 1 - i) for i in range(ta_size)]
    up = [(i, i + 1) for i in range(ha_size - 1)]
    down = [(i + 1, i) for i in range(ha_size - 1)]
    if wa_size == 2:
        ways = [([(0, 1), (1, 0)], [(0, 1), (1, 0)])]
    else:
        right = [(i, i + 1) for i in range(wa_size - 1)]
        left = [(i + 1, i) for i in range(wa_size - 1)]
        ways = [(right, left), (left, right)]
    tie = lax.optimization_barrier

    core = lax.ppermute(keyvals, "ta", core_pairs)
    first_rows, last_rows, outer, inner = cut(keyvals)
    cross = lax.ppermute(outer, "ta", cross_pairs)
    bottom = lax.ppermute(first_rows, "ha", down)
    top = lax.ppermute(last_rows, "ha", up)
    sent, core = tie((queries, core))
    visitors = [lax.ppermute(sent, "wa", there) for there, _ in ways]
    cross_last, cross_first = widened_rows(cross)
    cross_top = lax.ppermute(cross_last, "ha", up)
    cross_bottom = lax.ppermute(cross_first, "ha", down)
    last = lax.ppermute(inner, "ta", cross_pairs)
    bottom, top = tie((bottom, top))
    inner_bottom, inner_top = inner_rows(bottom, top)
    core_bottom = lax.ppermute(inner_bottom, "ta", core_pairs)
    inner_top, visitors = tie((inner_top, visitors))
    core_top = lax.ppermute(inner_top, "ta", core_pairs)

    early_third = (core, core_top, core_bottom)
    early = near_attention(True, ha_size, keyvals, top, bottom, early_third, visitors, [], 1)
    early_parts = [lax.ppermute(result, "wa", back) for result, (_, back) in zip(early, ways)]
    core_top, _ = tie((core_top, early[0]))
    early_third = (core, core_top, core_bottom)
    early_home = near_attention(True, ha_size, keyvals, top, bottom, early_third, [], [queries], 1)
    cross_top, cross_bottom, _ = tie((cross_top, cross_bottom, early_home[1]))
    late_third = (cross, cross_top, cross_bottom)
    late = near_attention(False, ha_size, keyvals, top, bottom, late_third, visitors, [], 1)
    late_parts = [lax.ppermute(result, "wa", back) for result, (_, back) in zip(late, ways)]
    cross_top, last, _ = tie((cross_top, last, late[0]))
    late_third = (cross, cross_top, cross_bottom)
    late_home = near_attention(False, ha_size, keyvals, top, bottom, late_third, [], [queries], LATE_COST)
    inner_corner = [lax.ppermute(value, "ta", core_pairs) for value in reversed(widened_rows(last))]
    cross_first, _ = tie((cross_first, late[0]))
    corner_first = lax.ppermute(cross_first, "ta", core_pairs)
    sent, early_parts, _ = tie((cross, early_parts, late_home[1]))
    corner_last = lax.ppermute(last_rows_of(sent), "ta", core_pairs)
    buffers = (core, cross, last, corner_first, corner_last, *inner_corner)
    own = far_attention(ta_size, far_frames, queries, buffers, (*early_home, *late_home))
    out = finish(wa_size, own, early_parts, None, FINISH_COST)
    out = finish(wa_size, own, late_parts, out, 1)
    return out.reshape(shape)


def solution(mesh):
    placed = (P("ta", "ha", "wa", None), P(None, "ta", "ha", "wa", None), P("ta", "ha", "wa", None))
    return jax.shard_map(
        per_device, mesh=mesh, in_specs=placed, out_specs=P("ta", "ha", "wa", None), check_vma=False
    )
```

```python
import functools

import jax
import jax.numpy as jnp
from jax import lax
from jax.experimental import pallas as pl
from jax.experimental.pallas import tpu as pltpu
from jax.sharding import PartitionSpec as P

TILE = 8
HEADS = 16
HD = 128
NFAR = 2
SPOT = TILE * TILE
NEGATIVE = -1e30
EXP_SCALE = HD ** (-0.5) * 1.4426950408889634
VMEM_LIMIT = 16 * 1024 * 1024
GROUP = 4
NEAR_GROUP = 8
FINISH_COST = 1
LATE_COST = 28 << 30


def contract_last(left, right):
    return lax.dot_general(left, right, (((1,), (1,)), ((), ())), preferred_element_type=jnp.float32)


def with_ones(values):
    return jnp.concatenate([values, jnp.ones_like(values)], axis=1)


def lane_index(rows):
    return lax.broadcasted_iota(jnp.int32, (rows, HD), 1)


def three_terms(value):
    high = value.astype(jnp.bfloat16).astype(jnp.float32)
    rest = value - high
    middle = rest.astype(jnp.bfloat16).astype(jnp.float32)
    return high, middle, rest - middle


def split_sums(value):
    high, middle, low = three_terms(value)
    return (high + pltpu.roll(middle, HEADS, 1) + pltpu.roll(low, 2 * HEADS, 1)).astype(jnp.bfloat16)


def store_sums(ref, value):
    turned = value.T[:HEADS]
    for i, term in enumerate(three_terms(turned)):
        start = HEADS * 2 * SPOT + i * HEADS
        ref[start : start + HEADS, :] = term.astype(jnp.bfloat16)


def load_sums(ref):
    start = HEADS * 2 * SPOT
    terms = [ref[start + i * HEADS : start + (i + 1) * HEADS, :].astype(jnp.float32) for i in range(3)]
    turned = terms[0] + (terms[1] + terms[2])
    return jnp.concatenate([turned, jnp.zeros((HD - HEADS, turned.shape[1]), jnp.float32)], axis=0).T


def kernel_cost(flops):
    return pl.CostEstimate(flops=flops, bytes_accessed=1, transcendentals=0)


def run_copies(pairs, sems):
    copies = [pltpu.make_async_copy(source, target, sems.at[i]) for i, (source, target) in enumerate(pairs)]
    for copy in copies:
        copy.start()
    for copy in copies:
        copy.wait()


def copying_call(kernel, shapes, copies, *operands):
    in_vmem = pl.BlockSpec(memory_space=pltpu.VMEM)
    return pl.pallas_call(
        kernel,
        out_shape=[jax.ShapeDtypeStruct(shape, operands[0].dtype) for shape in shapes],
        in_specs=[in_vmem] * len(operands),
        out_specs=[in_vmem] * len(shapes),
        scratch_shapes=[pltpu.SemaphoreType.DMA((copies,))],
        compiler_params=pltpu.CompilerParams(vmem_limit_bytes=VMEM_LIMIT),
        cost_estimate=kernel_cost(1),
    )(*operands)


FIRST, LAST = pl.ds(0, SPOT), pl.ds(SPOT, SPOT)


def cut_kernel(keyvals_ref, first_rows_ref, last_rows_ref, outer_ref, inner_ref, sems):
    outer = lax.axis_index("ta") % 2
    pairs = [
        (keyvals_ref.at[:, :, FIRST], first_rows_ref),
        (keyvals_ref.at[:, :, LAST], last_rows_ref),
        (keyvals_ref.at[:, outer], outer_ref),
        (keyvals_ref.at[:, 1 - outer], inner_ref),
    ]
    run_copies(pairs, sems)


def cut(keyvals):
    two, frames, tokens, features = keyvals.shape
    shapes = [(two, frames, SPOT, features)] * 2 + [(two, tokens, features)] * 2
    return copying_call(cut_kernel, shapes, 4, keyvals)


def last_rows_kernel(frame_ref, out_ref, sems):
    run_copies([(frame_ref.at[:, LAST], out_ref)], sems)


def last_rows_of(frame):
    two, _, features = frame.shape
    return copying_call(last_rows_kernel, [(two, SPOT, features)], 1, frame)[0]


def widened_rows_kernel(frame_ref, last_ref, first_ref, sems):
    features = frame_ref.shape[2]
    main, extra = pl.ds(0, features), pl.ds(features, HD)
    pairs = []
    for rows, out_ref in ((LAST, last_ref), (FIRST, first_ref)):
        pairs.append((frame_ref.at[:, rows], out_ref.at[:, :, main]))
        pairs.append((frame_ref.at[:, rows, pl.ds(0, HD)], out_ref.at[:, :, extra]))
    run_copies(pairs, sems)


def widened_rows(frame):
    two, _, features = frame.shape
    return copying_call(widened_rows_kernel, [(two, SPOT, features + HD)] * 2, 4, frame)


def inner_rows_kernel(bottom_ref, top_ref, out_bottom_ref, out_top_ref, sems):
    inner = 1 - lax.axis_index("ta") % 2
    run_copies([(bottom_ref.at[:, inner], out_bottom_ref), (top_ref.at[:, inner], out_top_ref)], sems)


def inner_rows(bottom, top):
    return copying_call(inner_rows_kernel, [top.shape[:1] + top.shape[2:]] * 2, 2, bottom, top)


def corrected_reciprocal(value):
    first = pl.reciprocal(value, approx=True)
    second = first * (2.0 - value * first)
    return second * (2.0 - value * second)


def near_kernel(sides, home, early, has_rows, own_ref, top_ref, bottom_ref, *refs):
    parity = lax.axis_index("ta") % 2
    ha = lax.axis_index("ha")
    valid = (ha > 0, ha < has_rows - 1)
    ext_ref, ext_top_ref, ext_bottom_ref, refs = refs[0], refs[1], refs[2], refs[3:]
    frame = 1 - parity if early else parity
    count = sides + home
    q_refs, out_refs = refs[:count], refs[count:]
    half = count * SPOT

    def middle(kind, lanes):
        parts = [own_ref[kind, 0, :, lanes], own_ref[kind, 1, :, lanes]]
        parts.append(ext_ref[kind, parity, :, lanes] if early else ext_ref[kind, :, lanes])
        return jnp.concatenate(parts, axis=0)

    def halo(a, kind, lanes, copies):
        ref, ext = ((top_ref, ext_top_ref), (bottom_ref, ext_bottom_ref))[a]
        blocks = [ref[kind, 0, :, lanes], ref[kind, 1, :, lanes]] + [ext[kind, :, lanes]] * copies
        return jnp.concatenate(blocks, axis=0)

    peaks = [jnp.zeros((half, HD), jnp.float32) for _ in range(2)]
    totals = [jnp.ones((half, HD), jnp.float32) for _ in range(2)]
    for first in range(0, HEADS, NEAR_GROUP):
        members = [slice(h * HD, (h + 1) * HD) for h in range(first, first + NEAR_GROUP)]
        scores = []
        for lanes in members:
            queries = [
                jnp.concatenate([ref[frame, a * SPOT : (a + 1) * SPOT, lanes] for ref in q_refs], axis=0)
                for a in range(2)
            ]
            near = contract_last(jnp.concatenate(queries, axis=0), middle(0, lanes))
            edges = [contract_last(queries[a], halo(a, 0, lanes, 2)) for a in range(2)]
            scores.append([(near[a * half : (a + 1) * half], edges[a]) for a in range(2)])
        weights = []
        for pairs in scores:
            for a, (near, edge) in enumerate(pairs):
                best = functools.reduce(jnp.maximum, [near[:, i * HD : (i + 1) * HD] for i in range(3)])
                edge_best = jnp.maximum(edge[:, : 2 * SPOT], edge[:, 2 * SPOT :])
                best = jnp.maximum(best, jnp.where(valid[a], edge_best, NEGATIVE))
                peak = jnp.max(best, axis=-1, keepdims=True)
                shift = jnp.where(valid[a], peak, -NEGATIVE)
                near = jnp.exp2((near - peak) * EXP_SCALE).astype(jnp.bfloat16)
                edge = jnp.exp2((edge[:, : 3 * SPOT] - shift) * EXP_SCALE).astype(jnp.bfloat16)
                weights.append((peak, near, edge))
        for i, lanes in enumerate(members):
            mask = lane_index(half) == first + i
            pair = weights[2 * i : 2 * i + 2]
            middle_weights = jnp.concatenate([near for _, near, _ in pair], axis=0)
            middle_sums = jnp.dot(middle_weights, with_ones(middle(1, lanes)), preferred_element_type=jnp.float32)
            for a, (peak, _, edge) in enumerate(pair):
                summed = jnp.dot(edge, with_ones(halo(a, 1, lanes, 1)), preferred_element_type=jnp.float32)
                summed = summed + middle_sums[a * half : (a + 1) * half]
                total = summed[:, HD:]
                peaks[a] = jnp.where(mask, peak, peaks[a])
                totals[a] = jnp.where(mask, total, totals[a])
                for s in range(count):
                    rows = slice(s * SPOT, (s + 1) * SPOT)
                    result = summed[rows, :HD]
                    if s < sides:
                        result = result * corrected_reciprocal(total[rows])
                    else:
                        filled = jnp.broadcast_to(peak[rows] * EXP_SCALE, (SPOT, HD))
                        out_refs[s + 3][a * SPOT : (a + 1) * SPOT, lanes] = filled
                        out_refs[s][a * SPOT : (a + 1) * SPOT, lanes] = result
                    if s < sides:
                        start = (first + i) * 2 * SPOT + a * SPOT
                        out_refs[s][start : start + SPOT, :] = result.astype(jnp.bfloat16)
    for s in range(count):
        rows = slice(s * SPOT, (s + 1) * SPOT)
        peak = jnp.concatenate([value[rows] for value in peaks], axis=0) * EXP_SCALE
        total = jnp.concatenate([value[rows] for value in totals], axis=0)
        if s < sides:
            store_sums(out_refs[s], peak + jnp.log2(total))
        else:
            out_refs[s + 1][...] = peak
            out_refs[s + 2][...] = total


def near_attention(early, has_rows, own, top, bottom, third, visitors, queries, cost):
    tokens, features = own.shape[2:]
    operands = [own, top, bottom, *third, *visitors, *queries]
    payload = jax.ShapeDtypeStruct((HEADS * (tokens + 3), HD), jnp.bfloat16)
    outs = [payload for _ in visitors]
    for _ in queries:
        outs += [jax.ShapeDtypeStruct((tokens, lanes), jnp.float32) for lanes in (features, HD, HD, features)]
    in_vmem = pl.BlockSpec(memory_space=pltpu.VMEM)
    return pl.pallas_call(
        functools.partial(near_kernel, len(visitors), len(queries), early, has_rows),
        out_shape=outs,
        in_specs=[in_vmem] * len(operands),
        out_specs=[in_vmem] * len(outs),
        compiler_params=pltpu.CompilerParams(vmem_limit_bytes=VMEM_LIMIT),
        cost_estimate=kernel_cost(cost),
    )(*operands)


def far_kernel(members, far_ref, q_ref, core_ref, *refs):
    cross_ref, cross_inner_ref, corner, corner_inner = refs[0], refs[1], refs[2:4], refs[4:6]
    near_refs, (out_ref, peak_ref, total_ref, held, sems) = (refs[6:10], refs[10:14]), refs[14:]
    ta = lax.axis_index("ta")
    parity = ta % 2

    def tile_copy(source, tile, j, slot, group):
        lanes = pl.ds(group * GROUP * HD, GROUP * HD)
        target = held.at[:, tile, pl.ds(j * SPOT, SPOT), lanes]
        return pltpu.make_async_copy(source.at[:, :, lanes], target, sems.at[slot, group])

    for f in range(2):
        for a in range(2):
            rows = pl.ds(a * SPOT, SPOT)
            for j in range(NFAR):
                slot = (f * 2 + a) * NFAR + j
                wanted = far_ref[f, a, 0, j]
                owner, place = wanted // 2, wanted % 2
                inner = place != owner % 2
                is_core, is_cross = owner == ta + 1 - 2 * parity, owner == members - 1 - ta
                is_corner = jnp.logical_not(jnp.logical_or(is_core, is_cross))
                sources = [
                    (jnp.logical_and(is_core, place == 0), core_ref.at[:, 0, rows]),
                    (jnp.logical_and(is_core, place == 1), core_ref.at[:, 1, rows]),
                    (jnp.logical_and(is_cross, jnp.logical_not(inner)), cross_ref.at[:, rows]),
                    (jnp.logical_and(is_cross, inner), cross_inner_ref.at[:, rows]),
                    (jnp.logical_and(is_corner, jnp.logical_not(inner)), corner[a]),
                    (jnp.logical_and(is_corner, inner), corner_inner[a]),
                ]
                for chosen, source in sources:

                    @pl.when(chosen)
                    def _(source=source, f=f, a=a, j=j, slot=slot):
                        for group in range(HEADS // GROUP):
                            tile_copy(source, f * 2 + a, j, slot, group).start()

    units = [(early, a) for early in range(2) for a in range(2)]
    frames = (1 - parity, parity)
    collected = [(jnp.zeros((SPOT, HD), jnp.float32), jnp.zeros((SPOT, HD), jnp.float32)) for _ in units]
    for first in range(0, HEADS, GROUP):
        for slot in range(4 * NFAR):
            tile_copy(corner[1], slot // NFAR, slot % NFAR, slot, first // GROUP).wait()
        work = [(h, u) for h in range(first, first + GROUP) for u in range(len(units))]
        scores = []
        for h, u in work:
            early, a = units[u]
            frame, lanes = frames[early], slice(h * HD, (h + 1) * HD)
            queries = q_ref[frame, a * SPOT : (a + 1) * SPOT, lanes]
            scores.append(contract_last(queries, held[0, frame * 2 + a, :, lanes]))
        weights = []
        for (h, u), value in zip(work, scores):
            early, a = units[u]
            near_peak = near_refs[early][3][a * SPOT : (a + 1) * SPOT, h * HD : (h + 1) * HD]
            value = value * EXP_SCALE
            peak = jnp.maximum(jnp.max(value, axis=-1, keepdims=True), near_peak)
            weights.append((peak, jnp.exp2(near_peak - peak), jnp.exp2(value - peak).astype(jnp.bfloat16)))
        for (h, u), (peak, near_scale, weight) in zip(work, weights):
            early, a = units[u]
            frame, lanes, tokens = frames[early], slice(h * HD, (h + 1) * HD), slice(a * SPOT, (a + 1) * SPOT)
            values = with_ones(held[1, frame * 2 + a, :, lanes])
            summed = jnp.dot(weight, values, preferred_element_type=jnp.float32)
            total = summed[:, HD:]
            out_ref[early, tokens, lanes] = summed[:, :HD] + near_scale * near_refs[early][0][tokens, lanes]
            mask = lane_index(SPOT) == h
            collected[u] = jnp.where(mask, peak, collected[u][0]), jnp.where(mask, total, collected[u][1])
    for (early, a), (peak, total) in zip(units, collected):
        tokens = slice(a * SPOT, (a + 1) * SPOT)
        near_scale = jnp.exp2(near_refs[early][1][tokens, :] - peak)
        peak_ref[early, tokens, :] = peak
        total_ref[early, tokens, :] = total + near_scale * near_refs[early][2][tokens, :]


def far_attention(members, far_frames, queries, buffers, near):
    tokens, features = queries.shape[1:]
    in_vmem = pl.BlockSpec(memory_space=pltpu.VMEM)
    in_specs = [pl.BlockSpec(memory_space=pltpu.SMEM), in_vmem]
    in_specs += [pl.BlockSpec(memory_space=pl.ANY)] * len(buffers) + [in_vmem] * len(near)
    return pl.pallas_call(
        functools.partial(far_kernel, members),
        out_shape=[jax.ShapeDtypeStruct((2, tokens, lanes), jnp.float32) for lanes in (features, HD, HD)],
        in_specs=in_specs,
        out_specs=[in_vmem] * 3,
        scratch_shapes=[
            pltpu.VMEM((2, 4, NFAR * SPOT, features), jnp.bfloat16),
            pltpu.SemaphoreType.DMA((4 * NFAR, HEADS // GROUP)),
        ],
        compiler_params=pltpu.CompilerParams(vmem_limit_bytes=VMEM_LIMIT),
        cost_estimate=kernel_cost(1),
    )(far_frames, queries, *buffers, *near)


def frame_scales(sides, columns, at, own_refs, parts):
    _, own_peak_ref, own_total_ref = own_refs
    wa = lax.axis_index("wa")
    logs = [own_peak_ref[at]]
    for s in range(sides):
        value = load_sums(parts[s])
        if columns > 2:
            value = jnp.where(wa < columns - 1 if s == 0 else wa > 0, value, NEGATIVE)
        logs.append(value)
    top = functools.reduce(jnp.maximum, logs)
    scales = [jnp.exp2(value - top) for value in logs]
    total = functools.reduce(jnp.add, [scales[0] * own_total_ref[at]] + scales[1:])
    heads = lane_index(top.shape[0]) < HEADS
    return [split_sums(jnp.where(heads, value / total, 0.0)) for value in scales]


def joined_head(h, at, own_ref, parts, scales):
    row = lax.broadcasted_iota(jnp.int32, (HD, HD), 0)
    spread = jnp.where(jnp.logical_and(row % HEADS == h, row < 3 * HEADS), 1.0, 0.0).astype(jnp.bfloat16)
    lanes = slice(h * HD, (h + 1) * HD)
    factors = [jnp.dot(value, spread, preferred_element_type=jnp.float32) for value in scales]
    joined = factors[0] * own_ref[at, :, lanes]
    for factor, part in zip(factors[1:], parts):
        joined = joined + factor * part[h * 2 * SPOT : (h + 1) * 2 * SPOT, :].astype(jnp.float32)
    return joined.astype(jnp.bfloat16)


def finish_early_kernel(sides, columns, *refs):
    own_refs, parts, out_ref = refs[:3], refs[3 : 3 + sides], refs[-1]
    scales = frame_scales(sides, columns, 0, own_refs, parts)
    for h in range(HEADS):
        out_ref[:, h * HD : (h + 1) * HD] = joined_head(h, 0, own_refs[0], parts, scales)


def finish_late_kernel(sides, columns, *refs):
    own_refs, parts, (early_ref, out_ref, held, sems) = refs[:3], refs[3 : 3 + sides], refs[3 + sides :]
    parity = lax.axis_index("ta") % 2
    copies = [pltpu.make_async_copy(early_ref, out_ref.at[1 - parity], sems.at[0])]
    copies[0].start()
    scales = frame_scales(sides, columns, 1, own_refs, parts)
    for first in range(0, HEADS, GROUP):
        for h in range(first, first + GROUP):
            held[:, h * HD : (h + 1) * HD] = joined_head(h, 1, own_refs[0], parts, scales)
        lanes = pl.ds(first * HD, GROUP * HD)
        copy = pltpu.make_async_copy(held.at[:, lanes], out_ref.at[parity, :, lanes], sems.at[1 + first // GROUP])
        copy.start()
        copies.append(copy)
    for copy in copies:
        copy.wait()


def finish(columns, own, parts, early_out, cost):
    sides = len(parts)
    frames, tokens, features = own[0].shape
    in_vmem = pl.BlockSpec(memory_space=pltpu.VMEM)
    early = early_out is None
    operands = [*own, *parts] + ([] if early else [early_out])
    one_frame = (tokens, features)
    if early:
        kernel, out_shape, out_spec, scratch = finish_early_kernel, one_frame, in_vmem, []
    else:
        kernel, out_shape, out_spec = finish_late_kernel, (frames, *one_frame), pl.BlockSpec(memory_space=pl.ANY)
        scratch = [pltpu.VMEM(one_frame, jnp.bfloat16), pltpu.SemaphoreType.DMA((1 + HEADS // GROUP,))]
    return pl.pallas_call(
        functools.partial(kernel, sides, columns),
        out_shape=jax.ShapeDtypeStruct(out_shape, jnp.bfloat16),
        in_specs=[in_vmem] * len(operands),
        out_specs=out_spec,
        scratch_shapes=scratch,
        compiler_params=pltpu.CompilerParams(vmem_limit_bytes=VMEM_LIMIT),
        cost_estimate=kernel_cost(cost),
    )(*operands)


def per_device(queries, keyvals, far_frames):
    shape = queries.shape
    frames, rows, columns, features = shape
    tokens = rows * columns
    ta_size, ha_size, wa_size = lax.axis_size("ta"), lax.axis_size("ha"), lax.axis_size("wa")
    queries = queries.reshape(frames, tokens, features)
    keyvals = keyvals.reshape(2, frames, tokens, features)

    core_pairs = [(i, i ^ 1) for i in range(ta_size)]
    cross_pairs = [(i, ta_size - 1 - i) for i in range(ta_size)]
    up = [(i, i + 1) for i in range(ha_size - 1)]
    down = [(i + 1, i) for i in range(ha_size - 1)]
    if wa_size == 2:
        ways = [([(0, 1), (1, 0)], [(0, 1), (1, 0)])]
    else:
        right = [(i, i + 1) for i in range(wa_size - 1)]
        left = [(i + 1, i) for i in range(wa_size - 1)]
        ways = [(right, left), (left, right)]
    tie = lax.optimization_barrier

    core = lax.ppermute(keyvals, "ta", core_pairs)
    first_rows, last_rows, outer, inner = cut(keyvals)
    cross = lax.ppermute(outer, "ta", cross_pairs)
    bottom = lax.ppermute(first_rows, "ha", down)
    top = lax.ppermute(last_rows, "ha", up)
    sent, core = tie((queries, core))
    visitors = [lax.ppermute(sent, "wa", there) for there, _ in ways]
    cross_last, cross_first = widened_rows(cross)
    cross_top = lax.ppermute(cross_last, "ha", up)
    cross_bottom = lax.ppermute(cross_first, "ha", down)
    last = lax.ppermute(inner, "ta", cross_pairs)
    bottom, top = tie((bottom, top))
    inner_bottom, inner_top = inner_rows(bottom, top)
    core_bottom = lax.ppermute(inner_bottom, "ta", core_pairs)
    inner_top, visitors = tie((inner_top, visitors))
    core_top = lax.ppermute(inner_top, "ta", core_pairs)

    early_third = (core, core_top, core_bottom)
    early = near_attention(True, ha_size, keyvals, top, bottom, early_third, visitors, [], 1)
    early_parts = [lax.ppermute(result, "wa", back) for result, (_, back) in zip(early, ways)]
    core_top, _ = tie((core_top, early[0]))
    early_third = (core, core_top, core_bottom)
    early_home = near_attention(True, ha_size, keyvals, top, bottom, early_third, [], [queries], 1)
    cross_top, cross_bottom, _ = tie((cross_top, cross_bottom, early_home[1]))
    late_third = (cross, cross_top, cross_bottom)
    late = near_attention(False, ha_size, keyvals, top, bottom, late_third, visitors, [], 1)
    late_parts = [lax.ppermute(result, "wa", back) for result, (_, back) in zip(late, ways)]
    cross_top, last, _ = tie((cross_top, last, late[0]))
    late_third = (cross, cross_top, cross_bottom)
    late_home = near_attention(False, ha_size, keyvals, top, bottom, late_third, [], [queries], LATE_COST)
    inner_corner = [lax.ppermute(value, "ta", core_pairs) for value in reversed(widened_rows(last))]
    cross_first, _ = tie((cross_first, late[0]))
    corner_first = lax.ppermute(cross_first, "ta", core_pairs)
    sent, early_parts, _ = tie((cross, early_parts, late_home[1]))
    corner_last = lax.ppermute(last_rows_of(sent), "ta", core_pairs)
    buffers = (core, cross, last, corner_first, corner_last, *inner_corner)
    own = far_attention(ta_size, far_frames, queries, buffers, (*early_home, *late_home))
    out = finish(wa_size, own, early_parts, None, FINISH_COST)
    out = finish(wa_size, own, late_parts, out, 1)
    return out.reshape(shape)


def solution(mesh):
    placed = (P("ta", "ha", "wa", None), P(None, "ta", "ha", "wa", None), P("ta", "ha", "wa", None))
    return jax.shard_map(
        per_device, mesh=mesh, in_specs=placed, out_specs=P("ta", "ha", "wa", None), check_vma=False
    )
```

```python
import functools

import jax
import jax.numpy as jnp
from jax import lax
from jax.experimental import pallas as pl
from jax.experimental.pallas import tpu as pltpu
from jax.sharding import PartitionSpec as P

TILE = 8
HEADS = 16
HD = 128
NFAR = 2
SPOT = TILE * TILE
NEGATIVE = -1e30
EXP_SCALE = HD ** (-0.5) * 1.4426950408889634
VMEM_LIMIT = 16 * 1024 * 1024
GROUP = 8
NEAR_GROUP = 16
FINISH_COST = 1
LATE_COST = 28 << 30


def contract_last(left, right):
    return lax.dot_general(left, right, (((1,), (1,)), ((), ())), preferred_element_type=jnp.float32)


def with_ones(values):
    return jnp.concatenate([values, jnp.ones_like(values)], axis=1)


def lane_index(rows):
    return lax.broadcasted_iota(jnp.int32, (rows, HD), 1)


def three_terms(value):
    high = value.astype(jnp.bfloat16).astype(jnp.float32)
    rest = value - high
    middle = rest.astype(jnp.bfloat16).astype(jnp.float32)
    return high, middle, rest - middle


def split_sums(value):
    high, middle, low = three_terms(value)
    return (high + pltpu.roll(middle, HEADS, 1) + pltpu.roll(low, 2 * HEADS, 1)).astype(jnp.bfloat16)


def store_sums(ref, value):
    turned = value.T[:HEADS]
    for i, term in enumerate(three_terms(turned)):
        start = HEADS * 2 * SPOT + i * HEADS
        ref[start : start + HEADS, :] = term.astype(jnp.bfloat16)


def load_sums(ref):
    start = HEADS * 2 * SPOT
    terms = [ref[start + i * HEADS : start + (i + 1) * HEADS, :].astype(jnp.float32) for i in range(3)]
    turned = terms[0] + (terms[1] + terms[2])
    return jnp.concatenate([turned, jnp.zeros((HD - HEADS, turned.shape[1]), jnp.float32)], axis=0).T


def kernel_cost(flops):
    return pl.CostEstimate(flops=flops, bytes_accessed=1, transcendentals=0)


def run_copies(pairs, sems):
    copies = [pltpu.make_async_copy(source, target, sems.at[i]) for i, (source, target) in enumerate(pairs)]
    for copy in copies:
        copy.start()
    for copy in copies:
        copy.wait()


def copying_call(kernel, shapes, copies, *operands):
    in_vmem = pl.BlockSpec(memory_space=pltpu.VMEM)
    return pl.pallas_call(
        kernel,
        out_shape=[jax.ShapeDtypeStruct(shape, operands[0].dtype) for shape in shapes],
        in_specs=[in_vmem] * len(operands),
        out_specs=[in_vmem] * len(shapes),
        scratch_shapes=[pltpu.SemaphoreType.DMA((copies,))],
        compiler_params=pltpu.CompilerParams(vmem_limit_bytes=VMEM_LIMIT),
        cost_estimate=kernel_cost(1),
    )(*operands)


FIRST, LAST = pl.ds(0, SPOT), pl.ds(SPOT, SPOT)


def cut_kernel(keyvals_ref, first_rows_ref, last_rows_ref, outer_ref, inner_ref, sems):
    outer = lax.axis_index("ta") % 2
    pairs = [
        (keyvals_ref.at[:, :, FIRST], first_rows_ref),
        (keyvals_ref.at[:, :, LAST], last_rows_ref),
        (keyvals_ref.at[:, outer], outer_ref),
        (keyvals_ref.at[:, 1 - outer], inner_ref),
    ]
    run_copies(pairs, sems)


def cut(keyvals):
    two, frames, tokens, features = keyvals.shape
    shapes = [(two, frames, SPOT, features)] * 2 + [(two, tokens, features)] * 2
    return copying_call(cut_kernel, shapes, 4, keyvals)


def last_rows_kernel(frame_ref, out_ref, sems):
    run_copies([(frame_ref.at[:, LAST], out_ref)], sems)


def last_rows_of(frame):
    two, _, features = frame.shape
    return copying_call(last_rows_kernel, [(two, SPOT, features)], 1, frame)[0]


def widened_rows_kernel(frame_ref, last_ref, first_ref, sems):
    features = frame_ref.shape[2]
    main, extra = pl.ds(0, features), pl.ds(features, HD)
    pairs = []
    for rows, out_ref in ((LAST, last_ref), (FIRST, first_ref)):
        pairs.append((frame_ref.at[:, rows], out_ref.at[:, :, main]))
        pairs.append((frame_ref.at[:, rows, pl.ds(0, HD)], out_ref.at[:, :, extra]))
    run_copies(pairs, sems)


def widened_rows(frame):
    two, _, features = frame.shape
    return copying_call(widened_rows_kernel, [(two, SPOT, features + HD)] * 2, 4, frame)


def inner_rows_kernel(bottom_ref, top_ref, out_bottom_ref, out_top_ref, sems):
    inner = 1 - lax.axis_index("ta") % 2
    run_copies([(bottom_ref.at[:, inner], out_bottom_ref), (top_ref.at[:, inner], out_top_ref)], sems)


def inner_rows(bottom, top):
    return copying_call(inner_rows_kernel, [top.shape[:1] + top.shape[2:]] * 2, 2, bottom, top)


def corrected_reciprocal(value):
    first = pl.reciprocal(value, approx=True)
    second = first * (2.0 - value * first)
    return second * (2.0 - value * second)


def near_kernel(sides, home, early, has_rows, own_ref, top_ref, bottom_ref, *refs):
    parity = lax.axis_index("ta") % 2
    ha = lax.axis_index("ha")
    valid = (ha > 0, ha < has_rows - 1)
    ext_ref, ext_top_ref, ext_bottom_ref, refs = refs[0], refs[1], refs[2], refs[3:]
    frame = 1 - parity if early else parity
    count = sides + home
    q_refs, out_refs = refs[:count], refs[count:]
    half = count * SPOT

    def middle(kind, lanes):
        parts = [own_ref[kind, 0, :, lanes], own_ref[kind, 1, :, lanes]]
        parts.append(ext_ref[kind, parity, :, lanes] if early else ext_ref[kind, :, lanes])
        return jnp.concatenate(parts, axis=0)

    def halo(a, kind, lanes, copies):
        ref, ext = ((top_ref, ext_top_ref), (bottom_ref, ext_bottom_ref))[a]
        blocks = [ref[kind, 0, :, lanes], ref[kind, 1, :, lanes]] + [ext[kind, :, lanes]] * copies
        return jnp.concatenate(blocks, axis=0)

    peaks = [jnp.zeros((half, HD), jnp.float32) for _ in range(2)]
    totals = [jnp.ones((half, HD), jnp.float32) for _ in range(2)]
    for first in range(0, HEADS, NEAR_GROUP):
        members = [slice(h * HD, (h + 1) * HD) for h in range(first, first + NEAR_GROUP)]
        scores = []
        for lanes in members:
            queries = [
                jnp.concatenate([ref[frame, a * SPOT : (a + 1) * SPOT, lanes] for ref in q_refs], axis=0)
                for a in range(2)
            ]
            near = contract_last(jnp.concatenate(queries, axis=0), middle(0, lanes))
            edges = [contract_last(queries[a], halo(a, 0, lanes, 2)) for a in range(2)]
            scores.append([(near[a * half : (a + 1) * half], edges[a]) for a in range(2)])
        weights = []
        for pairs in scores:
            for a, (near, edge) in enumerate(pairs):
                best = functools.reduce(jnp.maximum, [near[:, i * HD : (i + 1) * HD] for i in range(3)])
                edge_best = jnp.maximum(edge[:, : 2 * SPOT], edge[:, 2 * SPOT :])
                best = jnp.maximum(best, jnp.where(valid[a], edge_best, NEGATIVE))
                peak = jnp.max(best, axis=-1, keepdims=True)
                shift = jnp.where(valid[a], peak, -NEGATIVE)
                near = jnp.exp2((near - peak) * EXP_SCALE).astype(jnp.bfloat16)
                edge = jnp.exp2((edge[:, : 3 * SPOT] - shift) * EXP_SCALE).astype(jnp.bfloat16)
                weights.append((peak, near, edge))
        for i, lanes in enumerate(members):
            mask = lane_index(half) == first + i
            pair = weights[2 * i : 2 * i + 2]
            middle_weights = jnp.concatenate([near for _, near, _ in pair], axis=0)
            middle_sums = jnp.dot(middle_weights, with_ones(middle(1, lanes)), preferred_element_type=jnp.float32)
            for a, (peak, _, edge) in enumerate(pair):
                summed = jnp.dot(edge, with_ones(halo(a, 1, lanes, 1)), preferred_element_type=jnp.float32)
                summed = summed + middle_sums[a * half : (a + 1) * half]
                total = summed[:, HD:]
                peaks[a] = jnp.where(mask, peak, peaks[a])
                totals[a] = jnp.where(mask, total, totals[a])
                for s in range(count):
                    rows = slice(s * SPOT, (s + 1) * SPOT)
                    result = summed[rows, :HD]
                    if s < sides:
                        result = result * corrected_reciprocal(total[rows])
                    else:
                        filled = jnp.broadcast_to(peak[rows] * EXP_SCALE, (SPOT, HD))
                        out_refs[s + 3][a * SPOT : (a + 1) * SPOT, lanes] = filled
                        out_refs[s][a * SPOT : (a + 1) * SPOT, lanes] = result
                    if s < sides:
                        start = (first + i) * 2 * SPOT + a * SPOT
                        out_refs[s][start : start + SPOT, :] = result.astype(jnp.bfloat16)
    for s in range(count):
        rows = slice(s * SPOT, (s + 1) * SPOT)
        peak = jnp.concatenate([value[rows] for value in peaks], axis=0) * EXP_SCALE
        total = jnp.concatenate([value[rows] for value in totals], axis=0)
        if s < sides:
            store_sums(out_refs[s], peak + jnp.log2(total))
        else:
            out_refs[s + 1][...] = peak
            out_refs[s + 2][...] = total


def near_attention(early, has_rows, own, top, bottom, third, visitors, queries, cost):
    tokens, features = own.shape[2:]
    operands = [own, top, bottom, *third, *visitors, *queries]
    payload = jax.ShapeDtypeStruct((HEADS * (tokens + 3), HD), jnp.bfloat16)
    outs = [payload for _ in visitors]
    for _ in queries:
        outs += [jax.ShapeDtypeStruct((tokens, lanes), jnp.float32) for lanes in (features, HD, HD, features)]
    in_vmem = pl.BlockSpec(memory_space=pltpu.VMEM)
    return pl.pallas_call(
        functools.partial(near_kernel, len(visitors), len(queries), early, has_rows),
        out_shape=outs,
        in_specs=[in_vmem] * len(operands),
        out_specs=[in_vmem] * len(outs),
        compiler_params=pltpu.CompilerParams(vmem_limit_bytes=VMEM_LIMIT),
        cost_estimate=kernel_cost(cost),
    )(*operands)


def far_kernel(members, far_ref, q_ref, core_ref, *refs):
    cross_ref, cross_inner_ref, corner, corner_inner = refs[0], refs[1], refs[2:4], refs[4:6]
    near_refs, (out_ref, peak_ref, total_ref, held, sems) = (refs[6:10], refs[10:14]), refs[14:]
    ta = lax.axis_index("ta")
    parity = ta % 2

    def tile_copy(source, tile, j, slot, group):
        lanes = pl.ds(group * GROUP * HD, GROUP * HD)
        target = held.at[:, tile, pl.ds(j * SPOT, SPOT), lanes]
        return pltpu.make_async_copy(source.at[:, :, lanes], target, sems.at[slot, group])

    for f in range(2):
        for a in range(2):
            rows = pl.ds(a * SPOT, SPOT)
            for j in range(NFAR):
                slot = (f * 2 + a) * NFAR + j
                wanted = far_ref[f, a, 0, j]
                owner, place = wanted // 2, wanted % 2
                inner = place != owner % 2
                is_core, is_cross = owner == ta + 1 - 2 * parity, owner == members - 1 - ta
                is_corner = jnp.logical_not(jnp.logical_or(is_core, is_cross))
                sources = [
                    (jnp.logical_and(is_core, place == 0), core_ref.at[:, 0, rows]),
                    (jnp.logical_and(is_core, place == 1), core_ref.at[:, 1, rows]),
                    (jnp.logical_and(is_cross, jnp.logical_not(inner)), cross_ref.at[:, rows]),
                    (jnp.logical_and(is_cross, inner), cross_inner_ref.at[:, rows]),
                    (jnp.logical_and(is_corner, jnp.logical_not(inner)), corner[a]),
                    (jnp.logical_and(is_corner, inner), corner_inner[a]),
                ]
                for chosen, source in sources:

                    @pl.when(chosen)
                    def _(source=source, f=f, a=a, j=j, slot=slot):
                        for group in range(HEADS // GROUP):
                            tile_copy(source, f * 2 + a, j, slot, group).start()

    units = [(early, a) for early in range(2) for a in range(2)]
    frames = (1 - parity, parity)
    collected = [(jnp.zeros((SPOT, HD), jnp.float32), jnp.zeros((SPOT, HD), jnp.float32)) for _ in units]
    for first in range(0, HEADS, GROUP):
        for slot in range(4 * NFAR):
            tile_copy(corner[1], slot // NFAR, slot % NFAR, slot, first // GROUP).wait()
        work = [(h, u) for h in range(first, first + GROUP) for u in range(len(units))]
        scores = []
        for h, u in work:
            early, a = units[u]
            frame, lanes = frames[early], slice(h * HD, (h + 1) * HD)
            queries = q_ref[frame, a * SPOT : (a + 1) * SPOT, lanes]
            scores.append(contract_last(queries, held[0, frame * 2 + a, :, lanes]))
        weights = []
        for (h, u), value in zip(work, scores):
            early, a = units[u]
            near_peak = near_refs[early][3][a * SPOT : (a + 1) * SPOT, h * HD : (h + 1) * HD]
            value = value * EXP_SCALE
            peak = jnp.maximum(jnp.max(value, axis=-1, keepdims=True), near_peak)
            weights.append((peak, jnp.exp2(near_peak - peak), jnp.exp2(value - peak).astype(jnp.bfloat16)))
        for (h, u), (peak, near_scale, weight) in zip(work, weights):
            early, a = units[u]
            frame, lanes, tokens = frames[early], slice(h * HD, (h + 1) * HD), slice(a * SPOT, (a + 1) * SPOT)
            values = with_ones(held[1, frame * 2 + a, :, lanes])
            summed = jnp.dot(weight, values, preferred_element_type=jnp.float32)
            total = summed[:, HD:]
            out_ref[early, tokens, lanes] = summed[:, :HD] + near_scale * near_refs[early][0][tokens, lanes]
            mask = lane_index(SPOT) == h
            collected[u] = jnp.where(mask, peak, collected[u][0]), jnp.where(mask, total, collected[u][1])
    for (early, a), (peak, total) in zip(units, collected):
        tokens = slice(a * SPOT, (a + 1) * SPOT)
        near_scale = jnp.exp2(near_refs[early][1][tokens, :] - peak)
        peak_ref[early, tokens, :] = peak
        total_ref[early, tokens, :] = total + near_scale * near_refs[early][2][tokens, :]


def far_attention(members, far_frames, queries, buffers, near):
    tokens, features = queries.shape[1:]
    in_vmem = pl.BlockSpec(memory_space=pltpu.VMEM)
    in_specs = [pl.BlockSpec(memory_space=pltpu.SMEM), in_vmem]
    in_specs += [pl.BlockSpec(memory_space=pl.ANY)] * len(buffers) + [in_vmem] * len(near)
    return pl.pallas_call(
        functools.partial(far_kernel, members),
        out_shape=[jax.ShapeDtypeStruct((2, tokens, lanes), jnp.float32) for lanes in (features, HD, HD)],
        in_specs=in_specs,
        out_specs=[in_vmem] * 3,
        scratch_shapes=[
            pltpu.VMEM((2, 4, NFAR * SPOT, features), jnp.bfloat16),
            pltpu.SemaphoreType.DMA((4 * NFAR, HEADS // GROUP)),
        ],
        compiler_params=pltpu.CompilerParams(vmem_limit_bytes=VMEM_LIMIT),
        cost_estimate=kernel_cost(1),
    )(far_frames, queries, *buffers, *near)


def frame_scales(sides, columns, at, own_refs, parts):
    _, own_peak_ref, own_total_ref = own_refs
    wa = lax.axis_index("wa")
    logs = [own_peak_ref[at]]
    for s in range(sides):
        value = load_sums(parts[s])
        if columns > 2:
            value = jnp.where(wa < columns - 1 if s == 0 else wa > 0, value, NEGATIVE)
        logs.append(value)
    top = functools.reduce(jnp.maximum, logs)
    scales = [jnp.exp2(value - top) for value in logs]
    total = functools.reduce(jnp.add, [scales[0] * own_total_ref[at]] + scales[1:])
    heads = lane_index(top.shape[0]) < HEADS
    return [split_sums(jnp.where(heads, value / total, 0.0)) for value in scales]


def joined_head(h, at, own_ref, parts, scales):
    row = lax.broadcasted_iota(jnp.int32, (HD, HD), 0)
    spread = jnp.where(jnp.logical_and(row % HEADS == h, row < 3 * HEADS), 1.0, 0.0).astype(jnp.bfloat16)
    lanes = slice(h * HD, (h + 1) * HD)
    factors = [jnp.dot(value, spread, preferred_element_type=jnp.float32) for value in scales]
    joined = factors[0] * own_ref[at, :, lanes]
    for factor, part in zip(factors[1:], parts):
        joined = joined + factor * part[h * 2 * SPOT : (h + 1) * 2 * SPOT, :].astype(jnp.float32)
    return joined.astype(jnp.bfloat16)


def finish_early_kernel(sides, columns, *refs):
    own_refs, parts, out_ref = refs[:3], refs[3 : 3 + sides], refs[-1]
    scales = frame_scales(sides, columns, 0, own_refs, parts)
    for h in range(HEADS):
        out_ref[:, h * HD : (h + 1) * HD] = joined_head(h, 0, own_refs[0], parts, scales)


def finish_late_kernel(sides, columns, *refs):
    own_refs, parts, (early_ref, out_ref, held, sems) = refs[:3], refs[3 : 3 + sides], refs[3 + sides :]
    parity = lax.axis_index("ta") % 2
    copies = [pltpu.make_async_copy(early_ref, out_ref.at[1 - parity], sems.at[0])]
    copies[0].start()
    scales = frame_scales(sides, columns, 1, own_refs, parts)
    for first in range(0, HEADS, GROUP):
        for h in range(first, first + GROUP):
            held[:, h * HD : (h + 1) * HD] = joined_head(h, 1, own_refs[0], parts, scales)
        lanes = pl.ds(first * HD, GROUP * HD)
        copy = pltpu.make_async_copy(held.at[:, lanes], out_ref.at[parity, :, lanes], sems.at[1 + first // GROUP])
        copy.start()
        copies.append(copy)
    for copy in copies:
        copy.wait()


def finish(columns, own, parts, early_out, cost):
    sides = len(parts)
    frames, tokens, features = own[0].shape
    in_vmem = pl.BlockSpec(memory_space=pltpu.VMEM)
    early = early_out is None
    operands = [*own, *parts] + ([] if early else [early_out])
    one_frame = (tokens, features)
    if early:
        kernel, out_shape, out_spec, scratch = finish_early_kernel, one_frame, in_vmem, []
    else:
        kernel, out_shape, out_spec = finish_late_kernel, (frames, *one_frame), pl.BlockSpec(memory_space=pl.ANY)
        scratch = [pltpu.VMEM(one_frame, jnp.bfloat16), pltpu.SemaphoreType.DMA((1 + HEADS // GROUP,))]
    return pl.pallas_call(
        functools.partial(kernel, sides, columns),
        out_shape=jax.ShapeDtypeStruct(out_shape, jnp.bfloat16),
        in_specs=[in_vmem] * len(operands),
        out_specs=out_spec,
        scratch_shapes=scratch,
        compiler_params=pltpu.CompilerParams(vmem_limit_bytes=VMEM_LIMIT),
        cost_estimate=kernel_cost(cost),
    )(*operands)


def per_device(queries, keyvals, far_frames):
    shape = queries.shape
    frames, rows, columns, features = shape
    tokens = rows * columns
    ta_size, ha_size, wa_size = lax.axis_size("ta"), lax.axis_size("ha"), lax.axis_size("wa")
    queries = queries.reshape(frames, tokens, features)
    keyvals = keyvals.reshape(2, frames, tokens, features)

    core_pairs = [(i, i ^ 1) for i in range(ta_size)]
    cross_pairs = [(i, ta_size - 1 - i) for i in range(ta_size)]
    up = [(i, i + 1) for i in range(ha_size - 1)]
    down = [(i + 1, i) for i in range(ha_size - 1)]
    if wa_size == 2:
        ways = [([(0, 1), (1, 0)], [(0, 1), (1, 0)])]
    else:
        right = [(i, i + 1) for i in range(wa_size - 1)]
        left = [(i + 1, i) for i in range(wa_size - 1)]
        ways = [(right, left), (left, right)]
    tie = lax.optimization_barrier

    core = lax.ppermute(keyvals, "ta", core_pairs)
    first_rows, last_rows, outer, inner = cut(keyvals)
    cross = lax.ppermute(outer, "ta", cross_pairs)
    bottom = lax.ppermute(first_rows, "ha", down)
    top = lax.ppermute(last_rows, "ha", up)
    sent, core = tie((queries, core))
    visitors = [lax.ppermute(sent, "wa", there) for there, _ in ways]
    cross_last, cross_first = widened_rows(cross)
    cross_top = lax.ppermute(cross_last, "ha", up)
    cross_bottom = lax.ppermute(cross_first, "ha", down)
    last = lax.ppermute(inner, "ta", cross_pairs)
    bottom, top = tie((bottom, top))
    inner_bottom, inner_top = inner_rows(bottom, top)
    core_bottom = lax.ppermute(inner_bottom, "ta", core_pairs)
    inner_top, visitors = tie((inner_top, visitors))
    core_top = lax.ppermute(inner_top, "ta", core_pairs)

    early_third = (core, core_top, core_bottom)
    early = near_attention(True, ha_size, keyvals, top, bottom, early_third, visitors, [], 1)
    early_parts = [lax.ppermute(result, "wa", back) for result, (_, back) in zip(early, ways)]
    core_top, _ = tie((core_top, early[0]))
    early_third = (core, core_top, core_bottom)
    early_home = near_attention(True, ha_size, keyvals, top, bottom, early_third, [], [queries], 1)
    cross_top, cross_bottom, _ = tie((cross_top, cross_bottom, early_home[1]))
    late_third = (cross, cross_top, cross_bottom)
    late = near_attention(False, ha_size, keyvals, top, bottom, late_third, visitors, [], 1)
    late_parts = [lax.ppermute(result, "wa", back) for result, (_, back) in zip(late, ways)]
    cross_top, last, _ = tie((cross_top, last, late[0]))
    late_third = (cross, cross_top, cross_bottom)
    late_home = near_attention(False, ha_size, keyvals, top, bottom, late_third, [], [queries], LATE_COST)
    inner_corner = [lax.ppermute(value, "ta", core_pairs) for value in reversed(widened_rows(last))]
    cross_first, _ = tie((cross_first, late[0]))
    corner_first = lax.ppermute(cross_first, "ta", core_pairs)
    sent, early_parts, _ = tie((cross, early_parts, late_home[1]))
    corner_last = lax.ppermute(last_rows_of(sent), "ta", core_pairs)
    buffers = (core, cross, last, corner_first, corner_last, *inner_corner)
    own = far_attention(ta_size, far_frames, queries, buffers, (*early_home, *late_home))
    out = finish(wa_size, own, early_parts, None, FINISH_COST)
    out = finish(wa_size, own, late_parts, out, 1)
    return out.reshape(shape)


def solution(mesh):
    placed = (P("ta", "ha", "wa", None), P(None, "ta", "ha", "wa", None), P("ta", "ha", "wa", None))
    return jax.shard_map(
        per_device, mesh=mesh, in_specs=placed, out_specs=P("ta", "ha", "wa", None), check_vma=False
    )
```

```python
import functools

import jax
import jax.numpy as jnp
from jax import lax
from jax.experimental import pallas as pl
from jax.experimental.pallas import tpu as pltpu
from jax.sharding import PartitionSpec as P

TILE = 8
HEADS = 16
HD = 128
NFAR = 2
SPOT = TILE * TILE
NEGATIVE = -1e30
EXP_SCALE = HD ** (-0.5) * 1.4426950408889634
VMEM_LIMIT = 16 * 1024 * 1024
GROUP = 8
NEAR_GROUP = 8
FINISH_COST = 1
LATE_COST = 28 << 30


def contract_last(left, right):
    return lax.dot_general(left, right, (((1,), (1,)), ((), ())), preferred_element_type=jnp.float32)


def with_ones(values):
    return jnp.concatenate([values, jnp.ones_like(values)], axis=1)


def lane_index(rows):
    return lax.broadcasted_iota(jnp.int32, (rows, HD), 1)


def three_terms(value):
    high = value.astype(jnp.bfloat16).astype(jnp.float32)
    rest = value - high
    middle = rest.astype(jnp.bfloat16).astype(jnp.float32)
    return high, middle, rest - middle


def split_sums(value):
    high, middle, low = three_terms(value)
    return (high + pltpu.roll(middle, HEADS, 1) + pltpu.roll(low, 2 * HEADS, 1)).astype(jnp.bfloat16)


def store_sums(ref, value):
    turned = value.T[:HEADS]
    for i, term in enumerate(three_terms(turned)):
        start = HEADS * 2 * SPOT + i * HEADS
        ref[start : start + HEADS, :] = term.astype(jnp.bfloat16)


def load_sums(ref):
    start = HEADS * 2 * SPOT
    terms = [ref[start + i * HEADS : start + (i + 1) * HEADS, :].astype(jnp.float32) for i in range(3)]
    turned = terms[0] + (terms[1] + terms[2])
    return jnp.concatenate([turned, jnp.zeros((HD - HEADS, turned.shape[1]), jnp.float32)], axis=0).T


def kernel_cost(flops):
    return pl.CostEstimate(flops=flops, bytes_accessed=1, transcendentals=0)


def run_copies(pairs, sems):
    copies = [pltpu.make_async_copy(source, target, sems.at[i]) for i, (source, target) in enumerate(pairs)]
    for copy in copies:
        copy.start()
    for copy in copies:
        copy.wait()


def copying_call(kernel, shapes, copies, *operands):
    in_vmem = pl.BlockSpec(memory_space=pltpu.VMEM)
    return pl.pallas_call(
        kernel,
        out_shape=[jax.ShapeDtypeStruct(shape, operands[0].dtype) for shape in shapes],
        in_specs=[in_vmem] * len(operands),
        out_specs=[in_vmem] * len(shapes),
        scratch_shapes=[pltpu.SemaphoreType.DMA((copies,))],
        compiler_params=pltpu.CompilerParams(vmem_limit_bytes=VMEM_LIMIT),
        cost_estimate=kernel_cost(1),
    )(*operands)


FIRST, LAST = pl.ds(0, SPOT), pl.ds(SPOT, SPOT)


def cut_kernel(keyvals_ref, first_rows_ref, last_rows_ref, outer_ref, inner_ref, sems):
    outer = lax.axis_index("ta") % 2
    pairs = [
        (keyvals_ref.at[:, :, FIRST], first_rows_ref),
        (keyvals_ref.at[:, :, LAST], last_rows_ref),
        (keyvals_ref.at[:, outer], outer_ref),
        (keyvals_ref.at[:, 1 - outer], inner_ref),
    ]
    run_copies(pairs, sems)


def cut(keyvals):
    two, frames, tokens, features = keyvals.shape
    shapes = [(two, frames, SPOT, features)] * 2 + [(two, tokens, features)] * 2
    return copying_call(cut_kernel, shapes, 4, keyvals)


def last_rows_kernel(frame_ref, out_ref, sems):
    run_copies([(frame_ref.at[:, LAST], out_ref)], sems)


def last_rows_of(frame):
    two, _, features = frame.shape
    return copying_call(last_rows_kernel, [(two, SPOT, features)], 1, frame)[0]


def widened_rows_kernel(frame_ref, last_ref, first_ref, sems):
    features = frame_ref.shape[2]
    main, extra = pl.ds(0, features), pl.ds(features, HD)
    pairs = []
    for rows, out_ref in ((LAST, last_ref), (FIRST, first_ref)):
        pairs.append((frame_ref.at[:, rows], out_ref.at[:, :, main]))
        pairs.append((frame_ref.at[:, rows, pl.ds(0, HD)], out_ref.at[:, :, extra]))
    run_copies(pairs, sems)


def widened_rows(frame):
    two, _, features = frame.shape
    return copying_call(widened_rows_kernel, [(two, SPOT, features + HD)] * 2, 4, frame)


def inner_rows_kernel(bottom_ref, top_ref, out_bottom_ref, out_top_ref, sems):
    inner = 1 - lax.axis_index("ta") % 2
    run_copies([(bottom_ref.at[:, inner], out_bottom_ref), (top_ref.at[:, inner], out_top_ref)], sems)


def inner_rows(bottom, top):
    return copying_call(inner_rows_kernel, [top.shape[:1] + top.shape[2:]] * 2, 2, bottom, top)


def corrected_reciprocal(value):
    first = pl.reciprocal(value, approx=True)
    second = first * (2.0 - value * first)
    return second * (2.0 - value * second)


def near_kernel(sides, home, early, has_rows, own_ref, top_ref, bottom_ref, *refs):
    parity = lax.axis_index("ta") % 2
    ha = lax.axis_index("ha")
    valid = (ha > 0, ha < has_rows - 1)
    ext_ref, ext_top_ref, ext_bottom_ref, refs = refs[0], refs[1], refs[2], refs[3:]
    frame = 1 - parity if early else parity
    count = sides + home
    q_refs, out_refs = refs[:count], refs[count:]
    half = count * SPOT

    def middle(kind, lanes):
        parts = [own_ref[kind, 0, :, lanes], own_ref[kind, 1, :, lanes]]
        parts.append(ext_ref[kind, parity, :, lanes] if early else ext_ref[kind, :, lanes])
        return jnp.concatenate(parts, axis=0)

    def halo(a, kind, lanes, copies):
        ref, ext = ((top_ref, ext_top_ref), (bottom_ref, ext_bottom_ref))[a]
        blocks = [ref[kind, 0, :, lanes], ref[kind, 1, :, lanes]] + [ext[kind, :, lanes]] * copies
        return jnp.concatenate(blocks, axis=0)

    peaks = [jnp.zeros((half, HD), jnp.float32) for _ in range(2)]
    totals = [jnp.ones((half, HD), jnp.float32) for _ in range(2)]
    for first in range(0, HEADS, NEAR_GROUP):
        members = [slice(h * HD, (h + 1) * HD) for h in range(first, first + NEAR_GROUP)]
        scores = []
        for lanes in members:
            queries = [
                jnp.concatenate([ref[frame, a * SPOT : (a + 1) * SPOT, lanes] for ref in q_refs], axis=0)
                for a in range(2)
            ]
            near = contract_last(jnp.concatenate(queries, axis=0), middle(0, lanes))
            edges = [contract_last(queries[a], halo(a, 0, lanes, 2)) for a in range(2)]
            scores.append([(near[a * half : (a + 1) * half], edges[a]) for a in range(2)])
        weights = []
        for pairs in scores:
            for a, (near, edge) in enumerate(pairs):
                best = functools.reduce(jnp.maximum, [near[:, i * HD : (i + 1) * HD] for i in range(3)])
                edge_best = jnp.maximum(edge[:, : 2 * SPOT], edge[:, 2 * SPOT :])
                best = jnp.maximum(best, jnp.where(valid[a], edge_best, NEGATIVE))
                peak = jnp.max(best, axis=-1, keepdims=True)
                shift = jnp.where(valid[a], peak, -NEGATIVE)
                near = jnp.exp2((near - peak) * EXP_SCALE).astype(jnp.bfloat16)
                edge = jnp.exp2((edge[:, : 3 * SPOT] - shift) * EXP_SCALE).astype(jnp.bfloat16)
                weights.append((peak, near, edge))
        for i, lanes in enumerate(members):
            mask = lane_index(half) == first + i
            pair = weights[2 * i : 2 * i + 2]
            middle_weights = jnp.concatenate([near for _, near, _ in pair], axis=0)
            middle_sums = jnp.dot(middle_weights, with_ones(middle(1, lanes)), preferred_element_type=jnp.float32)
            for a, (peak, _, edge) in enumerate(pair):
                summed = jnp.dot(edge, with_ones(halo(a, 1, lanes, 1)), preferred_element_type=jnp.float32)
                summed = summed + middle_sums[a * half : (a + 1) * half]
                total = summed[:, HD:]
                peaks[a] = jnp.where(mask, peak, peaks[a])
                totals[a] = jnp.where(mask, total, totals[a])
                for s in range(count):
                    rows = slice(s * SPOT, (s + 1) * SPOT)
                    result = summed[rows, :HD]
                    if s < sides:
                        result = result * corrected_reciprocal(total[rows])
                    else:
                        filled = jnp.broadcast_to(peak[rows] * EXP_SCALE, (SPOT, HD))
                        out_refs[s + 3][a * SPOT : (a + 1) * SPOT, lanes] = filled
                        out_refs[s][a * SPOT : (a + 1) * SPOT, lanes] = result
                    if s < sides:
                        start = (first + i) * 2 * SPOT + a * SPOT
                        out_refs[s][start : start + SPOT, :] = result.astype(jnp.bfloat16)
    for s in range(count):
        rows = slice(s * SPOT, (s + 1) * SPOT)
        peak = jnp.concatenate([value[rows] for value in peaks], axis=0) * EXP_SCALE
        total = jnp.concatenate([value[rows] for value in totals], axis=0)
        if s < sides:
            store_sums(out_refs[s], peak + jnp.log2(total))
        else:
            out_refs[s + 1][...] = peak
            out_refs[s + 2][...] = total


def near_attention(early, has_rows, own, top, bottom, third, visitors, queries, cost):
    tokens, features = own.shape[2:]
    operands = [own, top, bottom, *third, *visitors, *queries]
    payload = jax.ShapeDtypeStruct((HEADS * (tokens + 3), HD), jnp.bfloat16)
    outs = [payload for _ in visitors]
    for _ in queries:
        outs += [jax.ShapeDtypeStruct((tokens, lanes), jnp.float32) for lanes in (features, HD, HD, features)]
    in_vmem = pl.BlockSpec(memory_space=pltpu.VMEM)
    return pl.pallas_call(
        functools.partial(near_kernel, len(visitors), len(queries), early, has_rows),
        out_shape=outs,
        in_specs=[in_vmem] * len(operands),
        out_specs=[in_vmem] * len(outs),
        compiler_params=pltpu.CompilerParams(vmem_limit_bytes=VMEM_LIMIT),
        cost_estimate=kernel_cost(cost),
    )(*operands)


def far_kernel(members, far_ref, q_ref, core_ref, *refs):
    cross_ref, cross_inner_ref, corner, corner_inner = refs[0], refs[1], refs[2:4], refs[4:6]
    near_refs, (out_ref, peak_ref, total_ref, held, sems) = (refs[6:10], refs[10:14]), refs[14:]
    ta = lax.axis_index("ta")
    parity = ta % 2

    def tile_copy(source, tile, j, slot, group):
        lanes = pl.ds(group * GROUP * HD, GROUP * HD)
        target = held.at[:, tile, pl.ds(j * SPOT, SPOT), lanes]
        return pltpu.make_async_copy(source.at[:, :, lanes], target, sems.at[slot, group])

    for f in range(2):
        for a in range(2):
            rows = pl.ds(a * SPOT, SPOT)
            for j in range(NFAR):
                slot = (f * 2 + a) * NFAR + j
                wanted = far_ref[f, a, 0, j]
                owner, place = wanted // 2, wanted % 2
                inner = place != owner % 2
                is_core, is_cross = owner == ta + 1 - 2 * parity, owner == members - 1 - ta
                is_corner = jnp.logical_not(jnp.logical_or(is_core, is_cross))
                sources = [
                    (jnp.logical_and(is_core, place == 0), core_ref.at[:, 0, rows]),
                    (jnp.logical_and(is_core, place == 1), core_ref.at[:, 1, rows]),
                    (jnp.logical_and(is_cross, jnp.logical_not(inner)), cross_ref.at[:, rows]),
                    (jnp.logical_and(is_cross, inner), cross_inner_ref.at[:, rows]),
                    (jnp.logical_and(is_corner, jnp.logical_not(inner)), corner[a]),
                    (jnp.logical_and(is_corner, inner), corner_inner[a]),
                ]
                for chosen, source in sources:

                    @pl.when(chosen)
                    def _(source=source, f=f, a=a, j=j, slot=slot):
                        for group in range(HEADS // GROUP):
                            tile_copy(source, f * 2 + a, j, slot, group).start()

    units = [(early, a) for early in range(2) for a in range(2)]
    frames = (1 - parity, parity)
    collected = [(jnp.zeros((SPOT, HD), jnp.float32), jnp.zeros((SPOT, HD), jnp.float32)) for _ in units]
    for first in range(0, HEADS, GROUP):
        for slot in range(4 * NFAR):
            tile_copy(corner[1], slot // NFAR, slot % NFAR, slot, first // GROUP).wait()
        work = [(h, u) for h in range(first, first + GROUP) for u in range(len(units))]
        scores = []
        for h, u in work:
            early, a = units[u]
            frame, lanes = frames[early], slice(h * HD, (h + 1) * HD)
            queries = q_ref[frame, a * SPOT : (a + 1) * SPOT, lanes]
            scores.append(contract_last(queries, held[0, frame * 2 + a, :, lanes]))
        weights = []
        for (h, u), value in zip(work, scores):
            early, a = units[u]
            near_peak = near_refs[early][3][a * SPOT : (a + 1) * SPOT, h * HD : (h + 1) * HD]
            value = value * EXP_SCALE
            peak = jnp.maximum(jnp.max(value, axis=-1, keepdims=True), near_peak)
            weights.append((peak, jnp.exp2(near_peak - peak), jnp.exp2(value - peak).astype(jnp.bfloat16)))
        for (h, u), (peak, near_scale, weight) in zip(work, weights):
            early, a = units[u]
            frame, lanes, tokens = frames[early], slice(h * HD, (h + 1) * HD), slice(a * SPOT, (a + 1) * SPOT)
            values = with_ones(held[1, frame * 2 + a, :, lanes])
            summed = jnp.dot(weight, values, preferred_element_type=jnp.float32)
            total = summed[:, HD:]
            out_ref[early, tokens, lanes] = summed[:, :HD] + near_scale * near_refs[early][0][tokens, lanes]
            mask = lane_index(SPOT) == h
            collected[u] = jnp.where(mask, peak, collected[u][0]), jnp.where(mask, total, collected[u][1])
    for (early, a), (peak, total) in zip(units, collected):
        tokens = slice(a * SPOT, (a + 1) * SPOT)
        near_scale = jnp.exp2(near_refs[early][1][tokens, :] - peak)
        peak_ref[early, tokens, :] = peak
        total_ref[early, tokens, :] = total + near_scale * near_refs[early][2][tokens, :]


def far_attention(members, far_frames, queries, buffers, near):
    tokens, features = queries.shape[1:]
    in_vmem = pl.BlockSpec(memory_space=pltpu.VMEM)
    in_specs = [pl.BlockSpec(memory_space=pltpu.SMEM), in_vmem]
    in_specs += [pl.BlockSpec(memory_space=pl.ANY)] * len(buffers) + [in_vmem] * len(near)
    return pl.pallas_call(
        functools.partial(far_kernel, members),
        out_shape=[jax.ShapeDtypeStruct((2, tokens, lanes), jnp.float32) for lanes in (features, HD, HD)],
        in_specs=in_specs,
        out_specs=[in_vmem] * 3,
        scratch_shapes=[
            pltpu.VMEM((2, 4, NFAR * SPOT, features), jnp.bfloat16),
            pltpu.SemaphoreType.DMA((4 * NFAR, HEADS // GROUP)),
        ],
        compiler_params=pltpu.CompilerParams(vmem_limit_bytes=VMEM_LIMIT),
        cost_estimate=kernel_cost(1),
    )(far_frames, queries, *buffers, *near)


def frame_scales(sides, columns, at, own_refs, parts):
    _, own_peak_ref, own_total_ref = own_refs
    wa = lax.axis_index("wa")
    logs = [own_peak_ref[at]]
    for s in range(sides):
        value = load_sums(parts[s])
        if columns > 2:
            value = jnp.where(wa < columns - 1 if s == 0 else wa > 0, value, NEGATIVE)
        logs.append(value)
    top = functools.reduce(jnp.maximum, logs)
    scales = [jnp.exp2(value - top) for value in logs]
    total = functools.reduce(jnp.add, [scales[0] * own_total_ref[at]] + scales[1:])
    heads = lane_index(top.shape[0]) < HEADS
    return [split_sums(jnp.where(heads, value / total, 0.0)) for value in scales]


def joined_head(h, at, own_ref, parts, scales):
    row = lax.broadcasted_iota(jnp.int32, (HD, HD), 0)
    spread = jnp.where(jnp.logical_and(row % HEADS == h, row < 3 * HEADS), 1.0, 0.0).astype(jnp.bfloat16)
    lanes = slice(h * HD, (h + 1) * HD)
    factors = [jnp.dot(value, spread, preferred_element_type=jnp.float32) for value in scales]
    joined = factors[0] * own_ref[at, :, lanes]
    for factor, part in zip(factors[1:], parts):
        joined = joined + factor * part[h * 2 * SPOT : (h + 1) * 2 * SPOT, :].astype(jnp.float32)
    return joined.astype(jnp.bfloat16)


def finish_early_kernel(sides, columns, *refs):
    own_refs, parts, out_ref = refs[:3], refs[3 : 3 + sides], refs[-1]
    scales = frame_scales(sides, columns, 0, own_refs, parts)
    for h in range(HEADS):
        out_ref[:, h * HD : (h + 1) * HD] = joined_head(h, 0, own_refs[0], parts, scales)


def finish_late_kernel(sides, columns, *refs):
    own_refs, parts, (early_ref, out_ref, held, sems) = refs[:3], refs[3 : 3 + sides], refs[3 + sides :]
    parity = lax.axis_index("ta") % 2
    copies = [pltpu.make_async_copy(early_ref, out_ref.at[1 - parity], sems.at[0])]
    copies[0].start()
    scales = frame_scales(sides, columns, 1, own_refs, parts)
    for first in range(0, HEADS, GROUP):
        for h in range(first, first + GROUP):
            held[:, h * HD : (h + 1) * HD] = joined_head(h, 1, own_refs[0], parts, scales)
        lanes = pl.ds(first * HD, GROUP * HD)
        copy = pltpu.make_async_copy(held.at[:, lanes], out_ref.at[parity, :, lanes], sems.at[1 + first // GROUP])
        copy.start()
        copies.append(copy)
    for copy in copies:
        copy.wait()


def finish(columns, own, parts, early_out, cost):
    sides = len(parts)
    frames, tokens, features = own[0].shape
    in_vmem = pl.BlockSpec(memory_space=pltpu.VMEM)
    early = early_out is None
    operands = [*own, *parts] + ([] if early else [early_out])
    one_frame = (tokens, features)
    if early:
        kernel, out_shape, out_spec, scratch = finish_early_kernel, one_frame, in_vmem, []
    else:
        kernel, out_shape, out_spec = finish_late_kernel, (frames, *one_frame), pl.BlockSpec(memory_space=pl.ANY)
        scratch = [pltpu.VMEM(one_frame, jnp.bfloat16), pltpu.SemaphoreType.DMA((1 + HEADS // GROUP,))]
    return pl.pallas_call(
        functools.partial(kernel, sides, columns),
        out_shape=jax.ShapeDtypeStruct(out_shape, jnp.bfloat16),
        in_specs=[in_vmem] * len(operands),
        out_specs=out_spec,
        scratch_shapes=scratch,
        compiler_params=pltpu.CompilerParams(vmem_limit_bytes=VMEM_LIMIT),
        cost_estimate=kernel_cost(cost),
    )(*operands)


def per_device(queries, keyvals, far_frames):
    shape = queries.shape
    frames, rows, columns, features = shape
    tokens = rows * columns
    ta_size, ha_size, wa_size = lax.axis_size("ta"), lax.axis_size("ha"), lax.axis_size("wa")
    queries = queries.reshape(frames, tokens, features)
    keyvals = keyvals.reshape(2, frames, tokens, features)

    core_pairs = [(i, i ^ 1) for i in range(ta_size)]
    cross_pairs = [(i, ta_size - 1 - i) for i in range(ta_size)]
    up = [(i, i + 1) for i in range(ha_size - 1)]
    down = [(i + 1, i) for i in range(ha_size - 1)]
    if wa_size == 2:
        ways = [([(0, 1), (1, 0)], [(0, 1), (1, 0)])]
    else:
        right = [(i, i + 1) for i in range(wa_size - 1)]
        left = [(i + 1, i) for i in range(wa_size - 1)]
        ways = [(right, left), (left, right)]
    tie = lax.optimization_barrier

    core = lax.ppermute(keyvals, "ta", core_pairs)
    first_rows, last_rows, outer, inner = cut(keyvals)
    cross = lax.ppermute(outer, "ta", cross_pairs)
    bottom = lax.ppermute(first_rows, "ha", down)
    top = lax.ppermute(last_rows, "ha", up)
    sent, core = tie((queries, core))
    visitors = [lax.ppermute(sent, "wa", there) for there, _ in ways]
    cross_last, cross_first = widened_rows(cross)
    cross_top = lax.ppermute(cross_last, "ha", up)
    cross_bottom = lax.ppermute(cross_first, "ha", down)
    last = lax.ppermute(inner, "ta", cross_pairs)
    bottom, top = tie((bottom, top))
    inner_bottom, inner_top = inner_rows(bottom, top)
    core_bottom = lax.ppermute(inner_bottom, "ta", core_pairs)
    inner_top, visitors = tie((inner_top, visitors))
    core_top = lax.ppermute(inner_top, "ta", core_pairs)

    early_third = (core, core_top, core_bottom)
    early = near_attention(True, ha_size, keyvals, top, bottom, early_third, visitors, [], 1)
    early_parts = [lax.ppermute(result, "wa", back) for result, (_, back) in zip(early, ways)]
    core_top, _ = tie((core_top, early[0]))
    early_third = (core, core_top, core_bottom)
    early_home = near_attention(True, ha_size, keyvals, top, bottom, early_third, [], [queries], 1)
    cross_top, cross_bottom, _ = tie((cross_top, cross_bottom, early_home[1]))
    late_third = (cross, cross_top, cross_bottom)
    late = near_attention(False, ha_size, keyvals, top, bottom, late_third, visitors, [], 1)
    late_parts = [lax.ppermute(result, "wa", back) for result, (_, back) in zip(late, ways)]
    cross_top, last, _ = tie((cross_top, last, late[0]))
    late_third = (cross, cross_top, cross_bottom)
    late_home = near_attention(False, ha_size, keyvals, top, bottom, late_third, [], [queries], LATE_COST)
    inner_corner = [lax.ppermute(value, "ta", core_pairs) for value in reversed(widened_rows(last))]
    cross_first, _ = tie((cross_first, late[0]))
    corner_first = lax.ppermute(cross_first, "ta", core_pairs)
    sent, early_parts, _ = tie((cross, early_parts, late_home[1]))
    corner_last = lax.ppermute(last_rows_of(sent), "ta", core_pairs)
    buffers = (core, cross, last, corner_first, corner_last, *inner_corner)
    own = far_attention(ta_size, far_frames, queries, buffers, (*early_home, *late_home))
    out = finish(wa_size, own, early_parts, None, FINISH_COST)
    out = finish(wa_size, own, late_parts, out, 1)
    return out.reshape(shape)


def solution(mesh):
    placed = (P("ta", "ha", "wa", None), P(None, "ta", "ha", "wa", None), P("ta", "ha", "wa", None))
    return jax.shard_map(
        per_device, mesh=mesh, in_specs=placed, out_specs=P("ta", "ha", "wa", None), check_vma=False
    )
```
